32 devices in a mesh: seq: 8 (over z, x), head: 4 (over y, core).
Axes of the slice: x: 2, y: 2, z: 4, core: 2. Of those that a mesh axis runs over, the one named last changes fastest.
Arguments:
- tokens: bfloat16 [2, 4096, 1536], P(None, 'seq'), may hold values from -6 to 6
- norm_gain: float32 [1536], replicated, may hold values from 0.5 to 1.5
- gate_input_weight: bfloat16 [1536, 2, 3072], P(None, None, 'head'), may hold values from -0.15625 to 0.15625
- coefficient_weight: bfloat16 [1536, 2, 128], P(None, None, 'head'), may hold values from -0.15625 to 0.15625
- step_weight: bfloat16 [1536, 48], P(None, 'head'), may hold values from -0.15625 to 0.15625
- conv_x: float32 [4, 3072], P(None, 'head'), may hold values from -0.6 to 0.6
- conv_bc: float32 [4, 2, 128], P(None, None, 'head'), may hold values from -0.6 to 0.6
- conv_bias_x: float32 [3072], P('head'), may hold values from -0.5 to 0.5
- conv_bias_bc: float32 [2, 128], P(None, 'head'), may hold values from -0.5 to 0.5
- dt_bias: float32 [48], P('head'), may hold values from -3 to -1
- a_log: float32 [48], P('head'), as said below
- d_skip: float32 [48], P('head'), may hold values from 0.5 to 1.5
- gate_gain: float32 [3072], P('head'), may hold values from 0.5 to 1.5
- output_weight: bfloat16 [3072, 1536], P('head'), may hold values from -0.109375 to 0.109375
- cotangent: bfloat16 [2, 4096, 1536], P(None, 'seq'), may hold values from -6 to 6
Outputs:
- block_out: bfloat16 [2, 4096, 1536], P(None, 'seq', 'head')
- grad_input: float32 [2, 4096, 1536], P(None, 'seq', 'head')
- grad_norm_gain: float32 [1536], P('head')
- grad_gate_input_weight: float32 [1536, 2, 3072], P(None, None, 'head')
- grad_coefficient_weight: float32 [1536, 2, 128], P(None, None, 'head')
- grad_step_weight: float32 [1536, 48], P(None, 'head')
- grad_conv_x: float32 [4, 3072], P(None, 'head')
- grad_conv_bc: float32 [4, 2, 128], P(None, None, 'head')
- grad_conv_bias_x: float32 [3072], P('head')
- grad_conv_bias_bc: float32 [2, 128], P(None, 'head')
- grad_dt_bias: float32 [48], P('head')
- grad_a_log: float32 [48], P('head')
- grad_d_skip: float32 [48], P('head')
- grad_gate_gain: float32 [3072], P('head')
- grad_w_out: float32 [3072, 1536], P('head')
The draws below stay inside these ranges and needn't reach their ends.
Inputs may be any that keep to these rules, and one draw needn't show every extreme that they name: Each head's a_log lies between log(0.3 / 4096) and log(2).
All inputs are finite; a program needn't handle non-finite values.
Results may differ from the reference program's by a relative error of at most 0.0095.
The reference program's roundings to bfloat16 on the way count: a program that leaves them out, or rounds other values in their place, can miss the bound.
Values may be sent and summed in bfloat16 or wider, within the bound.
A program may use at most 192 MiB of HBM per device.

```python
import math
from functools import partial
import jax
import jax.numpy as jnp
from jax import lax

D = 1536
HEADS = 48
HEAD_DIM = 64
STATE = 128
KER = 4
GROUP = 256
SEQS = 2
LEN = 4096
INNER = 3072


def draw_a_log(key, part):
    key = jax.random.fold_in(key, 11)
    pick_key, fast_key, slow_key = jax.random.split(key, 3)
    quick_share = 0.5
    quick_heads = jax.random.uniform(pick_key, (HEADS,), jnp.float32) < quick_share
    fast_rate = jax.random.uniform(fast_key, (HEADS,), jnp.float32, math.log(0.4), math.log(2.0))
    slow_rate = jax.random.uniform(slow_key, (HEADS,), jnp.float32, math.log(0.3), math.log(1.5)) - math.log(LEN)
    return jnp.where(quick_heads, fast_rate, slow_rate).astype(jnp.float32)


def block_scale(rng, extent, shards, least, high):
    def one(dim, shards_of):
        heights = jax.random.uniform(jax.random.fold_in(jax.random.fold_in(rng, 6), dim), (shards_of,), jnp.float32, least / len(shards), high / len(shards))
        return jnp.repeat(jnp.exp(heights), extent[dim] // shards_of).reshape((-1,) + (1,) * (len(extent) - dim - 1))

    factor_of = one(*shards[0])
    for cut in shards[1:]:
        factor_of = factor_of * one(*cut)
    return factor_of


def centred(rng, dims, deviation, limit, cuts=(), held_as=jnp.bfloat16):
    array = jax.random.normal(rng, dims, jnp.float32) * deviation
    if len(cuts) > 0:
        array = block_scale(rng, dims, cuts, -0.22, 0.18) * array
    return jnp.clip(array, min=-limit, max=limit).astype(held_as)


def setup_inputs(seed: int = 0) -> dict:
    streams_of = jax.random.split(jax.random.key(seed), 16)
    return {
        "tokens": centred(streams_of[0], (SEQS, LEN, D), 1.0, 6.0, ((1, 8),)),
        "norm_gain": jnp.clip(1.0 + 0.1 * jax.random.normal(streams_of[1], (D,), jnp.float32), 0.5, 1.5),
        "gate_input_weight": centred(streams_of[2], (D, 2, INNER), D ** -0.5, 0.15625, ((2, 4),)),
        "coefficient_weight": centred(streams_of[3], (D, 2, STATE), D ** -0.5, 0.15625, ((2, 4),)),
        "step_weight": centred(streams_of[4], (D, HEADS), D ** -0.5, 0.15625, ((1, 4),)),
        "conv_x": jnp.clip(jax.random.uniform(streams_of[5], (KER, INNER), jnp.float32, -0.6, 0.6) * block_scale(streams_of[5], (KER, INNER), ((1, 4),), -0.4, 0.0), -0.6, 0.6),
        "conv_bc": jnp.clip(jax.random.uniform(streams_of[6], (KER, 2, STATE), jnp.float32, -0.6, 0.6) * block_scale(streams_of[6], (KER, 2, STATE), ((2, 4),), -0.4, 0.0), -0.6, 0.6),
        "conv_bias_x": jnp.clip(jax.random.uniform(streams_of[7], (INNER,), jnp.float32, -0.5, 0.5) * block_scale(streams_of[7], (INNER,), ((0, 4),), -0.4, 0.0), -0.5, 0.5),
        "conv_bias_bc": jnp.clip(jax.random.uniform(streams_of[8], (2, STATE), jnp.float32, -0.5, 0.5) * block_scale(streams_of[8], (2, STATE), ((1, 4),), -0.4, 0.0), -0.5, 0.5),
        "dt_bias": jnp.clip(-3.0 + 2.0 * jax.random.uniform(streams_of[9], (HEADS,), jnp.float32) ** block_scale(streams_of[9], (HEADS,), ((0, 4),), -0.2, 0.2), -3.0, -1.0),
        "a_log": draw_a_log(jax.random.fold_in(streams_of[15], 71), 0),
        "d_skip": jnp.clip(0.5 + 1.0 * jax.random.uniform(streams_of[11], (HEADS,), jnp.float32) ** block_scale(streams_of[11], (HEADS,), ((0, 4),), -0.2, 0.2), 0.5, 1.5),
        "gate_gain": jnp.clip(1.0 + 0.1 * jax.random.normal(streams_of[12], (INNER,), jnp.float32), 0.5, 1.5),
        "output_weight": centred(streams_of[13], (INNER, D), INNER ** -0.5, 0.109375, ((0, 4),)),
        "cotangent": centred(streams_of[14], (SEQS, LEN, D), 1.0, 6.0, ((1, 8),)),
    }


EPSILON = 1e-05
EXACT_PRECISION = lax.Precision.HIGHEST

@jax.custom_vjp
def low(v):
    return lax.optimization_barrier(v.astype(jnp.bfloat16)).astype(jnp.float32)

@jax.custom_vjp
def low_back(v):
    return v

def low_keep(v):
    return (low(v), None)

def low_pass(kept, grad):
    return (grad,)

def back_keep(v):
    return (v, None)

def back_low(kept, grad):
    return (low(grad),)
low.defvjp(low_keep, low_pass)
low_back.defvjp(back_keep, back_low)

def silu_value(array_in):
    return array_in * jax.nn.sigmoid(array_in)

def group_step(carry_state, pieces):
    x_heads, b_rows, c_rows, log_decay, step_size = pieces
    cum_decay = jnp.cumsum(log_decay, axis=1)
    position = jnp.arange(log_decay.shape[1])
    lower_mask = (position[:, None] >= position[None, :])[None, :, :, None]
    gap_decay = cum_decay[:, :, None, :] - cum_decay[:, None, :, :]
    decay_mask = jnp.where(lower_mask, jnp.exp(jnp.where(lower_mask, gap_decay, 0.0)), 0.0)
    scores = jnp.einsum('sqn,skn->sqk', c_rows, b_rows, precision=EXACT_PRECISION)
    mixing = scores[:, :, :, None] * decay_mask * step_size[:, None, :, :]
    within = jnp.einsum('sqkh,skhp->sqhp', mixing, x_heads, precision=EXACT_PRECISION)
    carried = jnp.einsum('sqn,shpn->sqhp', c_rows, carry_state, precision=EXACT_PRECISION) * jnp.exp(cum_decay)[:, :, :, None]
    tail_weight = jnp.exp(cum_decay[:, -1:, :] - cum_decay) * step_size
    weighted = x_heads * tail_weight[:, :, :, None]
    fresh_state = jnp.einsum('skhp,skn->shpn', weighted, b_rows, precision=EXACT_PRECISION)
    new_state = jnp.exp(cum_decay[:, -1, :])[:, :, None, None] * carry_state + fresh_state
    return (new_state, within + carried)

def ssd_scan(x_heads, b_rows, c_rows, log_decay, step_size, carry_state):
    seq_count, block_len = (log_decay.shape[0], log_decay.shape[1])
    group_count = block_len // GROUP

    def grouped(array_in):
        return jnp.moveaxis(array_in.reshape((seq_count, group_count, GROUP) + array_in.shape[2:]), 1, 0)
    final_state, outputs = lax.scan(jax.checkpoint(group_step), carry_state, (grouped(x_heads), grouped(b_rows), grouped(c_rows), grouped(log_decay), grouped(step_size)))
    return (jnp.moveaxis(outputs, 0, 1).reshape(x_heads.shape), final_state)

def segment_step(params, carry, input_batch):
    norm_gain, gate_input_weight, coefficient_weight, step_weight, conv_x, conv_bc, conv_bias_x, conv_bias_bc, dt_bias, a_log, d_skip, gate_gain, output_weight = params
    tail_rows, carry_state = carry
    seq_count, block_len = (input_batch.shape[0], input_batch.shape[1])
    row_scale = lax.rsqrt(lax.optimization_barrier(jnp.mean(input_batch * input_batch, axis=-1, keepdims=True)) + EPSILON)
    normalized_input = low(input_batch * row_scale * norm_gain)
    gate_input_projected = low_back(jnp.einsum('rhp,pkw->rhkw', normalized_input, gate_input_weight, precision=EXACT_PRECISION))
    coefficient_projected = low_back(jnp.einsum('jxp,pyh->jxyh', normalized_input, coefficient_weight, precision=EXACT_PRECISION))
    step_unactivated = low_back(jnp.einsum('ajn,ng->ajg', normalized_input, step_weight, precision=EXACT_PRECISION))
    gate_pre = gate_input_projected[:, :, 0]
    conv_input = jnp.concatenate([gate_input_projected[:, :, 1], coefficient_projected.reshape(seq_count, block_len, 2 * STATE)], axis=-1)
    conv_taps = jnp.concatenate([conv_x, conv_bc.reshape(KER, 2 * STATE)], axis=-1)
    biases = jnp.concatenate([conv_bias_x, conv_bias_bc.reshape(2 * STATE)])
    extended = jnp.concatenate([tail_rows, conv_input], axis=1)
    conv_out = biases
    for tap_index in range(KER):
        conv_out = conv_out + conv_taps[tap_index] * extended[:, tap_index:tap_index + block_len]
    activated = low(silu_value(conv_out))
    x_heads = activated[:, :, :INNER].reshape(seq_count, block_len, HEADS, HEAD_DIM)
    b_rows = activated[:, :, INNER:INNER + STATE]
    c_rows = activated[:, :, INNER + STATE:]
    step_size = jax.nn.softplus(step_unactivated + dt_bias)
    log_decay = -jnp.exp(a_log) * step_size
    ssd_out, carry_state = ssd_scan(x_heads, b_rows, c_rows, log_decay, step_size, carry_state)
    ssd_out = ssd_out + d_skip[:, None] * x_heads
    gated = ssd_out.reshape(seq_count, block_len, INNER) * silu_value(gate_pre)
    gate_scale = lax.rsqrt(lax.optimization_barrier(jnp.mean(gated * gated, axis=-1, keepdims=True)) + EPSILON)
    normalized_gate_result = low(gated * gate_scale * gate_gain)
    residual_output = input_batch + jnp.einsum('qwy,yk->qwk', normalized_gate_result, output_weight, precision=EXACT_PRECISION)
    return ((extended[:, block_len:], carry_state), residual_output)

def forward(input_batch, *params):
    segment_len = min(1024, LEN)
    segment_count = LEN // segment_len
    pieces = jnp.moveaxis(input_batch.reshape(SEQS, segment_count, segment_len, D), 1, 0)
    initial = (jnp.zeros((SEQS, KER - 1, INNER + 2 * STATE), jnp.float32), jnp.zeros((SEQS, HEADS, HEAD_DIM, STATE), jnp.float32))
    _, outputs = lax.scan(jax.checkpoint(partial(segment_step, params)), initial, pieces)
    return jnp.moveaxis(outputs, 0, 1).reshape(SEQS, LEN, D)

def reference(tokens, norm_gain, gate_input_weight, coefficient_weight, step_weight, conv_x, conv_bc, conv_bias_x, conv_bias_bc, dt_bias, a_log, d_skip, gate_gain, output_weight, cotangent):
    params = tuple((array_in.astype(jnp.float32) for array_in in (norm_gain, gate_input_weight, coefficient_weight, step_weight, conv_x, conv_bc, conv_bias_x, conv_bias_bc, dt_bias, a_log, d_skip, gate_gain, output_weight)))
    residual_output, pull_back = jax.vjp(forward, tokens.astype(jnp.float32), *params)
    gradients = pull_back(cotangent.astype(jnp.float32))
    return (residual_output.astype(jnp.bfloat16), gradients[0], gradients[1], gradients[2], gradients[3], gradients[4], gradients[5], gradients[6], gradients[7], gradients[8], gradients[9], gradients[10], gradients[11], gradients[12], gradients[13])
```

```python
import functools

import jax
import jax.numpy as jnp
from jax import lax
from jax.experimental import pallas as pl
from jax.experimental.pallas import tpu as pltpu
from jax.sharding import PartitionSpec as P

KER = 4
GROUP = 256


EPSILON = 1e-05
EXACT_PRECISION = lax.Precision.HIGHEST


def from_behind(x, axis, by):
    length = lax.axis_size(axis)
    pairs = [(i, i + by) for i in range(length) if 0 <= i + by < length]
    return lax.ppermute(x, axis, pairs)


def prefix(part, axis, combine, identity, reverse):
    count = lax.axis_size(axis)
    place = lax.axis_index(axis)
    ahead = count - 1 - place if reverse else place
    gathered = jax.tree.map(lambda a: lax.all_gather(a, axis), part)
    state = jax.tree.map(lambda a, e: jnp.zeros_like(a) + jnp.asarray(e, a.dtype), part, identity)

    def one(step, state):
        source = count - 1 - step if reverse else step
        return combine(
            state, jax.tree.map(lambda a: lax.dynamic_index_in_dim(a, source, 0, False), gathered)
        )

    return lax.fori_loop(0, ahead, one, state)


def silu_value(array_in):
    return array_in * jax.nn.sigmoid(array_in)


def silu_slope(array_in):
    sigma_value = jax.nn.sigmoid(array_in)
    return sigma_value * (1.0 + array_in * (1.0 - sigma_value))


def group_step(carry_state, pieces):
    x_heads, b_rows, c_rows, log_decay, step_size = pieces
    cum_decay = jnp.cumsum(log_decay, axis=1)
    position = jnp.arange(log_decay.shape[1])
    lower_mask = (position[:, None] >= position[None, :])[None, :, :, None]
    gap_decay = cum_decay[:, :, None, :] - cum_decay[:, None, :, :]
    decay_mask = jnp.where(lower_mask, jnp.exp(jnp.where(lower_mask, gap_decay, 0.0)), 0.0)
    scores = jnp.einsum("sqn,skn->sqk", c_rows, b_rows, precision=EXACT_PRECISION)
    mixing = scores[:, :, :, None] * decay_mask * step_size[:, None, :, :]
    within = jnp.einsum("sqkh,skhp->sqhp", mixing, x_heads, precision=EXACT_PRECISION)
    carried = (
        jnp.einsum("sqn,shpn->sqhp", c_rows, carry_state, precision=EXACT_PRECISION)
        * jnp.exp(cum_decay)[:, :, :, None]
    )
    tail_weight = jnp.exp(cum_decay[:, -1:, :] - cum_decay) * step_size
    weighted = x_heads * tail_weight[:, :, :, None]
    fresh_state = jnp.einsum("skhp,skn->shpn", weighted, b_rows, precision=EXACT_PRECISION)
    new_state = jnp.exp(cum_decay[:, -1, :])[:, :, None, None] * carry_state + fresh_state
    return (new_state, within + carried)


def ssd_scan(x_heads, b_rows, c_rows, log_decay, step_size, carry_state):
    seq_count, block_len = (log_decay.shape[0], log_decay.shape[1])
    group_count = block_len // GROUP

    def grouped(array_in):
        return jnp.moveaxis(
            array_in.reshape((seq_count, group_count, GROUP) + array_in.shape[2:]), 1, 0
        )

    final_state, outputs = lax.scan(
        jax.checkpoint(group_step),
        carry_state,
        (
            grouped(x_heads),
            grouped(b_rows),
            grouped(c_rows),
            grouped(log_decay),
            grouped(step_size),
        ),
    )
    return (jnp.moveaxis(outputs, 0, 1).reshape(x_heads.shape), final_state)


def linked(earlier, later):
    return (earlier[0] * later[0], later[1] + later[0][:, :, None, None] * earlier[1])

MESH = pl.DeviceIdType.MESH


def ring_place(count):
    place = lax.axis_index("seq")
    row, col = place // 2, place % 2
    return jnp.where(col == 0, row, count - 1 - row)


def ring_device(rank, count):
    return jnp.where(rank < count // 2, 2 * rank, 2 * (count - 1 - rank) + 1)


def ring_kernel(count, plan, *refs):
    n_lhs = 1 + max(p[0] for p in plan)
    n_rhs = 1 + max(p[1] for p in plan)
    streams = len(plan)
    lhs, refs = refs[:n_lhs], refs[n_lhs:]
    rhs, refs = refs[:n_rhs], refs[n_rhs:]
    small_ref, refs = refs[0], refs[1:]
    outs, refs = refs[:streams], refs[streams:]
    small_out, refs = refs[0], refs[1:]
    bufs, refs = refs[:streams], refs[streams:]
    small_buf, rs_send, rs_recv, ag_send, ag_recv, sm_send, sm_recv = refs
    head = lax.axis_index("head")
    place = lax.axis_index("seq")
    rank = ring_place(count)
    peers = {
        1: (ring_device(lax.rem(rank + 1, count), count), head),
        -1: (ring_device(lax.rem(rank + count - 1, count), count), head),
    }
    barrier = pltpu.get_barrier_semaphore()

    def greet(i, _):
        other = lax.rem(place + i, count)
        pl.semaphore_signal(barrier, inc=1, device_id=(other, head), device_id_type=MESH)
        return 0

    lax.fori_loop(1, count, greet, 0)
    pl.semaphore_wait(barrier, count - 1)

    small_buf[place] = small_ref[...]

    def small_copy(i):
        other = lax.rem(place + i, count)
        return pltpu.make_async_remote_copy(
            src_ref=small_ref,
            dst_ref=small_buf.at[place],
            send_sem=sm_send.at[i],
            recv_sem=sm_recv.at[i],
            device_id=(other, head),
            device_id_type=MESH,
        )

    def small_start(i, _):
        small_copy(i).start()
        return 0

    lax.fori_loop(1, count, small_start, 0)

    def chunk_of(direction, step):
        return lax.rem(rank - direction * step + 2 * count, count)

    def partial(i, chunk):
        l, r, first, cols, _ = plan[i]
        rows = lhs[l].shape[0] // count
        left = lhs[l][pl.ds(pl.multiple_of(chunk * rows, rows), rows), :]
        return jnp.dot(left, rhs[r][:, first : first + cols], preferred_element_type=jnp.float32)

    def rs_copy(i, step):
        return pltpu.make_async_remote_copy(
            src_ref=bufs[i].at[step],
            dst_ref=bufs[i].at[step + 1],
            send_sem=rs_send.at[i, step],
            recv_sem=rs_recv.at[i, step],
            device_id=peers[plan[i][4]],
            device_id_type=MESH,
        )

    def ag_copy(i, step):
        rows = bufs[i].shape[1]
        chunk = chunk_of(plan[i][4], step - 1)
        block = outs[i].at[pl.ds(pl.multiple_of(chunk * rows, rows), rows)]
        return pltpu.make_async_remote_copy(
            src_ref=block,
            dst_ref=block,
            send_sem=ag_send.at[i, step],
            recv_sem=ag_recv.at[i, step],
            device_id=peers[plan[i][4]],
            device_id_type=MESH,
        )

    for i in range(streams):
        bufs[i][0] = partial(i, chunk_of(plan[i][4], 0)).astype(jnp.bfloat16)
        rs_copy(i, 0).start()

    def rs_step(step, _):
        for i in range(streams):
            own = partial(i, chunk_of(plan[i][4], step))
            rs_copy(i, step - 1).wait_recv()
            bufs[i][step] = (own + bufs[i][step].astype(jnp.float32)).astype(jnp.bfloat16)
            rs_copy(i, step).start()
        return 0

    lax.fori_loop(1, count - 1, rs_step, 0)
    for i in range(streams):
        chunk = chunk_of(plan[i][4], count - 1)
        rows = bufs[i].shape[1]
        own = partial(i, chunk)
        rs_copy(i, count - 2).wait_recv()
        done = (own + bufs[i][count - 1].astype(jnp.float32)).astype(jnp.bfloat16)
        outs[i][pl.ds(pl.multiple_of(chunk * rows, rows), rows), :] = done
        ag_copy(i, 0).start()

    def ag_step(step, _):
        for i in range(streams):
            ag_copy(i, step - 1).wait_recv()
            ag_copy(i, step).start()
        return 0

    lax.fori_loop(1, count - 1, ag_step, 0)
    for i in range(streams):
        ag_copy(i, count - 2).wait_recv()

    def small_wait(i, _):
        small_copy(i).wait()
        return 0

    lax.fori_loop(1, count, small_wait, 0)
    total = small_buf[0]
    for i in range(1, count):
        total = total + small_buf[i]
    small_out[...] = total

    def drain(step, _):
        for i in range(streams):
            rs_copy(i, step).wait_send()
            ag_copy(i, step).wait_send()
        return 0

    lax.fori_loop(0, count - 1, drain, 0)


def ring_sum(count, plan, lhs, rhs, small):
    rows = [lhs[p[0]].shape[0] for p in plan]
    vmem = pl.BlockSpec(memory_space=pltpu.VMEM)
    streams = len(plan)
    sems = pltpu.SemaphoreType.DMA((streams, count))
    return pl.pallas_call(
        functools.partial(ring_kernel, count, plan),
        out_shape=[jax.ShapeDtypeStruct((r, p[3]), jnp.bfloat16) for r, p in zip(rows, plan)]
        + [jax.ShapeDtypeStruct(small.shape, jnp.float32)],
        in_specs=[vmem] * (len(lhs) + len(rhs) + 1),
        out_specs=[vmem] * (streams + 1),
        scratch_shapes=[
            pltpu.VMEM((count, r // count, p[3]), jnp.bfloat16) for r, p in zip(rows, plan)
        ]
        + [
            pltpu.VMEM((count,) + small.shape, jnp.float32),
            sems,
            sems,
            sems,
            sems,
            pltpu.SemaphoreType.DMA((count,)),
            pltpu.SemaphoreType.DMA((count,)),
        ],
        compiler_params=pltpu.CompilerParams(
            collective_id=1, has_side_effects=True, vmem_limit_bytes=56 * 2**20
        ),
        name="weight_ring",
    )(*lhs, *rhs, small)


def body(
    tokens,
    norm_gain,
    gate_input_weight,
    coefficient_weight,
    step_weight,
    conv_x,
    conv_bc,
    conv_bias_x,
    conv_bias_bc,
    dt_bias,
    a_log,
    d_skip,
    gate_gain,
    output_weight,
    cotangent,
):
    seq_count, block_len, width = tokens.shape
    inner_len = gate_input_weight.shape[2]
    state_part = coefficient_weight.shape[2]
    head_count = step_weight.shape[1]
    head_dim = inner_len // head_count
    head_parts = lax.axis_size("head")
    my_head = lax.axis_index("head")
    col_count = width // head_parts
    state_full = state_part * head_parts
    edge_len = KER - 1
    input_batch = tokens.astype(jnp.float32)
    row_scale = lax.rsqrt(jnp.mean(input_batch * input_batch, axis=-1, keepdims=True) + EPSILON)
    unit_rows = input_batch * row_scale
    normalized_input = (unit_rows * norm_gain).astype(jnp.bfloat16)
    gate_input_projected = jnp.einsum(
        "rhp,pkw->rhkw", normalized_input, gate_input_weight, preferred_element_type=jnp.float32
    )
    coefficient_projected = jnp.einsum(
        "jxp,pyh->jxyh", normalized_input, coefficient_weight, preferred_element_type=jnp.float32
    )
    step_unactivated = jnp.einsum(
        "ajn,ng->ajg", normalized_input, step_weight, preferred_element_type=jnp.float32
    )
    gate_pre = gate_input_projected[:, :, 0]
    conv_input = jnp.concatenate(
        [
            gate_input_projected[:, :, 1],
            coefficient_projected.reshape(seq_count, block_len, 2 * state_part),
        ],
        axis=-1,
    )
    conv_taps = jnp.concatenate([conv_x, conv_bc.reshape(KER, 2 * state_part)], axis=-1)
    biases = jnp.concatenate([conv_bias_x, conv_bias_bc.reshape(2 * state_part)])
    edge_rows = from_behind(conv_input[:, block_len - edge_len :], "seq", 1)
    extended = jnp.concatenate([edge_rows, conv_input], axis=1)
    conv_out = biases
    for tap_index in range(KER):
        conv_out = conv_out + conv_taps[tap_index] * extended[:, tap_index : tap_index + block_len]
    activated = silu_value(conv_out).astype(jnp.bfloat16)
    bc_local = activated[:, :, inner_len:].reshape(seq_count, block_len, 2, state_part)
    bc_whole = lax.all_gather(bc_local, "head", axis=3, tiled=True).astype(jnp.float32)
    b_rows = bc_whole[:, :, 0]
    c_rows = bc_whole[:, :, 1]
    x_heads = (
        activated[:, :, :inner_len]
        .astype(jnp.float32)
        .reshape(seq_count, block_len, head_count, head_dim)
    )
    dt_input = step_unactivated + dt_bias
    step_size = jax.nn.softplus(dt_input)
    decay_speed = jnp.exp(a_log)
    log_decay = -decay_speed * step_size
    zero_state = jnp.zeros((seq_count, head_count, head_dim, state_full), jnp.float32)
    local_out, local_state = ssd_scan(x_heads, b_rows, c_rows, log_decay, step_size, zero_state)
    block_cum = jnp.cumsum(log_decay, axis=1)
    block_logs = block_cum[:, -1]
    block_decay = jnp.exp(block_logs)
    no_decay = jnp.ones_like(block_decay)
    incoming = prefix((block_decay, local_state), "seq", linked, (no_decay, zero_state), False)[1]
    decay_rows = jnp.exp(block_cum)[:, :, :, None]
    ssd_out = (
        local_out
        + jnp.einsum("sln,shpn->slhp", c_rows, incoming, precision=EXACT_PRECISION) * decay_rows
        + d_skip[:, None] * x_heads
    )
    ssd_flat = ssd_out.reshape(seq_count, block_len, inner_len)
    gate_act = silu_value(gate_pre)
    gated = ssd_flat * gate_act
    square_sum = lax.psum(jnp.sum(gated * gated, axis=-1), "head")
    gate_scale = lax.rsqrt(square_sum / (inner_len * head_parts) + EPSILON)[:, :, None]
    scaled_gate = gated * gate_scale
    normalized_gate_result = (scaled_gate * gate_gain).astype(jnp.bfloat16)
    mixer_result = jnp.einsum(
        "qwy,yk->qwk", normalized_gate_result, output_weight, preferred_element_type=jnp.float32
    )
    mixed = lax.psum_scatter(
        mixer_result.astype(jnp.bfloat16), "head", scatter_dimension=2, tiled=True
    ).astype(jnp.float32)
    own_inputs = lax.dynamic_slice_in_dim(input_batch, my_head * col_count, col_count, 2)
    block_out = (own_inputs + mixed).astype(jnp.bfloat16)
    grad_normalized_gate = jnp.einsum(
        "erz,qz->erq", cotangent, output_weight, preferred_element_type=jnp.float32
    )
    grad_gate_gain = jnp.sum(grad_normalized_gate * scaled_gate, axis=(0, 1))
    d_scaled = grad_normalized_gate * gate_gain
    cross_sum = lax.psum(jnp.sum(d_scaled * gated, axis=-1), "head")
    d_gated = (
        gate_scale * d_scaled
        - gated * gate_scale**3 * (cross_sum / (inner_len * head_parts))[:, :, None]
    )
    d_flat = d_gated * gate_act
    d_gate = (d_gated * ssd_flat * silu_slope(gate_pre)).astype(jnp.bfloat16)
    d_ssd = d_flat.reshape(seq_count, block_len, head_count, head_dim)
    grad_d_skip = jnp.sum(d_ssd * x_heads, axis=(0, 1, 3))
    d_entering = jnp.einsum("slhp,sln->shpn", d_ssd * decay_rows, c_rows, precision=EXACT_PRECISION)
    leaving = prefix((block_decay, d_entering), "seq", linked, (no_decay, zero_state), True)[1]
    _, pull_back = jax.vjp(ssd_scan, x_heads, b_rows, c_rows, log_decay, step_size, incoming)
    d_x_heads, d_b_rows, d_c_rows, d_log_decay, d_step, _ = pull_back((d_ssd, leaving))
    grad_a_log = jnp.sum(d_log_decay * log_decay, axis=(0, 1))
    d_step_all = d_step - decay_speed * d_log_decay
    d_dt_input = d_step_all * jax.nn.sigmoid(dt_input)
    grad_dt_bias = jnp.sum(d_dt_input, axis=(0, 1))
    grad_step_unactivated = d_dt_input.astype(jnp.bfloat16)
    d_bc_whole = jnp.stack([d_b_rows, d_c_rows], axis=2)
    d_bc_local = lax.psum_scatter(d_bc_whole, "head", scatter_dimension=3, tiled=True)
    d_x_total = (d_x_heads + d_skip[:, None] * d_ssd).reshape(seq_count, block_len, inner_len)
    d_activated = jnp.concatenate(
        [d_x_total, d_bc_local.reshape(seq_count, block_len, 2 * state_part)], axis=-1
    )
    d_conv = d_activated * silu_slope(conv_out)
    grad_taps = jnp.stack(
        [
            jnp.sum(d_conv * extended[:, tap_index : tap_index + block_len], axis=(0, 1))
            for tap_index in range(KER)
        ]
    )
    grad_biases = jnp.sum(d_conv, axis=(0, 1))
    d_extended = jnp.pad(conv_taps[0] * d_conv, ((0, 0), (0, edge_len), (0, 0)))
    for tap_index in range(1, KER):
        d_extended = d_extended + jnp.pad(
            conv_taps[tap_index] * d_conv, ((0, 0), (tap_index, edge_len - tap_index), (0, 0))
        )
    spill_rows = from_behind(d_extended[:, :edge_len], "seq", -1)
    d_input = (
        d_extended[:, edge_len:] + jnp.pad(spill_rows, ((0, 0), (block_len - edge_len, 0), (0, 0)))
    ).astype(jnp.bfloat16)
    grad_gate_input_projected = jnp.stack([d_gate, d_input[:, :, :inner_len]], axis=2)
    grad_coefficient_projected = d_input[:, :, inner_len:].reshape(
        seq_count, block_len, 2, state_part
    )
    grad_normalized = jnp.einsum(
        "ygtz,jtz->ygj",
        grad_gate_input_projected,
        gate_input_weight,
        preferred_element_type=jnp.float32,
    )
    grad_normalized = grad_normalized + jnp.einsum(
        "yrze,tze->yrt",
        grad_coefficient_projected,
        coefficient_weight,
        preferred_element_type=jnp.float32,
    )
    grad_normalized = grad_normalized + jnp.einsum(
        "yjw,zw->yjz", grad_step_unactivated, step_weight, preferred_element_type=jnp.float32
    )
    own_cotangent = lax.dynamic_slice_in_dim(cotangent, my_head * col_count, col_count, 2).astype(
        jnp.float32
    )
    own_units = lax.dynamic_slice_in_dim(unit_rows, my_head * col_count, col_count, 2)
    d_own = lax.psum_scatter(
        grad_normalized.astype(jnp.bfloat16), "head", scatter_dimension=2, tiled=True
    ).astype(jnp.float32)
    own_gain = lax.dynamic_slice_in_dim(norm_gain, my_head * col_count, col_count, 0)
    grad_norm_gain = jnp.sum(d_own * own_units, axis=(0, 1))
    d_units = d_own * own_gain
    row_sum = lax.psum(jnp.sum(d_units * own_inputs, axis=-1), "head")
    grad_input = (
        row_scale * d_units
        - own_inputs * row_scale**3 * (row_sum / width)[:, :, None]
        + own_cotangent
    )
    count = lax.axis_size("seq")
    rows = seq_count * block_len

    def padded(array_in):
        parts = count * 16
        return jnp.pad(array_in, ((0, -array_in.shape[0] % parts), (0, 0)))

    normed_t = padded(normalized_input.reshape(rows, width).T)
    gate_t = padded(normalized_gate_result.reshape(rows, inner_len).T)
    cot = cotangent.reshape(rows, width)
    d_gate2 = d_gate.reshape(rows, inner_len)
    narrow = jnp.concatenate(
        [
            d_input.reshape(rows, -1),
            grad_step_unactivated.reshape(rows, head_count),
        ],
        axis=1,
    )
    wide = -(-narrow.shape[1] // 128) * 128
    narrow = jnp.pad(narrow, ((0, 0), (0, wide - narrow.shape[1])))
    half, ihalf = width // 2, inner_len // 2
    plan = (
        (0, 0, 0, half, 1),
        (0, 0, half, half, -1),
        (1, 1, 0, ihalf, 1),
        (1, 1, ihalf, ihalf, -1),
        (1, 2, 0, ihalf, 1),
        (1, 2, ihalf, wide - ihalf, -1),
    )
    smalls = [
        grad_taps.reshape(-1),
        grad_biases,
        grad_dt_bias,
        grad_a_log,
        grad_d_skip,
        grad_gate_gain,
        grad_norm_gain,
    ]
    sizes = [a.shape[0] for a in smalls]
    flat = jnp.concatenate(smalls)
    lanes = -(-flat.shape[0] // 1024) * 8
    flat = jnp.pad(flat, (0, lanes * 128 - flat.shape[0])).reshape(lanes, 128)
    *sums, flat = ring_sum(count, plan, (gate_t, normed_t), (cot, d_gate2, narrow), flat)
    flat = flat.reshape(-1)
    cuts = []
    start = 0
    for size in sizes:
        cuts.append(flat[start : start + size])
        start += size
    taps, bias, g_dt, g_a, g_skip, g_gain, g_norm = cuts
    taps = taps.reshape(KER, -1)
    sums = [a.astype(jnp.float32) for a in sums]
    g_w_out = jnp.concatenate(sums[:2], axis=1)[:inner_len]
    g_gate = jnp.concatenate(sums[2:4], axis=1)[:width]
    g_narrow = jnp.concatenate(sums[4:], axis=1)[:width]
    g_in = jnp.stack([g_gate, g_narrow[:, :inner_len]], axis=1)
    split = inner_len + 2 * state_part
    g_coef = g_narrow[:, inner_len:split].reshape(width, 2, state_part)
    g_step = g_narrow[:, split : split + head_count]
    return (
        block_out,
        grad_input,
        g_norm,
        g_in,
        g_coef,
        g_step,
        taps[:, :inner_len],
        taps[:, inner_len:].reshape(KER, 2, state_part),
        bias[:inner_len],
        bias[inner_len:].reshape(2, state_part),
        g_dt,
        g_a,
        g_skip,
        g_gain,
        g_w_out,
    )


def solution(mesh):
    placed = (
        P(None, "seq", None),
        P(),
        P(None, None, "head"),
        P(None, None, "head"),
        P(None, "head"),
        P(None, "head"),
        P(None, None, "head"),
        P("head"),
        P(None, "head"),
        P("head"),
        P("head"),
        P("head"),
        P("head"),
        P("head", None),
        P(None, "seq", None),
    )
    return jax.shard_map(
        body,
        mesh=mesh,
        in_specs=placed,
        out_specs=(
            P(None, "seq", "head"),
            P(None, "seq", "head"),
            P("head"),
            P(None, None, "head"),
            P(None, None, "head"),
            P(None, "head"),
            P(None, "head"),
            P(None, None, "head"),
            P("head"),
            P(None, "head"),
            P("head"),
            P("head"),
            P("head"),
            P("head"),
            P("head", None),
        ),
        check_vma=False,
    )
```

```python
import functools

import jax
import jax.numpy as jnp
from jax import lax
from jax.experimental import pallas as pl
from jax.experimental.pallas import tpu as pltpu
from jax.sharding import PartitionSpec as P

KER = 4
EPSILON = 1e-05
CHUNK = 128
LANES = 128
MESH = pl.DeviceIdType.MESH
F32 = jnp.float32
BF16 = jnp.bfloat16
EXACT = lax.Precision.HIGHEST
VMEM_LIMIT = 60 * 2**20
NN = ((1,), (0,))
NT = ((1,), (1,))
TN = ((0,), (0,))


def mul(left, right, how, precision=None):
    return lax.dot_general(
        left, right, (how, ((), ())), precision=precision, preferred_element_type=F32
    )


def sigmoid(v):
    return 0.5 * jnp.tanh(0.5 * v) + 0.5


def softplus(v):
    e = jnp.exp(-jnp.abs(v))
    u = 1.0 + e
    near = u - 1.0
    log1p = jnp.where(near == 0.0, e, jnp.log(u) * (e / jnp.where(near == 0.0, 1.0, near)))
    return jnp.maximum(v, 0.0) + log1p


def iota(shape, dim):
    return lax.broadcasted_iota(jnp.int32, shape, dim)


def ds(start, size):
    return pl.ds(pl.multiple_of(start, size), size)


def pair_of(values, pair):
    low = values[:, 2 * pair : 2 * pair + 1]
    high = values[:, 2 * pair + 1 : 2 * pair + 2]
    return jnp.where(iota((values.shape[0], LANES), 1) < LANES // 2, low, high)


def spread(values, pairs):
    return jnp.concatenate([pair_of(values, p) for p in range(pairs)], axis=1)


def eights(v):
    return jnp.sum(v.reshape(v.shape[0] // 8, 8, v.shape[1]), axis=0)


def halves_of(v):
    high = v.astype(BF16)
    return high, (v - high.astype(F32)).astype(BF16)


def head_sums(v, gather):
    high, low = halves_of(v)
    return mul(high, gather, NN) + mul(low, gather, NN)


def remote(src, dst, send, recv, place, head):
    return pltpu.make_async_remote_copy(
        src_ref=src,
        dst_ref=dst,
        send_sem=send,
        recv_sem=recv,
        device_id=(place, head),
        device_id_type=MESH,
    )


def meet(count, parts):
    place, head = lax.axis_index("seq"), lax.axis_index("head")
    barrier = pltpu.get_barrier_semaphore()

    def along_seq(i, _):
        other = lax.rem(place + i, count)
        pl.semaphore_signal(barrier, inc=1, device_id=(other, head), device_id_type=MESH)
        return 0

    def along_head(i, _):
        other = lax.rem(head + i, parts)
        pl.semaphore_signal(barrier, inc=1, device_id=(place, other), device_id_type=MESH)
        return 0

    lax.fori_loop(1, count, along_seq, 0)
    lax.fori_loop(1, parts, along_head, 0)
    pl.semaphore_wait(barrier, count - 1 + parts - 1)


def loop(low, high, step):
    def one(i, _):
        step(i)
        return 0

    lax.fori_loop(low, high, one, 0)


def line_copy(count, src, dst, send, recv):
    place, head = lax.axis_index("seq"), lax.axis_index("head")

    def copy(i):
        other = lax.rem(place + i, count)
        return remote(src(other), dst(place), send.at[i], recv.at[i], other, head)

    return copy


def head_copy(parts, src, dst, send, recv):
    place, head = lax.axis_index("seq"), lax.axis_index("head")

    def copy(i):
        other = lax.rem(head + i, parts)
        return remote(src(other), dst(head), send.at[i], recv.at[i], place, other)

    return copy


def cut_of(count, seqs, state, inner):
    rows = max(16, seqs * state // count)
    lane_cuts = count * rows // (seqs * state)
    return rows, lane_cuts, inner // lane_cuts


def piece_of(k, count, seqs, state, inner):
    rows, lane_cuts, lanes = cut_of(count, seqs, state, inner)
    each = count // seqs
    seq, rest = k // each, lax.rem(k, each)
    row = pl.multiple_of(rest // lane_cuts * rows, rows)
    if lane_cuts == 1:
        return seq, pl.ds(row, rows), slice(None)
    lane = pl.multiple_of(lax.rem(rest, lane_cuts) * lanes, lanes)
    return seq, pl.ds(row, rows), pl.ds(lane, lanes)


def carry_exchange(dims, local, arrived, passed, incoming, decay_ref, sems, reverse):
    count, _, seqs, _, inner, _, state = dims
    place, head = lax.axis_index("seq"), lax.axis_index("head")
    send, recv, back_send, back_recv = sems
    piece = functools.partial(piece_of, count=count, seqs=seqs, state=state, inner=inner)
    rows, _, lanes = cut_of(count, seqs, state, inner)

    def at(ref, k):
        seq, row, lane = piece(k)
        return ref.at[seq, row, lane]

    out = line_copy(count, lambda other: at(local, other), lambda k: arrived.at[k], send, recv)

    def back(j):
        i = lax.rem(j - place + count, count)
        return remote(
            passed.at[j], at(incoming, place), back_send.at[i], back_recv.at[i], j, head
        )

    def start():
        loop(1, count, lambda i: out(i).start())
        seq, row, lane = piece(place)
        arrived[place] = local[seq, row, lane]

    def carry():
        seq, row, lane = piece(place)
        held = jnp.zeros((rows, lanes), F32)
        for step in range(count):
            j = count - 1 - step if reverse else step
            i = lax.rem(place - j + count, count)

            @pl.when(j != place)
            def _():
                out(i).wait_recv()

            passed[j] = held.astype(passed.dtype)

            @pl.when(j != place)
            def _():
                back(j).start()

            @pl.when(j == place)
            def _():
                incoming[seq, row, lane] = passed[j]

            decay = decay_ref[seq, pl.ds(j, 1), lane]
            held = decay * held + arrived[j].astype(F32)

    def finish():
        def one(i):
            out(i).wait_send()
            back(lax.rem(place + i, count)).wait()

        loop(1, count, one)

    return start, carry, finish


def forward_kernel(
    dims,
    x_ref,
    gate_ref,
    small_ref,
    chan_ref,
    vec_ref,
    unpack_ref,
    expand_ref,
    gather_ref,
    cot_ref,
    wout_ref,
    xact_ref,
    bc_ref,
    conv_ref,
    convbc_ref,
    dt_ref,
    cum_ref,
    states_ref,
    ng_ref,
    dgate_ref,
    dy_ref,
    dyy_ref,
    decay_ref,
    sums_ref,
    edge_x,
    edge_s,
    ext,
    extbc,
    bc_all,
    fresh,
    y_ref,
    dng_ref,
    gated_ref,
    decays,
    local,
    arrived,
    passed,
    incoming,
    rowsum,
    edge_send,
    edge_recv,
    dec_send,
    dec_recv,
    bc_send,
    bc_recv,
    st_send,
    st_recv,
    back_send,
    back_recv,
    row_send,
    row_recv,
):
    count, parts, seqs, block, inner, heads, state = dims
    place, head = lax.axis_index("seq"), lax.axis_index("head")
    chunks = block // CHUNK
    pairs = heads // 2
    total = seqs * chunks
    meet(count, parts)

    def edge_copies(ahead):
        copies = []
        for s in range(seqs):
            rows = pl.ds(s * block + block - 8, 8)
            for k, (src, dst) in enumerate(((x_ref, edge_x), (small_ref, edge_s))):
                copies.append(
                    remote(
                        src.at[rows], dst.at[s], edge_send.at[k, s], edge_recv.at[k, s], ahead, head
                    )
                )
        return copies

    after = lax.rem(place + 1, count)

    @pl.when(place < count - 1)
    def _():
        for c in edge_copies(after):
            c.start()

    lower = (iota((CHUNK, CHUNK), 0) >= iota((CHUNK, CHUNK), 1)).astype(F32)
    for s in range(seqs):

        def steps(c, logs):
            rows = ds((s * chunks + c) * CHUNK, CHUNK)
            dt = softplus(small_ref[rows, :] + vec_ref[5:6, :])
            cum = mul(lower, dt * vec_ref[6:7, :], NN, EXACT)
            dt_ref[rows, :] = dt
            cum_ref[rows, :] = cum
            return logs + cum[CHUNK - 1 :, :]

        logs = lax.fori_loop(0, chunks, steps, jnp.zeros((1, LANES), F32))
        decays[place, s : s + 1, :] = jnp.exp(logs)

    dec = line_copy(count, lambda _: decays.at[place], lambda k: decays.at[k], dec_send, dec_recv)
    loop(1, count, lambda i: dec(i).start())

    @pl.when(place > 0)
    def _():
        for c in edge_copies(after):
            c.wait_recv()

    @pl.when(place == 0)
    def _():
        edge_x[...] = jnp.zeros_like(edge_x)
        edge_s[...] = jnp.zeros_like(edge_s)

    def packed(low, high):
        return jnp.where(
            iota(low.shape, 1) < LANES // 2, pltpu.roll(low, LANES // 2, 1), high
        )

    extbc[0:8, :] = packed(edge_s[0], edge_s[1])
    extbc[8:, :] = packed(small_ref[0:block, :], small_ref[block:, :])
    conv = vec_ref[4:5, :]
    for k in range(KER):
        conv = conv + vec_ref[k : k + 1, :] * extbc[pl.ds(8 - (KER - 1) + k, block), :]
    convbc_ref[...] = conv
    bc_all[head] = (conv * sigmoid(conv)).astype(BF16)
    share = head_copy(parts, lambda _: bc_all.at[head], lambda k: bc_all.at[k], bc_send, bc_recv)
    loop(1, parts, lambda i: share(i).start())

    def x_chunk(t):
        rows = ds(t * CHUNK, CHUNK)
        s, c = t // chunks, lax.rem(t, chunks)
        before = pl.ds(pl.multiple_of(jnp.maximum(t * CHUNK - 8, 0), 8), 8)
        for b in range(inner // LANES):
            lane = slice(b * LANES, (b + 1) * LANES)
            ext[0:8, lane] = jnp.where(c == 0, edge_x[s, :, lane], x_ref[before, lane])
            ext[8:, lane] = x_ref[rows, lane]
            conv = chan_ref[4:5, lane]
            for k in range(KER):
                conv = conv + chan_ref[k : k + 1, lane] * ext[pl.ds(8 - (KER - 1) + k, CHUNK), lane]
            conv_ref[rows, lane] = conv
            xact_ref[rows, lane] = (conv * sigmoid(conv)).astype(BF16)

    loop(0, total, x_chunk)

    loop(1, parts, lambda i: share(i).wait())
    everything = jnp.concatenate([bc_all[k] for k in range(parts)], axis=1)
    for s in range(seqs):
        bc_ref[s * block : (s + 1) * block, :] = mul(everything, unpack_ref[s], NN).astype(BF16)

    for s in range(seqs):

        def add(c, held):
            t = s * chunks + c
            rows = ds(t * CHUNK, CHUNK)
            cum, dt = cum_ref[rows, :], dt_ref[rows, :]
            end = cum[CHUNK - 1 :, :]
            tail = jnp.exp(end - cum) * dt
            weighted = jnp.concatenate(
                [
                    (
                        xact_ref[rows, p * LANES : (p + 1) * LANES].astype(F32) * pair_of(tail, p)
                    ).astype(BF16)
                    for p in range(pairs)
                ],
                axis=1,
            )
            new = mul(bc_ref[rows, 0:state], weighted, TN)
            fresh[t] = new
            return spread(jnp.exp(end), pairs) * held + new

        held = lax.fori_loop(0, chunks, add, jnp.zeros((state, inner), F32))
        local[s] = held

    start, carry, finish = carry_exchange(
        dims,
        local,
        arrived,
        passed,
        incoming,
        decay_ref,
        (st_send, st_recv, back_send, back_recv),
        False,
    )
    start()

    def within(t):
        rows = ds(t * CHUNK, CHUNK)
        cum, dt = cum_ref[rows, :], dt_ref[rows, :]
        cum_t = cum.T
        scores = mul(bc_ref[rows, state:], bc_ref[rows, 0:state], NT)
        seen = iota((CHUNK, CHUNK), 0) >= iota((CHUNK, CHUNK), 1)
        side = iota((CHUNK, LANES), 1) < LANES // 2
        for p in range(pairs):
            lane = slice(p * LANES, (p + 1) * LANES)
            stepped = (xact_ref[rows, lane].astype(F32) * pair_of(dt, p)).astype(BF16)
            halves = []
            for h in (2 * p, 2 * p + 1):
                gap = cum[:, h : h + 1] - cum_t[h : h + 1, :]
                mixing = (scores * jnp.exp(jnp.where(seen, gap, -1e30))).astype(BF16)
                halves.append(mul(mixing, stepped, NN))
            y_ref[rows, lane] = jnp.where(side, halves[0], halves[1])

    loop(0, total, within)

    loop(1, count, lambda i: dec(i).wait())
    for s in range(seqs):
        decay_ref[s] = mul(decays[:, s, :], expand_ref[...], NN, EXACT)
    carry()

    wide = 2 * LANES

    def back_project(i):
        s, b = i // (inner // wide), lax.rem(i, inner // wide)
        rows, lane = ds(s * block, block), ds(b * wide, wide)
        dng_ref[rows, lane] = mul(cot_ref[rows, :], wout_ref[lane, :], NT)

    loop(0, seqs * (inner // wide), back_project)
    finish()

    for s in range(seqs):

        def gate(c, held):
            t = s * chunks + c
            rows = ds(t * CHUNK, CHUNK)
            cum = cum_ref[rows, :]
            grown = jnp.exp(cum)
            states_ref[t] = held
            high, low = halves_of(held)
            c_rows = bc_ref[rows, state:]
            carried = mul(c_rows, high, NN) + mul(c_rows, low, NN)
            square = jnp.zeros((CHUNK, LANES), F32)
            cross = jnp.zeros((CHUNK, LANES), F32)
            for p in range(pairs):
                lane = slice(p * LANES, (p + 1) * LANES)
                y = y_ref[rows, lane] + carried[:, lane] * pair_of(grown, p)
                y_ref[rows, lane] = y
                out = y + chan_ref[6:7, lane] * xact_ref[rows, lane].astype(F32)
                pre = gate_ref[rows, lane]
                gated = out * (pre * sigmoid(pre))
                gated_ref[rows, lane] = gated
                square = square + gated * gated
                cross = cross + dng_ref[rows, lane] * chan_ref[5:6, lane] * gated
            at = iota((CHUNK, LANES), 1)
            both = jnp.where(
                at == 0,
                jnp.sum(square, axis=1, keepdims=True),
                jnp.where(at == 1, jnp.sum(cross, axis=1, keepdims=True), 0.0),
            )
            rowsum[head, t] = both.T[0:8, :]
            return spread(grown[CHUNK - 1 :, :], pairs) * held + fresh[t]

        lax.fori_loop(0, chunks, gate, incoming[s].astype(F32))

    rows_copy = head_copy(
        parts, lambda _: rowsum.at[head], lambda k: rowsum.at[k], row_send, row_recv
    )
    loop(1, parts, lambda i: rows_copy(i).start())
    loop(1, parts, lambda i: rows_copy(i).wait())
    sums_ref[...] = jnp.zeros_like(sums_ref)
    channels = inner * parts

    def outputs(t):
        rows = ds(t * CHUNK, CHUNK)
        sums = rowsum[0, t]
        for k in range(1, parts):
            sums = sums + rowsum[k, t]
        turned = jnp.concatenate([sums, jnp.zeros((CHUNK - 8, LANES), F32)], axis=0).T
        scale = lax.rsqrt(turned[:, 0:1] / channels + EPSILON)
        pull = scale * scale * scale * (turned[:, 1:2] / channels)
        dyy = jnp.zeros((CHUNK, LANES), F32)
        for p in range(pairs):
            lane = slice(p * LANES, (p + 1) * LANES)
            pre = gate_ref[rows, lane]
            sg = sigmoid(pre)
            gated, y = gated_ref[rows, lane], y_ref[rows, lane]
            x = xact_ref[rows, lane].astype(F32)
            gain = chan_ref[5:6, lane]
            scaled = gated * scale
            ng_ref[rows, lane] = (scaled * gain).astype(BF16)
            dng = dng_ref[rows, lane]
            d_gated = scale * (dng * gain) - gated * pull
            d_ssd = d_gated * (pre * sg)
            out = y + chan_ref[6:7, lane] * x
            dgate_ref[rows, lane] = (d_gated * out * (sg * (1.0 + pre * (1.0 - sg)))).astype(BF16)
            dy = d_ssd.astype(BF16)
            dy_ref[rows, lane] = dy
            sums_ref[0:8, lane] += eights(dng * scaled)
            sums_ref[8:16, lane] += eights(d_ssd * x)
            dyy = dyy + head_sums(dy.astype(F32) * y, gather_ref[lane, :])
        dyy_ref[rows, :] = dyy

    loop(0, total, outputs)

    @pl.when(place < count - 1)
    def _():
        for c in edge_copies(after):
            c.wait_send()


def vmem(shape, kind):
    return pltpu.VMEM(shape, kind)


def forward(dims, *operands):
    count, parts, seqs, block, inner, heads, state = dims
    rows = seqs * block
    chunks = rows // CHUNK
    cut_rows, _, cut_lanes = cut_of(count, seqs, state, inner)
    spec = pl.BlockSpec(memory_space=pltpu.VMEM)
    line, ring = pltpu.SemaphoreType.DMA((count,)), pltpu.SemaphoreType.DMA((parts,))
    edge = pltpu.SemaphoreType.DMA((2, seqs))
    outs = [
        ((rows, inner), BF16),
        ((rows, 2 * state), BF16),
        ((rows, inner), F32),
        ((block, LANES), F32),
        ((rows, LANES), F32),
        ((rows, LANES), F32),
        ((chunks, state, inner), F32),
        ((rows, inner), BF16),
        ((rows, inner), BF16),
        ((rows, inner), BF16),
        ((rows, LANES), F32),
        ((seqs, count, inner), F32),
        ((16, inner), F32),
    ]
    return pl.pallas_call(
        functools.partial(forward_kernel, dims),
        out_shape=[jax.ShapeDtypeStruct(*o) for o in outs],
        in_specs=[spec] * len(operands),
        out_specs=[spec] * len(outs),
        scratch_shapes=[
            vmem((seqs, 8, inner), F32),
            vmem((seqs, 8, LANES), F32),
            vmem((CHUNK + 8, inner), F32),
            vmem((block + 8, LANES), F32),
            vmem((parts, block, LANES), BF16),
            vmem((chunks, state, inner), F32),
            vmem((rows, inner), F32),
            vmem((rows, inner), F32),
            vmem((rows, inner), F32),
            vmem((count, 8, LANES), F32),
            vmem((seqs, state, inner), F32),
            vmem((count, cut_rows, cut_lanes), F32),
            vmem((count, cut_rows, cut_lanes), F32),
            vmem((seqs, state, inner), F32),
            vmem((parts, chunks, 8, LANES), F32),
            edge,
            edge,
            line,
            line,
            ring,
            ring,
            line,
            line,
            line,
            line,
            ring,
            ring,
        ],
        compiler_params=pltpu.CompilerParams(
            collective_id=2, has_side_effects=True, vmem_limit_bytes=VMEM_LIMIT
        ),
        name="mixer_forward",
    )(*operands)


def backward_kernel(
    dims,
    dy_ref,
    xact_ref,
    bc_ref,
    conv_ref,
    convbc_ref,
    dt_ref,
    cum_ref,
    states_ref,
    dyy_ref,
    decay_ref,
    x_ref,
    small_ref,
    chan_ref,
    vec_ref,
    pack_ref,
    gather_ref,
    dx_ref,
    dsmall_ref,
    gx_ref,
    gbc_ref,
    gdt_ref,
    dconv,
    dconvbc,
    prebc,
    dbc,
    ddt,
    added,
    local,
    arrived,
    passed,
    incoming,
    bc_out,
    bc_in,
    edge_send,
    edge_recv,
    bc_send,
    bc_recv,
    st_send,
    st_recv,
    back_send,
    back_recv,
):
    count, parts, seqs, block, inner, heads, state = dims
    place, head = lax.axis_index("seq"), lax.axis_index("head")
    chunks = block // CHUNK
    pairs = heads // 2
    total = seqs * chunks
    meet(count, parts)
    gdt_ref[...] = jnp.zeros_like(gdt_ref)

    for s in range(seqs):

        def alone(i, held):
            t = s * chunks + chunks - 1 - i
            rows = ds(t * CHUNK, CHUNK)
            grown = jnp.exp(cum_ref[rows, :])
            weighted = jnp.concatenate(
                [
                    (
                        dy_ref[rows, p * LANES : (p + 1) * LANES].astype(F32) * pair_of(grown, p)
                    ).astype(BF16)
                    for p in range(pairs)
                ],
                axis=1,
            )
            new = mul(bc_ref[rows, state:], weighted, TN)
            added[t] = new
            return spread(grown[CHUNK - 1 :, :], pairs) * held + new

        held = lax.fori_loop(0, chunks, alone, jnp.zeros((state, inner), F32))
        local[s] = held.astype(BF16)

    start, carry, finish = carry_exchange(
        dims,
        local,
        arrived,
        passed,
        incoming,
        decay_ref,
        (st_send, st_recv, back_send, back_recv),
        True,
    )
    start()
    carry()
    finish()

    side = iota((CHUNK, LANES), 1) < LANES // 2
    seen = iota((CHUNK, CHUNK), 0) <= iota((CHUNK, CHUNK), 1)
    upper = seen.astype(F32)
    for s in range(seqs):

        def chunk(i, held):
            t = s * chunks + chunks - 1 - i
            rows = ds(t * CHUNK, CHUNK)
            out_rows = ds((s * chunks + chunks - 1 - i) * CHUNK, CHUNK)
            cum, dt = cum_ref[rows, :], dt_ref[rows, :]
            cum_t = cum.T
            grown = jnp.exp(cum)
            end = cum[CHUNK - 1 :, :]
            tail = jnp.exp(end - cum)
            b_rows, c_rows = bc_ref[rows, 0:state], bc_ref[rows, state:]
            scores = mul(b_rows, c_rows, NT)
            low = held.astype(BF16)
            begun = states_ref[t]
            begun_high, begun_low = halves_of(begun)
            pulled = mul(b_rows, low, NN)
            grad_scores = jnp.zeros((CHUNK, CHUNK), F32)
            d_x_sum = jnp.zeros((CHUNK, LANES), F32)
            d_fall = jnp.zeros((CHUNK, LANES), F32)
            into_x = []
            into_y = []
            last = []
            for p in range(pairs):
                lane = slice(p * LANES, (p + 1) * LANES)
                x, dy = xact_ref[rows, lane], dy_ref[rows, lane]
                xf, dyf = x.astype(F32), dy.astype(F32)
                dt_p, tail_p = pair_of(dt, p), pair_of(tail, p)
                stepped = xf * dt_p
                low_step = stepped.astype(BF16)
                halves = []
                for k, h in enumerate((2 * p, 2 * p + 1)):
                    gap = cum_t[h : h + 1, :] - cum[:, h : h + 1]
                    fade = jnp.exp(jnp.where(seen, gap, -1e30))
                    own = jnp.where(side if k == 0 else ~side, low_step, jnp.zeros_like(low_step))
                    grad_scores = grad_scores + mul(own, dy, NT) * fade
                    halves.append(mul((scores * fade).astype(BF16), dy, NN))
                from_state = pulled[:, lane] * tail_p
                d_step_x = jnp.where(side, halves[0], halves[1]) + from_state
                rounded = low_step.astype(F32)
                d_x_sum = d_x_sum + head_sums(xf * d_step_x, gather_ref[lane, :])
                d_fall = d_fall + head_sums(rounded * d_step_x, gather_ref[lane, :])
                into_x.append((stepped * tail_p).astype(BF16))
                into_y.append((dyf * pair_of(grown, p)).astype(BF16))
                last.append(jnp.sum(rounded * from_state, axis=0, keepdims=True))
                conv = conv_ref[rows, lane]
                sg = sigmoid(conv)
                d_act = dt_p * d_step_x + chan_ref[6:7, lane] * dyf
                dconv[s, ds((chunks - 1 - i) * CHUNK, CHUNK), lane] = d_act * (
                    sg * (1.0 + conv * (1.0 - sg))
                )
            low_scores = grad_scores.astype(BF16)
            d_b = mul(low_scores, c_rows, NN) + mul(jnp.concatenate(into_x, axis=1), low, NT)
            into_y = jnp.concatenate(into_y, axis=1)
            d_c = mul(low_scores, b_rows, TN) + mul(into_y, begun_high, NT)
            d_c = d_c + mul(into_y, begun_low, NT)
            dbc[out_rows, 0:state] = d_b.astype(BF16)
            dbc[out_rows, state:] = d_c.astype(BF16)
            fall = spread(grown[CHUNK - 1 :, :], pairs)
            ends = jnp.concatenate(last, axis=1) + fall * jnp.sum(
                held * begun, axis=0, keepdims=True
            )
            ends = head_sums(jnp.broadcast_to(ends, (8, inner)), gather_ref[...])[0:1, :]
            d_log = mul(upper, dyy_ref[rows, :] - d_fall, NN, EXACT) + ends
            d_step = d_x_sum + vec_ref[6:7, :] * d_log
            d_dt = d_step * sigmoid(small_ref[rows, :] + vec_ref[5:6, :])
            gdt_ref[0:8, :] += eights(d_dt)
            gdt_ref[8:16, :] += eights(d_log * (dt * vec_ref[6:7, :]))
            ddt[out_rows, :] = d_dt
            return fall * held + added[t]

        lax.fori_loop(0, chunks, chunk, incoming[s].astype(F32))

    def pack(k):
        piece = mul(dbc[0:block, :], pack_ref[k, 0], NN)
        return (piece + mul(dbc[block:, :], pack_ref[k, 1], NN)).astype(BF16)

    def pack_one(k):
        bc_out[k] = pack(k)

    loop(0, parts, pack_one)
    share = head_copy(parts, lambda k: bc_out.at[k], lambda k: bc_in.at[k], bc_send, bc_recv)
    loop(1, parts, lambda i: share(i).start())

    before = lax.rem(place + count - 1, count)

    def edge_copy(s):
        return remote(
            dconv.at[s, pl.ds(0, 8)],
            dconv.at[s, pl.ds(block, 8)],
            edge_send.at[s],
            edge_recv.at[s],
            before,
            head,
        )

    def edge_bc():
        return remote(
            dconvbc.at[pl.ds(0, 8)],
            dconvbc.at[pl.ds(block, 8)],
            edge_send.at[seqs],
            edge_recv.at[seqs],
            before,
            head,
        )

    @pl.when(place > 0)
    def _():
        for s in range(seqs):
            edge_copy(s).start()

    loop(1, parts, lambda i: share(i).wait())
    bc_in[head] = bc_out[head]
    d_act = bc_in[0].astype(F32)
    for k in range(1, parts):
        d_act = d_act + bc_in[k].astype(F32)
    conv = convbc_ref[...]
    sg = sigmoid(conv)
    dconvbc[0:block, :] = d_act * (sg * (1.0 + conv * (1.0 - sg)))

    @pl.when(place > 0)
    def _():
        edge_bc().start()

    @pl.when(place < count - 1)
    def _():
        for s in range(seqs):
            edge_copy(s).wait_recv()

    @pl.when(place == count - 1)
    def _():
        for s in range(seqs):
            dconv[s, block : block + 8, :] = jnp.zeros((8, inner), F32)

    gx_ref[...] = jnp.zeros_like(gx_ref)

    def x_chunk(t):
        rows = ds(t * CHUNK, CHUNK)
        s, c = t // chunks, lax.rem(t, chunks)
        for p in range(pairs):
            lane = slice(p * LANES, (p + 1) * LANES)
            x = x_ref[rows, lane]
            pre = jnp.zeros((CHUNK, LANES), F32)
            here = dconv[s, pl.ds(pl.multiple_of(c * CHUNK, CHUNK), CHUNK + 8), lane]
            for k in range(KER):
                off = KER - 1 - k
                d = pltpu.roll(here, CHUNK + 8 - off, 0)[:CHUNK] if off else here[:CHUNK]
                pre = pre + chan_ref[k : k + 1, lane] * d
                gx_ref[8 * k : 8 * k + 8, lane] += eights(x * d)
                if k == KER - 1:
                    gx_ref[8 * KER : 8 * KER + 8, lane] += eights(d)
            dx_ref[rows, lane] = pre.astype(BF16)

    loop(0, total, x_chunk)

    @pl.when(place < count - 1)
    def _():
        edge_bc().wait_recv()

    @pl.when(place == count - 1)
    def _():
        dconvbc[block : block + 8, :] = jnp.zeros((8, LANES), F32)

    low, high = small_ref[0:block, :], small_ref[block:, :]
    prebc[...] = jnp.where(
        iota(low.shape, 1) < LANES // 2, pltpu.roll(low, LANES // 2, 1), high
    )
    pre = jnp.zeros((block, LANES), F32)
    for k in range(KER):
        d = dconvbc[pl.ds(KER - 1 - k, block), :]
        pre = pre + vec_ref[k : k + 1, :] * d
        gbc_ref[8 * k : 8 * k + 8, :] = eights(prebc[...] * d)
    gbc_ref[8 * KER : 8 * KER + 8, :] = eights(dconvbc[0:block, :])
    at = iota((block, LANES), 1)
    for s in range(seqs):
        rows = slice(s * block, (s + 1) * block)
        mine = pre if s == seqs - 1 else pltpu.roll(pre, LANES // 2, 1)
        step = jnp.where(at < heads, ddt[rows, :], 0.0)
        dsmall_ref[rows, :] = jnp.where(at < LANES // 2, step, mine).astype(BF16)

    @pl.when(place > 0)
    def _():
        for s in range(seqs):
            edge_copy(s).wait_send()
        edge_bc().wait_send()


def backward(dims, *operands):
    count, parts, seqs, block, inner, heads, state = dims
    rows = seqs * block
    chunks = rows // CHUNK
    cut_rows, _, cut_lanes = cut_of(count, seqs, state, inner)
    spec = pl.BlockSpec(memory_space=pltpu.VMEM)
    line, ring = pltpu.SemaphoreType.DMA((count,)), pltpu.SemaphoreType.DMA((parts,))
    edge = pltpu.SemaphoreType.DMA((seqs + 1,))
    outs = [
        ((rows, inner), BF16),
        ((rows, LANES), BF16),
        ((8 * (KER + 1), inner), F32),
        ((8 * (KER + 1), LANES), F32),
        ((16, LANES), F32),
    ]
    return pl.pallas_call(
        functools.partial(backward_kernel, dims),
        out_shape=[jax.ShapeDtypeStruct(*o) for o in outs],
        in_specs=[spec] * len(operands),
        out_specs=[spec] * len(outs),
        scratch_shapes=[
            vmem((seqs, block + 8, inner), F32),
            vmem((block + 8, LANES), F32),
            vmem((block, LANES), F32),
            vmem((rows, 2 * state), BF16),
            vmem((rows, LANES), F32),
            vmem((chunks, state, inner), F32),
            vmem((seqs, state, inner), BF16),
            vmem((count, cut_rows, cut_lanes), BF16),
            vmem((count, cut_rows, cut_lanes), BF16),
            vmem((seqs, state, inner), BF16),
            vmem((parts, block, LANES), BF16),
            vmem((parts, block, LANES), BF16),
            edge,
            edge,
            ring,
            ring,
            line,
            line,
            line,
            line,
        ],
        compiler_params=pltpu.CompilerParams(
            collective_id=3, has_side_effects=True, vmem_limit_bytes=VMEM_LIMIT
        ),
        name="mixer_backward",
    )(*operands)


def ring_place(count):
    place = lax.axis_index("seq")
    row, col = place // 2, place % 2
    return jnp.where(col == 0, row, count - 1 - row)


def ring_device(rank, count):
    return jnp.where(rank < count // 2, 2 * rank, 2 * (count - 1 - rank) + 1)


def ring_kernel(count, plan, *refs):
    n_lhs = 1 + max(p[0] for p in plan)
    n_rhs = 1 + max(p[1] for p in plan)
    streams = len(plan)
    lhs, refs = refs[:n_lhs], refs[n_lhs:]
    rhs, refs = refs[:n_rhs], refs[n_rhs:]
    small_ref, refs = refs[0], refs[1:]
    outs, refs = refs[:streams], refs[streams:]
    small_out, refs = refs[0], refs[1:]
    bufs, refs = refs[:streams], refs[streams:]
    small_buf, rs_send, rs_recv, ag_send, ag_recv, sm_send, sm_recv = refs
    head = lax.axis_index("head")
    place = lax.axis_index("seq")
    rank = ring_place(count)
    peers = {
        1: (ring_device(lax.rem(rank + 1, count), count), head),
        -1: (ring_device(lax.rem(rank + count - 1, count), count), head),
    }
    barrier = pltpu.get_barrier_semaphore()

    def greet(i, _):
        other = lax.rem(place + i, count)
        pl.semaphore_signal(barrier, inc=1, device_id=(other, head), device_id_type=MESH)
        return 0

    lax.fori_loop(1, count, greet, 0)
    pl.semaphore_wait(barrier, count - 1)

    small_buf[place] = small_ref[...]

    def small_copy(i):
        other = lax.rem(place + i, count)
        return pltpu.make_async_remote_copy(
            src_ref=small_ref,
            dst_ref=small_buf.at[place],
            send_sem=sm_send.at[i],
            recv_sem=sm_recv.at[i],
            device_id=(other, head),
            device_id_type=MESH,
        )

    def small_start(i, _):
        small_copy(i).start()
        return 0

    lax.fori_loop(1, count, small_start, 0)

    def chunk_of(direction, step):
        return lax.rem(rank - direction * step + 2 * count, count)

    def partial(i, chunk):
        l, r, first, cols, _ = plan[i]
        rows = lhs[l].shape[0] // count
        left = lhs[l][pl.ds(pl.multiple_of(chunk * rows, rows), rows), :]
        return jnp.dot(left, rhs[r][:, first : first + cols], preferred_element_type=jnp.float32)

    def rs_copy(i, step):
        return pltpu.make_async_remote_copy(
            src_ref=bufs[i].at[step],
            dst_ref=bufs[i].at[step + 1],
            send_sem=rs_send.at[i, step],
            recv_sem=rs_recv.at[i, step],
            device_id=peers[plan[i][4]],
            device_id_type=MESH,
        )

    def ag_copy(i, step):
        rows = bufs[i].shape[1]
        chunk = chunk_of(plan[i][4], step - 1)
        block = outs[i].at[pl.ds(pl.multiple_of(chunk * rows, rows), rows)]
        return pltpu.make_async_remote_copy(
            src_ref=block,
            dst_ref=block,
            send_sem=ag_send.at[i, step],
            recv_sem=ag_recv.at[i, step],
            device_id=peers[plan[i][4]],
            device_id_type=MESH,
        )

    for i in range(streams):
        bufs[i][0] = partial(i, chunk_of(plan[i][4], 0)).astype(jnp.bfloat16)
        rs_copy(i, 0).start()

    def rs_step(step, _):
        for i in range(streams):
            own = partial(i, chunk_of(plan[i][4], step))
            rs_copy(i, step - 1).wait_recv()
            bufs[i][step] = (own + bufs[i][step].astype(jnp.float32)).astype(jnp.bfloat16)
            rs_copy(i, step).start()
        return 0

    lax.fori_loop(1, count - 1, rs_step, 0)
    for i in range(streams):
        chunk = chunk_of(plan[i][4], count - 1)
        rows = bufs[i].shape[1]
        own = partial(i, chunk)
        rs_copy(i, count - 2).wait_recv()
        done = (own + bufs[i][count - 1].astype(jnp.float32)).astype(jnp.bfloat16)
        outs[i][pl.ds(pl.multiple_of(chunk * rows, rows), rows), :] = done
        ag_copy(i, 0).start()

    def ag_step(step, _):
        for i in range(streams):
            ag_copy(i, step - 1).wait_recv()
            ag_copy(i, step).start()
        return 0

    lax.fori_loop(1, count - 1, ag_step, 0)
    for i in range(streams):
        ag_copy(i, count - 2).wait_recv()

    def small_wait(i, _):
        small_copy(i).wait()
        return 0

    lax.fori_loop(1, count, small_wait, 0)
    total = small_buf[0]
    for i in range(1, count):
        total = total + small_buf[i]
    small_out[...] = total

    def drain(step, _):
        for i in range(streams):
            rs_copy(i, step).wait_send()
            ag_copy(i, step).wait_send()
        return 0

    lax.fori_loop(0, count - 1, drain, 0)


def ring_sum(count, plan, lhs, rhs, small):
    rows = [lhs[p[0]].shape[0] for p in plan]
    vmem = pl.BlockSpec(memory_space=pltpu.VMEM)
    streams = len(plan)
    sems = pltpu.SemaphoreType.DMA((streams, count))
    return pl.pallas_call(
        functools.partial(ring_kernel, count, plan),
        out_shape=[jax.ShapeDtypeStruct((r, p[3]), jnp.bfloat16) for r, p in zip(rows, plan)]
        + [jax.ShapeDtypeStruct(small.shape, jnp.float32)],
        in_specs=[vmem] * (len(lhs) + len(rhs) + 1),
        out_specs=[vmem] * (streams + 1),
        scratch_shapes=[
            pltpu.VMEM((count, r // count, p[3]), jnp.bfloat16) for r, p in zip(rows, plan)
        ]
        + [
            pltpu.VMEM((count,) + small.shape, jnp.float32),
            sems,
            sems,
            sems,
            sems,
            pltpu.SemaphoreType.DMA((count,)),
            pltpu.SemaphoreType.DMA((count,)),
        ],
        compiler_params=pltpu.CompilerParams(
            collective_id=1, has_side_effects=True, vmem_limit_bytes=56 * 2**20
        ),
        name="weight_ring",
    )(*lhs, *rhs, small)


def body(
    tokens,
    norm_gain,
    gate_input_weight,
    coefficient_weight,
    step_weight,
    conv_x,
    conv_bc,
    conv_bias_x,
    conv_bias_bc,
    dt_bias,
    a_log,
    d_skip,
    gate_gain,
    output_weight,
    cotangent,
):
    seqs, block, width = tokens.shape
    inner = gate_input_weight.shape[2]
    state_part = coefficient_weight.shape[2]
    heads = step_weight.shape[1]
    count, parts = lax.axis_size("seq"), lax.axis_size("head")
    my_head = lax.axis_index("head")
    state = state_part * parts
    rows = seqs * block
    col_count = width // parts
    half = LANES // 2
    dims = (count, parts, seqs, block, inner, heads, state)

    input_batch = tokens.astype(F32).reshape(rows, width)
    row_scale = lax.rsqrt(jnp.mean(input_batch * input_batch, axis=-1, keepdims=True) + EPSILON)
    normed = (input_batch * row_scale * norm_gain).astype(BF16)
    projected = jnp.einsum(
        "rp,pkw->krw", normed, gate_input_weight, preferred_element_type=F32
    )
    gate_pre, x_pre = projected[0], projected[1]
    small_weight = jnp.concatenate(
        [
            step_weight,
            jnp.zeros((width, half - heads), BF16),
            coefficient_weight.reshape(width, 2 * state_part),
        ],
        axis=1,
    )
    small = jnp.dot(normed, small_weight, preferred_element_type=F32)

    chan = jnp.concatenate(
        [
            conv_x,
            conv_bias_x[None],
            gate_gain[None],
            jnp.repeat(d_skip, inner // heads)[None],
            jnp.zeros((1, inner), F32),
        ]
    )
    twice = jnp.concatenate(
        [conv_bc.reshape(KER, 2 * state_part), conv_bias_bc.reshape(1, 2 * state_part)]
    )
    per_head = jnp.stack([dt_bias, -jnp.exp(a_log), jnp.zeros_like(a_log)])
    vec = jnp.concatenate(
        [
            jnp.concatenate([twice, twice], axis=1),
            jnp.pad(per_head, ((0, 0), (0, LANES - heads))),
        ]
    )
    device, lane, channel = jnp.meshgrid(
        jnp.arange(parts), jnp.arange(LANES), jnp.arange(2 * state), indexing="ij"
    )
    is_c, at = channel // state, channel % state
    unpack = jnp.stack(
        [
            (lane == s * half + is_c * state_part + at - device * state_part)
            & (at // state_part == device)
            for s in range(seqs)
        ]
    ).astype(BF16)
    pack = unpack.transpose(1, 0, 3, 2)
    unpack = unpack.reshape(seqs, parts * LANES, 2 * state)
    expand = jnp.arange(LANES)[:, None] == jnp.arange(inner)[None, :] // (inner // heads)
    gather = expand.T.astype(BF16)
    expand = expand.astype(F32)
    cot = cotangent.reshape(rows, width)

    xact, bc, conv, convbc, dt, cum, states, ng, dgate, dy, dyy, decay, sums = forward(
        dims,
        x_pre,
        gate_pre,
        small,
        chan,
        vec,
        unpack,
        expand,
        gather,
        cot,
        output_weight,
    )
    dx, dsmall, gx, gbc, gdt = backward(
        dims,
        dy,
        xact,
        bc,
        conv,
        convbc,
        dt,
        cum,
        states,
        dyy,
        decay,
        x_pre,
        small,
        chan,
        vec,
        pack,
        gather,
    )

    mixer = jnp.dot(ng, output_weight, preferred_element_type=F32)
    mixed = lax.psum_scatter(
        mixer.astype(BF16), "head", scatter_dimension=1, tiled=True
    ).astype(F32)
    own_inputs = lax.dynamic_slice_in_dim(input_batch, my_head * col_count, col_count, 1)
    block_out = (own_inputs + mixed).astype(BF16)

    d_both = jnp.stack([dgate, dx], axis=1)
    grad_normed = jnp.einsum(
        "rkw,pkw->rp", d_both, gate_input_weight, preferred_element_type=F32
    ) + lax.dot_general(dsmall, small_weight, (((1,), (1,)), ((), ())), preferred_element_type=F32)
    d_own = lax.psum_scatter(
        grad_normed.astype(BF16), "head", scatter_dimension=1, tiled=True
    ).astype(F32)
    own_gain = lax.dynamic_slice_in_dim(norm_gain, my_head * col_count, col_count, 0)
    grad_norm_gain = jnp.sum(d_own * own_inputs * row_scale, axis=0)
    d_units = d_own * own_gain
    row_sum = lax.psum(jnp.sum(d_units * own_inputs, axis=-1, keepdims=True), "head")
    own_cot = lax.dynamic_slice_in_dim(cot, my_head * col_count, col_count, 1).astype(F32)
    grad_input = row_scale * d_units - own_inputs * row_scale**3 * (row_sum / width) + own_cot

    def padded(array_in):
        return jnp.pad(array_in, ((0, -array_in.shape[0] % (count * 16)), (0, 0)))

    normed_t, ng_t = padded(normed.T), padded(ng.T)
    narrow = jnp.concatenate([dx, dsmall], axis=1)
    hw, hi = width // 2, inner // 2
    plan = (
        (0, 0, 0, hw, 1),
        (0, 0, hw, hw, -1),
        (1, 1, 0, hi, 1),
        (1, 1, hi, hi, -1),
        (1, 2, 0, hi, 1),
        (1, 2, hi, hi + LANES, -1),
    )
    taps = gx.reshape(KER + 1, 8, inner).sum(1)
    taps_bc = gbc.reshape(KER + 1, 8, 2, half).sum((1, 2))
    gdt = gdt.reshape(2, 8, LANES).sum(1)[:, :heads]
    sums = sums.reshape(2, 8, inner).sum(1)
    skip = sums[1].reshape(heads, inner // heads).sum(1)
    smalls = [taps.reshape(-1), taps_bc.reshape(-1), gdt.reshape(-1), skip, sums[0], grad_norm_gain]
    sizes = [a.shape[0] for a in smalls]
    flat = jnp.concatenate(smalls)
    lines = -(-flat.shape[0] // 1024) * 8
    flat = jnp.pad(flat, (0, lines * LANES - flat.shape[0])).reshape(lines, LANES)
    *wide, flat = ring_sum(count, plan, (ng_t, normed_t), (cot, dgate, narrow), flat)
    flat = flat.reshape(-1)
    cuts = []
    begin = 0
    for size in sizes:
        cuts.append(flat[begin : begin + size])
        begin += size
    taps, taps_bc = cuts[0].reshape(KER + 1, inner), cuts[1].reshape(KER + 1, 2, state_part)
    g_dt, g_a = cuts[2].reshape(2, heads)
    wide = [a.astype(F32) for a in wide]
    g_w_out = jnp.concatenate(wide[:2], axis=1)[:inner]
    g_gate = jnp.concatenate(wide[2:4], axis=1)[:width]
    g_narrow = jnp.concatenate(wide[4:], axis=1)[:width]
    g_small = g_narrow[:, inner:]
    return (
        block_out.reshape(seqs, block, col_count),
        grad_input.reshape(seqs, block, col_count),
        cuts[5],
        jnp.stack([g_gate, g_narrow[:, :inner]], axis=1),
        g_small[:, half:].reshape(width, 2, state_part),
        g_small[:, :heads],
        taps[:KER],
        taps_bc[:KER],
        taps[KER],
        taps_bc[KER],
        g_dt,
        g_a,
        cuts[3],
        cuts[4],
        g_w_out,
    )


def solution(mesh):
    placed = (
        P(None, "seq", None),
        P(),
        P(None, None, "head"),
        P(None, None, "head"),
        P(None, "head"),
        P(None, "head"),
        P(None, None, "head"),
        P("head"),
        P(None, "head"),
        P("head"),
        P("head"),
        P("head"),
        P("head"),
        P("head", None),
        P(None, "seq", None),
    )
    return jax.shard_map(
        body,
        mesh=mesh,
        in_specs=placed,
        out_specs=(
            P(None, "seq", "head"),
            P(None, "seq", "head"),
            P("head"),
            P(None, None, "head"),
            P(None, None, "head"),
            P(None, "head"),
            P(None, "head"),
            P(None, None, "head"),
            P("head"),
            P(None, "head"),
            P("head"),
            P("head"),
            P("head"),
            P("head"),
            P("head", None),
        ),
        check_vma=False,
    )
```

```python
import functools

import jax
import jax.numpy as jnp
from jax import lax
from jax.experimental import pallas as pl
from jax.experimental.pallas import tpu as pltpu
from jax.sharding import PartitionSpec as P

KER = 4
EPSILON = 1e-05
CHUNK = 128
LANES = 128
MESH = pl.DeviceIdType.MESH
F32 = jnp.float32
BF16 = jnp.bfloat16
EXACT = lax.Precision.HIGHEST
VMEM_LIMIT = 60 * 2**20
NN = ((1,), (0,))
NT = ((1,), (1,))
TN = ((0,), (0,))


def mul(left, right, how, precision=None):
    return lax.dot_general(
        left, right, (how, ((), ())), precision=precision, preferred_element_type=F32
    )


def sigmoid(v):
    return 0.5 * jnp.tanh(0.5 * v) + 0.5


def softplus(v):
    e = jnp.exp(-jnp.abs(v))
    u = 1.0 + e
    near = u - 1.0
    log1p = jnp.where(near == 0.0, e, jnp.log(u) * (e / jnp.where(near == 0.0, 1.0, near)))
    return jnp.maximum(v, 0.0) + log1p


def iota(shape, dim):
    return lax.broadcasted_iota(jnp.int32, shape, dim)


def ds(start, size):
    return pl.ds(pl.multiple_of(start, size), size)


def pair_of(values, pair):
    low = values[:, 2 * pair : 2 * pair + 1]
    high = values[:, 2 * pair + 1 : 2 * pair + 2]
    return jnp.where(iota((values.shape[0], LANES), 1) < LANES // 2, low, high)


def spread(values, pairs):
    return jnp.concatenate([pair_of(values, p) for p in range(pairs)], axis=1)


def eights(v):
    return jnp.sum(v.reshape(v.shape[0] // 8, 8, v.shape[1]), axis=0)


def halves_of(v):
    high = v.astype(BF16)
    return high, (v - high.astype(F32)).astype(BF16)


def head_sums(v, gather):
    high, low = halves_of(v)
    return mul(high, gather, NN) + mul(low, gather, NN)


def remote(src, dst, send, recv, place, head):
    return pltpu.make_async_remote_copy(
        src_ref=src,
        dst_ref=dst,
        send_sem=send,
        recv_sem=recv,
        device_id=(place, head),
        device_id_type=MESH,
    )


def meet(count, parts):
    place, head = lax.axis_index("seq"), lax.axis_index("head")
    barrier = pltpu.get_barrier_semaphore()

    def along_seq(i, _):
        other = lax.rem(place + i, count)
        pl.semaphore_signal(barrier, inc=1, device_id=(other, head), device_id_type=MESH)
        return 0

    def along_head(i, _):
        other = lax.rem(head + i, parts)
        pl.semaphore_signal(barrier, inc=1, device_id=(place, other), device_id_type=MESH)
        return 0

    lax.fori_loop(1, count, along_seq, 0)
    lax.fori_loop(1, parts, along_head, 0)
    pl.semaphore_wait(barrier, count - 1 + parts - 1)


def loop(low, high, step):
    def one(i, _):
        step(i)
        return 0

    lax.fori_loop(low, high, one, 0)


def line_copy(count, src, dst, send, recv):
    place, head = lax.axis_index("seq"), lax.axis_index("head")

    def copy(i):
        other = lax.rem(place + i, count)
        return remote(src(other), dst(place), send.at[i], recv.at[i], other, head)

    return copy


def head_copy(parts, src, dst, send, recv):
    place, head = lax.axis_index("seq"), lax.axis_index("head")

    def copy(i):
        other = lax.rem(head + i, parts)
        return remote(src(other), dst(head), send.at[i], recv.at[i], place, other)

    return copy


def cut_of(count, seqs, state, inner):
    rows = max(16, seqs * state // count)
    lane_cuts = count * rows // (seqs * state)
    return rows, lane_cuts, inner // lane_cuts


def piece_of(k, count, seqs, state, inner):
    rows, lane_cuts, lanes = cut_of(count, seqs, state, inner)
    each = count // seqs
    seq, rest = k // each, lax.rem(k, each)
    row = pl.multiple_of(rest // lane_cuts * rows, rows)
    if lane_cuts == 1:
        return seq, pl.ds(row, rows), slice(None)
    lane = pl.multiple_of(lax.rem(rest, lane_cuts) * lanes, lanes)
    return seq, pl.ds(row, rows), pl.ds(lane, lanes)


def carry_exchange(dims, local, arrived, passed, incoming, decay_ref, sems, reverse):
    count, _, seqs, _, inner, _, state = dims
    place, head = lax.axis_index("seq"), lax.axis_index("head")
    send, recv, back_send, back_recv = sems
    piece = functools.partial(piece_of, count=count, seqs=seqs, state=state, inner=inner)
    rows, _, lanes = cut_of(count, seqs, state, inner)

    def at(ref, k):
        seq, row, lane = piece(k)
        return ref.at[seq, row, lane]

    out = line_copy(count, lambda other: at(local, other), lambda k: arrived.at[k], send, recv)

    def back(j):
        i = lax.rem(j - place + count, count)
        return remote(
            passed.at[j], at(incoming, place), back_send.at[i], back_recv.at[i], j, head
        )

    def start():
        loop(1, count, lambda i: out(i).start())
        seq, row, lane = piece(place)
        arrived[place] = local[seq, row, lane]

    def carry():
        seq, row, lane = piece(place)
        held = jnp.zeros((rows, lanes), F32)
        for step in range(count):
            j = count - 1 - step if reverse else step
            i = lax.rem(place - j + count, count)

            @pl.when(j != place)
            def _():
                out(i).wait_recv()

            passed[j] = held.astype(passed.dtype)

            @pl.when(j != place)
            def _():
                back(j).start()

            @pl.when(j == place)
            def _():
                incoming[seq, row, lane] = passed[j]

            decay = decay_ref[seq, pl.ds(j, 1), lane]
            held = decay * held + arrived[j].astype(F32)

    def finish():
        def one(i):
            out(i).wait_send()
            back(lax.rem(place + i, count)).wait()

        loop(1, count, one)

    return start, carry, finish


def forward_kernel(
    dims,
    x_ref,
    gate_ref,
    small_ref,
    chan_ref,
    vec_ref,
    unpack_ref,
    expand_ref,
    gather_ref,
    cot_ref,
    wout_ref,
    xact_ref,
    bc_ref,
    conv_ref,
    convbc_ref,
    dt_ref,
    cum_ref,
    states_ref,
    ng_ref,
    dgate_ref,
    dy_ref,
    dyy_ref,
    decay_ref,
    sums_ref,
    edge_x,
    edge_s,
    ext,
    extbc,
    bc_all,
    fresh,
    y_ref,
    dng_ref,
    gated_ref,
    decays,
    local,
    arrived,
    passed,
    incoming,
    rowsum,
    edge_send,
    edge_recv,
    dec_send,
    dec_recv,
    bc_send,
    bc_recv,
    st_send,
    st_recv,
    back_send,
    back_recv,
    row_send,
    row_recv,
):
    count, parts, seqs, block, inner, heads, state = dims
    place, head = lax.axis_index("seq"), lax.axis_index("head")
    chunks = block // CHUNK
    pairs = heads // 2
    total = seqs * chunks
    meet(count, parts)

    def edge_copies(ahead):
        copies = []
        for s in range(seqs):
            rows = pl.ds(s * block + block - 8, 8)
            for k, (src, dst) in enumerate(((x_ref, edge_x), (small_ref, edge_s))):
                copies.append(
                    remote(
                        src.at[rows], dst.at[s], edge_send.at[k, s], edge_recv.at[k, s], ahead, head
                    )
                )
        return copies

    after = lax.rem(place + 1, count)

    @pl.when(place < count - 1)
    def _():
        for c in edge_copies(after):
            c.start()

    lower = (iota((CHUNK, CHUNK), 0) >= iota((CHUNK, CHUNK), 1)).astype(F32)
    for s in range(seqs):

        def steps(c, logs):
            rows = ds((s * chunks + c) * CHUNK, CHUNK)
            dt = softplus(small_ref[rows, :] + vec_ref[5:6, :])
            cum = mul(lower, dt * vec_ref[6:7, :], NN, EXACT)
            dt_ref[rows, :] = dt
            cum_ref[rows, :] = cum
            return logs + cum[CHUNK - 1 :, :]

        logs = lax.fori_loop(0, chunks, steps, jnp.zeros((1, LANES), F32))
        decays[place, s : s + 1, :] = jnp.exp(logs)

    dec = line_copy(count, lambda _: decays.at[place], lambda k: decays.at[k], dec_send, dec_recv)
    loop(1, count, lambda i: dec(i).start())

    @pl.when(place > 0)
    def _():
        for c in edge_copies(after):
            c.wait_recv()

    @pl.when(place == 0)
    def _():
        edge_x[...] = jnp.zeros_like(edge_x)
        edge_s[...] = jnp.zeros_like(edge_s)

    def packed(low, high):
        return jnp.where(
            iota(low.shape, 1) < LANES // 2, pltpu.roll(low, LANES // 2, 1), high
        )

    extbc[0:8, :] = packed(edge_s[0], edge_s[1])
    extbc[8:, :] = packed(small_ref[0:block, :], small_ref[block:, :])
    conv = vec_ref[4:5, :]
    for k in range(KER):
        conv = conv + vec_ref[k : k + 1, :] * extbc[pl.ds(8 - (KER - 1) + k, block), :]
    convbc_ref[...] = conv
    bc_all[head] = (conv * sigmoid(conv)).astype(BF16)
    share = head_copy(parts, lambda _: bc_all.at[head], lambda k: bc_all.at[k], bc_send, bc_recv)
    loop(1, parts, lambda i: share(i).start())

    def x_chunk(t):
        rows = ds(t * CHUNK, CHUNK)
        s, c = t // chunks, lax.rem(t, chunks)
        before = pl.ds(pl.multiple_of(jnp.maximum(t * CHUNK - 8, 0), 8), 8)
        for b in range(inner // LANES):
            lane = slice(b * LANES, (b + 1) * LANES)
            ext[0:8, lane] = jnp.where(c == 0, edge_x[s, :, lane], x_ref[before, lane])
            ext[8:, lane] = x_ref[rows, lane]
            conv = chan_ref[4:5, lane]
            for k in range(KER):
                conv = conv + chan_ref[k : k + 1, lane] * ext[pl.ds(8 - (KER - 1) + k, CHUNK), lane]
            conv_ref[rows, lane] = conv
            xact_ref[rows, lane] = (conv * sigmoid(conv)).astype(BF16)

    loop(0, total, x_chunk)

    loop(1, parts, lambda i: share(i).wait())
    everything = jnp.concatenate([bc_all[k] for k in range(parts)], axis=1)
    for s in range(seqs):
        bc_ref[s * block : (s + 1) * block, :] = mul(everything, unpack_ref[s], NN).astype(BF16)

    for s in range(seqs):

        def add(c, held):
            t = s * chunks + c
            rows = ds(t * CHUNK, CHUNK)
            cum, dt = cum_ref[rows, :], dt_ref[rows, :]
            end = cum[CHUNK - 1 :, :]
            tail = jnp.exp(end - cum) * dt
            weighted = jnp.concatenate(
                [
                    (
                        xact_ref[rows, p * LANES : (p + 1) * LANES].astype(F32) * pair_of(tail, p)
                    ).astype(BF16)
                    for p in range(pairs)
                ],
                axis=1,
            )
            new = mul(bc_ref[rows, 0:state], weighted, TN)
            fresh[t] = new
            return spread(jnp.exp(end), pairs) * held + new

        held = lax.fori_loop(0, chunks, add, jnp.zeros((state, inner), F32))
        local[s] = held

    start, carry, finish = carry_exchange(
        dims,
        local,
        arrived,
        passed,
        incoming,
        decay_ref,
        (st_send, st_recv, back_send, back_recv),
        False,
    )
    start()

    def within(t):
        rows = ds(t * CHUNK, CHUNK)
        cum, dt = cum_ref[rows, :], dt_ref[rows, :]
        cum_t = cum.T
        scores = mul(bc_ref[rows, state:], bc_ref[rows, 0:state], NT)
        seen = iota((CHUNK, CHUNK), 0) >= iota((CHUNK, CHUNK), 1)
        side = iota((CHUNK, LANES), 1) < LANES // 2
        for p in range(pairs):
            lane = slice(p * LANES, (p + 1) * LANES)
            stepped = (xact_ref[rows, lane].astype(F32) * pair_of(dt, p)).astype(BF16)
            halves = []
            for h in (2 * p, 2 * p + 1):
                gap = cum[:, h : h + 1] - cum_t[h : h + 1, :]
                mixing = (scores * jnp.exp(jnp.where(seen, gap, -1e30))).astype(BF16)
                halves.append(mul(mixing, stepped, NN))
            y_ref[rows, lane] = jnp.where(side, halves[0], halves[1])

    loop(0, total, within)

    loop(1, count, lambda i: dec(i).wait())
    for s in range(seqs):
        decay_ref[s] = mul(decays[:, s, :], expand_ref[...], NN, EXACT)
    carry()

    wide = 2 * LANES

    def back_project(i):
        s, b = i // (inner // wide), lax.rem(i, inner // wide)
        rows, lane = ds(s * block, block), ds(b * wide, wide)
        dng_ref[rows, lane] = mul(cot_ref[rows, :], wout_ref[lane, :], NT)

    loop(0, seqs * (inner // wide), back_project)
    finish()

    for s in range(seqs):

        def gate(c, held):
            t = s * chunks + c
            rows = ds(t * CHUNK, CHUNK)
            cum = cum_ref[rows, :]
            grown = jnp.exp(cum)
            states_ref[t] = held
            high, low = halves_of(held)
            c_rows = bc_ref[rows, state:]
            carried = mul(c_rows, high, NN) + mul(c_rows, low, NN)
            square = jnp.zeros((CHUNK, LANES), F32)
            cross = jnp.zeros((CHUNK, LANES), F32)
            for p in range(pairs):
                lane = slice(p * LANES, (p + 1) * LANES)
                y = y_ref[rows, lane] + carried[:, lane] * pair_of(grown, p)
                y_ref[rows, lane] = y
                out = y + chan_ref[6:7, lane] * xact_ref[rows, lane].astype(F32)
                pre = gate_ref[rows, lane]
                gated = out * (pre * sigmoid(pre))
                gated_ref[rows, lane] = gated
                square = square + gated * gated
                cross = cross + dng_ref[rows, lane] * chan_ref[5:6, lane] * gated
            at = iota((CHUNK, LANES), 1)
            both = jnp.where(
                at == 0,
                jnp.sum(square, axis=1, keepdims=True),
                jnp.where(at == 1, jnp.sum(cross, axis=1, keepdims=True), 0.0),
            )
            rowsum[head, t] = both.T[0:8, :]
            return spread(grown[CHUNK - 1 :, :], pairs) * held + fresh[t]

        lax.fori_loop(0, chunks, gate, incoming[s].astype(F32))

    rows_copy = head_copy(
        parts, lambda _: rowsum.at[head], lambda k: rowsum.at[k], row_send, row_recv
    )
    loop(1, parts, lambda i: rows_copy(i).start())
    loop(1, parts, lambda i: rows_copy(i).wait())
    sums_ref[...] = jnp.zeros_like(sums_ref)
    channels = inner * parts

    def outputs(t):
        rows = ds(t * CHUNK, CHUNK)
        sums = rowsum[0, t]
        for k in range(1, parts):
            sums = sums + rowsum[k, t]
        turned = jnp.concatenate([sums, jnp.zeros((CHUNK - 8, LANES), F32)], axis=0).T
        scale = lax.rsqrt(turned[:, 0:1] / channels + EPSILON)
        pull = scale * scale * scale * (turned[:, 1:2] / channels)
        dyy = jnp.zeros((CHUNK, LANES), F32)
        for p in range(pairs):
            lane = slice(p * LANES, (p + 1) * LANES)
            pre = gate_ref[rows, lane]
            sg = sigmoid(pre)
            gated, y = gated_ref[rows, lane], y_ref[rows, lane]
            x = xact_ref[rows, lane].astype(F32)
            gain = chan_ref[5:6, lane]
            scaled = gated * scale
            ng_ref[rows, lane] = (scaled * gain).astype(BF16)
            dng = dng_ref[rows, lane]
            d_gated = scale * (dng * gain) - gated * pull
            d_ssd = d_gated * (pre * sg)
            out = y + chan_ref[6:7, lane] * x
            dgate_ref[rows, lane] = (d_gated * out * (sg * (1.0 + pre * (1.0 - sg)))).astype(BF16)
            dy = d_ssd.astype(BF16)
            dy_ref[rows, lane] = dy
            sums_ref[0:8, lane] += eights(dng * scaled)
            sums_ref[8:16, lane] += eights(d_ssd * x)
            dyy = dyy + head_sums(dy.astype(F32) * y, gather_ref[lane, :])
        dyy_ref[rows, :] = dyy

    loop(0, total, outputs)

    @pl.when(place < count - 1)
    def _():
        for c in edge_copies(after):
            c.wait_send()


def vmem(shape, kind):
    return pltpu.VMEM(shape, kind)


def forward(dims, *operands):
    count, parts, seqs, block, inner, heads, state = dims
    rows = seqs * block
    chunks = rows // CHUNK
    cut_rows, _, cut_lanes = cut_of(count, seqs, state, inner)
    spec = pl.BlockSpec(memory_space=pltpu.VMEM)
    line, ring = pltpu.SemaphoreType.DMA((count,)), pltpu.SemaphoreType.DMA((parts,))
    edge = pltpu.SemaphoreType.DMA((2, seqs))
    outs = [
        ((rows, inner), BF16),
        ((rows, 2 * state), BF16),
        ((rows, inner), F32),
        ((block, LANES), F32),
        ((rows, LANES), F32),
        ((rows, LANES), F32),
        ((chunks, state, inner), F32),
        ((rows, inner), BF16),
        ((rows, inner), BF16),
        ((rows, inner), BF16),
        ((rows, LANES), F32),
        ((seqs, count, inner), F32),
        ((16, inner), F32),
    ]
    return pl.pallas_call(
        functools.partial(forward_kernel, dims),
        out_shape=[jax.ShapeDtypeStruct(*o) for o in outs],
        in_specs=[spec] * len(operands),
        out_specs=[spec] * len(outs),
        scratch_shapes=[
            vmem((seqs, 8, inner), F32),
            vmem((seqs, 8, LANES), F32),
            vmem((CHUNK + 8, inner), F32),
            vmem((block + 8, LANES), F32),
            vmem((parts, block, LANES), BF16),
            vmem((chunks, state, inner), F32),
            vmem((rows, inner), F32),
            vmem((rows, inner), F32),
            vmem((rows, inner), F32),
            vmem((count, 8, LANES), F32),
            vmem((seqs, state, inner), F32),
            vmem((count, cut_rows, cut_lanes), F32),
            vmem((count, cut_rows, cut_lanes), F32),
            vmem((seqs, state, inner), F32),
            vmem((parts, chunks, 8, LANES), F32),
            edge,
            edge,
            line,
            line,
            ring,
            ring,
            line,
            line,
            line,
            line,
            ring,
            ring,
        ],
        compiler_params=pltpu.CompilerParams(
            collective_id=2, has_side_effects=True, vmem_limit_bytes=VMEM_LIMIT
        ),
        name="mixer_forward",
    )(*operands)


def ring_place(count):
    place = lax.axis_index("seq")
    row, col = place // 2, place % 2
    return jnp.where(col == 0, row, count - 1 - row)


def ring_device(rank, count):
    return jnp.where(rank < count // 2, 2 * rank, 2 * (count - 1 - rank) + 1)


def ring_steps(count, plan, outs, bufs, sems):
    rs_send, rs_recv, ag_send, ag_recv, keep_sem = sems
    head = lax.axis_index("head")
    rank = ring_place(count)
    peers = {
        1: ring_device(lax.rem(rank + 1, count), count),
        -1: ring_device(lax.rem(rank + count - 1, count), count),
    }

    def chunk_of(direction, step):
        return lax.rem(rank - direction * step + 2 * count, count)

    def partial(i, chunk):
        left, right, first, cols, _ = plan[i]
        rows = left.shape[0] // count
        return mul(left[ds(chunk * rows, rows), :], right[:, first : first + cols], NN)

    def block_of(i, chunk):
        return outs[i].at[ds(chunk * bufs[i].shape[1], bufs[i].shape[1])]

    def rs(i, step):
        return remote(
            bufs[i].at[step],
            bufs[i].at[step + 1],
            rs_send.at[i, step],
            rs_recv.at[i, step],
            peers[plan[i][4]],
            head,
        )

    def ag(i, step, first=False):
        there = block_of(i, chunk_of(plan[i][4], step - 1))
        here = bufs[i].at[count - 1] if first else there
        return remote(
            here, there, ag_send.at[i, step], ag_recv.at[i, step], peers[plan[i][4]], head
        )

    def keep(i):
        block = block_of(i, chunk_of(plan[i][4], count - 1))
        return pltpu.make_async_copy(bufs[i].at[count - 1], block, keep_sem.at[i])

    def begin(i):
        bufs[i][0] = partial(i, chunk_of(plan[i][4], 0)).astype(BF16)
        rs(i, 0).start()

    def bounds(slot, slots, steps):
        low = lax.div(steps * slot + slots - 1, slots)
        return 1 + low, 1 + lax.div(steps * (slot + 1) + slots - 1, slots)

    def advance(streams, slot, slots):
        def step_of(step):
            for i in streams:
                own = partial(i, chunk_of(plan[i][4], step))
                rs(i, step - 1).wait_recv()
                bufs[i][step] = (own + bufs[i][step].astype(F32)).astype(BF16)

                @pl.when(step < count - 1)
                def _():
                    rs(i, step).start()

                @pl.when(step == count - 1)
                def _():
                    ag(i, 0, True).start()
                    keep(i).start()

        loop(*bounds(slot, slots, count - 1), step_of)

    def pass_on(streams, slot, slots):
        def step_of(step):
            for i in streams:
                ag(i, step - 1).wait_recv()
                ag(i, step).start()

        loop(*bounds(slot, slots, count - 2), step_of)

    def pass_end(streams):
        for i in streams:
            ag(i, count - 2).wait_recv()

    def drain(streams):
        def one(step):
            for i in streams:
                rs(i, step).wait_send()
                ag(i, step).wait_send()

        loop(0, count - 1, one)
        for i in streams:
            keep(i).wait()

    return begin, advance, pass_on, pass_end, drain


def finish_kernel(gr, gl, xr, xl, wr, wl, gin_ref, wout_ref, small_ref):
    ihalf, half = gr.shape[1], wr.shape[1]
    gin_ref[:, 0, 0:ihalf] = gr[...].astype(F32)
    gin_ref[:, 0, ihalf:] = gl[...].astype(F32)
    gin_ref[:, 1, 0:ihalf] = xr[...].astype(F32)
    gin_ref[:, 1, ihalf:] = xl[:, 0:ihalf].astype(F32)
    small_ref[...] = xl[:, ihalf:].astype(F32).T
    wout_ref[:, 0:half] = wr[...].astype(F32)
    wout_ref[:, half:] = wl[...].astype(F32)


def finish_weights(width, inner, streams):
    steps = width // (2 * LANES)
    tall, low = width // steps, inner // steps
    wr, wl, gr, gl, xr, xl = streams

    def block(array_in, rows):
        return pl.BlockSpec((rows, array_in.shape[1]), lambda i: (i, 0))

    return pl.pallas_call(
        finish_kernel,
        grid=(steps,),
        in_specs=[block(a, tall) for a in (gr, gl, xr, xl)] + [block(a, low) for a in (wr, wl)],
        out_specs=[
            pl.BlockSpec((tall, 2, inner), lambda i: (i, 0, 0)),
            pl.BlockSpec((low, width), lambda i: (i, 0)),
            pl.BlockSpec((LANES, tall), lambda i: (0, i)),
        ],
        out_shape=[
            jax.ShapeDtypeStruct((width, 2, inner), F32),
            jax.ShapeDtypeStruct((inner, width), F32),
            jax.ShapeDtypeStruct((LANES, width), F32),
        ],
        compiler_params=pltpu.CompilerParams(vmem_limit_bytes=VMEM_LIMIT),
        name="finish_weights",
    )(gr, gl, xr, xl, wr, wl)


def backward_kernel(
    dims,
    dy_ref,
    xact_ref,
    bc_ref,
    conv_ref,
    convbc_ref,
    dt_ref,
    cum_ref,
    states_ref,
    dyy_ref,
    decay_ref,
    x_ref,
    small_ref,
    chan_ref,
    vec_ref,
    pack_ref,
    gather_ref,
    normed_t_ref,
    ng_t_ref,
    cot_ref,
    dgate_ref,
    small_weight_ref,
    sums_ref,
    gain_ref,
    row_scale_ref,
    tokens_ref,
    weight_ref,
    *rest,
):
    count, parts, seqs, block, inner, heads, state = dims
    outs, rest = rest[:6], rest[6:]
    grad_ref, total_ref, *rest = rest
    bufs, rest = rest[:6], rest[6:]
    (
        dx_ref,
        gx_ref,
        gbc_ref,
        gdt_ref,
        weights,
        conv_buf,
        dn_out,
        dn_in,
        token_buf,
        rowsum,
        shared,
        rs_send,
        rs_recv,
        ag_send,
        ag_recv,
        keep_sem,
        weight_sem,
        conv_sem,
        token_sem,
        dn_send,
        dn_recv,
        row_send,
        row_recv,
        sum_send,
        sum_recv,
        *rest,
    ) = rest
    (
        dconv,
        dconvbc,
        prebc,
        dbc,
        ddt,
        added,
        local,
        arrived,
        passed,
        incoming,
        bc_out,
        bc_in,
        edge_send,
        edge_recv,
        bc_send,
        bc_recv,
        st_send,
        st_recv,
        back_send,
        back_recv,
    ) = rest
    place, head = lax.axis_index("seq"), lax.axis_index("head")
    rank = ring_place(count)
    chunks = block // CHUNK
    pairs = heads // 2
    total = seqs * chunks
    rows_all = seqs * block
    width = cot_ref.shape[1]
    cols = width // parts
    half, ihalf = width // 2, inner // 2
    plan = (
        (ng_t_ref, cot_ref, 0, half, 1),
        (ng_t_ref, cot_ref, half, half, -1),
        (normed_t_ref, dgate_ref, 0, ihalf, 1),
        (normed_t_ref, dgate_ref, ihalf, ihalf, -1),
        (normed_t_ref, dx_ref, 0, ihalf, 1),
        (normed_t_ref, dx_ref, ihalf, ihalf + LANES, -1),
    )
    begin, advance, pass_on, pass_end, drain = ring_steps(
        count, plan, outs, bufs, (rs_send, rs_recv, ag_send, ag_recv, keep_sem)
    )
    out_streams, gate_streams, x_streams = (0, 1), (2, 3), (4, 5)
    meet(count, parts)
    gdt_ref[...] = jnp.zeros_like(gdt_ref)

    token_copy = pltpu.make_async_copy(
        tokens_ref.at[:, pl.ds(pl.multiple_of(head * cols, cols), cols)], token_buf, token_sem
    )
    token_copy.start()

    def weight_copy(i):
        other = lax.rem(head + i, parts)
        return pltpu.make_async_copy(
            weight_ref.at[:, pl.ds(pl.multiple_of(other * cols, cols), cols)],
            weights.at[lax.rem(i + 1, 2)],
            weight_sem.at[lax.rem(i + 1, 2)],
        )

    def conv_copy(q):
        t = q // chunks * chunks + chunks - 1 - lax.rem(q, chunks)
        slot = lax.rem(q, 2)
        return pltpu.make_async_copy(
            conv_ref.at[ds(t * CHUNK, CHUNK)], conv_buf.at[slot], conv_sem.at[slot]
        )

    conv_copy(0).start()
    weight_copy(1).start()
    for i in out_streams + gate_streams:
        begin(i)

    for s in range(seqs):

        def alone(i, held):
            t = s * chunks + chunks - 1 - i
            rows = ds(t * CHUNK, CHUNK)
            grown = jnp.exp(cum_ref[rows, :])
            weighted = jnp.concatenate(
                [
                    (
                        dy_ref[rows, p * LANES : (p + 1) * LANES].astype(F32) * pair_of(grown, p)
                    ).astype(BF16)
                    for p in range(pairs)
                ],
                axis=1,
            )
            new = mul(bc_ref[rows, state:], weighted, TN)
            added[t] = new
            return spread(grown[CHUNK - 1 :, :], pairs) * held + new

        held = lax.fori_loop(0, chunks, alone, jnp.zeros((state, inner), F32))
        local[s] = held.astype(BF16)

    start, carry, finish = carry_exchange(
        dims,
        local,
        arrived,
        passed,
        incoming,
        decay_ref,
        (st_send, st_recv, back_send, back_recv),
        True,
    )
    first = out_streams + gate_streams
    slots = 2 + total
    start()
    advance(first, 0, slots)
    carry()
    advance(first, 1, slots)
    finish()

    side = iota((CHUNK, LANES), 1) < LANES // 2
    seen = iota((CHUNK, CHUNK), 0) <= iota((CHUNK, CHUNK), 1)
    upper = seen.astype(F32)
    for s in range(seqs):

        def chunk(i, held):
            t = s * chunks + chunks - 1 - i
            rows = ds(t * CHUNK, CHUNK)
            out_rows = ds((s * chunks + chunks - 1 - i) * CHUNK, CHUNK)
            turn = s * chunks + i
            conv_copy(turn).wait()

            @pl.when(turn + 1 < total)
            def _():
                conv_copy(turn + 1).start()

            cum, dt = cum_ref[rows, :], dt_ref[rows, :]
            cum_t = cum.T
            grown = jnp.exp(cum)
            end = cum[CHUNK - 1 :, :]
            tail = jnp.exp(end - cum)
            b_rows, c_rows = bc_ref[rows, 0:state], bc_ref[rows, state:]
            scores = mul(b_rows, c_rows, NT)
            low = held.astype(BF16)
            begun = states_ref[t]
            begun_high, begun_low = halves_of(begun)
            pulled = mul(b_rows, low, NN)
            grad_scores = jnp.zeros((CHUNK, CHUNK), F32)
            d_x_sum = jnp.zeros((CHUNK, LANES), F32)
            d_fall = jnp.zeros((CHUNK, LANES), F32)
            into_x = []
            into_y = []
            last = []
            for p in range(pairs):
                lane = slice(p * LANES, (p + 1) * LANES)
                x, dy = xact_ref[rows, lane], dy_ref[rows, lane]
                xf, dyf = x.astype(F32), dy.astype(F32)
                dt_p, tail_p = pair_of(dt, p), pair_of(tail, p)
                stepped = xf * dt_p
                low_step = stepped.astype(BF16)
                halves = []
                for k, h in enumerate((2 * p, 2 * p + 1)):
                    gap = cum_t[h : h + 1, :] - cum[:, h : h + 1]
                    fade = jnp.exp(jnp.where(seen, gap, -1e30))
                    own = jnp.where(side if k == 0 else ~side, low_step, jnp.zeros_like(low_step))
                    grad_scores = grad_scores + mul(own, dy, NT) * fade
                    halves.append(mul((scores * fade).astype(BF16), dy, NN))
                from_state = pulled[:, lane] * tail_p
                d_step_x = jnp.where(side, halves[0], halves[1]) + from_state
                rounded = low_step.astype(F32)
                d_x_sum = d_x_sum + head_sums(xf * d_step_x, gather_ref[lane, :])
                d_fall = d_fall + head_sums(rounded * d_step_x, gather_ref[lane, :])
                into_x.append((stepped * tail_p).astype(BF16))
                into_y.append((dyf * pair_of(grown, p)).astype(BF16))
                last.append(jnp.sum(rounded * from_state, axis=0, keepdims=True))
                conv = conv_buf[lax.rem(turn, 2), :, lane]
                sg = sigmoid(conv)
                d_act = dt_p * d_step_x + chan_ref[6:7, lane] * dyf
                dconv[s, ds((chunks - 1 - i) * CHUNK, CHUNK), lane] = d_act * (
                    sg * (1.0 + conv * (1.0 - sg))
                )
            low_scores = grad_scores.astype(BF16)
            d_b = mul(low_scores, c_rows, NN) + mul(jnp.concatenate(into_x, axis=1), low, NT)
            into_y = jnp.concatenate(into_y, axis=1)
            d_c = mul(low_scores, b_rows, TN) + mul(into_y, begun_high, NT)
            d_c = d_c + mul(into_y, begun_low, NT)
            dbc[out_rows, 0:state] = d_b.astype(BF16)
            dbc[out_rows, state:] = d_c.astype(BF16)
            fall = spread(grown[CHUNK - 1 :, :], pairs)
            ends = jnp.concatenate(last, axis=1) + fall * jnp.sum(
                held * begun, axis=0, keepdims=True
            )
            ends = head_sums(jnp.broadcast_to(ends, (8, inner)), gather_ref[...])[0:1, :]
            d_log = mul(upper, dyy_ref[rows, :] - d_fall, NN, EXACT) + ends
            d_step = d_x_sum + vec_ref[6:7, :] * d_log
            d_dt = d_step * sigmoid(small_ref[rows, :] + vec_ref[5:6, :])
            gdt_ref[0:8, :] += eights(d_dt)
            gdt_ref[8:16, :] += eights(d_log * (dt * vec_ref[6:7, :]))
            ddt[out_rows, :] = d_dt
            advance(first, 2 + s * chunks + i, slots)
            return fall * held + added[t]

        lax.fori_loop(0, chunks, chunk, incoming[s].astype(F32))

    def pack(k):
        piece = mul(dbc[0:block, :], pack_ref[k, 0], NN)
        return (piece + mul(dbc[block:, :], pack_ref[k, 1], NN)).astype(BF16)

    def pack_one(k):
        bc_out[k] = pack(k)

    loop(0, parts, pack_one)
    share = head_copy(parts, lambda k: bc_out.at[k], lambda k: bc_in.at[k], bc_send, bc_recv)
    loop(1, parts, lambda i: share(i).start())

    before = lax.rem(place + count - 1, count)

    def edge_copy(s):
        return remote(
            dconv.at[s, pl.ds(0, 8)],
            dconv.at[s, pl.ds(block, 8)],
            edge_send.at[s],
            edge_recv.at[s],
            before,
            head,
        )

    def edge_bc():
        return remote(
            dconvbc.at[pl.ds(0, 8)],
            dconvbc.at[pl.ds(block, 8)],
            edge_send.at[seqs],
            edge_recv.at[seqs],
            before,
            head,
        )

    @pl.when(place > 0)
    def _():
        for s in range(seqs):
            edge_copy(s).start()

    loop(1, parts, lambda i: share(i).wait())
    bc_in[head] = bc_out[head]
    d_act = bc_in[0].astype(F32)
    for k in range(1, parts):
        d_act = d_act + bc_in[k].astype(F32)
    conv = convbc_ref[...]
    sg = sigmoid(conv)
    dconvbc[0:block, :] = d_act * (sg * (1.0 + conv * (1.0 - sg)))

    @pl.when(place > 0)
    def _():
        edge_bc().start()

    @pl.when(place < count - 1)
    def _():
        for s in range(seqs):
            edge_copy(s).wait_recv()

    @pl.when(place == count - 1)
    def _():
        for s in range(seqs):
            dconv[s, block : block + 8, :] = jnp.zeros((8, inner), F32)

    gx_ref[...] = jnp.zeros_like(gx_ref)

    def x_chunk(t):
        rows = ds(t * CHUNK, CHUNK)
        s, c = t // chunks, lax.rem(t, chunks)
        for p in range(pairs):
            lane = slice(p * LANES, (p + 1) * LANES)
            x = x_ref[rows, lane]
            pre = jnp.zeros((CHUNK, LANES), F32)
            here = dconv[s, pl.ds(pl.multiple_of(c * CHUNK, CHUNK), CHUNK + 8), lane]
            for k in range(KER):
                off = KER - 1 - k
                d = pltpu.roll(here, CHUNK + 8 - off, 0)[:CHUNK] if off else here[:CHUNK]
                pre = pre + chan_ref[k : k + 1, lane] * d
                gx_ref[8 * k : 8 * k + 8, lane] += eights(x * d)
                if k == KER - 1:
                    gx_ref[8 * KER : 8 * KER + 8, lane] += eights(d)
            dx_ref[rows, lane] = pre.astype(BF16)
        pass_on(out_streams, t, 2 * total)

    loop(0, total, x_chunk)

    @pl.when(place < count - 1)
    def _():
        edge_bc().wait_recv()

    @pl.when(place == count - 1)
    def _():
        dconvbc[block : block + 8, :] = jnp.zeros((8, LANES), F32)

    low, high = small_ref[0:block, :], small_ref[block:, :]
    prebc[...] = jnp.where(
        iota(low.shape, 1) < LANES // 2, pltpu.roll(low, LANES // 2, 1), high
    )
    pre = jnp.zeros((block, LANES), F32)
    for k in range(KER):
        d = dconvbc[pl.ds(KER - 1 - k, block), :]
        pre = pre + vec_ref[k : k + 1, :] * d
        gbc_ref[8 * k : 8 * k + 8, :] = eights(prebc[...] * d)
    gbc_ref[8 * KER : 8 * KER + 8, :] = eights(dconvbc[0:block, :])
    at = iota((block, LANES), 1)
    for s in range(seqs):
        rows = slice(s * block, (s + 1) * block)
        mine = pre if s == seqs - 1 else pltpu.roll(pre, LANES // 2, 1)
        step = jnp.where(at < heads, ddt[rows, :], 0.0)
        dx_ref[rows, inner:] = jnp.where(at < LANES // 2, step, mine).astype(BF16)

    for i in x_streams:
        begin(i)

    tall = 2 * CHUNK

    def dn_copy(i):
        other = lax.rem(head + i, parts)
        return remote(
            dn_out.at[other], dn_in.at[head], dn_send.at[i], dn_recv.at[i], place, other
        )

    def d_normed(i):
        other = lax.rem(head + i, parts)
        slot = lax.rem(i + 1, 2)

        @pl.when(i < parts)
        def _():
            weight_copy(i + 1).start()

        weight_copy(i).wait()
        mine = small_weight_ref[pl.ds(pl.multiple_of(other * cols, cols), cols), :]

        def some(r):
            rows = ds(r * tall, tall)
            part = mul(dgate_ref[rows, :], weights[slot, 0], NT)
            part = part + mul(dx_ref[rows, 0:inner], weights[slot, 1], NT)
            part = part + mul(dx_ref[rows, inner:], mine, NT)
            dn_out[other, rows, :] = part.astype(BF16)

        loop(0, rows_all // tall, some)

        @pl.when(i < parts)
        def _():
            dn_copy(i).start()

    def d_normed_step(i):
        d_normed(i)
        advance(x_streams, i - 1, parts)
        pass_on(out_streams, total + i - 1, 2 * total)

    loop(1, parts + 1, d_normed_step)
    for i in range(parts, total):
        pass_on(out_streams, total + i, 2 * total)
    slots = 2 * total + 2
    pass_on(gate_streams + x_streams, 0, slots)

    loop(1, parts, lambda i: dn_copy(i).wait())
    dn_in[head] = dn_out[head]
    token_copy.wait()
    my_cols = pl.ds(pl.multiple_of(head * cols, cols), cols)

    def own(t, grads):
        rows = ds(t * CHUNK, CHUNK)
        d = dn_in[0, rows, :].astype(F32)
        for k in range(1, parts):
            d = d + dn_in[k, rows, :].astype(F32)
        token = token_buf[rows, :].astype(F32)
        grads = grads + eights(d * (token * row_scale_ref[rows, :]))
        d = d * gain_ref[:, my_cols]
        grad_ref[rows, :] = d
        line = jnp.sum(d * token, axis=1, keepdims=True)
        line = jnp.where(iota((CHUNK, LANES), 1) == 0, line, 0.0)
        rowsum[head, t] = line.T[0:8, :]
        pass_on(gate_streams + x_streams, 1 + t, slots)
        return grads

    norm_grads = lax.fori_loop(0, total, own, jnp.zeros((8, cols), F32))
    rows_copy = head_copy(
        parts, lambda _: rowsum.at[head], lambda k: rowsum.at[k], row_send, row_recv
    )
    loop(1, parts, lambda i: rows_copy(i).start())

    def summed(ref, k):
        return jnp.sum(ref[8 * k : 8 * k + 8, :], axis=0, keepdims=True)

    shared[place] = jnp.zeros(shared.shape[1:], F32)
    for k in range(KER + 1):
        shared[place, k : k + 1, 0:inner] = summed(gx_ref, k)
        shared[place, k : k + 1, inner:] = summed(gbc_ref, k)
    for k in range(2):
        shared[place, KER + 1 + k : KER + 2 + k, 0:inner] = summed(sums_ref, k)
        shared[place, KER + 1 + k : KER + 2 + k, inner:] = summed(gdt_ref, k)
    shared[place, 7:8, 0:cols] = jnp.sum(norm_grads, axis=0, keepdims=True)
    sums_copy = line_copy(
        count, lambda _: shared.at[place], lambda k: shared.at[k], sum_send, sum_recv
    )
    loop(1, count, lambda i: sums_copy(i).start())
    pass_on(gate_streams + x_streams, 1 + total, slots)
    loop(1, parts, lambda i: rows_copy(i).wait())

    def finish_rows(t):
        rows = ds(t * CHUNK, CHUNK)
        sums = rowsum[0, t]
        for k in range(1, parts):
            sums = sums + rowsum[k, t]
        turned = jnp.concatenate([sums, jnp.zeros((CHUNK - 8, LANES), F32)], axis=0).T
        scale = row_scale_ref[rows, :]
        pull = scale * scale * scale * (turned[:, 0:1] / width)
        grad_ref[rows, :] = (
            scale * grad_ref[rows, :]
            - token_buf[rows, :].astype(F32) * pull
            + cot_ref[rows, my_cols].astype(F32)
        )
        pass_on(gate_streams + x_streams, 2 + total + t, slots)

    loop(0, total, finish_rows)
    loop(1, count, lambda i: sums_copy(i).wait())
    everything = shared[0]
    for k in range(1, count):
        everything = everything + shared[k]
    total_ref[...] = everything
    pass_end(out_streams + gate_streams + x_streams)
    drain(out_streams + gate_streams + x_streams)

    @pl.when(place > 0)
    def _():
        for s in range(seqs):
            edge_copy(s).wait_send()
        edge_bc().wait_send()


def backward(dims, *operands):
    count, parts, seqs, block, inner, heads, state = dims
    rows = seqs * block
    chunks = rows // CHUNK
    cut_rows, _, cut_lanes = cut_of(count, seqs, state, inner)
    normed_rows, ng_rows, width = (operands[k].shape[d] for k, d in ((16, 0), (17, 0), (18, 1)))
    cols = width // parts
    spec = pl.BlockSpec(memory_space=pltpu.VMEM)
    far = pl.BlockSpec(memory_space=pl.ANY)
    line, ring = pltpu.SemaphoreType.DMA((count,)), pltpu.SemaphoreType.DMA((parts,))
    edge = pltpu.SemaphoreType.DMA((seqs + 1,))
    half, ihalf = width // 2, inner // 2
    streams = [
        (ng_rows, half),
        (ng_rows, half),
        (normed_rows, ihalf),
        (normed_rows, ihalf),
        (normed_rows, ihalf),
        (normed_rows, ihalf + LANES),
    ]
    steps = pltpu.SemaphoreType.DMA((len(streams), count))
    outs = [(shape, BF16) for shape in streams]
    outs = outs + [((rows, cols), F32), ((8, inner + LANES), F32)]
    return pl.pallas_call(
        functools.partial(backward_kernel, dims),
        out_shape=[jax.ShapeDtypeStruct(*o) for o in outs],
        in_specs=[spec] * 3 + [far] + [spec] * (len(operands) - 6) + [far] * 2,
        out_specs=[far] * len(streams) + [spec] * 2,
        scratch_shapes=[vmem((count, r // count, c), BF16) for r, c in streams]
        + [
            vmem((rows, inner + LANES), BF16),
            vmem((8 * (KER + 1), inner), F32),
            vmem((8 * (KER + 1), LANES), F32),
            vmem((16, LANES), F32),
            vmem((2, 2, cols, inner), BF16),
            vmem((2, CHUNK, inner), F32),
            vmem((parts, rows, cols), BF16),
            vmem((parts, rows, cols), BF16),
            vmem((rows, cols), BF16),
            vmem((parts, chunks, 8, LANES), F32),
            vmem((count, 8, inner + LANES), F32),
            steps,
            steps,
            steps,
            steps,
            pltpu.SemaphoreType.DMA((len(streams),)),
            pltpu.SemaphoreType.DMA((2,)),
            pltpu.SemaphoreType.DMA((2,)),
            pltpu.SemaphoreType.DMA,
            ring,
            ring,
            ring,
            ring,
            line,
            line,
            vmem((seqs, block + 8, inner), F32),
            vmem((block + 8, LANES), F32),
            vmem((block, LANES), F32),
            vmem((rows, 2 * state), BF16),
            vmem((rows, LANES), F32),
            vmem((chunks, state, inner), F32),
            vmem((seqs, state, inner), BF16),
            vmem((count, cut_rows, cut_lanes), BF16),
            vmem((count, cut_rows, cut_lanes), BF16),
            vmem((seqs, state, inner), BF16),
            vmem((parts, block, LANES), BF16),
            vmem((parts, block, LANES), BF16),
            edge,
            edge,
            ring,
            ring,
            line,
            line,
            line,
            line,
        ],
        compiler_params=pltpu.CompilerParams(
            collective_id=3, has_side_effects=True, vmem_limit_bytes=VMEM_LIMIT
        ),
        name="mixer_backward",
    )(*operands)


def body(
    tokens,
    norm_gain,
    gate_input_weight,
    coefficient_weight,
    step_weight,
    conv_x,
    conv_bc,
    conv_bias_x,
    conv_bias_bc,
    dt_bias,
    a_log,
    d_skip,
    gate_gain,
    output_weight,
    cotangent,
):
    seqs, block, width = tokens.shape
    inner = gate_input_weight.shape[2]
    state_part = coefficient_weight.shape[2]
    heads = step_weight.shape[1]
    count, parts = lax.axis_size("seq"), lax.axis_size("head")
    my_head = lax.axis_index("head")
    state = state_part * parts
    rows = seqs * block
    col_count = width // parts
    half = LANES // 2
    dims = (count, parts, seqs, block, inner, heads, state)

    input_batch = tokens.astype(F32).reshape(rows, width)
    row_scale = lax.rsqrt(jnp.mean(input_batch * input_batch, axis=-1, keepdims=True) + EPSILON)
    normed = (input_batch * row_scale * norm_gain).astype(BF16)
    projected = jnp.einsum(
        "rp,pkw->krw", normed, gate_input_weight, preferred_element_type=F32
    )
    gate_pre, x_pre = projected[0], projected[1]
    small_weight = jnp.concatenate(
        [
            step_weight,
            jnp.zeros((width, half - heads), BF16),
            coefficient_weight.reshape(width, 2 * state_part),
        ],
        axis=1,
    )
    small = jnp.dot(normed, small_weight, preferred_element_type=F32)

    chan = jnp.concatenate(
        [
            conv_x,
            conv_bias_x[None],
            gate_gain[None],
            jnp.repeat(d_skip, inner // heads)[None],
            jnp.zeros((1, inner), F32),
        ]
    )
    twice = jnp.concatenate(
        [conv_bc.reshape(KER, 2 * state_part), conv_bias_bc.reshape(1, 2 * state_part)]
    )
    per_head = jnp.stack([dt_bias, -jnp.exp(a_log), jnp.zeros_like(a_log)])
    vec = jnp.concatenate(
        [
            jnp.concatenate([twice, twice], axis=1),
            jnp.pad(per_head, ((0, 0), (0, LANES - heads))),
        ]
    )
    device, lane, channel = jnp.meshgrid(
        jnp.arange(parts), jnp.arange(LANES), jnp.arange(2 * state), indexing="ij"
    )
    is_c, at = channel // state, channel % state
    unpack = jnp.stack(
        [
            (lane == s * half + is_c * state_part + at - device * state_part)
            & (at // state_part == device)
            for s in range(seqs)
        ]
    ).astype(BF16)
    pack = unpack.transpose(1, 0, 3, 2)
    unpack = unpack.reshape(seqs, parts * LANES, 2 * state)
    expand = jnp.arange(LANES)[:, None] == jnp.arange(inner)[None, :] // (inner // heads)
    gather = expand.T.astype(BF16)
    expand = expand.astype(F32)
    cot = cotangent.reshape(rows, width)

    xact, bc, conv, convbc, dt, cum, states, ng, dgate, dy, dyy, decay, sums = forward(
        dims,
        x_pre,
        gate_pre,
        small,
        chan,
        vec,
        unpack,
        expand,
        gather,
        cot,
        output_weight,
    )
    def padded(array_in):
        return jnp.pad(array_in, ((0, -array_in.shape[0] % (count * 16)), (0, 0)))

    mixer = jnp.dot(ng, output_weight, preferred_element_type=F32)
    mixed = lax.psum_scatter(
        mixer.astype(BF16), "head", scatter_dimension=1, tiled=True
    ).astype(F32)
    own_inputs = lax.dynamic_slice_in_dim(input_batch, my_head * col_count, col_count, 1)
    block_out = (own_inputs + mixed).astype(BF16)

    *streams, grad_input, sums = backward(
        dims,
        dy,
        xact,
        bc,
        conv,
        convbc,
        dt,
        cum,
        states,
        dyy,
        decay,
        x_pre,
        small,
        chan,
        vec,
        pack,
        gather,
        padded(normed.T),
        padded(ng.T),
        cot,
        dgate,
        small_weight,
        sums,
        norm_gain[None],
        row_scale,
        tokens.reshape(rows, width),
        gate_input_weight.transpose(1, 0, 2),
    )
    g_in, g_w_out, g_small = finish_weights(width, inner, streams)
    taps = sums[:, :inner]
    lanes = sums[:, inner:]
    taps_bc = (lanes[:, :half] + lanes[:, half:]).reshape(8, 2, state_part)
    return (
        block_out.reshape(seqs, block, col_count),
        grad_input.reshape(seqs, block, col_count),
        taps[KER + 3, :col_count],
        g_in,
        g_small[half:].reshape(2, state_part, width).transpose(2, 0, 1),
        g_small[:heads].T,
        taps[:KER],
        taps_bc[:KER],
        taps[KER],
        taps_bc[KER],
        lanes[KER + 1, :heads],
        lanes[KER + 2, :heads],
        taps[KER + 2].reshape(heads, inner // heads).sum(1),
        taps[KER + 1],
        g_w_out,
    )


def solution(mesh):
    placed = (
        P(None, "seq", None),
        P(),
        P(None, None, "head"),
        P(None, None, "head"),
        P(None, "head"),
        P(None, "head"),
        P(None, None, "head"),
        P("head"),
        P(None, "head"),
        P("head"),
        P("head"),
        P("head"),
        P("head"),
        P("head", None),
        P(None, "seq", None),
    )
    return jax.shard_map(
        body,
        mesh=mesh,
        in_specs=placed,
        out_specs=(
            P(None, "seq", "head"),
            P(None, "seq", "head"),
            P("head"),
            P(None, None, "head"),
            P(None, None, "head"),
            P(None, "head"),
            P(None, "head"),
            P(None, None, "head"),
            P("head"),
            P(None, "head"),
            P("head"),
            P("head"),
            P("head"),
            P("head"),
            P("head", None),
        ),
        check_vma=False,
    )
```

```python
import functools

import jax
import jax.numpy as jnp
import numpy as np
from jax import lax
from jax.experimental import pallas as pl
from jax.experimental.pallas import tpu as pltpu
from jax.sharding import PartitionSpec as P

KER = 4
EPSILON = 1e-05
CHUNK = 128
LANES = 128
MESH = pl.DeviceIdType.MESH
F32 = jnp.float32
BF16 = jnp.bfloat16
EXACT = lax.Precision.HIGHEST
VMEM_LIMIT = 60 * 2**20
NN = ((1,), (0,))
NT = ((1,), (1,))
TN = ((0,), (0,))


def mul(left, right, how, precision=None):
    return lax.dot_general(
        left, right, (how, ((), ())), precision=precision, preferred_element_type=F32
    )


def sigmoid(v):
    return 0.5 * jnp.tanh(0.5 * v) + 0.5


def softplus(v):
    e = jnp.exp(-jnp.abs(v))
    u = 1.0 + e
    near = u - 1.0
    log1p = jnp.where(near == 0.0, e, jnp.log(u) * (e / jnp.where(near == 0.0, 1.0, near)))
    return jnp.maximum(v, 0.0) + log1p


def iota(shape, dim):
    return lax.broadcasted_iota(jnp.int32, shape, dim)


def ds(start, size):
    return pl.ds(pl.multiple_of(start, size), size)


def pair_of(values, pair):
    low = values[:, 2 * pair : 2 * pair + 1]
    high = values[:, 2 * pair + 1 : 2 * pair + 2]
    return jnp.where(iota((values.shape[0], LANES), 1) < LANES // 2, low, high)


def spread(values, pairs):
    return jnp.concatenate([pair_of(values, p) for p in range(pairs)], axis=1)


def eights(v):
    return jnp.sum(v.reshape(v.shape[0] // 8, 8, v.shape[1]), axis=0)


def halves_of(v):
    high = v.astype(BF16)
    return high, (v - high.astype(F32)).astype(BF16)


def head_sums(v, gather):
    high, low = halves_of(v)
    return mul(high, gather, NN) + mul(low, gather, NN)


def remote(src, dst, send, recv, place, head):
    return pltpu.make_async_remote_copy(
        src_ref=src,
        dst_ref=dst,
        send_sem=send,
        recv_sem=recv,
        device_id=(place, head),
        device_id_type=MESH,
    )


def meet(count, parts):
    place, head = lax.axis_index("seq"), lax.axis_index("head")
    barrier = pltpu.get_barrier_semaphore()

    def along_seq(i, _):
        other = lax.rem(place + i, count)
        pl.semaphore_signal(barrier, inc=1, device_id=(other, head), device_id_type=MESH)
        return 0

    def along_head(i, _):
        other = lax.rem(head + i, parts)
        pl.semaphore_signal(barrier, inc=1, device_id=(place, other), device_id_type=MESH)
        return 0

    lax.fori_loop(1, count, along_seq, 0)
    lax.fori_loop(1, parts, along_head, 0)
    pl.semaphore_wait(barrier, count - 1 + parts - 1)


def loop(low, high, step):
    def one(i, _):
        step(i)
        return 0

    lax.fori_loop(low, high, one, 0)


def line_copy(count, src, dst, send, recv):
    place, head = lax.axis_index("seq"), lax.axis_index("head")

    def copy(i):
        other = lax.rem(place + i, count)
        return remote(src(other), dst(place), send.at[i], recv.at[i], other, head)

    return copy


def head_copy(parts, src, dst, send, recv):
    place, head = lax.axis_index("seq"), lax.axis_index("head")

    def copy(i):
        other = lax.rem(head + i, parts)
        return remote(src(other), dst(head), send.at[i], recv.at[i], place, other)

    return copy


def cut_of(count, seqs, state, inner):
    rows = max(16, seqs * state // count)
    lane_cuts = count * rows // (seqs * state)
    return rows, lane_cuts, inner // lane_cuts


def piece_of(k, count, seqs, state, inner):
    rows, lane_cuts, lanes = cut_of(count, seqs, state, inner)
    each = count // seqs
    seq, rest = k // each, lax.rem(k, each)
    row = pl.multiple_of(rest // lane_cuts * rows, rows)
    if lane_cuts == 1:
        return seq, pl.ds(row, rows), slice(None)
    lane = pl.multiple_of(lax.rem(rest, lane_cuts) * lanes, lanes)
    return seq, pl.ds(row, rows), pl.ds(lane, lanes)


def carry_exchange(dims, local, arrived, passed, incoming, decay_ref, sems, reverse):
    count, _, seqs, _, inner, _, state = dims
    place, head = lax.axis_index("seq"), lax.axis_index("head")
    send, recv, back_send, back_recv = sems
    piece = functools.partial(piece_of, count=count, seqs=seqs, state=state, inner=inner)
    rows, _, lanes = cut_of(count, seqs, state, inner)

    def at(ref, k):
        seq, row, lane = piece(k)
        return ref.at[seq, row, lane]

    out = line_copy(count, lambda other: at(local, other), lambda k: arrived.at[k], send, recv)

    def back(j):
        i = lax.rem(j - place + count, count)
        return remote(
            passed.at[j], at(incoming, place), back_send.at[i], back_recv.at[i], j, head
        )

    def start():
        loop(1, count, lambda i: out(i).start())
        seq, row, lane = piece(place)
        arrived[place] = local[seq, row, lane]

    def carry():
        seq, row, lane = piece(place)
        held = jnp.zeros((rows, lanes), F32)
        for step in range(count):
            j = count - 1 - step if reverse else step
            i = lax.rem(place - j + count, count)

            @pl.when(j != place)
            def _():
                out(i).wait_recv()

            passed[j] = held.astype(passed.dtype)

            @pl.when(j != place)
            def _():
                back(j).start()

            @pl.when(j == place)
            def _():
                incoming[seq, row, lane] = passed[j]

            decay = decay_ref[seq, pl.ds(j, 1), lane]
            held = decay * held + arrived[j].astype(F32)

    def finish():
        def one(i):
            out(i).wait_send()
            back(lax.rem(place + i, count)).wait()

        loop(1, count, one)

    return start, carry, finish


def forward_kernel(
    dims,
    x_ref,
    gate_far,
    small_ref,
    chan_ref,
    vec_ref,
    unpack_ref,
    expand_ref,
    gather_ref,
    cot_far,
    wout_far,
    xact_far,
    bc_far,
    conv_far,
    convbc_ref,
    dt_far,
    cum_far,
    states_far,
    ng_t_far,
    dgate_far,
    dy_far,
    dyy_far,
    decay_ref,
    sums_ref,
    gate_ref,
    cot_ref,
    wout_ref,
    xact_ref,
    bc_ref,
    conv_ref,
    dt_ref,
    cum_ref,
    states_ref,
    ng_t_ref,
    dgate_ref,
    dy_ref,
    dyy_ref,
    fetch_sem,
    keep_sem,
    edge_x,
    edge_s,
    ext,
    extbc,
    bc_all,
    fresh,
    y_ref,
    dng_ref,
    gated_ref,
    decays,
    local,
    arrived,
    passed,
    incoming,
    rowsum,
    edge_send,
    edge_recv,
    dec_send,
    dec_recv,
    bc_send,
    bc_recv,
    st_send,
    st_recv,
    back_send,
    back_recv,
    row_send,
    row_recv,
):
    count, parts, seqs, block, inner, heads, state = dims
    place, head = lax.axis_index("seq"), lax.axis_index("head")
    chunks = block // CHUNK
    pairs = heads // 2
    total = seqs * chunks
    fetches = [
        pltpu.make_async_copy(src, dst, fetch_sem.at[k])
        for k, (src, dst) in enumerate(
            ((cot_far, cot_ref), (wout_far, wout_ref), (gate_far, gate_ref))
        )
    ]
    for copy in fetches:
        copy.start()
    keeps = [
        pltpu.make_async_copy(src, dst, keep_sem.at[k])
        for k, (src, dst) in enumerate(
            (
                (xact_ref, xact_far),
                (bc_ref, bc_far),
                (conv_ref, conv_far),
                (dt_ref, dt_far),
                (cum_ref, cum_far),
                (states_ref, states_far),
                (ng_t_ref, ng_t_far),
                (dgate_ref, dgate_far),
                (dy_ref, dy_far),
                (dyy_ref, dyy_far),
            )
        )
    ]
    meet(count, parts)

    def edge_copies(ahead):
        copies = []
        for s in range(seqs):
            rows = pl.ds(s * block + block - 8, 8)
            for k, (src, dst) in enumerate(((x_ref, edge_x), (small_ref, edge_s))):
                copies.append(
                    remote(
                        src.at[rows], dst.at[s], edge_send.at[k, s], edge_recv.at[k, s], ahead, head
                    )
                )
        return copies

    after = lax.rem(place + 1, count)

    @pl.when(place < count - 1)
    def _():
        for c in edge_copies(after):
            c.start()

    lower = (iota((CHUNK, CHUNK), 0) >= iota((CHUNK, CHUNK), 1)).astype(F32)
    for s in range(seqs):

        def steps(c, logs):
            rows = ds((s * chunks + c) * CHUNK, CHUNK)
            dt = softplus(small_ref[rows, :] + vec_ref[5:6, :])
            cum = mul(lower, dt * vec_ref[6:7, :], NN, EXACT)
            dt_ref[rows, :] = dt
            cum_ref[rows, :] = cum
            return logs + cum[CHUNK - 1 :, :]

        logs = lax.fori_loop(0, chunks, steps, jnp.zeros((1, LANES), F32))
        decays[place, s : s + 1, :] = jnp.exp(logs)

    dec = line_copy(count, lambda _: decays.at[place], lambda k: decays.at[k], dec_send, dec_recv)
    loop(1, count, lambda i: dec(i).start())

    @pl.when(place > 0)
    def _():
        for c in edge_copies(after):
            c.wait_recv()

    @pl.when(place == 0)
    def _():
        edge_x[...] = jnp.zeros_like(edge_x)
        edge_s[...] = jnp.zeros_like(edge_s)

    def packed(low, high):
        return jnp.where(
            iota(low.shape, 1) < LANES // 2, pltpu.roll(low, LANES // 2, 1), high
        )

    extbc[0:8, :] = packed(edge_s[0], edge_s[1])
    extbc[8:, :] = packed(small_ref[0:block, :], small_ref[block:, :])
    conv = vec_ref[4:5, :]
    for k in range(KER):
        conv = conv + vec_ref[k : k + 1, :] * extbc[pl.ds(8 - (KER - 1) + k, block), :]
    convbc_ref[...] = conv
    bc_all[head] = (conv * sigmoid(conv)).astype(BF16)
    share = head_copy(parts, lambda _: bc_all.at[head], lambda k: bc_all.at[k], bc_send, bc_recv)
    loop(1, parts, lambda i: share(i).start())

    def x_chunk(t):
        rows = ds(t * CHUNK, CHUNK)
        s, c = t // chunks, lax.rem(t, chunks)
        before = pl.ds(pl.multiple_of(jnp.maximum(t * CHUNK - 8, 0), 8), 8)
        for b in range(inner // LANES):
            lane = slice(b * LANES, (b + 1) * LANES)
            ext[0:8, lane] = jnp.where(c == 0, edge_x[s, :, lane], x_ref[before, lane])
            ext[8:, lane] = x_ref[rows, lane]
            conv = chan_ref[4:5, lane]
            for k in range(KER):
                conv = conv + chan_ref[k : k + 1, lane] * ext[pl.ds(8 - (KER - 1) + k, CHUNK), lane]
            conv_ref[rows, lane] = conv
            xact_ref[rows, lane] = (conv * sigmoid(conv)).astype(BF16)

    loop(0, total, x_chunk)

    loop(1, parts, lambda i: share(i).wait())
    everything = jnp.concatenate([bc_all[k] for k in range(parts)], axis=1)
    for s in range(seqs):
        bc_ref[s * block : (s + 1) * block, :] = mul(everything, unpack_ref[s], NN).astype(BF16)

    for s in range(seqs):

        def add(c, held):
            t = s * chunks + c
            rows = ds(t * CHUNK, CHUNK)
            cum, dt = cum_ref[rows, :], dt_ref[rows, :]
            end = cum[CHUNK - 1 :, :]
            tail = jnp.exp(end - cum) * dt
            weighted = jnp.concatenate(
                [
                    (
                        xact_ref[rows, p * LANES : (p + 1) * LANES].astype(F32) * pair_of(tail, p)
                    ).astype(BF16)
                    for p in range(pairs)
                ],
                axis=1,
            )
            new = mul(bc_ref[rows, 0:state], weighted, TN)
            fresh[t] = new
            return spread(jnp.exp(end), pairs) * held + new

        held = lax.fori_loop(0, chunks, add, jnp.zeros((state, inner), F32))
        local[s] = held

    start, carry, finish = carry_exchange(
        dims,
        local,
        arrived,
        passed,
        incoming,
        decay_ref,
        (st_send, st_recv, back_send, back_recv),
        False,
    )
    start()
    for copy in keeps[:5]:
        copy.start()

    def within(t):
        rows = ds(t * CHUNK, CHUNK)
        cum, dt = cum_ref[rows, :], dt_ref[rows, :]
        cum_t = cum.T
        scores = mul(bc_ref[rows, state:], bc_ref[rows, 0:state], NT)
        seen = iota((CHUNK, CHUNK), 0) >= iota((CHUNK, CHUNK), 1)
        side = iota((CHUNK, LANES), 1) < LANES // 2
        for p in range(pairs):
            lane = slice(p * LANES, (p + 1) * LANES)
            stepped = (xact_ref[rows, lane].astype(F32) * pair_of(dt, p)).astype(BF16)
            halves = []
            for h in (2 * p, 2 * p + 1):
                gap = cum[:, h : h + 1] - cum_t[h : h + 1, :]
                mixing = (scores * jnp.exp(jnp.where(seen, gap, -1e30))).astype(BF16)
                halves.append(mul(mixing, stepped, NN))
            y_ref[rows, lane] = jnp.where(side, halves[0], halves[1])

    loop(0, total, within)

    loop(1, count, lambda i: dec(i).wait())
    for s in range(seqs):
        decay_ref[s] = mul(decays[:, s, :], expand_ref[...], NN, EXACT)
    carry()

    for copy in fetches:
        copy.wait()
    wide = 2 * LANES

    def back_project(i):
        s, b = i // (inner // wide), lax.rem(i, inner // wide)
        rows, lane = ds(s * block, block), ds(b * wide, wide)
        dng_ref[rows, lane] = mul(cot_ref[rows, :], wout_ref[lane, :], NT)

    loop(0, seqs * (inner // wide), back_project)
    finish()

    for s in range(seqs):

        def gate(c, held):
            t = s * chunks + c
            rows = ds(t * CHUNK, CHUNK)
            cum = cum_ref[rows, :]
            grown = jnp.exp(cum)
            states_ref[t] = held
            high, low = halves_of(held)
            c_rows = bc_ref[rows, state:]
            carried = mul(c_rows, high, NN) + mul(c_rows, low, NN)
            square = jnp.zeros((CHUNK, LANES), F32)
            cross = jnp.zeros((CHUNK, LANES), F32)
            for p in range(pairs):
                lane = slice(p * LANES, (p + 1) * LANES)
                y = y_ref[rows, lane] + carried[:, lane] * pair_of(grown, p)
                y_ref[rows, lane] = y
                out = y + chan_ref[6:7, lane] * xact_ref[rows, lane].astype(F32)
                pre = gate_ref[rows, lane]
                gated = out * (pre * sigmoid(pre))
                gated_ref[rows, lane] = gated
                square = square + gated * gated
                cross = cross + dng_ref[rows, lane] * chan_ref[5:6, lane] * gated
            at = iota((CHUNK, LANES), 1)
            both = jnp.where(
                at == 0,
                jnp.sum(square, axis=1, keepdims=True),
                jnp.where(at == 1, jnp.sum(cross, axis=1, keepdims=True), 0.0),
            )
            rowsum[head, t] = both.T[0:8, :]
            return spread(grown[CHUNK - 1 :, :], pairs) * held + fresh[t]

        lax.fori_loop(0, chunks, gate, incoming[s].astype(F32))

    keeps[5].start()
    rows_copy = head_copy(
        parts, lambda _: rowsum.at[head], lambda k: rowsum.at[k], row_send, row_recv
    )
    loop(1, parts, lambda i: rows_copy(i).start())
    loop(1, parts, lambda i: rows_copy(i).wait())
    sums_ref[...] = jnp.zeros_like(sums_ref)
    channels = inner * parts

    def outputs(t):
        rows = ds(t * CHUNK, CHUNK)
        sums = rowsum[0, t]
        for k in range(1, parts):
            sums = sums + rowsum[k, t]
        turned = jnp.concatenate([sums, jnp.zeros((CHUNK - 8, LANES), F32)], axis=0).T
        scale = lax.rsqrt(turned[:, 0:1] / channels + EPSILON)
        pull = scale * scale * scale * (turned[:, 1:2] / channels)
        dyy = jnp.zeros((CHUNK, LANES), F32)
        for p in range(pairs):
            lane = slice(p * LANES, (p + 1) * LANES)
            pre = gate_ref[rows, lane]
            sg = sigmoid(pre)
            gated, y = gated_ref[rows, lane], y_ref[rows, lane]
            x = xact_ref[rows, lane].astype(F32)
            gain = chan_ref[5:6, lane]
            scaled = gated * scale
            ng_t_ref[lane, rows] = (scaled * gain).T.astype(BF16)
            dng = dng_ref[rows, lane]
            d_gated = scale * (dng * gain) - gated * pull
            d_ssd = d_gated * (pre * sg)
            out = y + chan_ref[6:7, lane] * x
            dgate_ref[rows, lane] = (d_gated * out * (sg * (1.0 + pre * (1.0 - sg)))).astype(BF16)
            dy = d_ssd.astype(BF16)
            dy_ref[rows, lane] = dy
            sums_ref[0:8, lane] += eights(dng * scaled)
            sums_ref[8:16, lane] += eights(d_ssd * x)
            dyy = dyy + head_sums(dy.astype(F32) * y, gather_ref[lane, :])
        dyy_ref[rows, :] = dyy

    loop(0, total, outputs)
    for copy in keeps[6:]:
        copy.start()
    for copy in keeps:
        copy.wait()

    @pl.when(place < count - 1)
    def _():
        for c in edge_copies(after):
            c.wait_send()


def vmem(shape, kind):
    return pltpu.VMEM(shape, kind)


def forward(dims, *operands):
    count, parts, seqs, block, inner, heads, state = dims
    rows = seqs * block
    chunks = rows // CHUNK
    cut_rows, _, cut_lanes = cut_of(count, seqs, state, inner)
    spec, far = pl.BlockSpec(memory_space=pltpu.VMEM), pl.BlockSpec(memory_space=pl.ANY)
    fetched, kept = (1, 8, 9), (0, 1, 2, 4, 5, 6, 7, 8, 9, 10)
    line, ring = pltpu.SemaphoreType.DMA((count,)), pltpu.SemaphoreType.DMA((parts,))
    edge = pltpu.SemaphoreType.DMA((2, seqs))
    outs = [
        ((rows, inner), BF16),
        ((rows, 2 * state), BF16),
        ((rows, inner), F32),
        ((block, LANES), F32),
        ((rows, LANES), F32),
        ((rows, LANES), F32),
        ((chunks, state, inner), F32),
        ((inner, rows), BF16),
        ((rows, inner), BF16),
        ((rows, inner), BF16),
        ((rows, LANES), F32),
        ((seqs, count, inner), F32),
        ((16, inner), F32),
    ]
    return pl.pallas_call(
        functools.partial(forward_kernel, dims),
        out_shape=[jax.ShapeDtypeStruct(*o) for o in outs],
        in_specs=[far if k in fetched else spec for k in range(len(operands))],
        out_specs=[far if k in kept else spec for k in range(len(outs))],
        scratch_shapes=[vmem(operands[k].shape, operands[k].dtype) for k in fetched]
        + [vmem(*outs[k]) for k in kept]
        + [
            pltpu.SemaphoreType.DMA((len(fetched),)),
            pltpu.SemaphoreType.DMA((len(kept),)),
            vmem((seqs, 8, inner), F32),
            vmem((seqs, 8, LANES), F32),
            vmem((CHUNK + 8, inner), F32),
            vmem((block + 8, LANES), F32),
            vmem((parts, block, LANES), BF16),
            vmem((chunks, state, inner), F32),
            vmem((rows, inner), F32),
            vmem((rows, inner), F32),
            vmem((rows, inner), F32),
            vmem((count, 8, LANES), F32),
            vmem((seqs, state, inner), F32),
            vmem((count, cut_rows, cut_lanes), F32),
            vmem((count, cut_rows, cut_lanes), F32),
            vmem((seqs, state, inner), F32),
            vmem((parts, chunks, 8, LANES), F32),
            edge,
            edge,
            line,
            line,
            ring,
            ring,
            line,
            line,
            line,
            line,
            ring,
            ring,
        ],
        compiler_params=pltpu.CompilerParams(
            collective_id=2, has_side_effects=True, vmem_limit_bytes=VMEM_LIMIT
        ),
        name="mixer_forward",
    )(*operands)


def project_kernel(
    tokens_ref, gain_ref, weight_ref, small_weight_ref, gate_ref, x_ref, small_ref, turned_ref, scale_ref
):
    tokens = tokens_ref[...].astype(F32)
    scale = lax.rsqrt(jnp.mean(tokens * tokens, axis=1, keepdims=True) + EPSILON)
    scale_ref[...] = scale
    normed = tokens * scale * gain_ref[...]
    low = normed.astype(BF16)
    turned_ref[...] = low.T
    x_ref[...] = mul(low, weight_ref[1], NN)
    small_ref[...] = mul(low, small_weight_ref[...], NN)
    gate_ref[...] = mul(low, weight_ref[0], NN)


def project(tokens, gain, weights, small_weight):
    rows, width = tokens.shape
    inner = weights.shape[2]
    tall = 2 * CHUNK

    def by_rows(cols):
        return pl.BlockSpec((tall, cols), lambda i: (i, 0))

    def whole(array_in):
        return pl.BlockSpec(array_in.shape, lambda i: (0,) * array_in.ndim)

    return pl.pallas_call(
        project_kernel,
        grid=(rows // tall,),
        in_specs=[by_rows(width), whole(gain), whole(weights), whole(small_weight)],
        out_specs=[
            by_rows(inner),
            by_rows(inner),
            by_rows(LANES),
            pl.BlockSpec((width, tall), lambda i: (0, i)),
            by_rows(1),
        ],
        out_shape=[
            jax.ShapeDtypeStruct((rows, inner), F32),
            jax.ShapeDtypeStruct((rows, inner), F32),
            jax.ShapeDtypeStruct((rows, LANES), F32),
            jax.ShapeDtypeStruct((width, rows), BF16),
            jax.ShapeDtypeStruct((rows, 1), F32),
        ],
        compiler_params=pltpu.CompilerParams(vmem_limit_bytes=VMEM_LIMIT),
        name="project",
    )(tokens, gain, weights, small_weight)


def ring_place(count):
    place = lax.axis_index("seq")
    row, col = place // 2, place % 2
    return jnp.where(col == 0, row, count - 1 - row)


def ring_device(rank, count):
    return jnp.where(rank < count // 2, 2 * rank, 2 * (count - 1 - rank) + 1)


def ring_steps(count, plan, outs, bufs, stages, sems):
    rs_send, rs_recv, ag_send, ag_recv, keep_sem = sems
    far = count // 2
    head = lax.axis_index("head")
    rank = ring_place(count)
    arms = (1, -1)
    peers = [ring_device(lax.rem(rank + a + count, count), count) for a in arms]

    def chunk_at(distance):
        return lax.rem(rank + distance + 2 * count, count)

    def partial(i, chunk):
        left, right, cols, _ = plan[i]
        rows = left.shape[0] // count
        return mul(left[ds(chunk * rows, rows), :], right[:, 0:cols], NN)

    def half(i, arm):
        cols, cut = plan[i][2:]
        return slice(0, cut) if arm == 0 else slice(cut, cols)

    def block_of(i, chunk):
        rows = plan[i][0].shape[0] // count
        return outs[i].at[ds(chunk * rows, rows)]

    def rs(i, arm, step, first=False):
        here = stages[i] if first else bufs[i].at[arm, step - 1]
        there = bufs[i].at[arm, step]
        if first:
            here, there = here.at[:, half(i, arm)], there.at[:, half(i, arm)]
        return remote(
            here, there, rs_send.at[i, arm, step], rs_recv.at[i, arm, step], peers[arm], head
        )

    def ag(i, arm, step, kind="middle"):
        there = block_of(i, chunk_at(-arms[arm] * step))
        here = bufs[i].at[0, far - 1] if kind == "first" else there
        if kind == "last":
            here, there = here.at[:, half(i, arm)], there.at[:, half(i, arm)]
        return remote(
            here, there, ag_send.at[i, arm, step], ag_recv.at[i, arm, step], peers[arm], head
        )

    def keep(i):
        return pltpu.make_async_copy(
            bufs[i].at[0, far - 1], block_of(i, chunk_at(0)), keep_sem.at[i]
        )

    def begin(i):
        stages[i][...] = partial(i, chunk_at(far)).astype(BF16)
        for arm in range(2):
            rs(i, arm, 0, True).start()

    def advance(streams, slot, slots):
        def second(i, arm):
            own = partial(i, chunk_at(arms[arm] * (far - 1)))
            rs(i, arm, 0, True).wait_recv()
            mine, other = half(i, arm), half(i, 1 - arm)
            bufs[i][arm, 0, :, other] = own[:, other].astype(BF16)
            bufs[i][arm, 0, :, mine] = (
                own[:, mine] + bufs[i][arm, 0, :, mine].astype(F32)
            ).astype(BF16)
            rs(i, arm, 1).start()

        def later(i, arm, step):
            own = partial(i, chunk_at(arms[arm] * (far - step)))
            rs(i, arm, step - 1).wait_recv()
            bufs[i][arm, step - 1] = (own + bufs[i][arm, step - 1].astype(F32)).astype(BF16)
            rs(i, arm, step).start()

        def last(i):
            own = partial(i, chunk_at(0))
            for arm in range(2):
                rs(i, arm, far - 1).wait_recv()
                own = own + bufs[i][arm, far - 1].astype(F32)
            bufs[i][0, far - 1] = own.astype(BF16)
            for arm in range(2):
                ag(i, arm, 0, "first").start()
            keep(i).start()

        low, high = slot * far // slots, (slot + 1) * far // slots
        if low == 0 < high:
            for i in streams:
                for arm in range(2):
                    second(i, arm)

        def middle(step):
            for i in streams:
                for arm in range(2):
                    later(i, arm, step)

        if min(high, far - 1) > max(low, 1):
            loop(max(low, 1) + 1, min(high, far - 1) + 1, middle)
        if high == far:
            for i in streams:
                last(i)

    def pass_on(streams, slot, slots):
        def middle(step):
            for i in streams:
                for arm in range(2):
                    ag(i, arm, step - 1).wait_recv()
                    ag(i, arm, step).start()

        steps = far - 1
        low, high = slot * steps // slots, (slot + 1) * steps // slots
        if min(high, steps - 1) > low:
            loop(low + 1, min(high, steps - 1) + 1, middle)
        if low < high == steps:
            for i in streams:
                for arm in range(2):
                    ag(i, arm, steps - 1).wait_recv()
                    ag(i, arm, steps, "last").start()

    def pass_end(streams):
        for i in streams:
            for arm in range(2):
                ag(i, arm, far - 1, "last").wait_recv()

    def drain(streams):
        for i in streams:
            for arm in range(2):
                rs(i, arm, 0, True).wait_send()
                ag(i, arm, 0, "first").wait_send()
                ag(i, arm, far - 1, "last").wait_send()
            keep(i).wait()

        def one(step):
            for i in streams:
                for arm in range(2):
                    rs(i, arm, step).wait_send()

                    @pl.when(step < far - 1)
                    def _():
                        ag(i, arm, step).wait_send()

        loop(1, far, one)

    return begin, advance, pass_on, pass_end, drain


def finish_kernel(gate, narrow, out, gin_ref, wout_ref, small_ref):
    inner = gate.shape[1]
    gin_ref[:, 0, :] = gate[...].astype(F32)
    gin_ref[:, 1, :] = narrow[:, 0:inner].astype(F32)
    small_ref[...] = narrow[:, inner:].astype(F32).T
    wout_ref[...] = out[...].astype(F32)


def finish_weights(width, inner, streams):
    steps = width // (2 * LANES)
    tall, low = width // steps, inner // steps
    out, gate, narrow = streams

    def block(array_in, rows):
        return pl.BlockSpec((rows, array_in.shape[1]), lambda i: (i, 0))

    return pl.pallas_call(
        finish_kernel,
        grid=(steps,),
        in_specs=[block(gate, tall), block(narrow, tall), block(out, low)],
        out_specs=[
            pl.BlockSpec((tall, 2, inner), lambda i: (i, 0, 0)),
            pl.BlockSpec((low, width), lambda i: (i, 0)),
            pl.BlockSpec((LANES, tall), lambda i: (0, i)),
        ],
        out_shape=[
            jax.ShapeDtypeStruct((width, 2, inner), F32),
            jax.ShapeDtypeStruct((inner, width), F32),
            jax.ShapeDtypeStruct((LANES, width), F32),
        ],
        compiler_params=pltpu.CompilerParams(vmem_limit_bytes=VMEM_LIMIT),
        name="finish_weights",
    )(gate, narrow, out)


STEPS = 4


def backward_kernel(
    dims,
    dy_ref,
    xact_far,
    bc_ref,
    conv_ref,
    convbc_ref,
    dt_ref,
    cum_ref,
    states_far,
    dyy_ref,
    decay_ref,
    x_far,
    small_ref,
    chan_ref,
    vec_ref,
    pack_far,
    gather_ref,
    normed_t_far,
    ng_t_far,
    cot_far,
    dgate_far,
    small_weight_far,
    sums_ref,
    gain_ref,
    row_scale_ref,
    tokens_ref,
    weight_ref,
    *rest,
):
    count, parts, seqs, block, inner, heads, state = dims
    outs, rest = rest[:3], rest[3:]
    grad_ref, total_ref, *rest = rest
    bufs, rest = rest[:3], rest[3:]
    stages, rest = rest[:3], rest[3:]
    fetched, rest = rest[:7], rest[7:]
    fetch_sem, *rest = rest
    (
        dx_ref,
        gx_ref,
        gbc_ref,
        gdt_ref,
        weights,
        conv_buf,
        state_buf,
        dn_out,
        dn_in,
        token_buf,
        rowsum,
        shared,
        rs_send,
        rs_recv,
        ag_send,
        ag_recv,
        keep_sem,
        weight_sem,
        conv_sem,
        state_sem,
        x_sem,
        token_sem,
        dn_send,
        dn_recv,
        row_send,
        row_recv,
        sum_send,
        sum_recv,
        *rest,
    ) = rest
    (
        dconv,
        dconvbc,
        prebc,
        dbc,
        ddt,
        added,
        local,
        arrived,
        passed,
        incoming,
        bc_out,
        bc_in,
        edge_send,
        edge_recv,
        bc_send,
        bc_recv,
        st_send,
        st_recv,
        back_send,
        back_recv,
    ) = rest
    sources = (
        ng_t_far,
        cot_far,
        normed_t_far,
        dgate_far,
        xact_far,
        small_weight_far,
        pack_far,
    )
    fetches = [
        pltpu.make_async_copy(src, dst, fetch_sem.at[k])
        for k, (src, dst) in enumerate(zip(sources, fetched))
    ]
    for copy in fetches:
        copy.start()
    (
        ng_t_ref,
        cot_ref,
        normed_t_ref,
        dgate_ref,
        xact_ref,
        small_weight_ref,
        pack_ref,
    ) = fetched
    place, head = lax.axis_index("seq"), lax.axis_index("head")
    chunks = block // CHUNK
    pairs = heads // 2
    total = seqs * chunks
    rows_all = seqs * block
    width = cot_ref.shape[1]
    cols = width // parts
    plan = (
        (ng_t_ref, cot_ref, width, width // 2),
        (normed_t_ref, dgate_ref, inner, inner // 2),
        (normed_t_ref, dx_ref, inner + LANES, inner // 2),
    )
    begin, advance, pass_on, pass_end, drain = ring_steps(
        count, plan, outs, bufs, stages, (rs_send, rs_recv, ag_send, ag_recv, keep_sem)
    )
    out, gate, late = (0,), (1,), (2,)
    meet(count, parts)
    gdt_ref[...] = jnp.zeros_like(gdt_ref)

    token_copy = pltpu.make_async_copy(
        tokens_ref.at[:, pl.ds(pl.multiple_of(head * cols, cols), cols)], token_buf, token_sem
    )
    token_copy.start()

    def weight_copy(i):
        other = lax.rem(head + i, parts)
        return pltpu.make_async_copy(
            weight_ref.at[:, pl.ds(pl.multiple_of(other * cols, cols), cols)],
            weights.at[lax.rem(i + 1, 2)],
            weight_sem.at[lax.rem(i + 1, 2)],
        )

    def conv_copy(q):
        t = q // chunks * chunks + chunks - 1 - lax.rem(q, chunks)
        slot = lax.rem(q, 2)
        return pltpu.make_async_copy(
            conv_ref.at[ds(t * CHUNK, CHUNK)], conv_buf.at[slot], conv_sem.at[slot]
        )

    def state_copy(q):
        t = q // chunks * chunks + chunks - 1 - lax.rem(q, chunks)
        slot = lax.rem(q, 2)
        return pltpu.make_async_copy(states_far.at[t], state_buf.at[slot], state_sem.at[slot])

    conv_copy(0).start()
    state_copy(0).start()
    weight_copy(1).start()
    for copy in fetches[:4]:
        copy.wait()
    for i in out + gate:
        begin(i)

    for s in range(seqs):

        def alone(i, held):
            t = s * chunks + chunks - 1 - i
            rows = ds(t * CHUNK, CHUNK)
            grown = jnp.exp(cum_ref[rows, :])
            weighted = jnp.concatenate(
                [
                    (
                        dy_ref[rows, p * LANES : (p + 1) * LANES].astype(F32) * pair_of(grown, p)
                    ).astype(BF16)
                    for p in range(pairs)
                ],
                axis=1,
            )
            new = mul(bc_ref[rows, state:], weighted, TN)
            added[t] = new
            return spread(grown[CHUNK - 1 :, :], pairs) * held + new

        held = lax.fori_loop(0, chunks, alone, jnp.zeros((state, inner), F32))
        local[s] = held.astype(BF16)

    start, carry, finish = carry_exchange(
        dims,
        local,
        arrived,
        passed,
        incoming,
        decay_ref,
        (st_send, st_recv, back_send, back_recv),
        True,
    )
    start()
    advance(out, 0, STEPS)
    advance(gate, 0, STEPS)
    advance(out, 1, STEPS)
    carry()
    advance(gate, 1, STEPS)
    for copy in fetches[4:]:
        copy.wait()
    finish()
    advance(out, 2, STEPS)

    side = iota((CHUNK, LANES), 1) < LANES // 2
    seen = iota((CHUNK, CHUNK), 0) <= iota((CHUNK, CHUNK), 1)
    upper = seen.astype(F32)
    for s in range(seqs):

        def chunk(i, held):
            t = s * chunks + chunks - 1 - i
            rows = ds(t * CHUNK, CHUNK)
            out_rows = ds((s * chunks + chunks - 1 - i) * CHUNK, CHUNK)
            turn = s * chunks + i
            conv_copy(turn).wait()
            state_copy(turn).wait()

            @pl.when(turn + 1 < total)
            def _():
                conv_copy(turn + 1).start()
                state_copy(turn + 1).start()

            cum, dt = cum_ref[rows, :], dt_ref[rows, :]
            cum_t = cum.T
            grown = jnp.exp(cum)
            end = cum[CHUNK - 1 :, :]
            tail = jnp.exp(end - cum)
            b_rows, c_rows = bc_ref[rows, 0:state], bc_ref[rows, state:]
            scores = mul(b_rows, c_rows, NT)
            low = held.astype(BF16)
            begun = state_buf[lax.rem(turn, 2)]
            begun_high, begun_low = halves_of(begun)
            pulled = mul(b_rows, low, NN)
            grad_scores = jnp.zeros((CHUNK, CHUNK), F32)
            d_x_sum = jnp.zeros((CHUNK, LANES), F32)
            d_fall = jnp.zeros((CHUNK, LANES), F32)
            into_x = []
            into_y = []
            last = []
            for p in range(pairs):
                lane = slice(p * LANES, (p + 1) * LANES)
                x, dy = xact_ref[rows, lane], dy_ref[rows, lane]
                xf, dyf = x.astype(F32), dy.astype(F32)
                dt_p, tail_p = pair_of(dt, p), pair_of(tail, p)
                stepped = xf * dt_p
                low_step = stepped.astype(BF16)
                halves = []
                for k, h in enumerate((2 * p, 2 * p + 1)):
                    gap = cum_t[h : h + 1, :] - cum[:, h : h + 1]
                    fade = jnp.exp(jnp.where(seen, gap, -1e30))
                    own = jnp.where(side if k == 0 else ~side, low_step, jnp.zeros_like(low_step))
                    grad_scores = grad_scores + mul(own, dy, NT) * fade
                    halves.append(mul((scores * fade).astype(BF16), dy, NN))
                from_state = pulled[:, lane] * tail_p
                d_step_x = jnp.where(side, halves[0], halves[1]) + from_state
                rounded = low_step.astype(F32)
                d_x_sum = d_x_sum + head_sums(xf * d_step_x, gather_ref[lane, :])
                d_fall = d_fall + head_sums(rounded * d_step_x, gather_ref[lane, :])
                into_x.append((stepped * tail_p).astype(BF16))
                into_y.append((dyf * pair_of(grown, p)).astype(BF16))
                last.append(jnp.sum(rounded * from_state, axis=0, keepdims=True))
                conv = conv_buf[lax.rem(turn, 2), :, lane]
                sg = sigmoid(conv)
                d_act = dt_p * d_step_x + chan_ref[6:7, lane] * dyf
                dconv[s, ds((chunks - 1 - i) * CHUNK, CHUNK), lane] = d_act * (
                    sg * (1.0 + conv * (1.0 - sg))
                )
            low_scores = grad_scores.astype(BF16)
            d_b = mul(low_scores, c_rows, NN) + mul(jnp.concatenate(into_x, axis=1), low, NT)
            into_y = jnp.concatenate(into_y, axis=1)
            d_c = mul(low_scores, b_rows, TN) + mul(into_y, begun_high, NT)
            d_c = d_c + mul(into_y, begun_low, NT)
            dbc[out_rows, 0:state] = d_b.astype(BF16)
            dbc[out_rows, state:] = d_c.astype(BF16)
            fall = spread(grown[CHUNK - 1 :, :], pairs)
            ends = jnp.concatenate(last, axis=1) + fall * jnp.sum(
                held * begun, axis=0, keepdims=True
            )
            ends = head_sums(jnp.broadcast_to(ends, (8, inner)), gather_ref[...])[0:1, :]
            d_log = mul(upper, dyy_ref[rows, :] - d_fall, NN, EXACT) + ends
            d_step = d_x_sum + vec_ref[6:7, :] * d_log
            d_dt = d_step * sigmoid(small_ref[rows, :] + vec_ref[5:6, :])
            gdt_ref[0:8, :] += eights(d_dt)
            gdt_ref[8:16, :] += eights(d_log * (dt * vec_ref[6:7, :]))
            ddt[out_rows, :] = d_dt


            @pl.when(turn == total * 3 // 8)
            def _():
                advance(gate, 2, STEPS)

            @pl.when(turn == total * 6 // 8)
            def _():
                advance(out, 3, STEPS)

            return fall * held + added[t]

        lax.fori_loop(0, chunks, chunk, incoming[s].astype(F32))

    def pack(k):
        piece = mul(dbc[0:block, :], pack_ref[k, 0], NN)
        return (piece + mul(dbc[block:, :], pack_ref[k, 1], NN)).astype(BF16)

    def pack_one(k):
        bc_out[k] = pack(k)

    def x_copy(t):
        slot = lax.rem(t, 2)
        return pltpu.make_async_copy(
            x_far.at[ds(t * CHUNK, CHUNK)], conv_buf.at[slot], x_sem.at[slot]
        )

    x_copy(0).start()
    advance(gate, 3, STEPS)
    loop(0, parts, pack_one)
    share = head_copy(parts, lambda k: bc_out.at[k], lambda k: bc_in.at[k], bc_send, bc_recv)
    loop(1, parts, lambda i: share(i).start())

    before = lax.rem(place + count - 1, count)

    def edge_copy(s):
        return remote(
            dconv.at[s, pl.ds(0, 8)],
            dconv.at[s, pl.ds(block, 8)],
            edge_send.at[s],
            edge_recv.at[s],
            before,
            head,
        )

    def edge_bc():
        return remote(
            dconvbc.at[pl.ds(0, 8)],
            dconvbc.at[pl.ds(block, 8)],
            edge_send.at[seqs],
            edge_recv.at[seqs],
            before,
            head,
        )

    @pl.when(place > 0)
    def _():
        for s in range(seqs):
            edge_copy(s).start()

    pass_on(out, 0, 3)
    loop(1, parts, lambda i: share(i).wait())
    bc_in[head] = bc_out[head]
    d_act = bc_in[0].astype(F32)
    for k in range(1, parts):
        d_act = d_act + bc_in[k].astype(F32)
    conv = convbc_ref[...]
    sg = sigmoid(conv)
    dconvbc[0:block, :] = d_act * (sg * (1.0 + conv * (1.0 - sg)))

    @pl.when(place > 0)
    def _():
        edge_bc().start()

    @pl.when(place < count - 1)
    def _():
        for s in range(seqs):
            edge_copy(s).wait_recv()

    @pl.when(place == count - 1)
    def _():
        for s in range(seqs):
            dconv[s, block : block + 8, :] = jnp.zeros((8, inner), F32)

    gx_ref[...] = jnp.zeros_like(gx_ref)

    def x_chunk(t):
        rows = ds(t * CHUNK, CHUNK)
        s, c = t // chunks, lax.rem(t, chunks)
        x_copy(t).wait()

        @pl.when(t + 1 < total)
        def _():
            x_copy(t + 1).start()

        for p in range(pairs):
            lane = slice(p * LANES, (p + 1) * LANES)
            x = conv_buf[lax.rem(t, 2), :, lane]
            pre = jnp.zeros((CHUNK, LANES), F32)
            here = dconv[s, pl.ds(pl.multiple_of(c * CHUNK, CHUNK), CHUNK + 8), lane]
            for k in range(KER):
                off = KER - 1 - k
                d = pltpu.roll(here, CHUNK + 8 - off, 0)[:CHUNK] if off else here[:CHUNK]
                pre = pre + chan_ref[k : k + 1, lane] * d
                gx_ref[8 * k : 8 * k + 8, lane] += eights(x * d)
                if k == KER - 1:
                    gx_ref[8 * KER : 8 * KER + 8, lane] += eights(d)
            dx_ref[rows, lane] = pre.astype(BF16)

        @pl.when(t == total // 2)
        def _():
            pass_on(gate, 0, 3)

    loop(0, total, x_chunk)

    @pl.when(place < count - 1)
    def _():
        edge_bc().wait_recv()

    @pl.when(place == count - 1)
    def _():
        dconvbc[block : block + 8, :] = jnp.zeros((8, LANES), F32)

    low, high = small_ref[0:block, :], small_ref[block:, :]
    prebc[...] = jnp.where(
        iota(low.shape, 1) < LANES // 2, pltpu.roll(low, LANES // 2, 1), high
    )
    pre = jnp.zeros((block, LANES), F32)
    for k in range(KER):
        d = dconvbc[pl.ds(KER - 1 - k, block), :]
        pre = pre + vec_ref[k : k + 1, :] * d
        gbc_ref[8 * k : 8 * k + 8, :] = eights(prebc[...] * d)
    gbc_ref[8 * KER : 8 * KER + 8, :] = eights(dconvbc[0:block, :])
    at = iota((block, LANES), 1)
    for s in range(seqs):
        rows = slice(s * block, (s + 1) * block)
        mine = pre if s == seqs - 1 else pltpu.roll(pre, LANES // 2, 1)
        step = jnp.where(at < heads, ddt[rows, :], 0.0)
        dx_ref[rows, inner:] = jnp.where(at < LANES // 2, step, mine).astype(BF16)

    for i in late:
        begin(i)

    tall = 2 * CHUNK

    def dn_copy(i):
        other = lax.rem(head + i, parts)
        return remote(
            dn_out.at[other], dn_in.at[i - 1], dn_send.at[i], dn_recv.at[i], place, other
        )

    def d_normed(i):
        other = lax.rem(head + i, parts)
        slot = (i + 1) % 2
        if i < parts:
            weight_copy(i + 1).start()

        weight_copy(i).wait()
        mine = small_weight_ref[pl.ds(pl.multiple_of(other * cols, cols), cols), :]

        def some(r):
            rows = ds(r * tall, tall)
            part = mul(dgate_ref[rows, :], weights[slot, 0], NT)
            part = part + mul(dx_ref[rows, 0:inner], weights[slot, 1], NT)
            part = part + mul(dx_ref[rows, inner:], mine, NT)
            dn_out[other, rows, :] = part.astype(BF16)

        loop(0, rows_all // tall, some)

        if i < parts:
            dn_copy(i).start()

    between = ((out, 1), (gate, 1), (out, 2), (gate, 2))
    for k in range(STEPS):
        if k < parts:
            d_normed(k + 1)
        advance(late, k, STEPS)
        pass_on(*between[k], 3)
    for k in range(STEPS, parts):
        d_normed(k + 1)

    loop(1, parts, lambda i: dn_copy(i).wait())
    token_copy.wait()
    my_cols = pl.ds(pl.multiple_of(head * cols, cols), cols)

    def own(t, grads):
        rows = ds(t * CHUNK, CHUNK)
        d = dn_out[head, rows, :].astype(F32)
        for k in range(parts - 1):
            d = d + dn_in[k, rows, :].astype(F32)
        token = token_buf[rows, :].astype(F32)
        grads = grads + eights(d * (token * row_scale_ref[rows, :]))
        d = d * gain_ref[:, my_cols]
        grad_ref[rows, :] = d
        line = jnp.sum(d * token, axis=1, keepdims=True)
        line = jnp.where(iota((CHUNK, LANES), 1) == 0, line, 0.0)
        rowsum[head, t] = line.T[0:8, :]
        return grads

    norm_grads = lax.fori_loop(0, total, own, jnp.zeros((8, cols), F32))
    rows_copy = head_copy(
        parts, lambda _: rowsum.at[head], lambda k: rowsum.at[k], row_send, row_recv
    )
    loop(1, parts, lambda i: rows_copy(i).start())

    def summed(ref, k):
        return jnp.sum(ref[8 * k : 8 * k + 8, :], axis=0, keepdims=True)

    shared[place] = jnp.zeros(shared.shape[1:], F32)
    for k in range(KER + 1):
        shared[place, k : k + 1, 0:inner] = summed(gx_ref, k)
        shared[place, k : k + 1, inner:] = summed(gbc_ref, k)
    for k in range(2):
        shared[place, KER + 1 + k : KER + 2 + k, 0:inner] = summed(sums_ref, k)
        shared[place, KER + 1 + k : KER + 2 + k, inner:] = summed(gdt_ref, k)
    shared[place, 7:8, 0:cols] = jnp.sum(norm_grads, axis=0, keepdims=True)
    sums_copy = line_copy(
        count, lambda _: shared.at[place], lambda k: shared.at[k], sum_send, sum_recv
    )
    loop(1, count, lambda i: sums_copy(i).start())
    pass_on(late, 0, 3)
    loop(1, parts, lambda i: rows_copy(i).wait())

    def finish_rows(t):
        rows = ds(t * CHUNK, CHUNK)
        sums = rowsum[0, t]
        for k in range(1, parts):
            sums = sums + rowsum[k, t]
        turned = jnp.concatenate([sums, jnp.zeros((CHUNK - 8, LANES), F32)], axis=0).T
        scale = row_scale_ref[rows, :]
        pull = scale * scale * scale * (turned[:, 0:1] / width)
        grad_ref[rows, :] = (
            scale * grad_ref[rows, :]
            - token_buf[rows, :].astype(F32) * pull
            + cot_ref[rows, my_cols].astype(F32)
        )

    loop(0, total, finish_rows)
    pass_on(late, 1, 3)
    loop(1, count, lambda i: sums_copy(i).wait())
    everything = shared[0]
    for k in range(1, count):
        everything = everything + shared[k]
    total_ref[...] = everything
    pass_on(late, 2, 3)
    pass_end(out + gate + late)
    drain(out + gate + late)

    @pl.when(place > 0)
    def _():
        for s in range(seqs):
            edge_copy(s).wait_send()
        edge_bc().wait_send()


def backward(dims, *operands):
    count, parts, seqs, block, inner, heads, state = dims
    rows = seqs * block
    chunks = rows // CHUNK
    cut_rows, _, cut_lanes = cut_of(count, seqs, state, inner)
    normed_rows, ng_rows, width = (operands[k].shape[d] for k, d in ((16, 0), (17, 0), (18, 1)))
    cols = width // parts
    distant = (1, 3, 7, 10, 14, 16, 17, 18, 19, 20, 24, 25)
    fetched = [operands[k] for k in (17, 18, 16, 19, 1, 20, 14)]
    spec = pl.BlockSpec(memory_space=pltpu.VMEM)
    far = pl.BlockSpec(memory_space=pl.ANY)
    line, ring = pltpu.SemaphoreType.DMA((count,)), pltpu.SemaphoreType.DMA((parts,))
    edge = pltpu.SemaphoreType.DMA((seqs + 1,))
    streams = [(ng_rows, width), (normed_rows, inner), (normed_rows, inner + LANES)]
    steps = pltpu.SemaphoreType.DMA((len(streams), 2, count // 2))
    outs = [(shape, BF16) for shape in streams]
    outs = outs + [((rows, cols), F32), ((8, inner + LANES), F32)]
    return pl.pallas_call(
        functools.partial(backward_kernel, dims),
        out_shape=[jax.ShapeDtypeStruct(*o) for o in outs],
        in_specs=[far if k in distant else spec for k in range(len(operands))],
        out_specs=[far] * len(streams) + [spec] * 2,
        scratch_shapes=[vmem((2, count // 2, r // count, c), BF16) for r, c in streams]
        + [vmem((r // count, c), BF16) for r, c in streams]
        + [vmem(a.shape, a.dtype) for a in fetched]
        + [
            pltpu.SemaphoreType.DMA((len(fetched),)),
            vmem((rows, inner + LANES), BF16),
            vmem((8 * (KER + 1), inner), F32),
            vmem((8 * (KER + 1), LANES), F32),
            vmem((16, LANES), F32),
            vmem((2, 2, cols, inner), BF16),
            vmem((2, CHUNK, inner), F32),
            vmem((2, state, inner), F32),
            vmem((parts, rows, cols), BF16),
            vmem((parts - 1, rows, cols), BF16),
            vmem((rows, cols), BF16),
            vmem((parts, chunks, 8, LANES), F32),
            vmem((count, 8, inner + LANES), F32),
            steps,
            steps,
            steps,
            steps,
            pltpu.SemaphoreType.DMA((len(streams),)),
            pltpu.SemaphoreType.DMA((2,)),
            pltpu.SemaphoreType.DMA((2,)),
            pltpu.SemaphoreType.DMA((2,)),
            pltpu.SemaphoreType.DMA((2,)),
            pltpu.SemaphoreType.DMA,
            ring,
            ring,
            ring,
            ring,
            line,
            line,
            vmem((seqs, block + 8, inner), F32),
            vmem((block + 8, LANES), F32),
            vmem((block, LANES), F32),
            vmem((rows, 2 * state), BF16),
            vmem((rows, LANES), F32),
            vmem((chunks, state, inner), F32),
            vmem((seqs, state, inner), BF16),
            vmem((count, cut_rows, cut_lanes), BF16),
            vmem((count, cut_rows, cut_lanes), BF16),
            vmem((seqs, state, inner), BF16),
            vmem((parts, block, LANES), BF16),
            vmem((parts, block, LANES), BF16),
            edge,
            edge,
            ring,
            ring,
            line,
            line,
            line,
            line,
        ],
        compiler_params=pltpu.CompilerParams(
            collective_id=3, has_side_effects=True, vmem_limit_bytes=VMEM_LIMIT
        ),
        name="mixer_backward",
    )(*operands)


def body(
    tokens,
    norm_gain,
    gate_input_weight,
    coefficient_weight,
    step_weight,
    conv_x,
    conv_bc,
    conv_bias_x,
    conv_bias_bc,
    dt_bias,
    a_log,
    d_skip,
    gate_gain,
    output_weight,
    cotangent,
):
    seqs, block, width = tokens.shape
    inner = gate_input_weight.shape[2]
    state_part = coefficient_weight.shape[2]
    heads = step_weight.shape[1]
    count, parts = lax.axis_size("seq"), lax.axis_size("head")
    my_head = lax.axis_index("head")
    state = state_part * parts
    rows = seqs * block
    col_count = width // parts
    half = LANES // 2
    dims = (count, parts, seqs, block, inner, heads, state)

    flat_tokens = tokens.reshape(rows, width)
    small_weight = jnp.concatenate(
        [
            step_weight,
            jnp.zeros((width, half - heads), BF16),
            coefficient_weight.reshape(width, 2 * state_part),
        ],
        axis=1,
    )
    both_weights = gate_input_weight.transpose(1, 0, 2)
    gate_pre, x_pre, small, normed_t, row_scale = project(
        flat_tokens, norm_gain[None], both_weights, small_weight
    )

    chan = jnp.concatenate(
        [
            conv_x,
            conv_bias_x[None],
            gate_gain[None],
            jnp.repeat(d_skip, inner // heads)[None],
            jnp.zeros((1, inner), F32),
        ]
    )
    twice = jnp.concatenate(
        [conv_bc.reshape(KER, 2 * state_part), conv_bias_bc.reshape(1, 2 * state_part)]
    )
    per_head = jnp.stack([dt_bias, -jnp.exp(a_log), jnp.zeros_like(a_log)])
    vec = jnp.concatenate(
        [
            jnp.concatenate([twice, twice], axis=1),
            jnp.pad(per_head, ((0, 0), (0, LANES - heads))),
        ]
    )
    device, lane, channel = np.meshgrid(
        np.arange(parts), np.arange(LANES), np.arange(2 * state), indexing="ij"
    )
    is_c, at = channel // state, channel % state
    unpack = np.stack(
        [
            (lane == s * half + is_c * state_part + at - device * state_part)
            & (at // state_part == device)
            for s in range(seqs)
        ]
    ).astype(np.float32)
    pack = jnp.asarray(unpack.transpose(1, 0, 3, 2), BF16)
    unpack = jnp.asarray(unpack.reshape(seqs, parts * LANES, 2 * state), BF16)
    expand = np.arange(LANES)[:, None] == np.arange(inner)[None, :] // (inner // heads)
    gather = jnp.asarray(expand.T.astype(np.float32), BF16)
    expand = jnp.asarray(expand.astype(np.float32))
    cot = cotangent.reshape(rows, width)

    xact, bc, conv, convbc, dt, cum, states, ng_t, dgate, dy, dyy, decay, sums = forward(
        dims,
        x_pre,
        gate_pre,
        small,
        chan,
        vec,
        unpack,
        expand,
        gather,
        cot,
        output_weight,
    )
    def padded(array_in):
        return jnp.pad(array_in, ((0, -array_in.shape[0] % (count * 16)), (0, 0)))

    mixer = mul(ng_t, output_weight, TN)
    mixed = lax.psum_scatter(
        mixer.astype(BF16), "head", scatter_dimension=1, tiled=True
    ).astype(F32)
    own_inputs = lax.dynamic_slice_in_dim(flat_tokens, my_head * col_count, col_count, 1)
    block_out = (own_inputs.astype(F32) + mixed).astype(BF16)

    *streams, grad_input, sums = backward(
        dims,
        dy,
        xact,
        bc,
        conv,
        convbc,
        dt,
        cum,
        states,
        dyy,
        decay,
        x_pre,
        small,
        chan,
        vec,
        pack,
        gather,
        padded(normed_t),
        padded(ng_t),
        cot,
        dgate,
        small_weight,
        sums,
        norm_gain[None],
        row_scale,
        flat_tokens,
        both_weights,
    )
    g_in, g_w_out, g_small = finish_weights(width, inner, streams)
    taps = sums[:, :inner]
    lanes = sums[:, inner:]
    taps_bc = (lanes[:, :half] + lanes[:, half:]).reshape(8, 2, state_part)
    return (
        block_out.reshape(seqs, block, col_count),
        grad_input.reshape(seqs, block, col_count),
        taps[KER + 3, :col_count],
        g_in,
        g_small[half:].reshape(2, state_part, width).transpose(2, 0, 1),
        g_small[:heads].T,
        taps[:KER],
        taps_bc[:KER],
        taps[KER],
        taps_bc[KER],
        lanes[KER + 1, :heads],
        lanes[KER + 2, :heads],
        taps[KER + 2].reshape(heads, inner // heads).sum(1),
        taps[KER + 1],
        g_w_out,
    )


def solution(mesh):
    placed = (
        P(None, "seq", None),
        P(),
        P(None, None, "head"),
        P(None, None, "head"),
        P(None, "head"),
        P(None, "head"),
        P(None, None, "head"),
        P("head"),
        P(None, "head"),
        P("head"),
        P("head"),
        P("head"),
        P("head"),
        P("head", None),
        P(None, "seq", None),
    )
    return jax.shard_map(
        body,
        mesh=mesh,
        in_specs=placed,
        out_specs=(
            P(None, "seq", "head"),
            P(None, "seq", "head"),
            P("head"),
            P(None, None, "head"),
            P(None, None, "head"),
            P(None, "head"),
            P(None, "head"),
            P(None, None, "head"),
            P("head"),
            P(None, "head"),
            P("head"),
            P("head"),
            P("head"),
            P("head"),
            P("head", None),
        ),
        check_vma=False,
    )
```

```python
import functools

import jax
import jax.numpy as jnp
import numpy as np
from jax import lax
from jax.experimental import pallas as pl
from jax.experimental.pallas import tpu as pltpu
from jax.sharding import PartitionSpec as P

KER = 4
EPSILON = 1e-05
CHUNK = 128
LANES = 128
MESH = pl.DeviceIdType.MESH
F32 = jnp.float32
BF16 = jnp.bfloat16
EXACT = lax.Precision.HIGHEST
VMEM_LIMIT = 61 * 2**20
NN = ((1,), (0,))
NT = ((1,), (1,))
TN = ((0,), (0,))


def mul(left, right, how, precision=None):
    return lax.dot_general(
        left, right, (how, ((), ())), precision=precision, preferred_element_type=F32
    )


def sigmoid(v):
    return 0.5 * jnp.tanh(0.5 * v) + 0.5


def softplus(v):
    e = jnp.exp(-jnp.abs(v))
    u = 1.0 + e
    near = u - 1.0
    log1p = jnp.where(near == 0.0, e, jnp.log(u) * (e / jnp.where(near == 0.0, 1.0, near)))
    return jnp.maximum(v, 0.0) + log1p


def iota(shape, dim):
    return lax.broadcasted_iota(jnp.int32, shape, dim)


def ds(start, size):
    return pl.ds(pl.multiple_of(start, size), size)


def pair_of(values, pair):
    low = values[:, 2 * pair : 2 * pair + 1]
    high = values[:, 2 * pair + 1 : 2 * pair + 2]
    return jnp.where(iota((values.shape[0], LANES), 1) < LANES // 2, low, high)


def spread(values, pairs):
    return jnp.concatenate([pair_of(values, p) for p in range(pairs)], axis=1)


def eights(v):
    return jnp.sum(v.reshape(v.shape[0] // 8, 8, v.shape[1]), axis=0)


def halves_of(v):
    high = v.astype(BF16)
    return high, (v - high.astype(F32)).astype(BF16)


def head_sums(v, gather):
    high, low = halves_of(v)
    return mul(high, gather, NN) + mul(low, gather, NN)


def remote(src, dst, send, recv, place, head):
    return pltpu.make_async_remote_copy(
        src_ref=src,
        dst_ref=dst,
        send_sem=send,
        recv_sem=recv,
        device_id=(place, head),
        device_id_type=MESH,
    )


def meet(count, parts):
    place, head = lax.axis_index("seq"), lax.axis_index("head")
    barrier = pltpu.get_barrier_semaphore()

    def along_seq(i, _):
        other = lax.rem(place + i, count)
        pl.semaphore_signal(barrier, inc=1, device_id=(other, head), device_id_type=MESH)
        return 0

    def along_head(i, _):
        other = lax.rem(head + i, parts)
        pl.semaphore_signal(barrier, inc=1, device_id=(place, other), device_id_type=MESH)
        return 0

    lax.fori_loop(1, count, along_seq, 0)
    lax.fori_loop(1, parts, along_head, 0)
    pl.semaphore_wait(barrier, count - 1 + parts - 1)


def loop(low, high, step):
    def one(i, _):
        step(i)
        return 0

    lax.fori_loop(low, high, one, 0)


def line_copy(count, src, dst, send, recv):
    place, head = lax.axis_index("seq"), lax.axis_index("head")

    def copy(i):
        other = lax.rem(place + i, count)
        return remote(src(other), dst(place), send.at[i], recv.at[i], other, head)

    return copy


def head_copy(parts, src, dst, send, recv):
    place, head = lax.axis_index("seq"), lax.axis_index("head")

    def copy(i):
        other = lax.rem(head + i, parts)
        return remote(src(other), dst(head), send.at[i], recv.at[i], place, other)

    return copy


def cut_of(count, seqs, state, inner):
    rows = max(16, seqs * state // count)
    lane_cuts = count * rows // (seqs * state)
    return rows, lane_cuts, inner // lane_cuts


def piece_of(k, count, seqs, state, inner):
    rows, lane_cuts, lanes = cut_of(count, seqs, state, inner)
    each = count // seqs
    seq, rest = k // each, lax.rem(k, each)
    row = pl.multiple_of(rest // lane_cuts * rows, rows)
    if lane_cuts == 1:
        return seq, pl.ds(row, rows), slice(None)
    lane = pl.multiple_of(lax.rem(rest, lane_cuts) * lanes, lanes)
    return seq, pl.ds(row, rows), pl.ds(lane, lanes)


def carry_exchange(dims, local, arrived, passed, incoming, decay_ref, sems, reverse):
    count, _, seqs, _, inner, _, state = dims
    place, head = lax.axis_index("seq"), lax.axis_index("head")
    send, recv, back_send, back_recv = sems
    piece = functools.partial(piece_of, count=count, seqs=seqs, state=state, inner=inner)
    rows, _, lanes = cut_of(count, seqs, state, inner)

    def at(ref, k):
        seq, row, lane = piece(k)
        return ref.at[seq, row, lane]

    out = line_copy(count, lambda other: at(local, other), lambda k: arrived.at[k], send, recv)

    def back(j):
        i = lax.rem(j - place + count, count)
        return remote(
            passed.at[j], at(incoming, place), back_send.at[i], back_recv.at[i], j, head
        )

    def start():
        loop(1, count, lambda i: out(i).start())
        seq, row, lane = piece(place)
        arrived[place] = local[seq, row, lane]

    def carry():
        seq, row, lane = piece(place)
        held = jnp.zeros((rows, lanes), F32)
        for step in range(count):
            j = count - 1 - step if reverse else step
            i = lax.rem(place - j + count, count)

            @pl.when(j != place)
            def _():
                out(i).wait_recv()

            passed[j] = held.astype(passed.dtype)

            @pl.when(j != place)
            def _():
                back(j).start()

            @pl.when(j == place)
            def _():
                incoming[seq, row, lane] = passed[j]

            decay = decay_ref[seq, pl.ds(j, 1), lane]
            held = decay * held + arrived[j].astype(F32)

    def finish():
        def one(i):
            out(i).wait_send()
            back(lax.rem(place + i, count)).wait()

        loop(1, count, one)

    return start, carry, finish


def forward_kernel(
    dims,
    x_ref,
    gate_far,
    small_ref,
    chan_ref,
    vec_ref,
    unpack_ref,
    expand_ref,
    gather_ref,
    cot_far,
    wout_far,
    xact_far,
    bc_far,
    conv_far,
    convbc_ref,
    dt_far,
    cum_far,
    states_far,
    ng_t_far,
    dgate_far,
    dy_far,
    dyy_far,
    decay_ref,
    sums_ref,
    gate_ref,
    cot_ref,
    wout_ref,
    xact_ref,
    bc_ref,
    conv_ref,
    dt_ref,
    cum_ref,
    states_ref,
    ng_t_ref,
    dgate_ref,
    dy_ref,
    dyy_ref,
    fetch_sem,
    keep_sem,
    edge_x,
    edge_s,
    ext,
    extbc,
    bc_all,
    fresh,
    y_ref,
    dng_ref,
    gated_ref,
    decays,
    local,
    arrived,
    passed,
    incoming,
    rowsum,
    edge_send,
    edge_recv,
    dec_send,
    dec_recv,
    bc_send,
    bc_recv,
    st_send,
    st_recv,
    back_send,
    back_recv,
    row_send,
    row_recv,
):
    count, parts, seqs, block, inner, heads, state = dims
    place, head = lax.axis_index("seq"), lax.axis_index("head")
    chunks = block // CHUNK
    pairs = heads // 2
    total = seqs * chunks
    fetches = [
        pltpu.make_async_copy(src, dst, fetch_sem.at[k])
        for k, (src, dst) in enumerate(
            ((cot_far, cot_ref), (wout_far, wout_ref), (gate_far, gate_ref))
        )
    ]
    for copy in fetches:
        copy.start()
    keeps = [
        pltpu.make_async_copy(src, dst, keep_sem.at[k])
        for k, (src, dst) in enumerate(
            (
                (xact_ref, xact_far),
                (bc_ref, bc_far),
                (conv_ref, conv_far),
                (dt_ref, dt_far),
                (cum_ref, cum_far),
                (states_ref, states_far),
                (ng_t_ref, ng_t_far),
                (dgate_ref, dgate_far),
                (dy_ref, dy_far),
                (dyy_ref, dyy_far),
            )
        )
    ]
    meet(count, parts)

    def edge_copies(ahead):
        copies = []
        for s in range(seqs):
            rows = pl.ds(s * block + block - 8, 8)
            for k, (src, dst) in enumerate(((x_ref, edge_x), (small_ref, edge_s))):
                copies.append(
                    remote(
                        src.at[rows], dst.at[s], edge_send.at[k, s], edge_recv.at[k, s], ahead, head
                    )
                )
        return copies

    after = lax.rem(place + 1, count)

    @pl.when(place < count - 1)
    def _():
        for c in edge_copies(after):
            c.start()

    lower = (iota((CHUNK, CHUNK), 0) >= iota((CHUNK, CHUNK), 1)).astype(F32)
    for s in range(seqs):

        def steps(c, logs):
            rows = ds((s * chunks + c) * CHUNK, CHUNK)
            dt = softplus(small_ref[rows, :] + vec_ref[5:6, :])
            cum = mul(lower, dt * vec_ref[6:7, :], NN, EXACT)
            dt_ref[rows, :] = dt
            cum_ref[rows, :] = cum
            return logs + cum[CHUNK - 1 :, :]

        logs = lax.fori_loop(0, chunks, steps, jnp.zeros((1, LANES), F32))
        decays[place, s : s + 1, :] = jnp.exp(logs)

    dec = line_copy(count, lambda _: decays.at[place], lambda k: decays.at[k], dec_send, dec_recv)
    loop(1, count, lambda i: dec(i).start())

    @pl.when(place > 0)
    def _():
        for c in edge_copies(after):
            c.wait_recv()

    @pl.when(place == 0)
    def _():
        edge_x[...] = jnp.zeros_like(edge_x)
        edge_s[...] = jnp.zeros_like(edge_s)

    def packed(low, high):
        return jnp.where(
            iota(low.shape, 1) < LANES // 2, pltpu.roll(low, LANES // 2, 1), high
        )

    extbc[0:8, :] = packed(edge_s[0], edge_s[1])
    extbc[8:, :] = packed(small_ref[0:block, :], small_ref[block:, :])
    conv = vec_ref[4:5, :]
    for k in range(KER):
        conv = conv + vec_ref[k : k + 1, :] * extbc[pl.ds(8 - (KER - 1) + k, block), :]
    convbc_ref[...] = conv
    bc_all[head] = (conv * sigmoid(conv)).astype(BF16)
    share = head_copy(parts, lambda _: bc_all.at[head], lambda k: bc_all.at[k], bc_send, bc_recv)
    loop(1, parts, lambda i: share(i).start())

    def x_chunk(t):
        rows = ds(t * CHUNK, CHUNK)
        s, c = t // chunks, lax.rem(t, chunks)
        before = pl.ds(pl.multiple_of(jnp.maximum(t * CHUNK - 8, 0), 8), 8)
        for b in range(inner // LANES):
            lane = slice(b * LANES, (b + 1) * LANES)
            ext[0:8, lane] = jnp.where(c == 0, edge_x[s, :, lane], x_ref[before, lane])
            ext[8:, lane] = x_ref[rows, lane]
            conv = chan_ref[4:5, lane]
            for k in range(KER):
                conv = conv + chan_ref[k : k + 1, lane] * ext[pl.ds(8 - (KER - 1) + k, CHUNK), lane]
            conv_ref[rows, lane] = conv
            xact_ref[rows, lane] = (conv * sigmoid(conv)).astype(BF16)

    loop(0, total, x_chunk)

    loop(1, parts, lambda i: share(i).wait())
    everything = jnp.concatenate([bc_all[k] for k in range(parts)], axis=1)
    for s in range(seqs):
        bc_ref[s * block : (s + 1) * block, :] = mul(everything, unpack_ref[s], NN).astype(BF16)

    for s in range(seqs):

        def add(c, held):
            t = s * chunks + c
            rows = ds(t * CHUNK, CHUNK)
            cum, dt = cum_ref[rows, :], dt_ref[rows, :]
            end = cum[CHUNK - 1 :, :]
            tail = jnp.exp(end - cum) * dt
            weighted = jnp.concatenate(
                [
                    (
                        xact_ref[rows, p * LANES : (p + 1) * LANES].astype(F32) * pair_of(tail, p)
                    ).astype(BF16)
                    for p in range(pairs)
                ],
                axis=1,
            )
            new = mul(bc_ref[rows, 0:state], weighted, TN)
            fresh[t] = new
            return spread(jnp.exp(end), pairs) * held + new

        held = lax.fori_loop(0, chunks, add, jnp.zeros((state, inner), F32))
        local[s] = held

    start, carry, finish = carry_exchange(
        dims,
        local,
        arrived,
        passed,
        incoming,
        decay_ref,
        (st_send, st_recv, back_send, back_recv),
        False,
    )
    start()
    for copy in keeps[:5]:
        copy.start()

    def within(t):
        rows = ds(t * CHUNK, CHUNK)
        cum, dt = cum_ref[rows, :], dt_ref[rows, :]
        cum_t = cum.T
        scores = mul(bc_ref[rows, state:], bc_ref[rows, 0:state], NT)
        seen = iota((CHUNK, CHUNK), 0) >= iota((CHUNK, CHUNK), 1)
        side = iota((CHUNK, LANES), 1) < LANES // 2
        for p in range(pairs):
            lane = slice(p * LANES, (p + 1) * LANES)
            stepped = (xact_ref[rows, lane].astype(F32) * pair_of(dt, p)).astype(BF16)
            halves = []
            for h in (2 * p, 2 * p + 1):
                gap = cum[:, h : h + 1] - cum_t[h : h + 1, :]
                mixing = (scores * jnp.exp(jnp.where(seen, gap, -1e30))).astype(BF16)
                halves.append(mul(mixing, stepped, NN))
            y_ref[rows, lane] = jnp.where(side, halves[0], halves[1])

    loop(0, total, within)

    loop(1, count, lambda i: dec(i).wait())
    for s in range(seqs):
        decay_ref[s] = mul(decays[:, s, :], expand_ref[...], NN, EXACT)
    carry()

    for copy in fetches:
        copy.wait()
    wide = 2 * LANES

    def back_project(i):
        s, b = i // (inner // wide), lax.rem(i, inner // wide)
        rows, lane = ds(s * block, block), ds(b * wide, wide)
        dng_ref[rows, lane] = mul(cot_ref[rows, :], wout_ref[lane, :], NT)

    loop(0, seqs * (inner // wide), back_project)
    finish()

    for s in range(seqs):

        def gate(c, held):
            t = s * chunks + c
            rows = ds(t * CHUNK, CHUNK)
            cum = cum_ref[rows, :]
            grown = jnp.exp(cum)
            states_ref[t] = held
            high, low = halves_of(held)
            c_rows = bc_ref[rows, state:]
            carried = mul(c_rows, high, NN) + mul(c_rows, low, NN)
            square = jnp.zeros((CHUNK, LANES), F32)
            cross = jnp.zeros((CHUNK, LANES), F32)
            for p in range(pairs):
                lane = slice(p * LANES, (p + 1) * LANES)
                y = y_ref[rows, lane] + carried[:, lane] * pair_of(grown, p)
                y_ref[rows, lane] = y
                out = y + chan_ref[6:7, lane] * xact_ref[rows, lane].astype(F32)
                pre = gate_ref[rows, lane]
                gated = out * (pre * sigmoid(pre))
                gated_ref[rows, lane] = gated
                square = square + gated * gated
                cross = cross + dng_ref[rows, lane] * chan_ref[5:6, lane] * gated
            at = iota((CHUNK, LANES), 1)
            both = jnp.where(
                at == 0,
                jnp.sum(square, axis=1, keepdims=True),
                jnp.where(at == 1, jnp.sum(cross, axis=1, keepdims=True), 0.0),
            )
            rowsum[head, t] = both.T[0:8, :]
            return spread(grown[CHUNK - 1 :, :], pairs) * held + fresh[t]

        lax.fori_loop(0, chunks, gate, incoming[s].astype(F32))

    keeps[5].start()
    rows_copy = head_copy(
        parts, lambda _: rowsum.at[head], lambda k: rowsum.at[k], row_send, row_recv
    )
    loop(1, parts, lambda i: rows_copy(i).start())
    loop(1, parts, lambda i: rows_copy(i).wait())
    sums_ref[...] = jnp.zeros_like(sums_ref)
    channels = inner * parts

    def outputs(t):
        rows = ds(t * CHUNK, CHUNK)
        sums = rowsum[0, t]
        for k in range(1, parts):
            sums = sums + rowsum[k, t]
        turned = jnp.concatenate([sums, jnp.zeros((CHUNK - 8, LANES), F32)], axis=0).T
        scale = lax.rsqrt(turned[:, 0:1] / channels + EPSILON)
        pull = scale * scale * scale * (turned[:, 1:2] / channels)
        dyy = jnp.zeros((CHUNK, LANES), F32)
        for p in range(pairs):
            lane = slice(p * LANES, (p + 1) * LANES)
            pre = gate_ref[rows, lane]
            sg = sigmoid(pre)
            gated, y = gated_ref[rows, lane], y_ref[rows, lane]
            x = xact_ref[rows, lane].astype(F32)
            gain = chan_ref[5:6, lane]
            scaled = gated * scale
            ng_t_ref[lane, rows] = (scaled * gain).T.astype(BF16)
            dng = dng_ref[rows, lane]
            d_gated = scale * (dng * gain) - gated * pull
            d_ssd = d_gated * (pre * sg)
            out = y + chan_ref[6:7, lane] * x
            dgate_ref[rows, lane] = (d_gated * out * (sg * (1.0 + pre * (1.0 - sg)))).astype(BF16)
            dy = d_ssd.astype(BF16)
            dy_ref[rows, lane] = dy
            sums_ref[0:8, lane] += eights(dng * scaled)
            sums_ref[8:16, lane] += eights(d_ssd * x)
            dyy = dyy + head_sums(dy.astype(F32) * y, gather_ref[lane, :])
        dyy_ref[rows, :] = dyy

    loop(0, total, outputs)
    for copy in keeps[6:]:
        copy.start()
    for copy in keeps:
        copy.wait()

    @pl.when(place < count - 1)
    def _():
        for c in edge_copies(after):
            c.wait_send()


def vmem(shape, kind):
    return pltpu.VMEM(shape, kind)


def forward(dims, *operands):
    count, parts, seqs, block, inner, heads, state = dims
    rows = seqs * block
    chunks = rows // CHUNK
    cut_rows, _, cut_lanes = cut_of(count, seqs, state, inner)
    spec, far = pl.BlockSpec(memory_space=pltpu.VMEM), pl.BlockSpec(memory_space=pl.ANY)
    fetched, kept = (1, 8, 9), (0, 1, 2, 4, 5, 6, 7, 8, 9, 10)
    line, ring = pltpu.SemaphoreType.DMA((count,)), pltpu.SemaphoreType.DMA((parts,))
    edge = pltpu.SemaphoreType.DMA((2, seqs))
    outs = [
        ((rows, inner), BF16),
        ((rows, 2 * state), BF16),
        ((rows, inner), F32),
        ((block, LANES), F32),
        ((rows, LANES), F32),
        ((rows, LANES), F32),
        ((chunks, state, inner), F32),
        ((inner, rows), BF16),
        ((rows, inner), BF16),
        ((rows, inner), BF16),
        ((rows, LANES), F32),
        ((seqs, count, inner), F32),
        ((16, inner), F32),
    ]
    return pl.pallas_call(
        functools.partial(forward_kernel, dims),
        out_shape=[jax.ShapeDtypeStruct(*o) for o in outs],
        in_specs=[far if k in fetched else spec for k in range(len(operands))],
        out_specs=[far if k in kept else spec for k in range(len(outs))],
        scratch_shapes=[vmem(operands[k].shape, operands[k].dtype) for k in fetched]
        + [vmem(*outs[k]) for k in kept]
        + [
            pltpu.SemaphoreType.DMA((len(fetched),)),
            pltpu.SemaphoreType.DMA((len(kept),)),
            vmem((seqs, 8, inner), F32),
            vmem((seqs, 8, LANES), F32),
            vmem((CHUNK + 8, inner), F32),
            vmem((block + 8, LANES), F32),
            vmem((parts, block, LANES), BF16),
            vmem((chunks, state, inner), F32),
            vmem((rows, inner), F32),
            vmem((rows, inner), F32),
            vmem((rows, inner), F32),
            vmem((count, 8, LANES), F32),
            vmem((seqs, state, inner), F32),
            vmem((count, cut_rows, cut_lanes), F32),
            vmem((count, cut_rows, cut_lanes), F32),
            vmem((seqs, state, inner), F32),
            vmem((parts, chunks, 8, LANES), F32),
            edge,
            edge,
            line,
            line,
            ring,
            ring,
            line,
            line,
            line,
            line,
            ring,
            ring,
        ],
        compiler_params=pltpu.CompilerParams(
            collective_id=2, has_side_effects=True, vmem_limit_bytes=VMEM_LIMIT
        ),
        name="mixer_forward",
    )(*operands)


def project_kernel(
    tokens_ref, gain_ref, weight_ref, small_weight_ref, gate_ref, x_ref, small_ref, turned_ref, scale_ref
):
    tokens = tokens_ref[...].astype(F32)
    scale = lax.rsqrt(jnp.mean(tokens * tokens, axis=1, keepdims=True) + EPSILON)
    scale_ref[...] = scale
    normed = tokens * scale * gain_ref[...]
    low = normed.astype(BF16)
    turned_ref[...] = low.T
    x_ref[...] = mul(low, weight_ref[1], NN)
    small_ref[...] = mul(low, small_weight_ref[...], NN)
    gate_ref[...] = mul(low, weight_ref[0], NN)


def project(tokens, gain, weights, small_weight):
    rows, width = tokens.shape
    inner = weights.shape[2]
    tall = 2 * CHUNK

    def by_rows(cols):
        return pl.BlockSpec((tall, cols), lambda i: (i, 0))

    def whole(array_in):
        return pl.BlockSpec(array_in.shape, lambda i: (0,) * array_in.ndim)

    return pl.pallas_call(
        project_kernel,
        grid=(rows // tall,),
        in_specs=[by_rows(width), whole(gain), whole(weights), whole(small_weight)],
        out_specs=[
            by_rows(inner),
            by_rows(inner),
            by_rows(LANES),
            pl.BlockSpec((width, tall), lambda i: (0, i)),
            by_rows(1),
        ],
        out_shape=[
            jax.ShapeDtypeStruct((rows, inner), F32),
            jax.ShapeDtypeStruct((rows, inner), F32),
            jax.ShapeDtypeStruct((rows, LANES), F32),
            jax.ShapeDtypeStruct((width, rows), BF16),
            jax.ShapeDtypeStruct((rows, 1), F32),
        ],
        compiler_params=pltpu.CompilerParams(vmem_limit_bytes=VMEM_LIMIT),
        name="project",
    )(tokens, gain, weights, small_weight)


def ring_place(count):
    place = lax.axis_index("seq")
    row, col = place // 2, place % 2
    return jnp.where(col == 0, row, count - 1 - row)


def ring_device(rank, count):
    return jnp.where(rank < count // 2, 2 * rank, 2 * (count - 1 - rank) + 1)


def ring_steps(count, plan, outs, bufs, stages, sems):
    rs_send, rs_recv, ag_send, ag_recv, keep_sem = sems
    far = count // 2
    head = lax.axis_index("head")
    rank = ring_place(count)
    arms = (1, -1)
    peers = [ring_device(lax.rem(rank + a + count, count), count) for a in arms]

    def chunk_at(distance):
        return lax.rem(rank + distance + 2 * count, count)

    def partial(i, chunk):
        left, right, first, cols, _ = plan[i]
        rows = left.shape[0] // count
        return mul(left[ds(chunk * rows, rows), :], right[:, first : first + cols], NN)

    def half(i, arm):
        cols, cut = plan[i][3:]
        return slice(0, cut) if arm == 0 else slice(cut, cols)

    def block_of(i, chunk):
        rows = plan[i][0].shape[0] // count
        return outs[i].at[ds(chunk * rows, rows)]

    def rs(i, arm, step, first=False):
        here = stages[i] if first else bufs[i].at[arm, step - 1]
        there = bufs[i].at[arm, step]
        if first:
            here, there = here.at[:, half(i, arm)], there.at[:, half(i, arm)]
        return remote(
            here, there, rs_send.at[i, arm, step], rs_recv.at[i, arm, step], peers[arm], head
        )

    def ag(i, arm, step, kind="middle"):
        there = block_of(i, chunk_at(-arms[arm] * step))
        here = bufs[i].at[0, far - 1] if kind == "first" else there
        if kind == "last":
            here, there = here.at[:, half(i, arm)], there.at[:, half(i, arm)]
        return remote(
            here, there, ag_send.at[i, arm, step], ag_recv.at[i, arm, step], peers[arm], head
        )

    def keep(i):
        return pltpu.make_async_copy(
            bufs[i].at[0, far - 1], block_of(i, chunk_at(0)), keep_sem.at[i]
        )

    def begin(i):
        stages[i][...] = partial(i, chunk_at(far)).astype(BF16)
        for arm in range(2):
            rs(i, arm, 0, True).start()

    def advance(streams, slot, slots):
        def second(i, arm):
            own = partial(i, chunk_at(arms[arm] * (far - 1)))
            rs(i, arm, 0, True).wait_recv()
            mine, other = half(i, arm), half(i, 1 - arm)
            bufs[i][arm, 0, :, other] = own[:, other].astype(BF16)
            bufs[i][arm, 0, :, mine] = (
                own[:, mine] + bufs[i][arm, 0, :, mine].astype(F32)
            ).astype(BF16)
            rs(i, arm, 1).start()

        def later(i, arm, step):
            own = partial(i, chunk_at(arms[arm] * (far - step)))
            rs(i, arm, step - 1).wait_recv()
            bufs[i][arm, step - 1] = (own + bufs[i][arm, step - 1].astype(F32)).astype(BF16)
            rs(i, arm, step).start()

        def last(i):
            own = partial(i, chunk_at(0))
            for arm in range(2):
                rs(i, arm, far - 1).wait_recv()
                own = own + bufs[i][arm, far - 1].astype(F32)
            bufs[i][0, far - 1] = own.astype(BF16)
            for arm in range(2):
                ag(i, arm, 0, "first").start()
            keep(i).start()

        low, high = slot * far // slots, (slot + 1) * far // slots
        if low == 0 < high:
            for i in streams:
                for arm in range(2):
                    second(i, arm)

        def middle(step):
            for i in streams:
                for arm in range(2):
                    later(i, arm, step)

        if min(high, far - 1) > max(low, 1):
            loop(max(low, 1) + 1, min(high, far - 1) + 1, middle)
        if high == far:
            for i in streams:
                last(i)

    def pass_on(streams, slot, slots):
        def middle(step):
            for i in streams:
                for arm in range(2):
                    ag(i, arm, step - 1).wait_recv()
                    ag(i, arm, step).start()

        steps = far - 1
        low, high = slot * steps // slots, (slot + 1) * steps // slots
        if min(high, steps - 1) > low:
            loop(low + 1, min(high, steps - 1) + 1, middle)
        if low < high == steps:
            for i in streams:
                for arm in range(2):
                    ag(i, arm, steps - 1).wait_recv()
                    ag(i, arm, steps, "last").start()

    def pass_end(streams):
        for i in streams:
            for arm in range(2):
                ag(i, arm, far - 1, "last").wait_recv()

    def drain(streams):
        for i in streams:
            for arm in range(2):
                rs(i, arm, 0, True).wait_send()
                ag(i, arm, 0, "first").wait_send()
                ag(i, arm, far - 1, "last").wait_send()
            keep(i).wait()

        def one(step):
            for i in streams:
                for arm in range(2):
                    rs(i, arm, step).wait_send()

                    @pl.when(step < far - 1)
                    def _():
                        ag(i, arm, step).wait_send()

        loop(1, far, one)

    return begin, advance, pass_on, pass_end, drain


def finish_kernel(
    gate,
    narrow_low,
    narrow,
    out,
    sums_ref,
    gather_ref,
    block_far,
    input_far,
    gin_ref,
    wout_ref,
    coef_ref,
    step_ref,
    taps_ref,
    taps_bc_ref,
    bias_ref,
    bias_bc_ref,
    dt_ref,
    log_ref,
    skip_ref,
    gain_ref,
    norm_ref,
    block_out,
    input_out,
):
    inner, half = gate.shape[1], narrow_low.shape[1]
    heads, state_part = step_ref.shape[0], bias_bc_ref.shape[1]
    block_out[...] = block_far[...]
    input_out[...] = input_far[...]

    @pl.when(pl.program_id(0) == 0)
    def _():
        lanes = sums_ref[:, inner:]
        both = lanes + pltpu.roll(lanes, LANES // 2, 1)
        taps_ref[...] = sums_ref[0:KER, 0:inner]
        bias_ref[...] = sums_ref[KER : KER + 1, 0:inner]
        gain_ref[...] = sums_ref[KER + 1 : KER + 2, 0:inner]
        norm_ref[...] = sums_ref[KER + 3 : KER + 4, 0 : norm_ref.shape[1]]
        for k in range(2):
            at = slice(k * state_part, (k + 1) * state_part)
            taps_bc_ref[:, k, :] = both[0:KER, at]
            bias_bc_ref[k : k + 1, :] = both[KER : KER + 1, at]
        dt_ref[...] = lanes[KER + 1 : KER + 2, 0:heads]
        log_ref[...] = lanes[KER + 2 : KER + 3, 0:heads]
        skip_ref[...] = head_sums(sums_ref[:, 0:inner], gather_ref[...])[KER + 2 : KER + 3, 0:heads]

    gin_ref[:, 0, :] = gate[...].astype(F32)
    gin_ref[:, 1, 0:half] = narrow_low[...].astype(F32)
    gin_ref[:, 1, half:] = narrow[:, 0 : inner - half].astype(F32)
    small = narrow[:, inner - half :].astype(F32).T
    step_ref[...] = small[0:heads]
    for k in range(2):
        low = LANES // 2 + k * state_part
        coef_ref[k] = small[low : low + state_part]
    wout_ref[...] = out[...].astype(F32)


def finish(width, inner, heads, state_part, streams, sums, gather, block_out, grad_input):
    steps = 4
    tall, low, part = width // steps, inner // steps, grad_input.shape[0] // steps
    out, gate, narrow_low, narrow = streams
    cols = grad_input.shape[1]
    mine = pl.BlockSpec((part, cols), lambda i: (i, 0))

    def block(array_in, rows):
        return pl.BlockSpec((rows, array_in.shape[1]), lambda i: (i, 0))

    def whole(shape):
        return pl.BlockSpec(shape, lambda i: (0,) * len(shape))

    little = [
        (KER, inner),
        (KER, 2, state_part),
        (1, inner),
        (2, state_part),
        (1, heads),
        (1, heads),
        (1, heads),
        (1, inner),
        (1, cols),
    ]
    return pl.pallas_call(
        finish_kernel,
        grid=(steps,),
        in_specs=[block(gate, tall), block(narrow_low, tall), block(narrow, tall), block(out, low)]
        + [whole(sums.shape), whole(gather.shape), mine, mine],
        out_specs=[
            pl.BlockSpec((tall, 2, inner), lambda i: (i, 0, 0)),
            pl.BlockSpec((low, width), lambda i: (i, 0)),
            pl.BlockSpec((2, state_part, tall), lambda i: (0, 0, i)),
            pl.BlockSpec((heads, tall), lambda i: (0, i)),
        ]
        + [whole(s) for s in little]
        + [mine, mine],
        out_shape=[
            jax.ShapeDtypeStruct((width, 2, inner), F32),
            jax.ShapeDtypeStruct((inner, width), F32),
            jax.ShapeDtypeStruct((2, state_part, width), F32),
            jax.ShapeDtypeStruct((heads, width), F32),
        ]
        + [jax.ShapeDtypeStruct(s, F32) for s in little]
        + [
            jax.ShapeDtypeStruct(block_out.shape, BF16),
            jax.ShapeDtypeStruct(grad_input.shape, F32),
        ],
        compiler_params=pltpu.CompilerParams(vmem_limit_bytes=VMEM_LIMIT),
        name="finish",
    )(gate, narrow_low, narrow, out, sums, gather, block_out, grad_input)


STEPS = 4


def backward_kernel(
    dims,
    dy_ref,
    xact_far,
    bc_ref,
    conv_ref,
    convbc_ref,
    dt_ref,
    cum_ref,
    states_far,
    dyy_ref,
    decay_ref,
    x_far,
    small_ref,
    chan_ref,
    vec_ref,
    pack_far,
    gather_ref,
    normed_t_far,
    ng_t_far,
    cot_far,
    dgate_far,
    small_weight_far,
    sums_ref,
    gain_ref,
    row_scale_ref,
    tokens_ref,
    weight_ref,
    wout_far,
    *rest,
):
    count, parts, seqs, block, inner, heads, state = dims
    outs, rest = rest[:4], rest[4:]
    grad_ref, total_ref, mixed_ref, *rest = rest
    bufs, rest = rest[:4], rest[4:]
    stages, rest = rest[:4], rest[4:]
    fetched, rest = rest[:7], rest[7:]
    fetch_sem, *rest = rest
    (
        dx_ref,
        gx_ref,
        gbc_ref,
        gdt_ref,
        weights,
        conv_buf,
        state_buf,
        dn_out,
        dn_in,
        wout,
        mix_in,
        token_buf,
        rowsum,
        shared,
        rs_send,
        rs_recv,
        ag_send,
        ag_recv,
        keep_sem,
        weight_sem,
        conv_sem,
        state_sem,
        x_sem,
        token_sem,
        dn_send,
        dn_recv,
        wout_sem,
        mix_send,
        mix_recv,
        row_send,
        row_recv,
        sum_send,
        sum_recv,
        *rest,
    ) = rest
    (
        dconv,
        dconvbc,
        prebc,
        dbc,
        ddt,
        local,
        arrived,
        passed,
        incoming,
        bc_out,
        bc_in,
        edge_send,
        edge_recv,
        bc_send,
        bc_recv,
        st_send,
        st_recv,
        back_send,
        back_recv,
    ) = rest
    sources = (
        ng_t_far,
        cot_far,
        normed_t_far,
        dgate_far,
        xact_far,
        small_weight_far,
        pack_far,
    )
    fetches = [
        pltpu.make_async_copy(src, dst, fetch_sem.at[k])
        for k, (src, dst) in enumerate(zip(sources, fetched))
    ]
    for copy in fetches:
        copy.start()
    (
        ng_t_ref,
        cot_ref,
        normed_t_ref,
        dgate_ref,
        xact_ref,
        small_weight_ref,
        pack_ref,
    ) = fetched
    place, head = lax.axis_index("seq"), lax.axis_index("head")
    chunks = block // CHUNK
    pairs = heads // 2
    total = seqs * chunks
    rows_all = seqs * block
    width = cot_ref.shape[1]
    cols = width // parts
    plan = (
        (ng_t_ref, cot_ref, 0, width, width // 2),
        (normed_t_ref, dgate_ref, 0, inner, inner // 2),
        (normed_t_ref, dx_ref, 0, inner // 2, LANES),
        (normed_t_ref, dx_ref, inner // 2, inner // 2 + LANES, 2 * LANES),
    )
    begin, advance, pass_on, pass_end, drain = ring_steps(
        count, plan, outs, bufs, stages, (rs_send, rs_recv, ag_send, ag_recv, keep_sem)
    )
    out, gate, late = (0,), (1,), (2, 3)
    meet(count, parts)
    gdt_ref[...] = jnp.zeros_like(gdt_ref)

    token_copy = pltpu.make_async_copy(
        tokens_ref.at[:, pl.ds(pl.multiple_of(head * cols, cols), cols)], token_buf, token_sem
    )
    token_copy.start()

    def weight_copy(i):
        other = lax.rem(head + i, parts)
        return pltpu.make_async_copy(
            weight_ref.at[:, pl.ds(pl.multiple_of(other * cols, cols), cols)],
            weights.at[lax.rem(i + 1, 2)],
            weight_sem.at[lax.rem(i + 1, 2)],
        )

    def conv_copy(q):
        t = q // chunks * chunks + chunks - 1 - lax.rem(q, chunks)
        slot = lax.rem(q, 2)
        return pltpu.make_async_copy(
            conv_ref.at[ds(t * CHUNK, CHUNK)], conv_buf.at[slot], conv_sem.at[slot]
        )

    def state_copy(q):
        t = q // chunks * chunks + chunks - 1 - lax.rem(q, chunks)
        slot = lax.rem(q, 2)
        return pltpu.make_async_copy(states_far.at[t], state_buf.at[slot], state_sem.at[slot])

    conv_copy(0).start()
    state_copy(0).start()
    weight_copy(1).start()
    for copy in fetches[:4]:
        copy.wait()
    for i in out + gate:
        begin(i)

    tall = 2 * CHUNK

    def wout_copy(i):
        other = lax.rem(head + i, parts)
        return pltpu.make_async_copy(
            wout_far.at[:, pl.ds(pl.multiple_of(other * cols, cols), cols)],
            wout.at[i % 2],
            wout_sem.at[i % 2],
        )

    def mix_copy(i):
        other = lax.rem(head + i, parts)
        return remote(
            dn_out.at[other], mix_in.at[i - 1], mix_send.at[i], mix_recv.at[i], place, other
        )

    def mix(i):
        other = lax.rem(head + i, parts)
        if i < parts:
            wout_copy(i + 1).start()
        wout_copy(i).wait()

        def some(r):
            rows = ds(r * tall, tall)
            dn_out[other, rows, :] = mul(ng_t_ref[0:inner, rows], wout[i % 2], TN).astype(BF16)

        loop(0, rows_all // tall, some)
        if i < parts:
            mix_copy(i).start()

    wout_copy(1).start()

    for s in range(seqs):

        def alone(i, held):
            t = s * chunks + chunks - 1 - i
            rows = ds(t * CHUNK, CHUNK)
            grown = jnp.exp(cum_ref[rows, :])
            weighted = jnp.concatenate(
                [
                    (
                        dy_ref[rows, p * LANES : (p + 1) * LANES].astype(F32) * pair_of(grown, p)
                    ).astype(BF16)
                    for p in range(pairs)
                ],
                axis=1,
            )
            new = mul(bc_ref[rows, state:], weighted, TN)
            return spread(grown[CHUNK - 1 :, :], pairs) * held + new

        held = lax.fori_loop(0, chunks, alone, jnp.zeros((state, inner), F32))
        local[s] = held.astype(BF16)

    start, carry, finish = carry_exchange(
        dims,
        local,
        arrived,
        passed,
        incoming,
        decay_ref,
        (st_send, st_recv, back_send, back_recv),
        True,
    )
    start()
    advance(out, 0, STEPS)
    mix(1)
    advance(gate, 0, STEPS)
    mix(2)
    advance(out, 1, STEPS)
    carry()
    advance(gate, 1, STEPS)
    for copy in fetches[4:]:
        copy.wait()
    finish()
    mix(3)
    advance(out, 2, STEPS)
    for i in range(4, parts + 1):
        mix(i)

    side = iota((CHUNK, LANES), 1) < LANES // 2
    seen = iota((CHUNK, CHUNK), 0) <= iota((CHUNK, CHUNK), 1)
    upper = seen.astype(F32)
    for s in range(seqs):

        def chunk(i, held):
            t = s * chunks + chunks - 1 - i
            rows = ds(t * CHUNK, CHUNK)
            out_rows = ds((s * chunks + chunks - 1 - i) * CHUNK, CHUNK)
            turn = s * chunks + i
            conv_copy(turn).wait()
            state_copy(turn).wait()

            @pl.when(turn + 1 < total)
            def _():
                conv_copy(turn + 1).start()
                state_copy(turn + 1).start()

            cum, dt = cum_ref[rows, :], dt_ref[rows, :]
            cum_t = cum.T
            grown = jnp.exp(cum)
            end = cum[CHUNK - 1 :, :]
            tail = jnp.exp(end - cum)
            b_rows, c_rows = bc_ref[rows, 0:state], bc_ref[rows, state:]
            scores = mul(b_rows, c_rows, NT)
            low = held.astype(BF16)
            begun = state_buf[lax.rem(turn, 2)]
            begun_high, begun_low = halves_of(begun)
            pulled = mul(b_rows, low, NN)
            grad_scores = jnp.zeros((CHUNK, CHUNK), F32)
            d_x_sum = jnp.zeros((CHUNK, LANES), F32)
            d_fall = jnp.zeros((CHUNK, LANES), F32)
            into_x = []
            into_y = []
            last = []
            for p in range(pairs):
                lane = slice(p * LANES, (p + 1) * LANES)
                x, dy = xact_ref[rows, lane], dy_ref[rows, lane]
                xf, dyf = x.astype(F32), dy.astype(F32)
                dt_p, tail_p = pair_of(dt, p), pair_of(tail, p)
                stepped = xf * dt_p
                low_step = stepped.astype(BF16)
                halves = []
                for k, h in enumerate((2 * p, 2 * p + 1)):
                    gap = cum_t[h : h + 1, :] - cum[:, h : h + 1]
                    fade = jnp.exp(jnp.where(seen, gap, -1e30))
                    own = jnp.where(side if k == 0 else ~side, low_step, jnp.zeros_like(low_step))
                    grad_scores = grad_scores + mul(own, dy, NT) * fade
                    halves.append(mul((scores * fade).astype(BF16), dy, NN))
                from_state = pulled[:, lane] * tail_p
                d_step_x = jnp.where(side, halves[0], halves[1]) + from_state
                rounded = low_step.astype(F32)
                d_x_sum = d_x_sum + head_sums(xf * d_step_x, gather_ref[lane, :])
                d_fall = d_fall + head_sums(rounded * d_step_x, gather_ref[lane, :])
                into_x.append((stepped * tail_p).astype(BF16))
                into_y.append((dyf * pair_of(grown, p)).astype(BF16))
                last.append(jnp.sum(rounded * from_state, axis=0, keepdims=True))
                conv = conv_buf[lax.rem(turn, 2), :, lane]
                sg = sigmoid(conv)
                d_act = dt_p * d_step_x + chan_ref[6:7, lane] * dyf
                dconv[s, ds((chunks - 1 - i) * CHUNK, CHUNK), lane] = d_act * (
                    sg * (1.0 + conv * (1.0 - sg))
                )
            low_scores = grad_scores.astype(BF16)
            d_b = mul(low_scores, c_rows, NN) + mul(jnp.concatenate(into_x, axis=1), low, NT)
            into_y = jnp.concatenate(into_y, axis=1)
            d_c = mul(low_scores, b_rows, TN) + mul(into_y, begun_high, NT)
            d_c = d_c + mul(into_y, begun_low, NT)
            dbc[out_rows, 0:state] = d_b.astype(BF16)
            dbc[out_rows, state:] = d_c.astype(BF16)
            fall = spread(grown[CHUNK - 1 :, :], pairs)
            ends = jnp.concatenate(last, axis=1) + fall * jnp.sum(
                held * begun, axis=0, keepdims=True
            )
            ends = head_sums(jnp.broadcast_to(ends, (8, inner)), gather_ref[...])[0:1, :]
            d_log = mul(upper, dyy_ref[rows, :] - d_fall, NN, EXACT) + ends
            d_step = d_x_sum + vec_ref[6:7, :] * d_log
            d_dt = d_step * sigmoid(small_ref[rows, :] + vec_ref[5:6, :])
            gdt_ref[0:8, :] += eights(d_dt)
            gdt_ref[8:16, :] += eights(d_log * (dt * vec_ref[6:7, :]))
            ddt[out_rows, :] = d_dt


            @pl.when(turn == total * 3 // 8)
            def _():
                advance(gate, 2, STEPS)

            @pl.when(turn == total * 6 // 8)
            def _():
                advance(out, 3, STEPS)

            return fall * held + mul(c_rows, into_y, TN)

        lax.fori_loop(0, chunks, chunk, incoming[s].astype(F32))

    def pack(k):
        piece = mul(dbc[0:block, :], pack_ref[k, 0], NN)
        return (piece + mul(dbc[block:, :], pack_ref[k, 1], NN)).astype(BF16)

    def pack_one(k):
        bc_out[k] = pack(k)

    def x_copy(t):
        slot = lax.rem(t, 2)
        return pltpu.make_async_copy(
            x_far.at[ds(t * CHUNK, CHUNK)], conv_buf.at[slot], x_sem.at[slot]
        )

    x_copy(0).start()
    advance(gate, 3, STEPS)
    loop(0, parts, pack_one)
    share = head_copy(parts, lambda k: bc_out.at[k], lambda k: bc_in.at[k], bc_send, bc_recv)
    loop(1, parts, lambda i: share(i).start())

    before = lax.rem(place + count - 1, count)

    def edge_copy(s):
        return remote(
            dconv.at[s, pl.ds(0, 8)],
            dconv.at[s, pl.ds(block, 8)],
            edge_send.at[s],
            edge_recv.at[s],
            before,
            head,
        )

    def edge_bc():
        return remote(
            dconvbc.at[pl.ds(0, 8)],
            dconvbc.at[pl.ds(block, 8)],
            edge_send.at[seqs],
            edge_recv.at[seqs],
            before,
            head,
        )

    @pl.when(place > 0)
    def _():
        for s in range(seqs):
            edge_copy(s).start()

    pass_on(out, 0, 3)
    loop(1, parts, lambda i: share(i).wait())
    bc_in[head] = bc_out[head]
    d_act = bc_in[0].astype(F32)
    for k in range(1, parts):
        d_act = d_act + bc_in[k].astype(F32)
    conv = convbc_ref[...]
    sg = sigmoid(conv)
    dconvbc[0:block, :] = d_act * (sg * (1.0 + conv * (1.0 - sg)))

    @pl.when(place > 0)
    def _():
        edge_bc().start()

    @pl.when(place < count - 1)
    def _():
        for s in range(seqs):
            edge_copy(s).wait_recv()

    @pl.when(place == count - 1)
    def _():
        for s in range(seqs):
            dconv[s, block : block + 8, :] = jnp.zeros((8, inner), F32)

    gx_ref[...] = jnp.zeros_like(gx_ref)

    def x_chunk(t):
        rows = ds(t * CHUNK, CHUNK)
        s, c = t // chunks, lax.rem(t, chunks)
        x_copy(t).wait()

        @pl.when(t + 1 < total)
        def _():
            x_copy(t + 1).start()

        for p in range(pairs):
            lane = slice(p * LANES, (p + 1) * LANES)
            x = conv_buf[lax.rem(t, 2), :, lane]
            pre = jnp.zeros((CHUNK, LANES), F32)
            here = dconv[s, pl.ds(pl.multiple_of(c * CHUNK, CHUNK), CHUNK + 8), lane]
            for k in range(KER):
                off = KER - 1 - k
                d = pltpu.roll(here, CHUNK + 8 - off, 0)[:CHUNK] if off else here[:CHUNK]
                pre = pre + chan_ref[k : k + 1, lane] * d
                gx_ref[8 * k : 8 * k + 8, lane] += eights(x * d)
                if k == KER - 1:
                    gx_ref[8 * KER : 8 * KER + 8, lane] += eights(d)
            dx_ref[rows, lane] = pre.astype(BF16)

        @pl.when(t == total // 2)
        def _():
            pass_on(gate, 0, 3)

    loop(0, total, x_chunk)

    @pl.when(place < count - 1)
    def _():
        edge_bc().wait_recv()

    @pl.when(place == count - 1)
    def _():
        dconvbc[block : block + 8, :] = jnp.zeros((8, LANES), F32)

    low, high = small_ref[0:block, :], small_ref[block:, :]
    prebc[...] = jnp.where(
        iota(low.shape, 1) < LANES // 2, pltpu.roll(low, LANES // 2, 1), high
    )
    pre = jnp.zeros((block, LANES), F32)
    for k in range(KER):
        d = dconvbc[pl.ds(KER - 1 - k, block), :]
        pre = pre + vec_ref[k : k + 1, :] * d
        gbc_ref[8 * k : 8 * k + 8, :] = eights(prebc[...] * d)
    gbc_ref[8 * KER : 8 * KER + 8, :] = eights(dconvbc[0:block, :])
    at = iota((block, LANES), 1)
    for s in range(seqs):
        rows = slice(s * block, (s + 1) * block)
        mine = pre if s == seqs - 1 else pltpu.roll(pre, LANES // 2, 1)
        step = jnp.where(at < heads, ddt[rows, :], 0.0)
        dx_ref[rows, inner:] = jnp.where(at < LANES // 2, step, mine).astype(BF16)

    for i in late:
        begin(i)

    loop(1, parts, lambda i: mix_copy(i).wait())
    token_copy.wait()

    def add_up(t):
        rows = ds(t * CHUNK, CHUNK)
        d = dn_out[head, rows, :].astype(F32)
        for k in range(parts - 1):
            d = d + mix_in[k, rows, :].astype(F32)
        mixed_ref[rows, :] = (token_buf[rows, :].astype(F32) + d).astype(BF16)

    loop(0, total, add_up)


    def dn_copy(i):
        other = lax.rem(head + i, parts)
        return remote(
            dn_out.at[other], dn_in.at[i - 1], dn_send.at[i], dn_recv.at[i], place, other
        )

    def d_normed(i):
        other = lax.rem(head + i, parts)
        slot = (i + 1) % 2
        if i < parts:
            weight_copy(i + 1).start()

        weight_copy(i).wait()
        mine = small_weight_ref[pl.ds(pl.multiple_of(other * cols, cols), cols), :]

        def some(r):
            rows = ds(r * tall, tall)
            part = mul(dgate_ref[rows, :], weights[slot, 0], NT)
            part = part + mul(dx_ref[rows, 0:inner], weights[slot, 1], NT)
            part = part + mul(dx_ref[rows, inner:], mine, NT)
            dn_out[other, rows, :] = part.astype(BF16)

        loop(0, rows_all // tall, some)

        if i < parts:
            dn_copy(i).start()

    between = ((out, 1), (gate, 1), (out, 2), (gate, 2))
    for k in range(STEPS):
        if k < parts:
            d_normed(k + 1)
        advance(late, k, STEPS)
        pass_on(*between[k], 3)
    for k in range(STEPS, parts):
        d_normed(k + 1)

    loop(1, parts, lambda i: dn_copy(i).wait())
    my_cols = pl.ds(pl.multiple_of(head * cols, cols), cols)

    def own(t, grads):
        rows = ds(t * CHUNK, CHUNK)
        d = dn_out[head, rows, :].astype(F32)
        for k in range(parts - 1):
            d = d + dn_in[k, rows, :].astype(F32)
        token = token_buf[rows, :].astype(F32)
        grads = grads + eights(d * (token * row_scale_ref[rows, :]))
        d = d * gain_ref[:, my_cols]
        grad_ref[rows, :] = d
        line = jnp.sum(d * token, axis=1, keepdims=True)
        line = jnp.where(iota((CHUNK, LANES), 1) == 0, line, 0.0)
        rowsum[head, t] = line.T[0:8, :]
        return grads

    norm_grads = lax.fori_loop(0, total, own, jnp.zeros((8, cols), F32))
    rows_copy = head_copy(
        parts, lambda _: rowsum.at[head], lambda k: rowsum.at[k], row_send, row_recv
    )
    loop(1, parts, lambda i: rows_copy(i).start())

    def summed(ref, k):
        return jnp.sum(ref[8 * k : 8 * k + 8, :], axis=0, keepdims=True)

    shared[place] = jnp.zeros(shared.shape[1:], F32)
    for k in range(KER + 1):
        shared[place, k : k + 1, 0:inner] = summed(gx_ref, k)
        shared[place, k : k + 1, inner:] = summed(gbc_ref, k)
    for k in range(2):
        shared[place, KER + 1 + k : KER + 2 + k, 0:inner] = summed(sums_ref, k)
        shared[place, KER + 1 + k : KER + 2 + k, inner:] = summed(gdt_ref, k)
    shared[place, 7:8, 0:cols] = jnp.sum(norm_grads, axis=0, keepdims=True)
    sums_copy = line_copy(
        count, lambda _: shared.at[place], lambda k: shared.at[k], sum_send, sum_recv
    )
    loop(1, count, lambda i: sums_copy(i).start())
    pass_on(late, 0, 3)
    loop(1, parts, lambda i: rows_copy(i).wait())

    def finish_rows(t):
        rows = ds(t * CHUNK, CHUNK)
        sums = rowsum[0, t]
        for k in range(1, parts):
            sums = sums + rowsum[k, t]
        turned = jnp.concatenate([sums, jnp.zeros((CHUNK - 8, LANES), F32)], axis=0).T
        scale = row_scale_ref[rows, :]
        pull = scale * scale * scale * (turned[:, 0:1] / width)
        grad_ref[rows, :] = (
            scale * grad_ref[rows, :]
            - token_buf[rows, :].astype(F32) * pull
            + cot_ref[rows, my_cols].astype(F32)
        )

    loop(0, total, finish_rows)
    pass_on(late, 1, 3)
    loop(1, count, lambda i: sums_copy(i).wait())
    everything = shared[0]
    for k in range(1, count):
        everything = everything + shared[k]
    total_ref[...] = everything
    pass_on(late, 2, 3)
    pass_end(out + gate + late)
    drain(out + gate + late)

    @pl.when(place > 0)
    def _():
        for s in range(seqs):
            edge_copy(s).wait_send()
        edge_bc().wait_send()


def backward(dims, *operands):
    count, parts, seqs, block, inner, heads, state = dims
    rows = seqs * block
    chunks = rows // CHUNK
    cut_rows, _, cut_lanes = cut_of(count, seqs, state, inner)
    normed_rows, ng_rows, width = (operands[k].shape[d] for k, d in ((16, 0), (17, 0), (18, 1)))
    cols = width // parts
    distant = (1, 3, 7, 10, 14, 16, 17, 18, 19, 20, 24, 25, 26)
    fetched = [operands[k] for k in (17, 18, 16, 19, 1, 20, 14)]
    spec = pl.BlockSpec(memory_space=pltpu.VMEM)
    far = pl.BlockSpec(memory_space=pl.ANY)
    line, ring = pltpu.SemaphoreType.DMA((count,)), pltpu.SemaphoreType.DMA((parts,))
    edge = pltpu.SemaphoreType.DMA((seqs + 1,))
    streams = [
        (ng_rows, width),
        (normed_rows, inner),
        (normed_rows, inner // 2),
        (normed_rows, inner // 2 + LANES),
    ]
    steps = pltpu.SemaphoreType.DMA((len(streams), 2, count // 2))
    outs = [(shape, BF16) for shape in streams]
    outs = outs + [((rows, cols), F32), ((8, inner + LANES), F32), ((rows, cols), BF16)]
    return pl.pallas_call(
        functools.partial(backward_kernel, dims),
        out_shape=[jax.ShapeDtypeStruct(*o) for o in outs],
        in_specs=[far if k in distant else spec for k in range(len(operands))],
        out_specs=[far] * len(streams) + [spec] * 3,
        scratch_shapes=[vmem((2, count // 2, r // count, c), BF16) for r, c in streams]
        + [vmem((r // count, c), BF16) for r, c in streams]
        + [vmem(a.shape, a.dtype) for a in fetched]
        + [
            pltpu.SemaphoreType.DMA((len(fetched),)),
            vmem((rows, inner + LANES), BF16),
            vmem((8 * (KER + 1), inner), F32),
            vmem((8 * (KER + 1), LANES), F32),
            vmem((16, LANES), F32),
            vmem((2, 2, cols, inner), BF16),
            vmem((2, CHUNK, inner), F32),
            vmem((2, state, inner), F32),
            vmem((parts, rows, cols), BF16),
            vmem((parts - 1, rows, cols), BF16),
            vmem((2, inner, cols), BF16),
            vmem((parts - 1, rows, cols), BF16),
            vmem((rows, cols), BF16),
            vmem((parts, chunks, 8, LANES), F32),
            vmem((count, 8, inner + LANES), F32),
            steps,
            steps,
            steps,
            steps,
            pltpu.SemaphoreType.DMA((len(streams),)),
            pltpu.SemaphoreType.DMA((2,)),
            pltpu.SemaphoreType.DMA((2,)),
            pltpu.SemaphoreType.DMA((2,)),
            pltpu.SemaphoreType.DMA((2,)),
            pltpu.SemaphoreType.DMA,
            ring,
            ring,
            pltpu.SemaphoreType.DMA((2,)),
            ring,
            ring,
            ring,
            ring,
            line,
            line,
            vmem((seqs, block + 8, inner), F32),
            vmem((block + 8, LANES), F32),
            vmem((block, LANES), F32),
            vmem((rows, 2 * state), BF16),
            vmem((rows, LANES), F32),
            vmem((seqs, state, inner), BF16),
            vmem((count, cut_rows, cut_lanes), BF16),
            vmem((count, cut_rows, cut_lanes), BF16),
            vmem((seqs, state, inner), BF16),
            vmem((parts, block, LANES), BF16),
            vmem((parts, block, LANES), BF16),
            edge,
            edge,
            ring,
            ring,
            line,
            line,
            line,
            line,
        ],
        compiler_params=pltpu.CompilerParams(
            collective_id=3, has_side_effects=True, vmem_limit_bytes=VMEM_LIMIT
        ),
        name="mixer_backward",
    )(*operands)


def body(
    tokens,
    norm_gain,
    gate_input_weight,
    coefficient_weight,
    step_weight,
    conv_x,
    conv_bc,
    conv_bias_x,
    conv_bias_bc,
    dt_bias,
    a_log,
    d_skip,
    gate_gain,
    output_weight,
    cotangent,
):
    seqs, block, width = tokens.shape
    inner = gate_input_weight.shape[2]
    state_part = coefficient_weight.shape[2]
    heads = step_weight.shape[1]
    count, parts = lax.axis_size("seq"), lax.axis_size("head")
    state = state_part * parts
    rows = seqs * block
    col_count = width // parts
    half = LANES // 2
    dims = (count, parts, seqs, block, inner, heads, state)

    flat_tokens = tokens.reshape(rows, width)
    small_weight = jnp.concatenate(
        [
            step_weight,
            jnp.zeros((width, half - heads), BF16),
            coefficient_weight.reshape(width, 2 * state_part),
        ],
        axis=1,
    )
    both_weights = gate_input_weight.transpose(1, 0, 2)
    gate_pre, x_pre, small, normed_t, row_scale = project(
        flat_tokens, norm_gain[None], both_weights, small_weight
    )

    chan = jnp.concatenate(
        [
            conv_x,
            conv_bias_x[None],
            gate_gain[None],
            jnp.repeat(d_skip, inner // heads)[None],
            jnp.zeros((1, inner), F32),
        ]
    )
    twice = jnp.concatenate(
        [conv_bc.reshape(KER, 2 * state_part), conv_bias_bc.reshape(1, 2 * state_part)]
    )
    per_head = jnp.stack([dt_bias, -jnp.exp(a_log), jnp.zeros_like(a_log)])
    vec = jnp.concatenate(
        [
            jnp.concatenate([twice, twice], axis=1),
            jnp.pad(per_head, ((0, 0), (0, LANES - heads))),
        ]
    )
    device, lane, channel = np.meshgrid(
        np.arange(parts), np.arange(LANES), np.arange(2 * state), indexing="ij"
    )
    is_c, at = channel // state, channel % state
    unpack = np.stack(
        [
            (lane == s * half + is_c * state_part + at - device * state_part)
            & (at // state_part == device)
            for s in range(seqs)
        ]
    ).astype(np.float32)
    pack = jnp.asarray(unpack.transpose(1, 0, 3, 2), BF16)
    unpack = jnp.asarray(unpack.reshape(seqs, parts * LANES, 2 * state), BF16)
    expand = np.arange(LANES)[:, None] == np.arange(inner)[None, :] // (inner // heads)
    gather = jnp.asarray(expand.T.astype(np.float32), BF16)
    expand = jnp.asarray(expand.astype(np.float32))
    cot = cotangent.reshape(rows, width)

    xact, bc, conv, convbc, dt, cum, states, ng_t, dgate, dy, dyy, decay, sums = forward(
        dims,
        x_pre,
        gate_pre,
        small,
        chan,
        vec,
        unpack,
        expand,
        gather,
        cot,
        output_weight,
    )
    def padded(array_in):
        return jnp.pad(array_in, ((0, -array_in.shape[0] % (count * 16)), (0, 0)))

    *streams, grad_input, sums, block_out = backward(
        dims,
        dy,
        xact,
        bc,
        conv,
        convbc,
        dt,
        cum,
        states,
        dyy,
        decay,
        x_pre,
        small,
        chan,
        vec,
        pack,
        gather,
        padded(normed_t),
        padded(ng_t),
        cot,
        dgate,
        small_weight,
        sums,
        norm_gain[None],
        row_scale,
        flat_tokens,
        both_weights,
        output_weight,
    )
    (
        g_in,
        g_w_out,
        g_coef,
        g_step,
        taps,
        taps_bc,
        bias,
        bias_bc,
        g_dt,
        g_log,
        g_skip,
        g_gain,
        g_norm,
        block_out,
        grad_input,
    ) = finish(
        width, inner, heads, state_part, streams, sums, gather, block_out, grad_input
    )
    return (
        block_out.reshape(seqs, block, col_count),
        grad_input.reshape(seqs, block, col_count),
        g_norm[0],
        g_in,
        g_coef.transpose(2, 0, 1),
        g_step.T,
        taps,
        taps_bc,
        bias[0],
        bias_bc,
        g_dt[0],
        g_log[0],
        g_skip[0],
        g_gain[0],
        g_w_out,
    )


def solution(mesh):
    placed = (
        P(None, "seq", None),
        P(),
        P(None, None, "head"),
        P(None, None, "head"),
        P(None, "head"),
        P(None, "head"),
        P(None, None, "head"),
        P("head"),
        P(None, "head"),
        P("head"),
        P("head"),
        P("head"),
        P("head"),
        P("head", None),
        P(None, "seq", None),
    )
    return jax.shard_map(
        body,
        mesh=mesh,
        in_specs=placed,
        out_specs=(
            P(None, "seq", "head"),
            P(None, "seq", "head"),
            P("head"),
            P(None, None, "head"),
            P(None, None, "head"),
            P(None, "head"),
            P(None, "head"),
            P(None, None, "head"),
            P("head"),
            P(None, "head"),
            P("head"),
            P("head"),
            P("head"),
            P("head"),
            P("head", None),
        ),
        check_vma=False,
    )
```

```python
import functools

import jax
import jax.numpy as jnp
import numpy as np
from jax import lax
from jax.experimental import pallas as pl
from jax.experimental.pallas import tpu as pltpu
from jax.sharding import PartitionSpec as P

KER = 4
EPSILON = 1e-05
CHUNK = 128
LANES = 128
MESH = pl.DeviceIdType.MESH
F32 = jnp.float32
BF16 = jnp.bfloat16
EXACT = lax.Precision.HIGHEST
VMEM_LIMIT = 61 * 2**20
NN = ((1,), (0,))
NT = ((1,), (1,))
TN = ((0,), (0,))


def mul(left, right, how, precision=None):
    return lax.dot_general(
        left, right, (how, ((), ())), precision=precision, preferred_element_type=F32
    )


def sigmoid(v):
    return 0.5 * jnp.tanh(0.5 * v) + 0.5


def softplus(v):
    e = jnp.exp(-jnp.abs(v))
    u = 1.0 + e
    near = u - 1.0
    log1p = jnp.where(near == 0.0, e, jnp.log(u) * (e / jnp.where(near == 0.0, 1.0, near)))
    return jnp.maximum(v, 0.0) + log1p


def iota(shape, dim):
    return lax.broadcasted_iota(jnp.int32, shape, dim)


def ds(start, size):
    return pl.ds(pl.multiple_of(start, size), size)


def pair_of(values, pair):
    low = values[:, 2 * pair : 2 * pair + 1]
    high = values[:, 2 * pair + 1 : 2 * pair + 2]
    return jnp.where(iota((values.shape[0], LANES), 1) < LANES // 2, low, high)


def spread(values, pairs):
    return jnp.concatenate([pair_of(values, p) for p in range(pairs)], axis=1)


def eights(v):
    return jnp.sum(v.reshape(v.shape[0] // 8, 8, v.shape[1]), axis=0)


def halves_of(v):
    high = v.astype(BF16)
    return high, (v - high.astype(F32)).astype(BF16)


def head_sums(v, gather):
    high, low = halves_of(v)
    return mul(high, gather, NN) + mul(low, gather, NN)


def remote(src, dst, send, recv, place, head):
    return pltpu.make_async_remote_copy(
        src_ref=src,
        dst_ref=dst,
        send_sem=send,
        recv_sem=recv,
        device_id=(place, head),
        device_id_type=MESH,
    )


def meet(count, parts):
    place, head = lax.axis_index("seq"), lax.axis_index("head")
    barrier = pltpu.get_barrier_semaphore()

    def along_seq(i, _):
        other = lax.rem(place + i, count)
        pl.semaphore_signal(barrier, inc=1, device_id=(other, head), device_id_type=MESH)
        return 0

    def along_head(i, _):
        other = lax.rem(head + i, parts)
        pl.semaphore_signal(barrier, inc=1, device_id=(place, other), device_id_type=MESH)
        return 0

    lax.fori_loop(1, count, along_seq, 0)
    lax.fori_loop(1, parts, along_head, 0)
    pl.semaphore_wait(barrier, count - 1 + parts - 1)


def loop(low, high, step):
    def one(i, _):
        step(i)
        return 0

    lax.fori_loop(low, high, one, 0)


def line_copy(count, src, dst, send, recv):
    place, head = lax.axis_index("seq"), lax.axis_index("head")

    def copy(i):
        other = lax.rem(place + i, count)
        return remote(src(other), dst(place), send.at[i], recv.at[i], other, head)

    return copy


def head_copy(parts, src, dst, send, recv):
    place, head = lax.axis_index("seq"), lax.axis_index("head")

    def copy(i):
        other = lax.rem(head + i, parts)
        return remote(src(other), dst(head), send.at[i], recv.at[i], place, other)

    return copy


def cut_of(count, seqs, state):
    group = count // 2
    return group, seqs * state // group


def carry_exchange(dims, local, arrived, passed, total, incoming, decay_ref, sems, reverse):
    count, _, seqs, _, inner, _, state = dims
    place, head = lax.axis_index("seq"), lax.axis_index("head")
    send, recv, back_send, back_recv, over_send, over_recv = sems
    group, rows = cut_of(count, seqs, state)
    base, me = place // group * group, lax.rem(place, group)
    leads = place >= group if reverse else place < group
    each = group // seqs

    def at(ref, k):
        return ref.at[k // each, ds(lax.rem(k, each) * rows, rows)]

    def out(i):
        other = lax.rem(me + i, group)
        return remote(at(local, other), arrived.at[me], send.at[i], recv.at[i], base + other, head)

    def back(j):
        i = lax.rem(j - me + group, group)
        return remote(
            passed.at[j], at(incoming, me), back_send.at[i], back_recv.at[i], base + j, head
        )

    def over():
        other = lax.rem(place + group, count)
        return remote(total.at[0], total.at[1], over_send, over_recv, other, head)

    def start():
        loop(1, group, lambda i: out(i).start())
        arrived[me] = local[me // each, ds(lax.rem(me, each) * rows, rows)]

    def carry():
        @pl.when(leads)
        def _():
            total[1] = jnp.zeros((rows, inner), total.dtype)

        @pl.when(~leads)
        def _():
            over().wait_recv()

        held = total[1].astype(F32)
        seq = me // each
        for step in range(group):
            j = group - 1 - step if reverse else step

            @pl.when(j != me)
            def _():
                out(lax.rem(me - j + group, group)).wait_recv()

            passed[j] = held.astype(passed.dtype)

            @pl.when(j != me)
            def _():
                back(j).start()

            @pl.when(j == me)
            def _():
                incoming[seq, ds(lax.rem(me, each) * rows, rows)] = passed[j]

            held = decay_ref[seq, pl.ds(base + j, 1), :] * held + arrived[j].astype(F32)

        @pl.when(leads)
        def _():
            total[0] = held.astype(total.dtype)
            over().start()

    def finish():
        def one(i):
            out(i).wait_send()
            back(lax.rem(me + i, group)).wait()

        loop(1, group, one)

        @pl.when(leads)
        def _():
            over().wait_send()

    return start, carry, finish


def forward_kernel(
    dims,
    x_ref,
    gate_far,
    small_ref,
    chan_ref,
    vec_ref,
    unpack_ref,
    expand_ref,
    gather_ref,
    cot_far,
    wout_far,
    xact_far,
    bc_far,
    conv_far,
    convbc_ref,
    dt_far,
    cum_far,
    states_far,
    ng_t_far,
    dgate_far,
    dy_far,
    dyy_far,
    decay_ref,
    sums_ref,
    gate_ref,
    cot_ref,
    wout_ref,
    xact_ref,
    bc_ref,
    conv_ref,
    dt_ref,
    cum_ref,
    states_ref,
    ng_t_ref,
    dgate_ref,
    dy_ref,
    dyy_ref,
    fetch_sem,
    keep_sem,
    edge_x,
    edge_s,
    ext,
    extbc,
    bc_all,
    fresh,
    y_ref,
    dng_ref,
    gated_ref,
    decays,
    local,
    arrived,
    passed,
    handed,
    incoming,
    rowsum,
    edge_send,
    edge_recv,
    dec_send,
    dec_recv,
    bc_send,
    bc_recv,
    st_send,
    st_recv,
    back_send,
    back_recv,
    over_send,
    over_recv,
    row_send,
    row_recv,
):
    count, parts, seqs, block, inner, heads, state = dims
    place, head = lax.axis_index("seq"), lax.axis_index("head")
    chunks = block // CHUNK
    pairs = heads // 2
    total = seqs * chunks
    fetches = [
        pltpu.make_async_copy(src, dst, fetch_sem.at[k])
        for k, (src, dst) in enumerate(
            ((cot_far, cot_ref), (wout_far, wout_ref), (gate_far, gate_ref))
        )
    ]
    for copy in fetches:
        copy.start()
    keeps = [
        pltpu.make_async_copy(src, dst, keep_sem.at[k])
        for k, (src, dst) in enumerate(
            (
                (xact_ref, xact_far),
                (bc_ref, bc_far),
                (conv_ref, conv_far),
                (dt_ref, dt_far),
                (cum_ref, cum_far),
                (states_ref, states_far),
                (ng_t_ref, ng_t_far),
                (dgate_ref, dgate_far),
                (dy_ref, dy_far),
                (dyy_ref, dyy_far),
            )
        )
    ]
    meet(count, parts)

    def edge_copies(ahead):
        copies = []
        for s in range(seqs):
            rows = pl.ds(s * block + block - 8, 8)
            for k, (src, dst) in enumerate(((x_ref, edge_x), (small_ref, edge_s))):
                copies.append(
                    remote(
                        src.at[rows], dst.at[s], edge_send.at[k, s], edge_recv.at[k, s], ahead, head
                    )
                )
        return copies

    after = lax.rem(place + 1, count)

    @pl.when(place < count - 1)
    def _():
        for c in edge_copies(after):
            c.start()

    lower = (iota((CHUNK, CHUNK), 0) >= iota((CHUNK, CHUNK), 1)).astype(F32)
    for s in range(seqs):

        def steps(c, logs):
            rows = ds((s * chunks + c) * CHUNK, CHUNK)
            dt = softplus(small_ref[rows, :] + vec_ref[5:6, :])
            cum = mul(lower, dt * vec_ref[6:7, :], NN, EXACT)
            dt_ref[rows, :] = dt
            cum_ref[rows, :] = cum
            return logs + cum[CHUNK - 1 :, :]

        logs = lax.fori_loop(0, chunks, steps, jnp.zeros((1, LANES), F32))
        decays[place, s : s + 1, :] = jnp.exp(logs)

    dec = line_copy(count, lambda _: decays.at[place], lambda k: decays.at[k], dec_send, dec_recv)
    loop(1, count, lambda i: dec(i).start())

    @pl.when(place > 0)
    def _():
        for c in edge_copies(after):
            c.wait_recv()

    @pl.when(place == 0)
    def _():
        edge_x[...] = jnp.zeros_like(edge_x)
        edge_s[...] = jnp.zeros_like(edge_s)

    def packed(low, high):
        return jnp.where(
            iota(low.shape, 1) < LANES // 2, pltpu.roll(low, LANES // 2, 1), high
        )

    extbc[0:8, :] = packed(edge_s[0], edge_s[1])
    extbc[8:, :] = packed(small_ref[0:block, :], small_ref[block:, :])
    conv = vec_ref[4:5, :]
    for k in range(KER):
        conv = conv + vec_ref[k : k + 1, :] * extbc[pl.ds(8 - (KER - 1) + k, block), :]
    convbc_ref[...] = conv
    bc_all[head] = (conv * sigmoid(conv)).astype(BF16)
    share = head_copy(parts, lambda _: bc_all.at[head], lambda k: bc_all.at[k], bc_send, bc_recv)
    loop(1, parts, lambda i: share(i).start())

    def x_chunk(t):
        rows = ds(t * CHUNK, CHUNK)
        s, c = t // chunks, lax.rem(t, chunks)
        before = pl.ds(pl.multiple_of(jnp.maximum(t * CHUNK - 8, 0), 8), 8)
        for b in range(inner // LANES):
            lane = slice(b * LANES, (b + 1) * LANES)
            ext[0:8, lane] = jnp.where(c == 0, edge_x[s, :, lane], x_ref[before, lane])
            ext[8:, lane] = x_ref[rows, lane]
            conv = chan_ref[4:5, lane]
            for k in range(KER):
                conv = conv + chan_ref[k : k + 1, lane] * ext[pl.ds(8 - (KER - 1) + k, CHUNK), lane]
            conv_ref[rows, lane] = conv
            xact_ref[rows, lane] = (conv * sigmoid(conv)).astype(BF16)

    loop(0, total, x_chunk)

    loop(1, parts, lambda i: share(i).wait())
    everything = jnp.concatenate([bc_all[k] for k in range(parts)], axis=1)
    for s in range(seqs):
        bc_ref[s * block : (s + 1) * block, :] = mul(everything, unpack_ref[s], NN).astype(BF16)

    for s in range(seqs):

        def add(c, held):
            t = s * chunks + c
            rows = ds(t * CHUNK, CHUNK)
            cum, dt = cum_ref[rows, :], dt_ref[rows, :]
            end = cum[CHUNK - 1 :, :]
            tail = jnp.exp(end - cum) * dt
            weighted = jnp.concatenate(
                [
                    (
                        xact_ref[rows, p * LANES : (p + 1) * LANES].astype(F32) * pair_of(tail, p)
                    ).astype(BF16)
                    for p in range(pairs)
                ],
                axis=1,
            )
            new = mul(bc_ref[rows, 0:state], weighted, TN)
            fresh[t] = new
            return spread(jnp.exp(end), pairs) * held + new

        held = lax.fori_loop(0, chunks, add, jnp.zeros((state, inner), F32))
        local[s] = held

    start, carry, finish = carry_exchange(
        dims,
        local,
        arrived,
        passed,
        handed,
        incoming,
        decay_ref,
        (st_send, st_recv, back_send, back_recv, over_send, over_recv),
        False,
    )
    start()
    for copy in keeps[:5]:
        copy.start()

    def within(t):
        rows = ds(t * CHUNK, CHUNK)
        cum, dt = cum_ref[rows, :], dt_ref[rows, :]
        cum_t = cum.T
        scores = mul(bc_ref[rows, state:], bc_ref[rows, 0:state], NT)
        seen = iota((CHUNK, CHUNK), 0) >= iota((CHUNK, CHUNK), 1)
        side = iota((CHUNK, LANES), 1) < LANES // 2
        for p in range(pairs):
            lane = slice(p * LANES, (p + 1) * LANES)
            stepped = (xact_ref[rows, lane].astype(F32) * pair_of(dt, p)).astype(BF16)
            halves = []
            for h in (2 * p, 2 * p + 1):
                gap = cum[:, h : h + 1] - cum_t[h : h + 1, :]
                mixing = (scores * jnp.exp(jnp.where(seen, gap, -1e30))).astype(BF16)
                halves.append(mul(mixing, stepped, NN))
            y_ref[rows, lane] = jnp.where(side, halves[0], halves[1])

    loop(0, total, within)

    loop(1, count, lambda i: dec(i).wait())
    for s in range(seqs):
        decay_ref[s] = mul(decays[:, s, :], expand_ref[...], NN, EXACT)
    carry()

    for copy in fetches:
        copy.wait()
    wide = 2 * LANES

    def back_project(i):
        s, b = i // (inner // wide), lax.rem(i, inner // wide)
        rows, lane = ds(s * block, block), ds(b * wide, wide)
        dng_ref[rows, lane] = mul(cot_ref[rows, :], wout_ref[lane, :], NT)

    loop(0, seqs * (inner // wide), back_project)
    finish()

    for s in range(seqs):

        def gate(c, held):
            t = s * chunks + c
            rows = ds(t * CHUNK, CHUNK)
            cum = cum_ref[rows, :]
            grown = jnp.exp(cum)
            states_ref[t] = held
            high, low = halves_of(held)
            c_rows = bc_ref[rows, state:]
            carried = mul(c_rows, high, NN) + mul(c_rows, low, NN)
            square = jnp.zeros((CHUNK, LANES), F32)
            cross = jnp.zeros((CHUNK, LANES), F32)
            for p in range(pairs):
                lane = slice(p * LANES, (p + 1) * LANES)
                y = y_ref[rows, lane] + carried[:, lane] * pair_of(grown, p)
                y_ref[rows, lane] = y
                out = y + chan_ref[6:7, lane] * xact_ref[rows, lane].astype(F32)
                pre = gate_ref[rows, lane]
                gated = out * (pre * sigmoid(pre))
                gated_ref[rows, lane] = gated
                square = square + gated * gated
                cross = cross + dng_ref[rows, lane] * chan_ref[5:6, lane] * gated
            at = iota((CHUNK, LANES), 1)
            both = jnp.where(
                at == 0,
                jnp.sum(square, axis=1, keepdims=True),
                jnp.where(at == 1, jnp.sum(cross, axis=1, keepdims=True), 0.0),
            )
            rowsum[head, t] = both.T[0:8, :]
            return spread(grown[CHUNK - 1 :, :], pairs) * held + fresh[t]

        lax.fori_loop(0, chunks, gate, incoming[s].astype(F32))

    keeps[5].start()
    rows_copy = head_copy(
        parts, lambda _: rowsum.at[head], lambda k: rowsum.at[k], row_send, row_recv
    )
    loop(1, parts, lambda i: rows_copy(i).start())
    loop(1, parts, lambda i: rows_copy(i).wait())
    sums_ref[...] = jnp.zeros_like(sums_ref)
    channels = inner * parts

    def outputs(t):
        rows = ds(t * CHUNK, CHUNK)
        sums = rowsum[0, t]
        for k in range(1, parts):
            sums = sums + rowsum[k, t]
        turned = jnp.concatenate([sums, jnp.zeros((CHUNK - 8, LANES), F32)], axis=0).T
        scale = lax.rsqrt(turned[:, 0:1] / channels + EPSILON)
        pull = scale * scale * scale * (turned[:, 1:2] / channels)
        dyy = jnp.zeros((CHUNK, LANES), F32)
        for p in range(pairs):
            lane = slice(p * LANES, (p + 1) * LANES)
            pre = gate_ref[rows, lane]
            sg = sigmoid(pre)
            gated, y = gated_ref[rows, lane], y_ref[rows, lane]
            x = xact_ref[rows, lane].astype(F32)
            gain = chan_ref[5:6, lane]
            scaled = gated * scale
            ng_t_ref[lane, rows] = (scaled * gain).T.astype(BF16)
            dng = dng_ref[rows, lane]
            d_gated = scale * (dng * gain) - gated * pull
            d_ssd = d_gated * (pre * sg)
            out = y + chan_ref[6:7, lane] * x
            dgate_ref[rows, lane] = (d_gated * out * (sg * (1.0 + pre * (1.0 - sg)))).astype(BF16)
            dy = d_ssd.astype(BF16)
            dy_ref[rows, lane] = dy
            sums_ref[0:8, lane] += eights(dng * scaled)
            sums_ref[8:16, lane] += eights(d_ssd * x)
            dyy = dyy + head_sums(dy.astype(F32) * y, gather_ref[lane, :])
        dyy_ref[rows, :] = dyy

    loop(0, total, outputs)
    for copy in keeps[6:]:
        copy.start()
    for copy in keeps:
        copy.wait()

    @pl.when(place < count - 1)
    def _():
        for c in edge_copies(after):
            c.wait_send()


def vmem(shape, kind):
    return pltpu.VMEM(shape, kind)


def forward(dims, *operands):
    count, parts, seqs, block, inner, heads, state = dims
    rows = seqs * block
    chunks = rows // CHUNK
    group, cut_rows = cut_of(count, seqs, state)
    spec, far = pl.BlockSpec(memory_space=pltpu.VMEM), pl.BlockSpec(memory_space=pl.ANY)
    fetched, kept = (1, 8, 9), (0, 1, 2, 4, 5, 6, 7, 8, 9, 10)
    line, ring = pltpu.SemaphoreType.DMA((count,)), pltpu.SemaphoreType.DMA((parts,))
    edge = pltpu.SemaphoreType.DMA((2, seqs))
    outs = [
        ((rows, inner), BF16),
        ((rows, 2 * state), BF16),
        ((rows, inner), F32),
        ((block, LANES), F32),
        ((rows, LANES), F32),
        ((rows, LANES), F32),
        ((chunks, state, inner), F32),
        ((inner, rows), BF16),
        ((rows, inner), BF16),
        ((rows, inner), BF16),
        ((rows, LANES), F32),
        ((seqs, count, inner), F32),
        ((16, inner), F32),
    ]
    return pl.pallas_call(
        functools.partial(forward_kernel, dims),
        out_shape=[jax.ShapeDtypeStruct(*o) for o in outs],
        in_specs=[far if k in fetched else spec for k in range(len(operands))],
        out_specs=[far if k in kept else spec for k in range(len(outs))],
        scratch_shapes=[vmem(operands[k].shape, operands[k].dtype) for k in fetched]
        + [vmem(*outs[k]) for k in kept]
        + [
            pltpu.SemaphoreType.DMA((len(fetched),)),
            pltpu.SemaphoreType.DMA((len(kept),)),
            vmem((seqs, 8, inner), F32),
            vmem((seqs, 8, LANES), F32),
            vmem((CHUNK + 8, inner), F32),
            vmem((block + 8, LANES), F32),
            vmem((parts, block, LANES), BF16),
            vmem((chunks, state, inner), F32),
            vmem((rows, inner), F32),
            vmem((rows, inner), F32),
            vmem((rows, inner), F32),
            vmem((count, 8, LANES), F32),
            vmem((seqs, state, inner), F32),
            vmem((group, cut_rows, inner), F32),
            vmem((group, cut_rows, inner), F32),
            vmem((2, cut_rows, inner), F32),
            vmem((seqs, state, inner), F32),
            vmem((parts, chunks, 8, LANES), F32),
            edge,
            edge,
            line,
            line,
            ring,
            ring,
            line,
            line,
            line,
            line,
            pltpu.SemaphoreType.DMA,
            pltpu.SemaphoreType.DMA,
            ring,
            ring,
        ],
        compiler_params=pltpu.CompilerParams(
            collective_id=2, has_side_effects=True, vmem_limit_bytes=VMEM_LIMIT
        ),
        name="mixer_forward",
    )(*operands)


def project_kernel(
    tokens_ref,
    gain_ref,
    weight_ref,
    step_ref,
    coef_ref,
    taps_ref,
    taps_bc_ref,
    bias_ref,
    bias_bc_ref,
    dt_bias_ref,
    a_log_ref,
    skip_ref,
    gate_gain_ref,
    gate_ref,
    x_ref,
    small_ref,
    turned_ref,
    scale_ref,
    small_weight_ref,
    chan_ref,
    vec_ref,
    gain_row,
):
    heads, state_part = step_ref.shape[0], coef_ref.shape[1]

    def flat(ref):
        return jnp.concatenate([ref[k : k + 1, :] for k in range(ref.shape[0])], axis=1)

    @pl.when(pl.program_id(0) == 0)
    def _():
        small_weight_ref[...] = jnp.zeros_like(small_weight_ref)
        small_weight_ref[0:heads, :] = step_ref[...]
        for k in range(2):
            low = LANES // 2 + k * state_part
            small_weight_ref[low : low + state_part, :] = coef_ref[k]
        gain_row[...] = flat(gain_ref)
        chan_ref[...] = jnp.zeros_like(chan_ref)
        chan_ref[0:KER, :] = taps_ref[...]
        chan_ref[4:5, :] = flat(bias_ref)
        chan_ref[5:6, :] = flat(gate_gain_ref)
        chan_ref[6:7, :] = spread(skip_ref[...], heads // 2)
        vec_ref[...] = jnp.zeros_like(vec_ref)
        for k in range(4):
            at = slice(k * state_part, (k + 1) * state_part)
            vec_ref[0:KER, at] = taps_bc_ref[:, k % 2, :]
            vec_ref[4:5, at] = bias_bc_ref[k % 2 : k % 2 + 1, :]
        vec_ref[5:6, 0:heads] = dt_bias_ref[...]
        vec_ref[6:7, 0:heads] = -jnp.exp(a_log_ref[...])

    tokens = tokens_ref[...].astype(F32)
    scale = lax.rsqrt(jnp.mean(tokens * tokens, axis=1, keepdims=True) + EPSILON)
    scale_ref[...] = scale
    low = (tokens * scale * gain_row[...]).astype(BF16)
    turned_ref[...] = low.T
    x_ref[...] = mul(low, weight_ref[1], NN)
    small_ref[...] = mul(low, small_weight_ref[...], NT)
    gate_ref[...] = mul(low, weight_ref[0], NN)


def project(tokens, gain, weights, *params):
    rows, width = tokens.shape
    inner = weights.shape[2]
    tall = 2 * CHUNK

    def by_rows(cols):
        return pl.BlockSpec((tall, cols), lambda i: (i, 0))

    def whole(shape):
        return pl.BlockSpec(shape, lambda i: (0,) * len(shape))

    return pl.pallas_call(
        project_kernel,
        grid=(rows // tall,),
        in_specs=[by_rows(width)] + [whole(a.shape) for a in (gain, weights) + params],
        out_specs=[
            by_rows(inner),
            by_rows(inner),
            by_rows(LANES),
            pl.BlockSpec((width, tall), lambda i: (0, i)),
            by_rows(1),
            whole((LANES, width)),
            whole((8, inner)),
            whole((8, LANES)),
        ],
        out_shape=[
            jax.ShapeDtypeStruct((rows, inner), F32),
            jax.ShapeDtypeStruct((rows, inner), F32),
            jax.ShapeDtypeStruct((rows, LANES), F32),
            jax.ShapeDtypeStruct((width, rows), BF16),
            jax.ShapeDtypeStruct((rows, 1), F32),
            jax.ShapeDtypeStruct((LANES, width), BF16),
            jax.ShapeDtypeStruct((8, inner), F32),
            jax.ShapeDtypeStruct((8, LANES), F32),
        ],
        scratch_shapes=[pltpu.VMEM((1, width), F32)],
        compiler_params=pltpu.CompilerParams(vmem_limit_bytes=VMEM_LIMIT),
        name="project",
    )(tokens, gain, weights, *params)


def ring_place(count):
    place = lax.axis_index("seq")
    row, col = place // 2, place % 2
    return jnp.where(col == 0, row, count - 1 - row)


def ring_device(rank, count):
    return jnp.where(rank < count // 2, 2 * rank, 2 * (count - 1 - rank) + 1)


def ring_steps(count, plan, outs, bufs, stages, sems):
    rs_send, rs_recv, ag_send, ag_recv, keep_sem = sems
    far = count // 2
    head = lax.axis_index("head")
    rank = ring_place(count)
    arms = (1, -1)
    peers = [ring_device(lax.rem(rank + a + count, count), count) for a in arms]

    def chunk_at(distance):
        return lax.rem(rank + distance + 2 * count, count)

    def partial(i, chunk):
        left, right, first, cols, _ = plan[i]
        rows = left.shape[0] // count
        return mul(left[ds(chunk * rows, rows), :], right[:, first : first + cols], NN)

    def half(i, arm):
        cols, cut = plan[i][3:]
        return slice(0, cut) if arm == 0 else slice(cut, cols)

    def block_of(i, chunk):
        rows = plan[i][0].shape[0] // count
        return outs[i].at[ds(chunk * rows, rows)]

    def rs(i, arm, step, first=False):
        here = stages[i] if first else bufs[i].at[arm, step - 1]
        there = bufs[i].at[arm, step]
        if first:
            here, there = here.at[:, half(i, arm)], there.at[:, half(i, arm)]
        return remote(
            here, there, rs_send.at[i, arm, step], rs_recv.at[i, arm, step], peers[arm], head
        )

    def ag(i, arm, step, kind="middle"):
        there = block_of(i, chunk_at(-arms[arm] * step))
        here = bufs[i].at[0, far - 1] if kind == "first" else there
        if kind == "last":
            here, there = here.at[:, half(i, arm)], there.at[:, half(i, arm)]
        return remote(
            here, there, ag_send.at[i, arm, step], ag_recv.at[i, arm, step], peers[arm], head
        )

    def keep(i):
        return pltpu.make_async_copy(
            bufs[i].at[0, far - 1], block_of(i, chunk_at(0)), keep_sem.at[i]
        )

    def begin(i):
        stages[i][...] = partial(i, chunk_at(far)).astype(BF16)
        for arm in range(2):
            rs(i, arm, 0, True).start()

    def advance(streams, slot, slots):
        def second(i, arm):
            own = partial(i, chunk_at(arms[arm] * (far - 1)))
            rs(i, arm, 0, True).wait_recv()
            mine, other = half(i, arm), half(i, 1 - arm)
            bufs[i][arm, 0, :, other] = own[:, other].astype(BF16)
            bufs[i][arm, 0, :, mine] = (
                own[:, mine] + bufs[i][arm, 0, :, mine].astype(F32)
            ).astype(BF16)
            rs(i, arm, 1).start()

        def later(i, arm, step):
            own = partial(i, chunk_at(arms[arm] * (far - step)))
            rs(i, arm, step - 1).wait_recv()
            bufs[i][arm, step - 1] = (own + bufs[i][arm, step - 1].astype(F32)).astype(BF16)
            rs(i, arm, step).start()

        def last(i):
            own = partial(i, chunk_at(0))
            for arm in range(2):
                rs(i, arm, far - 1).wait_recv()
                own = own + bufs[i][arm, far - 1].astype(F32)
            bufs[i][0, far - 1] = own.astype(BF16)
            for arm in range(2):
                ag(i, arm, 0, "first").start()
            keep(i).start()

        low, high = slot * far // slots, (slot + 1) * far // slots
        if low == 0 < high:
            for i in streams:
                for arm in range(2):
                    second(i, arm)

        def middle(step):
            for i in streams:
                for arm in range(2):
                    later(i, arm, step)

        if min(high, far - 1) > max(low, 1):
            loop(max(low, 1) + 1, min(high, far - 1) + 1, middle)
        if high == far:
            for i in streams:
                last(i)

    def pass_on(streams, slot, slots):
        def middle(step):
            for i in streams:
                for arm in range(2):
                    ag(i, arm, step - 1).wait_recv()
                    ag(i, arm, step).start()

        steps = far - 1
        low, high = slot * steps // slots, (slot + 1) * steps // slots
        if min(high, steps - 1) > low:
            loop(low + 1, min(high, steps - 1) + 1, middle)
        if low < high == steps:
            for i in streams:
                for arm in range(2):
                    ag(i, arm, steps - 1).wait_recv()
                    ag(i, arm, steps, "last").start()

    def pass_end(streams):
        for i in streams:
            for arm in range(2):
                ag(i, arm, far - 1, "last").wait_recv()

    def drain(streams):
        for i in streams:
            for arm in range(2):
                rs(i, arm, 0, True).wait_send()
                ag(i, arm, 0, "first").wait_send()
                ag(i, arm, far - 1, "last").wait_send()
            keep(i).wait()

        def one(step):
            for i in streams:
                for arm in range(2):
                    rs(i, arm, step).wait_send()

                    @pl.when(step < far - 1)
                    def _():
                        ag(i, arm, step).wait_send()

        loop(1, far, one)

    return begin, advance, pass_on, pass_end, drain


def finish_kernel(
    gate,
    narrow_low,
    narrow,
    out,
    sums_ref,
    gather_ref,
    block_far,
    input_far,
    gin_ref,
    wout_ref,
    coef_ref,
    step_ref,
    taps_ref,
    taps_bc_ref,
    bias_ref,
    bias_bc_ref,
    dt_ref,
    log_ref,
    skip_ref,
    gain_ref,
    norm_ref,
    block_out,
    input_out,
):
    inner, half = gate.shape[1], narrow_low.shape[1]
    heads, state_part = step_ref.shape[0], bias_bc_ref.shape[1]
    block_out[...] = block_far[...]
    input_out[...] = input_far[...]

    @pl.when(pl.program_id(0) == 0)
    def _():
        lanes = sums_ref[:, inner:]
        both = lanes + pltpu.roll(lanes, LANES // 2, 1)
        taps_ref[...] = sums_ref[0:KER, 0:inner]
        for ref, row in ((bias_ref, KER), (gain_ref, KER + 1), (norm_ref, KER + 3)):
            for k in range(ref.shape[0]):
                ref[k : k + 1, :] = sums_ref[row : row + 1, k * LANES : (k + 1) * LANES]
        for k in range(2):
            at = slice(k * state_part, (k + 1) * state_part)
            taps_bc_ref[:, k, :] = both[0:KER, at]
            bias_bc_ref[k : k + 1, :] = both[KER : KER + 1, at]
        dt_ref[...] = lanes[KER + 1 : KER + 2, 0:heads]
        log_ref[...] = lanes[KER + 2 : KER + 3, 0:heads]
        skip_ref[...] = head_sums(sums_ref[:, 0:inner], gather_ref[...])[KER + 2 : KER + 3, 0:heads]

    gin_ref[:, 0, :] = gate[...].astype(F32)
    gin_ref[:, 1, 0:half] = narrow_low[...].astype(F32)
    gin_ref[:, 1, half:] = narrow[:, 0 : inner - half].astype(F32)
    small = narrow[:, inner - half :].astype(F32).T
    step_ref[...] = small[0:heads]
    for k in range(2):
        low = LANES // 2 + k * state_part
        coef_ref[k] = small[low : low + state_part]
    wout_ref[...] = out[...].astype(F32)


def finish(width, inner, heads, state_part, streams, sums, gather, block_out, grad_input):
    steps = 4
    tall, low, part = width // steps, inner // steps, grad_input.shape[0] // steps
    out, gate, narrow_low, narrow = streams
    cols = grad_input.shape[1]
    mine = pl.BlockSpec((part, cols), lambda i: (i, 0))

    def block(array_in, rows):
        return pl.BlockSpec((rows, array_in.shape[1]), lambda i: (i, 0))

    def whole(shape):
        return pl.BlockSpec(shape, lambda i: (0,) * len(shape))

    little = [
        (KER, inner),
        (KER, 2, state_part),
        (inner // LANES, LANES),
        (2, state_part),
        (1, heads),
        (1, heads),
        (1, heads),
        (inner // LANES, LANES),
        (cols // LANES, LANES),
    ]
    return pl.pallas_call(
        finish_kernel,
        grid=(steps,),
        in_specs=[block(gate, tall), block(narrow_low, tall), block(narrow, tall), block(out, low)]
        + [whole(sums.shape), whole(gather.shape), mine, mine],
        out_specs=[
            pl.BlockSpec((tall, 2, inner), lambda i: (i, 0, 0)),
            pl.BlockSpec((low, width), lambda i: (i, 0)),
            pl.BlockSpec((2, state_part, tall), lambda i: (0, 0, i)),
            pl.BlockSpec((heads, tall), lambda i: (0, i)),
        ]
        + [whole(s) for s in little]
        + [mine, mine],
        out_shape=[
            jax.ShapeDtypeStruct((width, 2, inner), F32),
            jax.ShapeDtypeStruct((inner, width), F32),
            jax.ShapeDtypeStruct((2, state_part, width), F32),
            jax.ShapeDtypeStruct((heads, width), F32),
        ]
        + [jax.ShapeDtypeStruct(s, F32) for s in little]
        + [
            jax.ShapeDtypeStruct(block_out.shape, BF16),
            jax.ShapeDtypeStruct(grad_input.shape, F32),
        ],
        compiler_params=pltpu.CompilerParams(vmem_limit_bytes=VMEM_LIMIT),
        name="finish",
    )(gate, narrow_low, narrow, out, sums, gather, block_out, grad_input)


STEPS = 4


def backward_kernel(
    dims,
    dy_ref,
    xact_far,
    bc_ref,
    conv_ref,
    convbc_ref,
    dt_ref,
    cum_ref,
    states_far,
    dyy_ref,
    decay_ref,
    x_far,
    small_ref,
    chan_ref,
    vec_ref,
    pack_far,
    gather_ref,
    normed_t_far,
    ng_t_far,
    cot_far,
    dgate_far,
    small_weight_far,
    sums_ref,
    gain_ref,
    row_scale_ref,
    tokens_ref,
    weight_ref,
    wout_far,
    *rest,
):
    count, parts, seqs, block, inner, heads, state = dims
    outs, rest = rest[:4], rest[4:]
    grad_ref, total_ref, mixed_ref, *rest = rest
    bufs, rest = rest[:4], rest[4:]
    stages, rest = rest[:4], rest[4:]
    fetched, rest = rest[:7], rest[7:]
    fetch_sem, *rest = rest
    (
        dx_ref,
        gx_ref,
        gbc_ref,
        gdt_ref,
        weights,
        conv_buf,
        state_buf,
        dn_out,
        dn_in,
        wout,
        mix_in,
        token_buf,
        rowsum,
        shared,
        rs_send,
        rs_recv,
        ag_send,
        ag_recv,
        keep_sem,
        weight_sem,
        conv_sem,
        state_sem,
        x_sem,
        token_sem,
        dn_send,
        dn_recv,
        wout_sem,
        mix_send,
        mix_recv,
        row_send,
        row_recv,
        sum_send,
        sum_recv,
        *rest,
    ) = rest
    (
        dconv,
        dconvbc,
        prebc,
        dbc,
        ddt,
        local,
        arrived,
        passed,
        handed,
        incoming,
        bc_out,
        bc_in,
        edge_send,
        edge_recv,
        bc_send,
        bc_recv,
        st_send,
        st_recv,
        back_send,
        back_recv,
        over_send,
        over_recv,
    ) = rest
    sources = (
        ng_t_far,
        cot_far,
        normed_t_far,
        dgate_far,
        xact_far,
        small_weight_far,
        pack_far,
    )
    fetches = [
        pltpu.make_async_copy(src, dst, fetch_sem.at[k])
        for k, (src, dst) in enumerate(zip(sources, fetched))
    ]
    for copy in fetches:
        copy.start()
    (
        ng_t_ref,
        cot_ref,
        normed_t_ref,
        dgate_ref,
        xact_ref,
        small_weight_ref,
        pack_ref,
    ) = fetched
    place, head = lax.axis_index("seq"), lax.axis_index("head")
    chunks = block // CHUNK
    pairs = heads // 2
    total = seqs * chunks
    rows_all = seqs * block
    width = cot_ref.shape[1]
    cols = width // parts
    plan = (
        (ng_t_ref, cot_ref, 0, width, width // 2),
        (normed_t_ref, dgate_ref, 0, inner, inner // 2),
        (normed_t_ref, dx_ref, 0, inner // 2, LANES),
        (normed_t_ref, dx_ref, inner // 2, inner // 2 + LANES, 2 * LANES),
    )
    begin, advance, pass_on, pass_end, drain = ring_steps(
        count, plan, outs, bufs, stages, (rs_send, rs_recv, ag_send, ag_recv, keep_sem)
    )
    out, gate, late = (0,), (1,), (2, 3)
    meet(count, parts)
    gdt_ref[...] = jnp.zeros_like(gdt_ref)

    token_copy = pltpu.make_async_copy(
        tokens_ref.at[:, pl.ds(pl.multiple_of(head * cols, cols), cols)], token_buf, token_sem
    )
    token_copy.start()

    def weight_copy(i):
        other = lax.rem(head + i, parts)
        return pltpu.make_async_copy(
            weight_ref.at[:, pl.ds(pl.multiple_of(other * cols, cols), cols)],
            weights.at[lax.rem(i + 1, 2)],
            weight_sem.at[lax.rem(i + 1, 2)],
        )

    def conv_copy(q):
        t = q // chunks * chunks + chunks - 1 - lax.rem(q, chunks)
        slot = lax.rem(q, 2)
        return pltpu.make_async_copy(
            conv_ref.at[ds(t * CHUNK, CHUNK)], conv_buf.at[slot], conv_sem.at[slot]
        )

    def state_copy(q):
        t = q // chunks * chunks + chunks - 1 - lax.rem(q, chunks)
        slot = lax.rem(q, 2)
        return pltpu.make_async_copy(states_far.at[t], state_buf.at[slot], state_sem.at[slot])

    conv_copy(0).start()
    state_copy(0).start()
    weight_copy(1).start()
    for copy in fetches[:4]:
        copy.wait()
    for i in out + gate:
        begin(i)

    tall = 2 * CHUNK

    def wout_copy(i):
        other = lax.rem(head + i, parts)
        return pltpu.make_async_copy(
            wout_far.at[:, pl.ds(pl.multiple_of(other * cols, cols), cols)],
            wout.at[i % 2],
            wout_sem.at[i % 2],
        )

    def mix_copy(i):
        other = lax.rem(head + i, parts)
        return remote(
            dn_out.at[other], mix_in.at[i - 1], mix_send.at[i], mix_recv.at[i], place, other
        )

    def mix(i):
        other = lax.rem(head + i, parts)
        if i < parts:
            wout_copy(i + 1).start()
        wout_copy(i).wait()

        def some(r):
            rows = ds(r * tall, tall)
            dn_out[other, rows, :] = mul(ng_t_ref[0:inner, rows], wout[i % 2], TN).astype(BF16)

        loop(0, rows_all // tall, some)
        if i < parts:
            mix_copy(i).start()

    wout_copy(1).start()

    for s in range(seqs):

        def alone(i, held):
            t = s * chunks + chunks - 1 - i
            rows = ds(t * CHUNK, CHUNK)
            grown = jnp.exp(cum_ref[rows, :])
            weighted = jnp.concatenate(
                [
                    (
                        dy_ref[rows, p * LANES : (p + 1) * LANES].astype(F32) * pair_of(grown, p)
                    ).astype(BF16)
                    for p in range(pairs)
                ],
                axis=1,
            )
            new = mul(bc_ref[rows, state:], weighted, TN)
            return spread(grown[CHUNK - 1 :, :], pairs) * held + new

        held = lax.fori_loop(0, chunks, alone, jnp.zeros((state, inner), F32))
        local[s] = held.astype(BF16)

    start, carry, finish = carry_exchange(
        dims,
        local,
        arrived,
        passed,
        handed,
        incoming,
        decay_ref,
        (st_send, st_recv, back_send, back_recv, over_send, over_recv),
        True,
    )
    start()
    advance(out, 0, STEPS)
    mix(1)
    advance(gate, 0, STEPS)
    mix(2)
    advance(out, 1, STEPS)
    carry()
    advance(gate, 1, STEPS)
    for copy in fetches[4:]:
        copy.wait()
    finish()
    mix(3)
    advance(out, 2, STEPS)
    for i in range(4, parts + 1):
        mix(i)

    side = iota((CHUNK, LANES), 1) < LANES // 2
    seen = iota((CHUNK, CHUNK), 0) <= iota((CHUNK, CHUNK), 1)
    upper = seen.astype(F32)
    for s in range(seqs):

        def chunk(i, held):
            t = s * chunks + chunks - 1 - i
            rows = ds(t * CHUNK, CHUNK)
            out_rows = ds((s * chunks + chunks - 1 - i) * CHUNK, CHUNK)
            turn = s * chunks + i
            conv_copy(turn).wait()
            state_copy(turn).wait()

            @pl.when(turn + 1 < total)
            def _():
                conv_copy(turn + 1).start()
                state_copy(turn + 1).start()

            cum, dt = cum_ref[rows, :], dt_ref[rows, :]
            cum_t = cum.T
            grown = jnp.exp(cum)
            end = cum[CHUNK - 1 :, :]
            tail = jnp.exp(end - cum)
            b_rows, c_rows = bc_ref[rows, 0:state], bc_ref[rows, state:]
            scores = mul(b_rows, c_rows, NT)
            low = held.astype(BF16)
            begun = state_buf[lax.rem(turn, 2)]
            begun_high, begun_low = halves_of(begun)
            pulled = mul(b_rows, low, NN)
            grad_scores = jnp.zeros((CHUNK, CHUNK), F32)
            d_x_sum = jnp.zeros((CHUNK, LANES), F32)
            d_fall = jnp.zeros((CHUNK, LANES), F32)
            into_x = []
            into_y = []
            last = []
            for p in range(pairs):
                lane = slice(p * LANES, (p + 1) * LANES)
                x, dy = xact_ref[rows, lane], dy_ref[rows, lane]
                xf, dyf = x.astype(F32), dy.astype(F32)
                dt_p, tail_p = pair_of(dt, p), pair_of(tail, p)
                stepped = xf * dt_p
                low_step = stepped.astype(BF16)
                halves = []
                for k, h in enumerate((2 * p, 2 * p + 1)):
                    gap = cum_t[h : h + 1, :] - cum[:, h : h + 1]
                    fade = jnp.exp(jnp.where(seen, gap, -1e30))
                    own = jnp.where(side if k == 0 else ~side, low_step, jnp.zeros_like(low_step))
                    grad_scores = grad_scores + mul(own, dy, NT) * fade
                    halves.append(mul((scores * fade).astype(BF16), dy, NN))
                from_state = pulled[:, lane] * tail_p
                d_step_x = jnp.where(side, halves[0], halves[1]) + from_state
                rounded = low_step.astype(F32)
                d_x_sum = d_x_sum + head_sums(xf * d_step_x, gather_ref[lane, :])
                d_fall = d_fall + head_sums(rounded * d_step_x, gather_ref[lane, :])
                into_x.append((stepped * tail_p).astype(BF16))
                into_y.append((dyf * pair_of(grown, p)).astype(BF16))
                last.append(jnp.sum(rounded * from_state, axis=0, keepdims=True))
                conv = conv_buf[lax.rem(turn, 2), :, lane]
                sg = sigmoid(conv)
                d_act = dt_p * d_step_x + chan_ref[6:7, lane] * dyf
                dconv[s, ds((chunks - 1 - i) * CHUNK, CHUNK), lane] = d_act * (
                    sg * (1.0 + conv * (1.0 - sg))
                )
            low_scores = grad_scores.astype(BF16)
            d_b = mul(low_scores, c_rows, NN) + mul(jnp.concatenate(into_x, axis=1), low, NT)
            into_y = jnp.concatenate(into_y, axis=1)
            d_c = mul(low_scores, b_rows, TN) + mul(into_y, begun_high, NT)
            d_c = d_c + mul(into_y, begun_low, NT)
            dbc[out_rows, 0:state] = d_b.astype(BF16)
            dbc[out_rows, state:] = d_c.astype(BF16)
            fall = spread(grown[CHUNK - 1 :, :], pairs)
            ends = jnp.concatenate(last, axis=1) + fall * jnp.sum(
                held * begun, axis=0, keepdims=True
            )
            ends = head_sums(jnp.broadcast_to(ends, (8, inner)), gather_ref[...])[0:1, :]
            d_log = mul(upper, dyy_ref[rows, :] - d_fall, NN, EXACT) + ends
            d_step = d_x_sum + vec_ref[6:7, :] * d_log
            d_dt = d_step * sigmoid(small_ref[rows, :] + vec_ref[5:6, :])
            gdt_ref[0:8, :] += eights(d_dt)
            gdt_ref[8:16, :] += eights(d_log * (dt * vec_ref[6:7, :]))
            ddt[out_rows, :] = d_dt


            @pl.when(turn == total * 3 // 8)
            def _():
                advance(gate, 2, STEPS)

            @pl.when(turn == total * 6 // 8)
            def _():
                advance(out, 3, STEPS)

            return fall * held + mul(c_rows, into_y, TN)

        lax.fori_loop(0, chunks, chunk, incoming[s].astype(F32))

    def pack(k):
        piece = mul(dbc[0:block, :], pack_ref[k, 0], NN)
        return (piece + mul(dbc[block:, :], pack_ref[k, 1], NN)).astype(BF16)

    def pack_one(k):
        bc_out[k] = pack(k)

    def x_copy(t):
        slot = lax.rem(t, 2)
        return pltpu.make_async_copy(
            x_far.at[ds(t * CHUNK, CHUNK)], conv_buf.at[slot], x_sem.at[slot]
        )

    x_copy(0).start()
    advance(gate, 3, STEPS)
    loop(0, parts, pack_one)
    share = head_copy(parts, lambda k: bc_out.at[k], lambda k: bc_in.at[k], bc_send, bc_recv)
    loop(1, parts, lambda i: share(i).start())

    before = lax.rem(place + count - 1, count)

    def edge_copy(s):
        return remote(
            dconv.at[s, pl.ds(0, 8)],
            dconv.at[s, pl.ds(block, 8)],
            edge_send.at[s],
            edge_recv.at[s],
            before,
            head,
        )

    def edge_bc():
        return remote(
            dconvbc.at[pl.ds(0, 8)],
            dconvbc.at[pl.ds(block, 8)],
            edge_send.at[seqs],
            edge_recv.at[seqs],
            before,
            head,
        )

    @pl.when(place > 0)
    def _():
        for s in range(seqs):
            edge_copy(s).start()

    pass_on(out, 0, 3)
    loop(1, parts, lambda i: share(i).wait())
    bc_in[head] = bc_out[head]
    d_act = bc_in[0].astype(F32)
    for k in range(1, parts):
        d_act = d_act + bc_in[k].astype(F32)
    conv = convbc_ref[...]
    sg = sigmoid(conv)
    dconvbc[0:block, :] = d_act * (sg * (1.0 + conv * (1.0 - sg)))

    @pl.when(place > 0)
    def _():
        edge_bc().start()

    @pl.when(place < count - 1)
    def _():
        for s in range(seqs):
            edge_copy(s).wait_recv()

    @pl.when(place == count - 1)
    def _():
        for s in range(seqs):
            dconv[s, block : block + 8, :] = jnp.zeros((8, inner), F32)

    gx_ref[...] = jnp.zeros_like(gx_ref)

    def x_chunk(t):
        rows = ds(t * CHUNK, CHUNK)
        s, c = t // chunks, lax.rem(t, chunks)
        x_copy(t).wait()

        @pl.when(t + 1 < total)
        def _():
            x_copy(t + 1).start()

        for p in range(pairs):
            lane = slice(p * LANES, (p + 1) * LANES)
            x = conv_buf[lax.rem(t, 2), :, lane]
            pre = jnp.zeros((CHUNK, LANES), F32)
            here = dconv[s, pl.ds(pl.multiple_of(c * CHUNK, CHUNK), CHUNK + 8), lane]
            for k in range(KER):
                off = KER - 1 - k
                d = pltpu.roll(here, CHUNK + 8 - off, 0)[:CHUNK] if off else here[:CHUNK]
                pre = pre + chan_ref[k : k + 1, lane] * d
                gx_ref[8 * k : 8 * k + 8, lane] += eights(x * d)
                if k == KER - 1:
                    gx_ref[8 * KER : 8 * KER + 8, lane] += eights(d)
            dx_ref[rows, lane] = pre.astype(BF16)

        @pl.when(t == total // 2)
        def _():
            pass_on(gate, 0, 3)

    loop(0, total, x_chunk)

    @pl.when(place < count - 1)
    def _():
        edge_bc().wait_recv()

    @pl.when(place == count - 1)
    def _():
        dconvbc[block : block + 8, :] = jnp.zeros((8, LANES), F32)

    low, high = small_ref[0:block, :], small_ref[block:, :]
    prebc[...] = jnp.where(
        iota(low.shape, 1) < LANES // 2, pltpu.roll(low, LANES // 2, 1), high
    )
    pre = jnp.zeros((block, LANES), F32)
    for k in range(KER):
        d = dconvbc[pl.ds(KER - 1 - k, block), :]
        pre = pre + vec_ref[k : k + 1, :] * d
        gbc_ref[8 * k : 8 * k + 8, :] = eights(prebc[...] * d)
    gbc_ref[8 * KER : 8 * KER + 8, :] = eights(dconvbc[0:block, :])
    at = iota((block, LANES), 1)
    for s in range(seqs):
        rows = slice(s * block, (s + 1) * block)
        mine = pre if s == seqs - 1 else pltpu.roll(pre, LANES // 2, 1)
        step = jnp.where(at < heads, ddt[rows, :], 0.0)
        dx_ref[rows, inner:] = jnp.where(at < LANES // 2, step, mine).astype(BF16)

    for i in late:
        begin(i)

    loop(1, parts, lambda i: mix_copy(i).wait())
    token_copy.wait()

    def add_up(t):
        rows = ds(t * CHUNK, CHUNK)
        d = dn_out[head, rows, :].astype(F32)
        for k in range(parts - 1):
            d = d + mix_in[k, rows, :].astype(F32)
        mixed_ref[rows, :] = (token_buf[rows, :].astype(F32) + d).astype(BF16)

    loop(0, total, add_up)


    def dn_copy(i):
        other = lax.rem(head + i, parts)
        return remote(
            dn_out.at[other], dn_in.at[i - 1], dn_send.at[i], dn_recv.at[i], place, other
        )

    def d_normed(i):
        other = lax.rem(head + i, parts)
        slot = (i + 1) % 2
        if i < parts:
            weight_copy(i + 1).start()

        weight_copy(i).wait()
        mine = small_weight_ref[:, pl.ds(pl.multiple_of(other * cols, cols), cols)]

        def some(r):
            rows = ds(r * tall, tall)
            part = mul(dgate_ref[rows, :], weights[slot, 0], NT)
            part = part + mul(dx_ref[rows, 0:inner], weights[slot, 1], NT)
            part = part + mul(dx_ref[rows, inner:], mine, NN)
            dn_out[other, rows, :] = part.astype(BF16)

        loop(0, rows_all // tall, some)

        if i < parts:
            dn_copy(i).start()

    between = ((out, 1), (gate, 1), (out, 2), (gate, 2))
    for k in range(STEPS):
        if k < parts:
            d_normed(k + 1)
        advance(late, k, STEPS)
        pass_on(*between[k], 3)
    for k in range(STEPS, parts):
        d_normed(k + 1)

    loop(1, parts, lambda i: dn_copy(i).wait())
    my_cols = pl.ds(pl.multiple_of(head * cols, cols), cols)

    def own(t, grads):
        rows = ds(t * CHUNK, CHUNK)
        d = dn_out[head, rows, :].astype(F32)
        for k in range(parts - 1):
            d = d + dn_in[k, rows, :].astype(F32)
        token = token_buf[rows, :].astype(F32)
        grads = grads + eights(d * (token * row_scale_ref[rows, :]))
        d = d * gain_ref[:, my_cols]
        grad_ref[rows, :] = d
        line = jnp.sum(d * token, axis=1, keepdims=True)
        line = jnp.where(iota((CHUNK, LANES), 1) == 0, line, 0.0)
        rowsum[head, t] = line.T[0:8, :]
        return grads

    norm_grads = lax.fori_loop(0, total, own, jnp.zeros((8, cols), F32))
    rows_copy = head_copy(
        parts, lambda _: rowsum.at[head], lambda k: rowsum.at[k], row_send, row_recv
    )
    loop(1, parts, lambda i: rows_copy(i).start())

    def summed(ref, k):
        return jnp.sum(ref[8 * k : 8 * k + 8, :], axis=0, keepdims=True)

    shared[place] = jnp.zeros(shared.shape[1:], F32)
    for k in range(KER + 1):
        shared[place, k : k + 1, 0:inner] = summed(gx_ref, k)
        shared[place, k : k + 1, inner:] = summed(gbc_ref, k)
    for k in range(2):
        shared[place, KER + 1 + k : KER + 2 + k, 0:inner] = summed(sums_ref, k)
        shared[place, KER + 1 + k : KER + 2 + k, inner:] = summed(gdt_ref, k)
    shared[place, 7:8, 0:cols] = jnp.sum(norm_grads, axis=0, keepdims=True)
    sums_copy = line_copy(
        count, lambda _: shared.at[place], lambda k: shared.at[k], sum_send, sum_recv
    )
    loop(1, count, lambda i: sums_copy(i).start())
    pass_on(late, 0, 3)
    loop(1, parts, lambda i: rows_copy(i).wait())

    def finish_rows(t):
        rows = ds(t * CHUNK, CHUNK)
        sums = rowsum[0, t]
        for k in range(1, parts):
            sums = sums + rowsum[k, t]
        turned = jnp.concatenate([sums, jnp.zeros((CHUNK - 8, LANES), F32)], axis=0).T
        scale = row_scale_ref[rows, :]
        pull = scale * scale * scale * (turned[:, 0:1] / width)
        grad_ref[rows, :] = (
            scale * grad_ref[rows, :]
            - token_buf[rows, :].astype(F32) * pull
            + cot_ref[rows, my_cols].astype(F32)
        )

    loop(0, total, finish_rows)
    pass_on(late, 1, 3)
    loop(1, count, lambda i: sums_copy(i).wait())
    everything = shared[0]
    for k in range(1, count):
        everything = everything + shared[k]
    total_ref[...] = everything
    pass_on(late, 2, 3)
    pass_end(out + gate + late)
    drain(out + gate + late)

    @pl.when(place > 0)
    def _():
        for s in range(seqs):
            edge_copy(s).wait_send()
        edge_bc().wait_send()


def backward(dims, *operands):
    count, parts, seqs, block, inner, heads, state = dims
    rows = seqs * block
    chunks = rows // CHUNK
    group, cut_rows = cut_of(count, seqs, state)
    normed_rows, ng_rows, width = (operands[k].shape[d] for k, d in ((16, 0), (17, 0), (18, 1)))
    cols = width // parts
    distant = (1, 3, 7, 10, 14, 16, 17, 18, 19, 20, 24, 25, 26)
    fetched = [operands[k] for k in (17, 18, 16, 19, 1, 20, 14)]
    spec = pl.BlockSpec(memory_space=pltpu.VMEM)
    far = pl.BlockSpec(memory_space=pl.ANY)
    line, ring = pltpu.SemaphoreType.DMA((count,)), pltpu.SemaphoreType.DMA((parts,))
    edge = pltpu.SemaphoreType.DMA((seqs + 1,))
    streams = [
        (ng_rows, width),
        (normed_rows, inner),
        (normed_rows, inner // 2),
        (normed_rows, inner // 2 + LANES),
    ]
    steps = pltpu.SemaphoreType.DMA((len(streams), 2, count // 2))
    outs = [(shape, BF16) for shape in streams]
    outs = outs + [((rows, cols), F32), ((8, inner + LANES), F32), ((rows, cols), BF16)]
    return pl.pallas_call(
        functools.partial(backward_kernel, dims),
        out_shape=[jax.ShapeDtypeStruct(*o) for o in outs],
        in_specs=[far if k in distant else spec for k in range(len(operands))],
        out_specs=[far] * len(streams) + [spec] * 3,
        scratch_shapes=[vmem((2, count // 2, r // count, c), BF16) for r, c in streams]
        + [vmem((r // count, c), BF16) for r, c in streams]
        + [vmem(a.shape, a.dtype) for a in fetched]
        + [
            pltpu.SemaphoreType.DMA((len(fetched),)),
            vmem((rows, inner + LANES), BF16),
            vmem((8 * (KER + 1), inner), F32),
            vmem((8 * (KER + 1), LANES), F32),
            vmem((16, LANES), F32),
            vmem((2, 2, cols, inner), BF16),
            vmem((2, CHUNK, inner), F32),
            vmem((2, state, inner), F32),
            vmem((parts, rows, cols), BF16),
            vmem((parts - 1, rows, cols), BF16),
            vmem((2, inner, cols), BF16),
            vmem((parts - 1, rows, cols), BF16),
            vmem((rows, cols), BF16),
            vmem((parts, chunks, 8, LANES), F32),
            vmem((count, 8, inner + LANES), F32),
            steps,
            steps,
            steps,
            steps,
            pltpu.SemaphoreType.DMA((len(streams),)),
            pltpu.SemaphoreType.DMA((2,)),
            pltpu.SemaphoreType.DMA((2,)),
            pltpu.SemaphoreType.DMA((2,)),
            pltpu.SemaphoreType.DMA((2,)),
            pltpu.SemaphoreType.DMA,
            ring,
            ring,
            pltpu.SemaphoreType.DMA((2,)),
            ring,
            ring,
            ring,
            ring,
            line,
            line,
            vmem((seqs, block + 8, inner), F32),
            vmem((block + 8, LANES), F32),
            vmem((block, LANES), F32),
            vmem((rows, 2 * state), BF16),
            vmem((rows, LANES), F32),
            vmem((seqs, state, inner), BF16),
            vmem((group, cut_rows, inner), BF16),
            vmem((group, cut_rows, inner), BF16),
            vmem((2, cut_rows, inner), BF16),
            vmem((seqs, state, inner), BF16),
            vmem((parts, block, LANES), BF16),
            vmem((parts, block, LANES), BF16),
            edge,
            edge,
            ring,
            ring,
            line,
            line,
            line,
            line,
            pltpu.SemaphoreType.DMA,
            pltpu.SemaphoreType.DMA,
        ],
        compiler_params=pltpu.CompilerParams(
            collective_id=3, has_side_effects=True, vmem_limit_bytes=VMEM_LIMIT
        ),
        name="mixer_backward",
    )(*operands)


def body(
    tokens,
    norm_gain,
    gate_input_weight,
    coefficient_weight,
    step_weight,
    conv_x,
    conv_bc,
    conv_bias_x,
    conv_bias_bc,
    dt_bias,
    a_log,
    d_skip,
    gate_gain,
    output_weight,
    cotangent,
):
    seqs, block, width = tokens.shape
    inner = gate_input_weight.shape[2]
    state_part = coefficient_weight.shape[2]
    heads = step_weight.shape[1]
    count, parts = lax.axis_size("seq"), lax.axis_size("head")
    state = state_part * parts
    rows = seqs * block
    col_count = width // parts
    half = LANES // 2
    dims = (count, parts, seqs, block, inner, heads, state)

    flat_tokens = tokens.reshape(rows, width)
    both_weights = gate_input_weight.transpose(1, 0, 2)
    gate_pre, x_pre, small, normed_t, row_scale, small_weight, chan, vec = project(
        flat_tokens,
        norm_gain.reshape(-1, LANES),
        both_weights,
        step_weight.T,
        coefficient_weight.transpose(1, 2, 0),
        conv_x,
        conv_bc,
        conv_bias_x.reshape(-1, LANES),
        conv_bias_bc,
        dt_bias.reshape(1, heads),
        a_log.reshape(1, heads),
        d_skip.reshape(1, heads),
        gate_gain.reshape(-1, LANES),
    )
    device, lane, channel = np.meshgrid(
        np.arange(parts), np.arange(LANES), np.arange(2 * state), indexing="ij"
    )
    is_c, at = channel // state, channel % state
    unpack = np.stack(
        [
            (lane == s * half + is_c * state_part + at - device * state_part)
            & (at // state_part == device)
            for s in range(seqs)
        ]
    ).astype(np.float32)
    pack = jnp.asarray(unpack.transpose(1, 0, 3, 2), BF16)
    unpack = jnp.asarray(unpack.reshape(seqs, parts * LANES, 2 * state), BF16)
    expand = np.arange(LANES)[:, None] == np.arange(inner)[None, :] // (inner // heads)
    gather = jnp.asarray(expand.T.astype(np.float32), BF16)
    expand = jnp.asarray(expand.astype(np.float32))
    cot = cotangent.reshape(rows, width)

    xact, bc, conv, convbc, dt, cum, states, ng_t, dgate, dy, dyy, decay, sums = forward(
        dims,
        x_pre,
        gate_pre,
        small,
        chan,
        vec,
        unpack,
        expand,
        gather,
        cot,
        output_weight,
    )
    def padded(array_in):
        return jnp.pad(array_in, ((0, -array_in.shape[0] % (count * 16)), (0, 0)))

    *streams, grad_input, sums, block_out = backward(
        dims,
        dy,
        xact,
        bc,
        conv,
        convbc,
        dt,
        cum,
        states,
        dyy,
        decay,
        x_pre,
        small,
        chan,
        vec,
        pack,
        gather,
        padded(normed_t),
        padded(ng_t),
        cot,
        dgate,
        small_weight,
        sums,
        norm_gain[None],
        row_scale,
        flat_tokens,
        both_weights,
        output_weight,
    )
    (
        g_in,
        g_w_out,
        g_coef,
        g_step,
        taps,
        taps_bc,
        bias,
        bias_bc,
        g_dt,
        g_log,
        g_skip,
        g_gain,
        g_norm,
        block_out,
        grad_input,
    ) = finish(
        width, inner, heads, state_part, streams, sums, gather, block_out, grad_input
    )
    return (
        block_out.reshape(seqs, block, col_count),
        grad_input.reshape(seqs, block, col_count),
        g_norm.reshape(-1),
        g_in,
        g_coef.transpose(2, 0, 1),
        g_step.T,
        taps,
        taps_bc,
        bias.reshape(-1),
        bias_bc,
        g_dt.reshape(-1),
        g_log.reshape(-1),
        g_skip.reshape(-1),
        g_gain.reshape(-1),
        g_w_out,
    )


def solution(mesh):
    placed = (
        P(None, "seq", None),
        P(),
        P(None, None, "head"),
        P(None, None, "head"),
        P(None, "head"),
        P(None, "head"),
        P(None, None, "head"),
        P("head"),
        P(None, "head"),
        P("head"),
        P("head"),
        P("head"),
        P("head"),
        P("head", None),
        P(None, "seq", None),
    )
    return jax.shard_map(
        body,
        mesh=mesh,
        in_specs=placed,
        out_specs=(
            P(None, "seq", "head"),
            P(None, "seq", "head"),
            P("head"),
            P(None, None, "head"),
            P(None, None, "head"),
            P(None, "head"),
            P(None, "head"),
            P(None, None, "head"),
            P("head"),
            P(None, "head"),
            P("head"),
            P("head"),
            P("head"),
            P("head"),
            P("head", None),
        ),
        check_vma=False,
    )
```

```python
import functools

import jax
import jax.numpy as jnp
import numpy as np
from jax import lax
from jax.experimental import pallas as pl
from jax.experimental.pallas import tpu as pltpu
from jax.sharding import PartitionSpec as P

KER = 4
EPSILON = 1e-05
CHUNK = 128
LANES = 128
MESH = pl.DeviceIdType.MESH
F32 = jnp.float32
BF16 = jnp.bfloat16
EXACT = lax.Precision.HIGHEST
VMEM_LIMIT = 61 * 2**20
NN = ((1,), (0,))
NT = ((1,), (1,))
TN = ((0,), (0,))


def mul(left, right, how, precision=None):
    return lax.dot_general(
        left, right, (how, ((), ())), precision=precision, preferred_element_type=F32
    )


def sigmoid(v):
    return 0.5 * jnp.tanh(0.5 * v) + 0.5


def softplus(v):
    e = jnp.exp(-jnp.abs(v))
    u = 1.0 + e
    near = u - 1.0
    log1p = jnp.where(near == 0.0, e, jnp.log(u) * (e / jnp.where(near == 0.0, 1.0, near)))
    return jnp.maximum(v, 0.0) + log1p


def iota(shape, dim):
    return lax.broadcasted_iota(jnp.int32, shape, dim)


def ds(start, size):
    return pl.ds(pl.multiple_of(start, size), size)


def pair_of(values, pair):
    low = values[:, 2 * pair : 2 * pair + 1]
    high = values[:, 2 * pair + 1 : 2 * pair + 2]
    return jnp.where(iota((values.shape[0], LANES), 1) < LANES // 2, low, high)


def spread(values, pairs):
    return jnp.concatenate([pair_of(values, p) for p in range(pairs)], axis=1)


def eights(v):
    return jnp.sum(v.reshape(v.shape[0] // 8, 8, v.shape[1]), axis=0)


def halves_of(v):
    high = v.astype(BF16)
    return high, (v - high.astype(F32)).astype(BF16)


def head_sums(v, gather):
    high, low = halves_of(v)
    return mul(high, gather, NN) + mul(low, gather, NN)


def remote(src, dst, send, recv, place, head):
    return pltpu.make_async_remote_copy(
        src_ref=src,
        dst_ref=dst,
        send_sem=send,
        recv_sem=recv,
        device_id=(place, head),
        device_id_type=MESH,
    )


def meet(count, parts):
    place, head = lax.axis_index("seq"), lax.axis_index("head")
    barrier = pltpu.get_barrier_semaphore()

    def along_seq(i, _):
        other = lax.rem(place + i, count)
        pl.semaphore_signal(barrier, inc=1, device_id=(other, head), device_id_type=MESH)
        return 0

    def along_head(i, _):
        other = lax.rem(head + i, parts)
        pl.semaphore_signal(barrier, inc=1, device_id=(place, other), device_id_type=MESH)
        return 0

    lax.fori_loop(1, count, along_seq, 0)
    lax.fori_loop(1, parts, along_head, 0)
    pl.semaphore_wait(barrier, count - 1 + parts - 1)


def loop(low, high, step):
    def one(i, _):
        step(i)
        return 0

    lax.fori_loop(low, high, one, 0)


def line_copy(count, src, dst, send, recv):
    place, head = lax.axis_index("seq"), lax.axis_index("head")

    def copy(i):
        other = lax.rem(place + i, count)
        return remote(src(other), dst(place), send.at[i], recv.at[i], other, head)

    return copy


def head_copy(parts, src, dst, send, recv):
    place, head = lax.axis_index("seq"), lax.axis_index("head")

    def copy(i):
        other = lax.rem(head + i, parts)
        return remote(src(other), dst(head), send.at[i], recv.at[i], place, other)

    return copy


def cut_of(count, seqs, state):
    group = count // 2
    return group, seqs * state // group


def carry_exchange(dims, local, arrived, passed, total, incoming, decay_ref, sems, reverse):
    count, _, seqs, _, inner, _, state = dims
    place, head = lax.axis_index("seq"), lax.axis_index("head")
    send, recv, back_send, back_recv, over_send, over_recv = sems
    group, rows = cut_of(count, seqs, state)
    base, me = place // group * group, lax.rem(place, group)
    leads = place >= group if reverse else place < group
    each = group // seqs

    def at(ref, k):
        return ref.at[k // each, ds(lax.rem(k, each) * rows, rows)]

    def out(i):
        other = lax.rem(me + i, group)
        return remote(at(local, other), arrived.at[me], send.at[i], recv.at[i], base + other, head)

    def back(j):
        i = lax.rem(j - me + group, group)
        return remote(
            passed.at[j], at(incoming, me), back_send.at[i], back_recv.at[i], base + j, head
        )

    def over():
        other = lax.rem(place + group, count)
        return remote(total.at[0], total.at[1], over_send, over_recv, other, head)

    def start():
        loop(1, group, lambda i: out(i).start())
        arrived[me] = local[me // each, ds(lax.rem(me, each) * rows, rows)]

    def carry():
        @pl.when(leads)
        def _():
            total[1] = jnp.zeros((rows, inner), total.dtype)

        @pl.when(~leads)
        def _():
            over().wait_recv()

        held = total[1].astype(F32)
        seq = me // each
        for step in range(group):
            j = group - 1 - step if reverse else step

            @pl.when(j != me)
            def _():
                out(lax.rem(me - j + group, group)).wait_recv()

            passed[j] = held.astype(passed.dtype)

            @pl.when(j != me)
            def _():
                back(j).start()

            @pl.when(j == me)
            def _():
                incoming[seq, ds(lax.rem(me, each) * rows, rows)] = passed[j]

            held = decay_ref[seq, pl.ds(base + j, 1), :] * held + arrived[j].astype(F32)

        @pl.when(leads)
        def _():
            total[0] = held.astype(total.dtype)
            over().start()

    def finish():
        def one(i):
            out(i).wait_send()
            back(lax.rem(me + i, group)).wait()

        loop(1, group, one)

        @pl.when(leads)
        def _():
            over().wait_send()

    return start, carry, finish


def forward_kernel(
    dims,
    x_ref,
    normed_t_far,
    weight_far,
    small_ref,
    chan_ref,
    vec_ref,
    unpack_ref,
    expand_ref,
    gather_ref,
    cot_far,
    wout_far,
    xact_far,
    bc_far,
    conv_far,
    convbc_ref,
    dt_far,
    cum_far,
    states_far,
    ng_t_far,
    dgate_far,
    dy_far,
    dyy_far,
    decay_ref,
    sums_ref,
    normed_t_ref,
    weight_ref,
    cot_ref,
    wout_ref,
    gate_ref,
    xact_ref,
    bc_ref,
    conv_ref,
    dt_ref,
    cum_ref,
    states_ref,
    ng_t_ref,
    dgate_ref,
    dy_ref,
    dyy_ref,
    fetch_sem,
    keep_sem,
    edge_x,
    edge_s,
    ext,
    extbc,
    bc_all,
    fresh,
    y_ref,
    dng_ref,
    gated_ref,
    decays,
    local,
    arrived,
    passed,
    handed,
    incoming,
    rowsum,
    edge_send,
    edge_recv,
    dec_send,
    dec_recv,
    bc_send,
    bc_recv,
    st_send,
    st_recv,
    back_send,
    back_recv,
    over_send,
    over_recv,
    row_send,
    row_recv,
):
    count, parts, seqs, block, inner, heads, state = dims
    place, head = lax.axis_index("seq"), lax.axis_index("head")
    chunks = block // CHUNK
    pairs = heads // 2
    total = seqs * chunks
    fetches = [
        pltpu.make_async_copy(src, dst, fetch_sem.at[k])
        for k, (src, dst) in enumerate(
            (
                (cot_far, cot_ref),
                (wout_far, wout_ref),
                (normed_t_far, normed_t_ref),
                (weight_far.at[0], weight_ref),
            )
        )
    ]
    for copy in fetches:
        copy.start()
    keeps = [
        pltpu.make_async_copy(src, dst, keep_sem.at[k])
        for k, (src, dst) in enumerate(
            (
                (xact_ref, xact_far),
                (bc_ref, bc_far),
                (conv_ref, conv_far),
                (dt_ref, dt_far),
                (cum_ref, cum_far),
                (states_ref, states_far),
                (ng_t_ref, ng_t_far),
                (dgate_ref, dgate_far),
                (dy_ref, dy_far),
                (dyy_ref, dyy_far),
            )
        )
    ]
    meet(count, parts)

    def edge_copies(ahead):
        copies = []
        for s in range(seqs):
            rows = pl.ds(s * block + block - 8, 8)
            for k, (src, dst) in enumerate(((x_ref, edge_x), (small_ref, edge_s))):
                copies.append(
                    remote(
                        src.at[rows], dst.at[s], edge_send.at[k, s], edge_recv.at[k, s], ahead, head
                    )
                )
        return copies

    after = lax.rem(place + 1, count)

    @pl.when(place < count - 1)
    def _():
        for c in edge_copies(after):
            c.start()

    lower = (iota((CHUNK, CHUNK), 0) >= iota((CHUNK, CHUNK), 1)).astype(F32)
    for s in range(seqs):

        def steps(c, logs):
            rows = ds((s * chunks + c) * CHUNK, CHUNK)
            dt = softplus(small_ref[rows, :] + vec_ref[5:6, :])
            cum = mul(lower, dt * vec_ref[6:7, :], NN, EXACT)
            dt_ref[rows, :] = dt
            cum_ref[rows, :] = cum
            return logs + cum[CHUNK - 1 :, :]

        logs = lax.fori_loop(0, chunks, steps, jnp.zeros((1, LANES), F32))
        decays[place, s : s + 1, :] = jnp.exp(logs)

    dec = line_copy(count, lambda _: decays.at[place], lambda k: decays.at[k], dec_send, dec_recv)
    loop(1, count, lambda i: dec(i).start())

    @pl.when(place > 0)
    def _():
        for c in edge_copies(after):
            c.wait_recv()

    @pl.when(place == 0)
    def _():
        edge_x[...] = jnp.zeros_like(edge_x)
        edge_s[...] = jnp.zeros_like(edge_s)

    def packed(low, high):
        return jnp.where(
            iota(low.shape, 1) < LANES // 2, pltpu.roll(low, LANES // 2, 1), high
        )

    extbc[0:8, :] = packed(edge_s[0], edge_s[1])
    extbc[8:, :] = packed(small_ref[0:block, :], small_ref[block:, :])
    conv = vec_ref[4:5, :]
    for k in range(KER):
        conv = conv + vec_ref[k : k + 1, :] * extbc[pl.ds(8 - (KER - 1) + k, block), :]
    convbc_ref[...] = conv
    bc_all[head] = (conv * sigmoid(conv)).astype(BF16)
    share = head_copy(parts, lambda _: bc_all.at[head], lambda k: bc_all.at[k], bc_send, bc_recv)
    loop(1, parts, lambda i: share(i).start())

    def x_chunk(t):
        rows = ds(t * CHUNK, CHUNK)
        s, c = t // chunks, lax.rem(t, chunks)
        before = pl.ds(pl.multiple_of(jnp.maximum(t * CHUNK - 8, 0), 8), 8)
        for b in range(inner // LANES):
            lane = slice(b * LANES, (b + 1) * LANES)
            ext[0:8, lane] = jnp.where(c == 0, edge_x[s, :, lane], x_ref[before, lane])
            ext[8:, lane] = x_ref[rows, lane]
            conv = chan_ref[4:5, lane]
            for k in range(KER):
                conv = conv + chan_ref[k : k + 1, lane] * ext[pl.ds(8 - (KER - 1) + k, CHUNK), lane]
            conv_ref[rows, lane] = conv
            xact_ref[rows, lane] = (conv * sigmoid(conv)).astype(BF16)

    loop(0, total, x_chunk)

    loop(1, parts, lambda i: share(i).wait())
    everything = jnp.concatenate([bc_all[k] for k in range(parts)], axis=1)
    for s in range(seqs):
        bc_ref[s * block : (s + 1) * block, :] = mul(everything, unpack_ref[s], NN).astype(BF16)

    for s in range(seqs):

        def add(c, held):
            t = s * chunks + c
            rows = ds(t * CHUNK, CHUNK)
            cum, dt = cum_ref[rows, :], dt_ref[rows, :]
            end = cum[CHUNK - 1 :, :]
            tail = jnp.exp(end - cum) * dt
            weighted = jnp.concatenate(
                [
                    (
                        xact_ref[rows, p * LANES : (p + 1) * LANES].astype(F32) * pair_of(tail, p)
                    ).astype(BF16)
                    for p in range(pairs)
                ],
                axis=1,
            )
            new = mul(bc_ref[rows, 0:state], weighted, TN)
            fresh[t] = new
            return spread(jnp.exp(end), pairs) * held + new

        held = lax.fori_loop(0, chunks, add, jnp.zeros((state, inner), F32))
        local[s] = held.astype(local.dtype)

    start, carry, finish = carry_exchange(
        dims,
        local,
        arrived,
        passed,
        handed,
        incoming,
        decay_ref,
        (st_send, st_recv, back_send, back_recv, over_send, over_recv),
        False,
    )
    start()
    for copy in keeps[:5]:
        copy.start()

    def within(t):
        rows = ds(t * CHUNK, CHUNK)
        cum, dt = cum_ref[rows, :], dt_ref[rows, :]
        cum_t = cum.T
        scores = mul(bc_ref[rows, state:], bc_ref[rows, 0:state], NT)
        seen = iota((CHUNK, CHUNK), 0) >= iota((CHUNK, CHUNK), 1)
        side = iota((CHUNK, LANES), 1) < LANES // 2
        for p in range(pairs):
            lane = slice(p * LANES, (p + 1) * LANES)
            stepped = (xact_ref[rows, lane].astype(F32) * pair_of(dt, p)).astype(BF16)
            halves = []
            for h in (2 * p, 2 * p + 1):
                gap = cum[:, h : h + 1] - cum_t[h : h + 1, :]
                mixing = (scores * jnp.exp(jnp.where(seen, gap, -1e30))).astype(BF16)
                halves.append(mul(mixing, stepped, NN))
            y_ref[rows, lane] = jnp.where(side, halves[0], halves[1])

    loop(0, total, within)

    loop(1, count, lambda i: dec(i).wait())
    for s in range(seqs):
        decay_ref[s] = mul(decays[:, s, :], expand_ref[...], NN, EXACT)
    for copy in fetches:
        copy.wait()
    wide = 2 * LANES
    leads = place < count // 2

    def back_project(i):
        s, b = i // (inner // wide), lax.rem(i, inner // wide)
        rows, lane = ds(s * block, block), ds(b * wide, wide)
        dng_ref[rows, lane] = mul(cot_ref[rows, :], wout_ref[lane, :], NT)

    def gate_project(i):
        rows = ds(i * wide, wide)
        gate_ref[rows, :] = mul(normed_t_ref[:, rows], weight_ref[...], TN)

    def meanwhile():
        loop(0, seqs * (inner // wide), back_project)
        loop(0, seqs * block // wide, gate_project)

    @pl.when(~leads)
    def _():
        meanwhile()

    carry()

    @pl.when(leads)
    def _():
        meanwhile()

    finish()

    for s in range(seqs):

        def gate(c, held):
            t = s * chunks + c
            rows = ds(t * CHUNK, CHUNK)
            cum = cum_ref[rows, :]
            grown = jnp.exp(cum)
            states_ref[t] = held
            high, low = halves_of(held)
            c_rows = bc_ref[rows, state:]
            carried = mul(c_rows, high, NN) + mul(c_rows, low, NN)
            square = jnp.zeros((CHUNK, LANES), F32)
            cross = jnp.zeros((CHUNK, LANES), F32)
            for p in range(pairs):
                lane = slice(p * LANES, (p + 1) * LANES)
                y = y_ref[rows, lane] + carried[:, lane] * pair_of(grown, p)
                y_ref[rows, lane] = y
                out = y + chan_ref[6:7, lane] * xact_ref[rows, lane].astype(F32)
                pre = gate_ref[rows, lane]
                gated = out * (pre * sigmoid(pre))
                gated_ref[rows, lane] = gated
                square = square + gated * gated
                cross = cross + dng_ref[rows, lane] * chan_ref[5:6, lane] * gated
            at = iota((CHUNK, LANES), 1)
            both = jnp.where(
                at == 0,
                jnp.sum(square, axis=1, keepdims=True),
                jnp.where(at == 1, jnp.sum(cross, axis=1, keepdims=True), 0.0),
            )
            rowsum[head, t] = both.T[0:8, :]
            return spread(grown[CHUNK - 1 :, :], pairs) * held + fresh[t]

        lax.fori_loop(0, chunks, gate, incoming[s].astype(F32))

    keeps[5].start()
    rows_copy = head_copy(
        parts, lambda _: rowsum.at[head], lambda k: rowsum.at[k], row_send, row_recv
    )
    loop(1, parts, lambda i: rows_copy(i).start())
    loop(1, parts, lambda i: rows_copy(i).wait())
    sums_ref[...] = jnp.zeros_like(sums_ref)
    channels = inner * parts

    def outputs(t):
        rows = ds(t * CHUNK, CHUNK)
        sums = rowsum[0, t]
        for k in range(1, parts):
            sums = sums + rowsum[k, t]
        turned = jnp.concatenate([sums, jnp.zeros((CHUNK - 8, LANES), F32)], axis=0).T
        scale = lax.rsqrt(turned[:, 0:1] / channels + EPSILON)
        pull = scale * scale * scale * (turned[:, 1:2] / channels)
        dyy = jnp.zeros((CHUNK, LANES), F32)
        for p in range(pairs):
            lane = slice(p * LANES, (p + 1) * LANES)
            pre = gate_ref[rows, lane]
            sg = sigmoid(pre)
            gated, y = gated_ref[rows, lane], y_ref[rows, lane]
            x = xact_ref[rows, lane].astype(F32)
            gain = chan_ref[5:6, lane]
            scaled = gated * scale
            ng_t_ref[lane, rows] = (scaled * gain).T.astype(BF16)
            dng = dng_ref[rows, lane]
            d_gated = scale * (dng * gain) - gated * pull
            d_ssd = d_gated * (pre * sg)
            out = y + chan_ref[6:7, lane] * x
            dgate_ref[rows, lane] = (d_gated * out * (sg * (1.0 + pre * (1.0 - sg)))).astype(BF16)
            dy = d_ssd.astype(BF16)
            dy_ref[rows, lane] = dy
            sums_ref[0:8, lane] += eights(dng * scaled)
            sums_ref[8:16, lane] += eights(d_ssd * x)
            dyy = dyy + head_sums(dy.astype(F32) * y, gather_ref[lane, :])
        dyy_ref[rows, :] = dyy

    loop(0, total, outputs)
    for copy in keeps[6:]:
        copy.start()
    for copy in keeps:
        copy.wait()

    @pl.when(place < count - 1)
    def _():
        for c in edge_copies(after):
            c.wait_send()


def vmem(shape, kind):
    return pltpu.VMEM(shape, kind)


def forward(dims, *operands):
    count, parts, seqs, block, inner, heads, state = dims
    rows = seqs * block
    chunks = rows // CHUNK
    group, cut_rows = cut_of(count, seqs, state)
    spec, far = pl.BlockSpec(memory_space=pltpu.VMEM), pl.BlockSpec(memory_space=pl.ANY)
    fetched, kept = (1, 2, 9, 10), (0, 1, 2, 4, 5, 6, 7, 8, 9, 10)
    line, ring = pltpu.SemaphoreType.DMA((count,)), pltpu.SemaphoreType.DMA((parts,))
    edge = pltpu.SemaphoreType.DMA((2, seqs))
    outs = [
        ((rows, inner), BF16),
        ((rows, 2 * state), BF16),
        ((rows, inner), F32),
        ((block, LANES), F32),
        ((rows, LANES), F32),
        ((rows, LANES), F32),
        ((chunks, state, inner), F32),
        ((inner, rows), BF16),
        ((rows, inner), BF16),
        ((rows, inner), BF16),
        ((rows, LANES), F32),
        ((seqs, count, inner), F32),
        ((16, inner), F32),
    ]
    return pl.pallas_call(
        functools.partial(forward_kernel, dims),
        out_shape=[jax.ShapeDtypeStruct(*o) for o in outs],
        in_specs=[far if k in fetched else spec for k in range(len(operands))],
        out_specs=[far if k in kept else spec for k in range(len(outs))],
        scratch_shapes=[vmem(operands[k].shape[-2:], operands[k].dtype) for k in fetched]
        + [vmem((rows, inner), F32)]
        + [vmem(*outs[k]) for k in kept]
        + [
            pltpu.SemaphoreType.DMA((len(fetched),)),
            pltpu.SemaphoreType.DMA((len(kept),)),
            vmem((seqs, 8, inner), F32),
            vmem((seqs, 8, LANES), F32),
            vmem((CHUNK + 8, inner), F32),
            vmem((block + 8, LANES), F32),
            vmem((parts, block, LANES), BF16),
            vmem((chunks, state, inner), F32),
            vmem((rows, inner), F32),
            vmem((rows, inner), F32),
            vmem((rows, inner), F32),
            vmem((count, 8, LANES), F32),
            vmem((seqs, state, inner), BF16),
            vmem((group, cut_rows, inner), BF16),
            vmem((group, cut_rows, inner), F32),
            vmem((2, cut_rows, inner), F32),
            vmem((seqs, state, inner), F32),
            vmem((parts, chunks, 8, LANES), F32),
            edge,
            edge,
            line,
            line,
            ring,
            ring,
            line,
            line,
            line,
            line,
            pltpu.SemaphoreType.DMA,
            pltpu.SemaphoreType.DMA,
            ring,
            ring,
        ],
        compiler_params=pltpu.CompilerParams(
            collective_id=2, has_side_effects=True, vmem_limit_bytes=VMEM_LIMIT
        ),
        name="mixer_forward",
    )(*operands)


def project_kernel(
    tokens_ref,
    gain_ref,
    weight_ref,
    step_ref,
    coef_ref,
    taps_ref,
    taps_bc_ref,
    bias_ref,
    bias_bc_ref,
    dt_bias_ref,
    a_log_ref,
    skip_ref,
    gate_gain_ref,
    x_ref,
    small_ref,
    turned_ref,
    scale_ref,
    small_weight_ref,
    chan_ref,
    vec_ref,
    gain_row,
):
    heads, state_part = step_ref.shape[0], coef_ref.shape[1]

    def flat(ref):
        return jnp.concatenate([ref[k : k + 1, :] for k in range(ref.shape[0])], axis=1)

    @pl.when(pl.program_id(0) == 0)
    def _():
        small_weight_ref[...] = jnp.zeros_like(small_weight_ref)
        small_weight_ref[0:heads, :] = step_ref[...]
        for k in range(2):
            low = LANES // 2 + k * state_part
            small_weight_ref[low : low + state_part, :] = coef_ref[k]
        gain_row[...] = flat(gain_ref)
        chan_ref[...] = jnp.zeros_like(chan_ref)
        chan_ref[0:KER, :] = taps_ref[...]
        chan_ref[4:5, :] = flat(bias_ref)
        chan_ref[5:6, :] = flat(gate_gain_ref)
        chan_ref[6:7, :] = spread(skip_ref[...], heads // 2)
        vec_ref[...] = jnp.zeros_like(vec_ref)
        for k in range(4):
            at = slice(k * state_part, (k + 1) * state_part)
            vec_ref[0:KER, at] = taps_bc_ref[:, k % 2, :]
            vec_ref[4:5, at] = bias_bc_ref[k % 2 : k % 2 + 1, :]
        vec_ref[5:6, 0:heads] = dt_bias_ref[...]
        vec_ref[6:7, 0:heads] = -jnp.exp(a_log_ref[...])

    tokens = tokens_ref[...].astype(F32)
    scale = lax.rsqrt(jnp.mean(tokens * tokens, axis=1, keepdims=True) + EPSILON)
    scale_ref[...] = scale
    low = (tokens * scale * gain_row[...]).astype(BF16)
    turned_ref[...] = low.T
    x_ref[...] = mul(low, weight_ref[0], NN)
    small_ref[...] = mul(low, small_weight_ref[...], NT)


def project(tokens, gain, weights, *params):
    rows, width = tokens.shape
    inner = weights.shape[2]
    tall = 2 * CHUNK

    def by_rows(cols):
        return pl.BlockSpec((tall, cols), lambda i: (i, 0))

    def whole(shape):
        return pl.BlockSpec(shape, lambda i: (0,) * len(shape))

    return pl.pallas_call(
        project_kernel,
        grid=(rows // tall,),
        in_specs=[
            by_rows(width),
            whole(gain.shape),
            pl.BlockSpec((1, width, inner), lambda i: (1, 0, 0)),
        ]
        + [whole(a.shape) for a in params],
        out_specs=[
            by_rows(inner),
            by_rows(LANES),
            pl.BlockSpec((width, tall), lambda i: (0, i)),
            by_rows(1),
            whole((LANES, width)),
            whole((8, inner)),
            whole((8, LANES)),
            whole((1, width)),
        ],
        out_shape=[
            jax.ShapeDtypeStruct((rows, inner), F32),
            jax.ShapeDtypeStruct((rows, LANES), F32),
            jax.ShapeDtypeStruct((width, rows), BF16),
            jax.ShapeDtypeStruct((rows, 1), F32),
            jax.ShapeDtypeStruct((LANES, width), BF16),
            jax.ShapeDtypeStruct((8, inner), F32),
            jax.ShapeDtypeStruct((8, LANES), F32),
            jax.ShapeDtypeStruct((1, width), F32),
        ],
        compiler_params=pltpu.CompilerParams(vmem_limit_bytes=VMEM_LIMIT),
        name="project",
    )(tokens, gain, weights, *params)


def ring_place(count):
    place = lax.axis_index("seq")
    row, col = place // 2, place % 2
    return jnp.where(col == 0, row, count - 1 - row)


def ring_device(rank, count):
    return jnp.where(rank < count // 2, 2 * rank, 2 * (count - 1 - rank) + 1)


def ring_steps(count, plan, outs, bufs, stages, sems):
    rs_send, rs_recv, ag_send, ag_recv, keep_sem = sems
    far = count // 2
    head = lax.axis_index("head")
    rank = ring_place(count)
    arms = (1, -1)
    peers = [ring_device(lax.rem(rank + a + count, count), count) for a in arms]

    def chunk_at(distance):
        return lax.rem(rank + distance + 2 * count, count)

    def partial(i, chunk):
        left, right, first, cols, _ = plan[i]
        rows = left.shape[0] // count
        return mul(left[ds(chunk * rows, rows), :], right[:, first : first + cols], NN)

    def half(i, arm):
        cols, cut = plan[i][3:]
        return slice(0, cut) if arm == 0 else slice(cut, cols)

    def block_of(i, chunk):
        rows = plan[i][0].shape[0] // count
        return outs[i].at[ds(chunk * rows, rows)]

    def rs(i, arm, step, first=False):
        here = stages[i] if first else bufs[i].at[arm, step - 1]
        there = bufs[i].at[arm, step]
        if first:
            here, there = here.at[:, half(i, arm)], there.at[:, half(i, arm)]
        return remote(
            here, there, rs_send.at[i, arm, step], rs_recv.at[i, arm, step], peers[arm], head
        )

    def ag(i, arm, step, kind="middle"):
        there = block_of(i, chunk_at(-arms[arm] * step))
        here = bufs[i].at[0, far - 1] if kind == "first" else there
        if kind == "last":
            here, there = here.at[:, half(i, arm)], there.at[:, half(i, arm)]
        return remote(
            here, there, ag_send.at[i, arm, step], ag_recv.at[i, arm, step], peers[arm], head
        )

    def keep(i):
        return pltpu.make_async_copy(
            bufs[i].at[0, far - 1], block_of(i, chunk_at(0)), keep_sem.at[i]
        )

    def begin(i):
        stages[i][...] = partial(i, chunk_at(far)).astype(BF16)
        for arm in range(2):
            rs(i, arm, 0, True).start()

    def advance(streams, slot, slots):
        def second(i, arm):
            own = partial(i, chunk_at(arms[arm] * (far - 1)))
            rs(i, arm, 0, True).wait_recv()
            mine, other = half(i, arm), half(i, 1 - arm)
            bufs[i][arm, 0, :, other] = own[:, other].astype(BF16)
            bufs[i][arm, 0, :, mine] = (
                own[:, mine] + bufs[i][arm, 0, :, mine].astype(F32)
            ).astype(BF16)
            rs(i, arm, 1).start()

        def later(i, arm, step):
            own = partial(i, chunk_at(arms[arm] * (far - step)))
            rs(i, arm, step - 1).wait_recv()
            bufs[i][arm, step - 1] = (own + bufs[i][arm, step - 1].astype(F32)).astype(BF16)
            rs(i, arm, step).start()

        def last(i):
            own = partial(i, chunk_at(0))
            for arm in range(2):
                rs(i, arm, far - 1).wait_recv()
                own = own + bufs[i][arm, far - 1].astype(F32)
            bufs[i][0, far - 1] = own.astype(BF16)
            for arm in range(2):
                ag(i, arm, 0, "first").start()
            keep(i).start()

        low, high = slot * far // slots, (slot + 1) * far // slots
        if low == 0 < high:
            for i in streams:
                for arm in range(2):
                    second(i, arm)

        def middle(step):
            for i in streams:
                for arm in range(2):
                    later(i, arm, step)

        if min(high, far - 1) > max(low, 1):
            loop(max(low, 1) + 1, min(high, far - 1) + 1, middle)
        if high == far:
            for i in streams:
                last(i)

    def pass_on(streams, slot, slots):
        def middle(step):
            for i in streams:
                for arm in range(2):
                    ag(i, arm, step - 1).wait_recv()
                    ag(i, arm, step).start()

        steps = far - 1
        low, high = slot * steps // slots, (slot + 1) * steps // slots
        if min(high, steps - 1) > low:
            loop(low + 1, min(high, steps - 1) + 1, middle)
        if low < high == steps:
            for i in streams:
                for arm in range(2):
                    ag(i, arm, steps - 1).wait_recv()
                    ag(i, arm, steps, "last").start()

    def pass_end(streams):
        for i in streams:
            for arm in range(2):
                ag(i, arm, far - 1, "last").wait_recv()

    def drain(streams):
        for i in streams:
            for arm in range(2):
                rs(i, arm, 0, True).wait_send()
                ag(i, arm, 0, "first").wait_send()
                ag(i, arm, far - 1, "last").wait_send()
            keep(i).wait()

        def one(step):
            for i in streams:
                for arm in range(2):
                    rs(i, arm, step).wait_send()

                    @pl.when(step < far - 1)
                    def _():
                        ag(i, arm, step).wait_send()

        loop(1, far, one)

    return begin, advance, pass_on, pass_end, drain


def finish_kernel(
    gate,
    narrow_low,
    narrow,
    out,
    sums_ref,
    gather_ref,
    block_far,
    input_far,
    gin_ref,
    wout_ref,
    coef_ref,
    step_ref,
    taps_ref,
    taps_bc_ref,
    bias_ref,
    bias_bc_ref,
    dt_ref,
    log_ref,
    skip_ref,
    gain_ref,
    norm_ref,
    block_out,
    input_out,
):
    inner, half = gate.shape[1], narrow_low.shape[1]
    heads, state_part = step_ref.shape[0], bias_bc_ref.shape[1]
    block_out[...] = block_far[...]
    input_out[...] = input_far[...]

    @pl.when(pl.program_id(0) == 0)
    def _():
        lanes = sums_ref[:, inner:]
        both = lanes + pltpu.roll(lanes, LANES // 2, 1)
        taps_ref[...] = sums_ref[0:KER, 0:inner]
        for ref, row in ((bias_ref, KER), (gain_ref, KER + 1), (norm_ref, KER + 3)):
            for k in range(ref.shape[0]):
                ref[k : k + 1, :] = sums_ref[row : row + 1, k * LANES : (k + 1) * LANES]
        for k in range(2):
            at = slice(k * state_part, (k + 1) * state_part)
            taps_bc_ref[:, k, :] = both[0:KER, at]
            bias_bc_ref[k : k + 1, :] = both[KER : KER + 1, at]
        dt_ref[...] = lanes[KER + 1 : KER + 2, 0:heads]
        log_ref[...] = lanes[KER + 2 : KER + 3, 0:heads]
        skip_ref[...] = head_sums(sums_ref[:, 0:inner], gather_ref[...])[KER + 2 : KER + 3, 0:heads]

    gin_ref[:, 0, :] = gate[...].astype(F32)
    gin_ref[:, 1, 0:half] = narrow_low[...].astype(F32)
    gin_ref[:, 1, half:] = narrow[:, 0 : inner - half].astype(F32)
    small = narrow[:, inner - half :].astype(F32).T
    step_ref[...] = small[0:heads]
    for k in range(2):
        low = LANES // 2 + k * state_part
        coef_ref[k] = small[low : low + state_part]
    wout_ref[...] = out[...].astype(F32)


def finish(width, inner, heads, state_part, streams, sums, gather, block_out, grad_input):
    steps = 4
    tall, low, part = width // steps, inner // steps, grad_input.shape[0] // steps
    out, gate, narrow_low, narrow = streams
    cols = grad_input.shape[1]
    mine = pl.BlockSpec((part, cols), lambda i: (i, 0))

    def block(array_in, rows):
        return pl.BlockSpec((rows, array_in.shape[1]), lambda i: (i, 0))

    def whole(shape):
        return pl.BlockSpec(shape, lambda i: (0,) * len(shape))

    little = [
        (KER, inner),
        (KER, 2, state_part),
        (inner // LANES, LANES),
        (2, state_part),
        (1, heads),
        (1, heads),
        (1, heads),
        (inner // LANES, LANES),
        (cols // LANES, LANES),
    ]
    return pl.pallas_call(
        finish_kernel,
        grid=(steps,),
        in_specs=[block(gate, tall), block(narrow_low, tall), block(narrow, tall), block(out, low)]
        + [whole(sums.shape), whole(gather.shape), mine, mine],
        out_specs=[
            pl.BlockSpec((tall, 2, inner), lambda i: (i, 0, 0)),
            pl.BlockSpec((low, width), lambda i: (i, 0)),
            pl.BlockSpec((2, state_part, tall), lambda i: (0, 0, i)),
            pl.BlockSpec((heads, tall), lambda i: (0, i)),
        ]
        + [whole(s) for s in little]
        + [mine, mine],
        out_shape=[
            jax.ShapeDtypeStruct((width, 2, inner), F32),
            jax.ShapeDtypeStruct((inner, width), F32),
            jax.ShapeDtypeStruct((2, state_part, width), F32),
            jax.ShapeDtypeStruct((heads, width), F32),
        ]
        + [jax.ShapeDtypeStruct(s, F32) for s in little]
        + [
            jax.ShapeDtypeStruct(block_out.shape, BF16),
            jax.ShapeDtypeStruct(grad_input.shape, F32),
        ],
        compiler_params=pltpu.CompilerParams(vmem_limit_bytes=VMEM_LIMIT),
        name="finish",
    )(gate, narrow_low, narrow, out, sums, gather, block_out, grad_input)


STEPS = 4


def backward_kernel(
    dims,
    dy_ref,
    xact_far,
    bc_ref,
    conv_ref,
    convbc_ref,
    dt_ref,
    cum_ref,
    states_far,
    dyy_ref,
    decay_ref,
    x_far,
    small_ref,
    chan_ref,
    vec_ref,
    pack_far,
    gather_ref,
    normed_t_far,
    ng_t_far,
    cot_far,
    dgate_far,
    small_weight_far,
    sums_ref,
    gain_ref,
    row_scale_ref,
    tokens_ref,
    weight_ref,
    wout_far,
    *rest,
):
    count, parts, seqs, block, inner, heads, state = dims
    outs, rest = rest[:4], rest[4:]
    grad_ref, total_ref, mixed_ref, *rest = rest
    bufs, rest = rest[:4], rest[4:]
    stages, rest = rest[:4], rest[4:]
    fetched, rest = rest[:7], rest[7:]
    fetch_sem, *rest = rest
    (
        dx_ref,
        gx_ref,
        gbc_ref,
        gdt_ref,
        weights,
        conv_buf,
        state_buf,
        dn_out,
        dn_in,
        wout,
        mix_in,
        token_buf,
        rowsum,
        shared,
        rs_send,
        rs_recv,
        ag_send,
        ag_recv,
        keep_sem,
        weight_sem,
        conv_sem,
        state_sem,
        x_sem,
        token_sem,
        dn_send,
        dn_recv,
        wout_sem,
        mix_send,
        mix_recv,
        row_send,
        row_recv,
        sum_send,
        sum_recv,
        *rest,
    ) = rest
    (
        dconv,
        dconvbc,
        prebc,
        dbc,
        ddt,
        local,
        arrived,
        passed,
        handed,
        incoming,
        bc_out,
        bc_in,
        edge_send,
        edge_recv,
        bc_send,
        bc_recv,
        st_send,
        st_recv,
        back_send,
        back_recv,
        over_send,
        over_recv,
    ) = rest
    sources = (
        ng_t_far,
        cot_far,
        normed_t_far,
        dgate_far,
        xact_far,
        small_weight_far,
        pack_far,
    )
    fetches = [
        pltpu.make_async_copy(src, dst, fetch_sem.at[k])
        for k, (src, dst) in enumerate(zip(sources, fetched))
    ]
    for copy in fetches:
        copy.start()
    (
        ng_t_ref,
        cot_ref,
        normed_t_ref,
        dgate_ref,
        xact_ref,
        small_weight_ref,
        pack_ref,
    ) = fetched
    place, head = lax.axis_index("seq"), lax.axis_index("head")
    chunks = block // CHUNK
    pairs = heads // 2
    total = seqs * chunks
    rows_all = seqs * block
    width = cot_ref.shape[1]
    cols = width // parts
    plan = (
        (ng_t_ref, cot_ref, 0, width, width // 2),
        (normed_t_ref, dgate_ref, 0, inner, inner // 2),
        (normed_t_ref, dx_ref, 0, inner // 2, LANES),
        (normed_t_ref, dx_ref, inner // 2, inner // 2 + LANES, 2 * LANES),
    )
    begin, advance, pass_on, pass_end, drain = ring_steps(
        count, plan, outs, bufs, stages, (rs_send, rs_recv, ag_send, ag_recv, keep_sem)
    )
    out, gate, late = (0,), (1,), (2, 3)
    meet(count, parts)
    gdt_ref[...] = jnp.zeros_like(gdt_ref)

    token_copy = pltpu.make_async_copy(
        tokens_ref.at[:, pl.ds(pl.multiple_of(head * cols, cols), cols)], token_buf, token_sem
    )
    token_copy.start()

    def weight_copy(i):
        other = lax.rem(head + i, parts)
        return pltpu.make_async_copy(
            weight_ref.at[:, pl.ds(pl.multiple_of(other * cols, cols), cols)],
            weights.at[lax.rem(i + 1, 2)],
            weight_sem.at[lax.rem(i + 1, 2)],
        )

    def conv_copy(q):
        t = q // chunks * chunks + chunks - 1 - lax.rem(q, chunks)
        slot = lax.rem(q, 2)
        return pltpu.make_async_copy(
            conv_ref.at[ds(t * CHUNK, CHUNK)], conv_buf.at[slot], conv_sem.at[slot]
        )

    def state_copy(q):
        t = q // chunks * chunks + chunks - 1 - lax.rem(q, chunks)
        slot = lax.rem(q, 2)
        return pltpu.make_async_copy(states_far.at[t], state_buf.at[slot], state_sem.at[slot])

    conv_copy(0).start()
    state_copy(0).start()
    weight_copy(1).start()

    tall = 2 * CHUNK

    def wout_copy(i):
        other = lax.rem(head + i, parts)
        return pltpu.make_async_copy(
            wout_far.at[:, pl.ds(pl.multiple_of(other * cols, cols), cols)],
            wout.at[i % 2],
            wout_sem.at[i % 2],
        )

    def mix_copy(i):
        other = lax.rem(head + i, parts)
        return remote(
            dn_out.at[other], mix_in.at[i - 1], mix_send.at[i], mix_recv.at[i], place, other
        )

    def mix(i):
        other = lax.rem(head + i, parts)
        if i < parts:
            wout_copy(i + 1).start()
        wout_copy(i).wait()

        def some(r):
            rows = ds(r * tall, tall)
            dn_out[other, rows, :] = mul(ng_t_ref[0:inner, rows], wout[i % 2], TN).astype(BF16)

        loop(0, rows_all // tall, some)
        if i < parts:
            mix_copy(i).start()

    wout_copy(1).start()

    for s in range(seqs):

        def alone(i, held):
            t = s * chunks + chunks - 1 - i
            rows = ds(t * CHUNK, CHUNK)
            grown = jnp.exp(cum_ref[rows, :])
            weighted = jnp.concatenate(
                [
                    (
                        dy_ref[rows, p * LANES : (p + 1) * LANES].astype(F32) * pair_of(grown, p)
                    ).astype(BF16)
                    for p in range(pairs)
                ],
                axis=1,
            )
            new = mul(bc_ref[rows, state:], weighted, TN)
            return spread(grown[CHUNK - 1 :, :], pairs) * held + new

        held = lax.fori_loop(0, chunks, alone, jnp.zeros((state, inner), F32))
        local[s] = held.astype(BF16)
        if s == 0:
            for copy in fetches[:4]:
                copy.wait()
            for i in out + gate:
                begin(i)

    start, carry, finish = carry_exchange(
        dims,
        local,
        arrived,
        passed,
        handed,
        incoming,
        decay_ref,
        (st_send, st_recv, back_send, back_recv, over_send, over_recv),
        True,
    )
    leads = place >= count // 2
    start()
    advance(out, 0, STEPS)

    @pl.when(leads)
    def _():
        carry()

    mix(1)
    advance(gate, 0, STEPS)
    mix(2)
    advance(out, 1, STEPS)
    advance(gate, 1, STEPS)

    @pl.when(~leads)
    def _():
        carry()

    mix(3)
    advance(out, 2, STEPS)
    for i in range(4, parts + 1):
        mix(i)
    for copy in fetches[4:]:
        copy.wait()
    finish()

    side = iota((CHUNK, LANES), 1) < LANES // 2
    seen = iota((CHUNK, CHUNK), 0) <= iota((CHUNK, CHUNK), 1)
    upper = seen.astype(F32)
    for s in range(seqs):

        def chunk(i, held):
            t = s * chunks + chunks - 1 - i
            rows = ds(t * CHUNK, CHUNK)
            out_rows = ds((s * chunks + chunks - 1 - i) * CHUNK, CHUNK)
            turn = s * chunks + i
            conv_copy(turn).wait()
            state_copy(turn).wait()

            @pl.when(turn + 1 < total)
            def _():
                conv_copy(turn + 1).start()
                state_copy(turn + 1).start()

            cum, dt = cum_ref[rows, :], dt_ref[rows, :]
            cum_t = cum.T
            grown = jnp.exp(cum)
            end = cum[CHUNK - 1 :, :]
            tail = jnp.exp(end - cum)
            b_rows, c_rows = bc_ref[rows, 0:state], bc_ref[rows, state:]
            scores = mul(b_rows, c_rows, NT)
            low = held.astype(BF16)
            begun = state_buf[lax.rem(turn, 2)]
            begun_high, begun_low = halves_of(begun)
            pulled = mul(b_rows, low, NN)
            grad_scores = jnp.zeros((CHUNK, CHUNK), F32)
            d_x_sum = jnp.zeros((CHUNK, LANES), F32)
            d_fall = jnp.zeros((CHUNK, LANES), F32)
            into_x = []
            into_y = []
            last = []
            for p in range(pairs):
                lane = slice(p * LANES, (p + 1) * LANES)
                x, dy = xact_ref[rows, lane], dy_ref[rows, lane]
                xf, dyf = x.astype(F32), dy.astype(F32)
                dt_p, tail_p = pair_of(dt, p), pair_of(tail, p)
                stepped = xf * dt_p
                low_step = stepped.astype(BF16)
                halves = []
                for k, h in enumerate((2 * p, 2 * p + 1)):
                    gap = cum_t[h : h + 1, :] - cum[:, h : h + 1]
                    fade = jnp.exp(jnp.where(seen, gap, -1e30))
                    own = jnp.where(side if k == 0 else ~side, low_step, jnp.zeros_like(low_step))
                    grad_scores = grad_scores + mul(own, dy, NT) * fade
                    halves.append(mul((scores * fade).astype(BF16), dy, NN))
                from_state = pulled[:, lane] * tail_p
                d_step_x = jnp.where(side, halves[0], halves[1]) + from_state
                rounded = low_step.astype(F32)
                d_x_sum = d_x_sum + head_sums(xf * d_step_x, gather_ref[lane, :])
                d_fall = d_fall + head_sums(rounded * d_step_x, gather_ref[lane, :])
                into_x.append(halves_of(stepped * tail_p))
                into_y.append(halves_of(dyf * pair_of(grown, p)))
                last.append(jnp.sum(rounded * from_state, axis=0, keepdims=True))
                conv = conv_buf[lax.rem(turn, 2), :, lane]
                sg = sigmoid(conv)
                d_act = dt_p * d_step_x + chan_ref[6:7, lane] * dyf
                dconv[s, ds((chunks - 1 - i) * CHUNK, CHUNK), lane] = d_act * (
                    sg * (1.0 + conv * (1.0 - sg))
                )
            low_scores = grad_scores.astype(BF16)
            x_high, x_low = (jnp.concatenate([v[k] for v in into_x], axis=1) for k in range(2))
            y_high, y_low = (jnp.concatenate([v[k] for v in into_y], axis=1) for k in range(2))
            d_b = mul(low_scores, c_rows, NN) + mul(x_high, low, NT) + mul(x_low, low, NT)
            d_c = mul(low_scores, b_rows, TN) + mul(y_high, begun_high, NT)
            d_c = d_c + mul(y_high, begun_low, NT) + mul(y_low, begun_high, NT)
            dbc[out_rows, 0:state] = d_b.astype(BF16)
            dbc[out_rows, state:] = d_c.astype(BF16)
            fall = spread(grown[CHUNK - 1 :, :], pairs)
            ends = jnp.concatenate(last, axis=1) + fall * jnp.sum(
                held * begun, axis=0, keepdims=True
            )
            ends = head_sums(jnp.broadcast_to(ends, (8, inner)), gather_ref[...])[0:1, :]
            d_log = mul(upper, dyy_ref[rows, :] - d_fall, NN, EXACT) + ends
            d_step = d_x_sum + vec_ref[6:7, :] * d_log
            d_dt = d_step * sigmoid(small_ref[rows, :] + vec_ref[5:6, :])
            gdt_ref[0:8, :] += eights(d_dt)
            gdt_ref[8:16, :] += eights(d_log * (dt * vec_ref[6:7, :]))
            ddt[out_rows, :] = d_dt


            @pl.when(turn == total * 3 // 8)
            def _():
                advance(gate, 2, STEPS)

            @pl.when(turn == total * 6 // 8)
            def _():
                advance(out, 3, STEPS)

            return fall * held + mul(c_rows, y_high, TN)

        lax.fori_loop(0, chunks, chunk, incoming[s].astype(F32))

    def pack(k):
        piece = mul(dbc[0:block, :], pack_ref[k, 0], NN)
        return (piece + mul(dbc[block:, :], pack_ref[k, 1], NN)).astype(BF16)

    def pack_one(k):
        bc_out[k] = pack(k)

    def x_copy(t):
        slot = lax.rem(t, 2)
        return pltpu.make_async_copy(
            x_far.at[ds(t * CHUNK, CHUNK)], conv_buf.at[slot], x_sem.at[slot]
        )

    x_copy(0).start()
    advance(gate, 3, STEPS)
    loop(0, parts, pack_one)
    share = head_copy(parts, lambda k: bc_out.at[k], lambda k: bc_in.at[k], bc_send, bc_recv)
    loop(1, parts, lambda i: share(i).start())

    before = lax.rem(place + count - 1, count)

    def edge_copy(s):
        return remote(
            dconv.at[s, pl.ds(0, 8)],
            dconv.at[s, pl.ds(block, 8)],
            edge_send.at[s],
            edge_recv.at[s],
            before,
            head,
        )

    def edge_bc():
        return remote(
            dconvbc.at[pl.ds(0, 8)],
            dconvbc.at[pl.ds(block, 8)],
            edge_send.at[seqs],
            edge_recv.at[seqs],
            before,
            head,
        )

    @pl.when(place > 0)
    def _():
        for s in range(seqs):
            edge_copy(s).start()

    pass_on(out, 0, 3)
    loop(1, parts, lambda i: share(i).wait())
    bc_in[head] = bc_out[head]
    d_act = bc_in[0].astype(F32)
    for k in range(1, parts):
        d_act = d_act + bc_in[k].astype(F32)
    conv = convbc_ref[...]
    sg = sigmoid(conv)
    dconvbc[0:block, :] = d_act * (sg * (1.0 + conv * (1.0 - sg)))

    @pl.when(place > 0)
    def _():
        edge_bc().start()

    @pl.when(place < count - 1)
    def _():
        for s in range(seqs):
            edge_copy(s).wait_recv()

    @pl.when(place == count - 1)
    def _():
        for s in range(seqs):
            dconv[s, block : block + 8, :] = jnp.zeros((8, inner), F32)

    gx_ref[...] = jnp.zeros_like(gx_ref)

    def x_chunk(t):
        rows = ds(t * CHUNK, CHUNK)
        s, c = t // chunks, lax.rem(t, chunks)
        x_copy(t).wait()

        @pl.when(t + 1 < total)
        def _():
            x_copy(t + 1).start()

        for p in range(pairs):
            lane = slice(p * LANES, (p + 1) * LANES)
            x = conv_buf[lax.rem(t, 2), :, lane]
            pre = jnp.zeros((CHUNK, LANES), F32)
            here = dconv[s, pl.ds(pl.multiple_of(c * CHUNK, CHUNK), CHUNK + 8), lane]
            for k in range(KER):
                off = KER - 1 - k
                d = pltpu.roll(here, CHUNK + 8 - off, 0)[:CHUNK] if off else here[:CHUNK]
                pre = pre + chan_ref[k : k + 1, lane] * d
                gx_ref[8 * k : 8 * k + 8, lane] += eights(x * d)
                if k == KER - 1:
                    gx_ref[8 * KER : 8 * KER + 8, lane] += eights(d)
            dx_ref[rows, lane] = pre.astype(BF16)

        @pl.when(t == total // 2)
        def _():
            pass_on(gate, 0, 3)

    loop(0, total, x_chunk)

    @pl.when(place < count - 1)
    def _():
        edge_bc().wait_recv()

    @pl.when(place == count - 1)
    def _():
        dconvbc[block : block + 8, :] = jnp.zeros((8, LANES), F32)

    low, high = small_ref[0:block, :], small_ref[block:, :]
    prebc[...] = jnp.where(
        iota(low.shape, 1) < LANES // 2, pltpu.roll(low, LANES // 2, 1), high
    )
    pre = jnp.zeros((block, LANES), F32)
    for k in range(KER):
        d = dconvbc[pl.ds(KER - 1 - k, block), :]
        pre = pre + vec_ref[k : k + 1, :] * d
        gbc_ref[8 * k : 8 * k + 8, :] = eights(prebc[...] * d)
    gbc_ref[8 * KER : 8 * KER + 8, :] = eights(dconvbc[0:block, :])
    at = iota((block, LANES), 1)
    for s in range(seqs):
        rows = slice(s * block, (s + 1) * block)
        mine = pre if s == seqs - 1 else pltpu.roll(pre, LANES // 2, 1)
        step = jnp.where(at < heads, ddt[rows, :], 0.0)
        dx_ref[rows, inner:] = jnp.where(at < LANES // 2, step, mine).astype(BF16)

    for i in late:
        begin(i)

    loop(1, parts, lambda i: mix_copy(i).wait())
    token_copy.wait()

    def add_up(t):
        rows = ds(t * CHUNK, CHUNK)
        d = dn_out[head, rows, :].astype(F32)
        for k in range(parts - 1):
            d = d + mix_in[k, rows, :].astype(F32)
        mixed_ref[rows, :] = (token_buf[rows, :].astype(F32) + d).astype(BF16)

    loop(0, total, add_up)


    def dn_copy(i):
        other = lax.rem(head + i, parts)
        return remote(
            dn_out.at[other], dn_in.at[i - 1], dn_send.at[i], dn_recv.at[i], place, other
        )

    def d_normed(i):
        other = lax.rem(head + i, parts)
        slot = (i + 1) % 2
        if i < parts:
            weight_copy(i + 1).start()

        weight_copy(i).wait()
        mine = small_weight_ref[:, pl.ds(pl.multiple_of(other * cols, cols), cols)]

        def some(r):
            rows = ds(r * tall, tall)
            part = mul(dgate_ref[rows, :], weights[slot, 0], NT)
            part = part + mul(dx_ref[rows, 0:inner], weights[slot, 1], NT)
            part = part + mul(dx_ref[rows, inner:], mine, NN)
            dn_out[other, rows, :] = part.astype(BF16)

        loop(0, rows_all // tall, some)

        if i < parts:
            dn_copy(i).start()

    between = ((out, 1), (), (out, 2), ())
    for k in range(STEPS):
        if k < parts:
            d_normed(k + 1)
        advance(late, k, STEPS)
        if between[k]:
            pass_on(*between[k], 3)
    for k in range(STEPS, parts):
        d_normed(k + 1)

    loop(1, parts, lambda i: dn_copy(i).wait())
    my_cols = pl.ds(pl.multiple_of(head * cols, cols), cols)

    def own(t, grads):
        rows = ds(t * CHUNK, CHUNK)
        d = dn_out[head, rows, :].astype(F32)
        for k in range(parts - 1):
            d = d + dn_in[k, rows, :].astype(F32)
        token = token_buf[rows, :].astype(F32)
        grads = grads + eights(d * (token * row_scale_ref[rows, :]))
        d = d * gain_ref[:, my_cols]
        grad_ref[rows, :] = d
        line = jnp.sum(d * token, axis=1, keepdims=True)
        line = jnp.where(iota((CHUNK, LANES), 1) == 0, line, 0.0)
        rowsum[head, t] = line.T[0:8, :]
        return grads

    norm_grads = lax.fori_loop(0, total, own, jnp.zeros((8, cols), F32))
    rows_copy = head_copy(
        parts, lambda _: rowsum.at[head], lambda k: rowsum.at[k], row_send, row_recv
    )
    loop(1, parts, lambda i: rows_copy(i).start())

    def summed(ref, k):
        return jnp.sum(ref[8 * k : 8 * k + 8, :], axis=0, keepdims=True)

    shared[place] = jnp.zeros(shared.shape[1:], F32)
    for k in range(KER + 1):
        shared[place, k : k + 1, 0:inner] = summed(gx_ref, k)
        shared[place, k : k + 1, inner:] = summed(gbc_ref, k)
    for k in range(2):
        shared[place, KER + 1 + k : KER + 2 + k, 0:inner] = summed(sums_ref, k)
        shared[place, KER + 1 + k : KER + 2 + k, inner:] = summed(gdt_ref, k)
    shared[place, 7:8, 0:cols] = jnp.sum(norm_grads, axis=0, keepdims=True)
    sums_copy = line_copy(
        count, lambda _: shared.at[place], lambda k: shared.at[k], sum_send, sum_recv
    )
    loop(1, count, lambda i: sums_copy(i).start())
    pass_on(late, 0, 3)
    pass_on(gate, 1, 3)
    loop(1, parts, lambda i: rows_copy(i).wait())

    def finish_rows(t):
        rows = ds(t * CHUNK, CHUNK)
        sums = rowsum[0, t]
        for k in range(1, parts):
            sums = sums + rowsum[k, t]
        turned = jnp.concatenate([sums, jnp.zeros((CHUNK - 8, LANES), F32)], axis=0).T
        scale = row_scale_ref[rows, :]
        pull = scale * scale * scale * (turned[:, 0:1] / width)
        grad_ref[rows, :] = (
            scale * grad_ref[rows, :]
            - token_buf[rows, :].astype(F32) * pull
            + cot_ref[rows, my_cols].astype(F32)
        )

    loop(0, total, finish_rows)
    pass_on(late, 1, 3)
    pass_on(gate, 2, 3)
    loop(1, count, lambda i: sums_copy(i).wait())
    everything = shared[0]
    for k in range(1, count):
        everything = everything + shared[k]
    total_ref[...] = everything
    pass_on(late, 2, 3)
    pass_end(out + gate + late)
    drain(out + gate + late)

    @pl.when(place > 0)
    def _():
        for s in range(seqs):
            edge_copy(s).wait_send()
        edge_bc().wait_send()


def backward(dims, *operands):
    count, parts, seqs, block, inner, heads, state = dims
    rows = seqs * block
    chunks = rows // CHUNK
    group, cut_rows = cut_of(count, seqs, state)
    normed_rows, ng_rows, width = (operands[k].shape[d] for k, d in ((16, 0), (17, 0), (18, 1)))
    cols = width // parts
    distant = (1, 3, 7, 10, 14, 16, 17, 18, 19, 20, 24, 25, 26)
    fetched = [operands[k] for k in (17, 18, 16, 19, 1, 20, 14)]
    spec = pl.BlockSpec(memory_space=pltpu.VMEM)
    far = pl.BlockSpec(memory_space=pl.ANY)
    line, ring = pltpu.SemaphoreType.DMA((count,)), pltpu.SemaphoreType.DMA((parts,))
    edge = pltpu.SemaphoreType.DMA((seqs + 1,))
    streams = [
        (ng_rows, width),
        (normed_rows, inner),
        (normed_rows, inner // 2),
        (normed_rows, inner // 2 + LANES),
    ]
    steps = pltpu.SemaphoreType.DMA((len(streams), 2, count // 2))
    outs = [(shape, BF16) for shape in streams]
    outs = outs + [((rows, cols), F32), ((8, inner + LANES), F32), ((rows, cols), BF16)]
    return pl.pallas_call(
        functools.partial(backward_kernel, dims),
        out_shape=[jax.ShapeDtypeStruct(*o) for o in outs],
        in_specs=[far if k in distant else spec for k in range(len(operands))],
        out_specs=[far] * len(streams) + [spec] * 3,
        scratch_shapes=[vmem((2, count // 2, r // count, c), BF16) for r, c in streams]
        + [vmem((r // count, c), BF16) for r, c in streams]
        + [vmem(a.shape, a.dtype) for a in fetched]
        + [
            pltpu.SemaphoreType.DMA((len(fetched),)),
            vmem((rows, inner + LANES), BF16),
            vmem((8 * (KER + 1), inner), F32),
            vmem((8 * (KER + 1), LANES), F32),
            vmem((16, LANES), F32),
            vmem((2, 2, cols, inner), BF16),
            vmem((2, CHUNK, inner), F32),
            vmem((2, state, inner), F32),
            vmem((parts, rows, cols), BF16),
            vmem((parts - 1, rows, cols), BF16),
            vmem((2, inner, cols), BF16),
            vmem((parts - 1, rows, cols), BF16),
            vmem((rows, cols), BF16),
            vmem((parts, chunks, 8, LANES), F32),
            vmem((count, 8, inner + LANES), F32),
            steps,
            steps,
            steps,
            steps,
            pltpu.SemaphoreType.DMA((len(streams),)),
            pltpu.SemaphoreType.DMA((2,)),
            pltpu.SemaphoreType.DMA((2,)),
            pltpu.SemaphoreType.DMA((2,)),
            pltpu.SemaphoreType.DMA((2,)),
            pltpu.SemaphoreType.DMA,
            ring,
            ring,
            pltpu.SemaphoreType.DMA((2,)),
            ring,
            ring,
            ring,
            ring,
            line,
            line,
            vmem((seqs, block + 8, inner), F32),
            vmem((block + 8, LANES), F32),
            vmem((block, LANES), F32),
            vmem((rows, 2 * state), BF16),
            vmem((rows, LANES), F32),
            vmem((seqs, state, inner), BF16),
            vmem((group, cut_rows, inner), BF16),
            vmem((group, cut_rows, inner), BF16),
            vmem((2, cut_rows, inner), BF16),
            vmem((seqs, state, inner), BF16),
            vmem((parts, block, LANES), BF16),
            vmem((parts, block, LANES), BF16),
            edge,
            edge,
            ring,
            ring,
            line,
            line,
            line,
            line,
            pltpu.SemaphoreType.DMA,
            pltpu.SemaphoreType.DMA,
        ],
        compiler_params=pltpu.CompilerParams(
            collective_id=3, has_side_effects=True, vmem_limit_bytes=VMEM_LIMIT
        ),
        name="mixer_backward",
    )(*operands)


def body(
    tokens,
    norm_gain,
    gate_input_weight,
    coefficient_weight,
    step_weight,
    conv_x,
    conv_bc,
    conv_bias_x,
    conv_bias_bc,
    dt_bias,
    a_log,
    d_skip,
    gate_gain,
    output_weight,
    cotangent,
):
    seqs, block, width = tokens.shape
    inner = gate_input_weight.shape[2]
    state_part = coefficient_weight.shape[2]
    heads = step_weight.shape[1]
    count, parts = lax.axis_size("seq"), lax.axis_size("head")
    state = state_part * parts
    rows = seqs * block
    col_count = width // parts
    half = LANES // 2
    dims = (count, parts, seqs, block, inner, heads, state)

    flat_tokens = tokens.reshape(rows, width)
    both_weights = gate_input_weight.transpose(1, 0, 2)
    x_pre, small, normed_t, row_scale, small_weight, chan, vec, gain = project(
        flat_tokens,
        norm_gain.reshape(-1, LANES),
        both_weights,
        step_weight.T,
        coefficient_weight.transpose(1, 2, 0),
        conv_x,
        conv_bc,
        conv_bias_x.reshape(-1, LANES),
        conv_bias_bc,
        dt_bias.reshape(1, heads),
        a_log.reshape(1, heads),
        d_skip.reshape(1, heads),
        gate_gain.reshape(-1, LANES),
    )
    device, lane, channel = np.meshgrid(
        np.arange(parts), np.arange(LANES), np.arange(2 * state), indexing="ij"
    )
    is_c, at = channel // state, channel % state
    unpack = np.stack(
        [
            (lane == s * half + is_c * state_part + at - device * state_part)
            & (at // state_part == device)
            for s in range(seqs)
        ]
    ).astype(np.float32)
    pack = jnp.asarray(unpack.transpose(1, 0, 3, 2), BF16)
    unpack = jnp.asarray(unpack.reshape(seqs, parts * LANES, 2 * state), BF16)
    expand = np.arange(LANES)[:, None] == np.arange(inner)[None, :] // (inner // heads)
    gather = jnp.asarray(expand.T.astype(np.float32), BF16)
    expand = jnp.asarray(expand.astype(np.float32))
    cot = cotangent.reshape(rows, width)

    xact, bc, conv, convbc, dt, cum, states, ng_t, dgate, dy, dyy, decay, sums = forward(
        dims,
        x_pre,
        normed_t,
        both_weights,
        small,
        chan,
        vec,
        unpack,
        expand,
        gather,
        cot,
        output_weight,
    )
    def padded(array_in):
        return jnp.pad(array_in, ((0, -array_in.shape[0] % (count * 16)), (0, 0)))

    *streams, grad_input, sums, block_out = backward(
        dims,
        dy,
        xact,
        bc,
        conv,
        convbc,
        dt,
        cum,
        states,
        dyy,
        decay,
        x_pre,
        small,
        chan,
        vec,
        pack,
        gather,
        padded(normed_t),
        padded(ng_t),
        cot,
        dgate,
        small_weight,
        sums,
        gain,
        row_scale,
        flat_tokens,
        both_weights,
        output_weight,
    )
    (
        g_in,
        g_w_out,
        g_coef,
        g_step,
        taps,
        taps_bc,
        bias,
        bias_bc,
        g_dt,
        g_log,
        g_skip,
        g_gain,
        g_norm,
        block_out,
        grad_input,
    ) = finish(
        width, inner, heads, state_part, streams, sums, gather, block_out, grad_input
    )
    return (
        block_out.reshape(seqs, block, col_count),
        grad_input.reshape(seqs, block, col_count),
        g_norm.reshape(-1),
        g_in,
        g_coef.transpose(2, 0, 1),
        g_step.T,
        taps,
        taps_bc,
        bias.reshape(-1),
        bias_bc,
        g_dt.reshape(-1),
        g_log.reshape(-1),
        g_skip.reshape(-1),
        g_gain.reshape(-1),
        g_w_out,
    )


def solution(mesh):
    placed = (
        P(None, "seq", None),
        P(),
        P(None, None, "head"),
        P(None, None, "head"),
        P(None, "head"),
        P(None, "head"),
        P(None, None, "head"),
        P("head"),
        P(None, "head"),
        P("head"),
        P("head"),
        P("head"),
        P("head"),
        P("head", None),
        P(None, "seq", None),
    )
    return jax.shard_map(
        body,
        mesh=mesh,
        in_specs=placed,
        out_specs=(
            P(None, "seq", "head"),
            P(None, "seq", "head"),
            P("head"),
            P(None, None, "head"),
            P(None, None, "head"),
            P(None, "head"),
            P(None, "head"),
            P(None, None, "head"),
            P("head"),
            P(None, "head"),
            P("head"),
            P("head"),
            P("head"),
            P("head"),
            P("head", None),
        ),
        check_vma=False,
    )
```

```python
import functools

import jax
import jax.numpy as jnp
import numpy as np
from jax import lax
from jax.experimental import pallas as pl
from jax.experimental.pallas import tpu as pltpu
from jax.sharding import PartitionSpec as P

KER = 4
EPSILON = 1e-05
CHUNK = 128
LANES = 128
MESH = pl.DeviceIdType.MESH
F32 = jnp.float32
BF16 = jnp.bfloat16
EXACT = lax.Precision.HIGHEST
VMEM_LIMIT = 61 * 2**20
NN = ((1,), (0,))
NT = ((1,), (1,))
TN = ((0,), (0,))


def mul(left, right, how, precision=None):
    return lax.dot_general(
        left, right, (how, ((), ())), precision=precision, preferred_element_type=F32
    )


def sigmoid(v):
    return 0.5 * jnp.tanh(0.5 * v) + 0.5


def softplus(v):
    e = jnp.exp(-jnp.abs(v))
    u = 1.0 + e
    near = u - 1.0
    log1p = jnp.where(near == 0.0, e, jnp.log(u) * (e / jnp.where(near == 0.0, 1.0, near)))
    return jnp.maximum(v, 0.0) + log1p


def iota(shape, dim):
    return lax.broadcasted_iota(jnp.int32, shape, dim)


def ds(start, size):
    return pl.ds(pl.multiple_of(start, size), size)


def pair_of(values, pair):
    low = values[:, 2 * pair : 2 * pair + 1]
    high = values[:, 2 * pair + 1 : 2 * pair + 2]
    return jnp.where(iota((values.shape[0], LANES), 1) < LANES // 2, low, high)


def spread(values, pairs):
    return jnp.concatenate([pair_of(values, p) for p in range(pairs)], axis=1)


def eights(v):
    return jnp.sum(v.reshape(v.shape[0] // 8, 8, v.shape[1]), axis=0)


def halves_of(v):
    high = v.astype(BF16)
    return high, (v - high.astype(F32)).astype(BF16)


def head_sums(v, gather):
    high, low = halves_of(v)
    return mul(high, gather, NN) + mul(low, gather, NN)


def remote(src, dst, send, recv, place, head):
    return pltpu.make_async_remote_copy(
        src_ref=src,
        dst_ref=dst,
        send_sem=send,
        recv_sem=recv,
        device_id=(place, head),
        device_id_type=MESH,
    )


def meet(count, parts):
    place, head = lax.axis_index("seq"), lax.axis_index("head")
    barrier = pltpu.get_barrier_semaphore()

    def along_seq(i, _):
        other = lax.rem(place + i, count)
        pl.semaphore_signal(barrier, inc=1, device_id=(other, head), device_id_type=MESH)
        return 0

    def along_head(i, _):
        other = lax.rem(head + i, parts)
        pl.semaphore_signal(barrier, inc=1, device_id=(place, other), device_id_type=MESH)
        return 0

    lax.fori_loop(1, count, along_seq, 0)
    lax.fori_loop(1, parts, along_head, 0)
    pl.semaphore_wait(barrier, count - 1 + parts - 1)


def loop(low, high, step):
    def one(i, _):
        step(i)
        return 0

    lax.fori_loop(low, high, one, 0)


def line_copy(count, src, dst, send, recv):
    place, head = lax.axis_index("seq"), lax.axis_index("head")

    def copy(i):
        other = lax.rem(place + i, count)
        return remote(src(other), dst(place), send.at[i], recv.at[i], other, head)

    return copy


def head_copy(parts, src, dst, send, recv):
    place, head = lax.axis_index("seq"), lax.axis_index("head")

    def copy(i):
        other = lax.rem(head + i, parts)
        return remote(src(other), dst(head), send.at[i], recv.at[i], place, other)

    return copy


def cut_of(count, seqs, state):
    group = count // 2
    return group, seqs * state // group


def carry_exchange(dims, local, arrived, passed, total, incoming, decay_ref, sems, reverse):
    count, _, seqs, _, inner, _, state = dims
    place, head = lax.axis_index("seq"), lax.axis_index("head")
    send, recv, back_send, back_recv, over_send, over_recv = sems
    group, rows = cut_of(count, seqs, state)
    base, me = place // group * group, lax.rem(place, group)
    leads = place >= group if reverse else place < group
    each = group // seqs

    def at(ref, k):
        return ref.at[k // each, ds(lax.rem(k, each) * rows, rows)]

    def out(i):
        other = lax.rem(me + i, group)
        return remote(at(local, other), arrived.at[me], send.at[i], recv.at[i], base + other, head)

    def back(j):
        i = lax.rem(j - me + group, group)
        return remote(
            passed.at[j], at(incoming, me), back_send.at[i], back_recv.at[i], base + j, head
        )

    def over():
        other = lax.rem(place + group, count)
        return remote(total.at[0], total.at[1], over_send, over_recv, other, head)

    def start():
        loop(1, group, lambda i: out(i).start())
        arrived[me] = local[me // each, ds(lax.rem(me, each) * rows, rows)]

    def carry():
        @pl.when(leads)
        def _():
            total[1] = jnp.zeros((rows, inner), total.dtype)

        @pl.when(~leads)
        def _():
            over().wait_recv()

        held = total[1].astype(F32)
        seq = me // each
        for step in range(group):
            j = group - 1 - step if reverse else step

            @pl.when(j != me)
            def _():
                out(lax.rem(me - j + group, group)).wait_recv()

            passed[j] = held.astype(passed.dtype)

            @pl.when(j != me)
            def _():
                back(j).start()

            @pl.when(j == me)
            def _():
                incoming[seq, ds(lax.rem(me, each) * rows, rows)] = passed[j]

            held = decay_ref[seq, pl.ds(base + j, 1), :] * held + arrived[j].astype(F32)

        @pl.when(leads)
        def _():
            total[0] = held.astype(total.dtype)
            over().start()

    def finish():
        def one(i):
            out(i).wait_send()
            back(lax.rem(me + i, group)).wait()

        loop(1, group, one)

        @pl.when(leads)
        def _():
            over().wait_send()

    return start, carry, finish


def forward_kernel(
    dims,
    x_ref,
    normed_t_far,
    weight_far,
    small_ref,
    chan_ref,
    vec_ref,
    unpack_ref,
    expand_ref,
    gather_ref,
    cot_far,
    wout_far,
    xact_far,
    bc_far,
    conv_far,
    convbc_ref,
    dt_far,
    cum_far,
    states_far,
    ng_t_far,
    dgate_far,
    dy_far,
    dyy_far,
    decay_ref,
    sums_ref,
    normed_t_ref,
    weight_ref,
    cot_ref,
    wout_ref,
    gate_ref,
    xact_ref,
    bc_ref,
    conv_ref,
    dt_ref,
    cum_ref,
    states_ref,
    ng_t_ref,
    dgate_ref,
    dy_ref,
    dyy_ref,
    fetch_sem,
    keep_sem,
    edge_x,
    edge_s,
    ext,
    extbc,
    bc_all,
    fresh,
    y_ref,
    dng_ref,
    gated_ref,
    decays,
    local,
    arrived,
    passed,
    handed,
    incoming,
    rowsum,
    edge_send,
    edge_recv,
    dec_send,
    dec_recv,
    bc_send,
    bc_recv,
    st_send,
    st_recv,
    back_send,
    back_recv,
    over_send,
    over_recv,
    row_send,
    row_recv,
):
    count, parts, seqs, block, inner, heads, state = dims
    place, head = lax.axis_index("seq"), lax.axis_index("head")
    chunks = block // CHUNK
    pairs = heads // 2
    total = seqs * chunks
    fetches = [
        pltpu.make_async_copy(src, dst, fetch_sem.at[k])
        for k, (src, dst) in enumerate(
            (
                (cot_far, cot_ref),
                (wout_far, wout_ref),
                (normed_t_far, normed_t_ref),
                (weight_far.at[0], weight_ref),
            )
        )
    ]
    for copy in fetches:
        copy.start()
    keeps = [
        pltpu.make_async_copy(src, dst, keep_sem.at[k])
        for k, (src, dst) in enumerate(
            (
                (xact_ref, xact_far),
                (bc_ref, bc_far),
                (conv_ref, conv_far),
                (dt_ref, dt_far),
                (cum_ref, cum_far),
                (states_ref, states_far),
                (ng_t_ref, ng_t_far),
                (dgate_ref, dgate_far),
                (dy_ref, dy_far),
                (dyy_ref, dyy_far),
            )
        )
    ]
    meet(count, parts)

    def edge_copies(ahead):
        copies = []
        for s in range(seqs):
            rows = pl.ds(s * block + block - 8, 8)
            for k, (src, dst) in enumerate(((x_ref, edge_x), (small_ref, edge_s))):
                copies.append(
                    remote(
                        src.at[rows], dst.at[s], edge_send.at[k, s], edge_recv.at[k, s], ahead, head
                    )
                )
        return copies

    after = lax.rem(place + 1, count)

    @pl.when(place < count - 1)
    def _():
        for c in edge_copies(after):
            c.start()

    lower = (iota((CHUNK, CHUNK), 0) >= iota((CHUNK, CHUNK), 1)).astype(F32)
    for s in range(seqs):

        def steps(c, logs):
            rows = ds((s * chunks + c) * CHUNK, CHUNK)
            dt = softplus(small_ref[rows, :] + vec_ref[5:6, :])
            cum = mul(lower, dt * vec_ref[6:7, :], NN, EXACT)
            dt_ref[rows, :] = dt
            cum_ref[rows, :] = cum
            return logs + cum[CHUNK - 1 :, :]

        logs = lax.fori_loop(0, chunks, steps, jnp.zeros((1, LANES), F32))
        decays[place, s : s + 1, :] = jnp.exp(logs)

    dec = line_copy(count, lambda _: decays.at[place], lambda k: decays.at[k], dec_send, dec_recv)
    loop(1, count, lambda i: dec(i).start())

    @pl.when(place > 0)
    def _():
        for c in edge_copies(after):
            c.wait_recv()

    @pl.when(place == 0)
    def _():
        edge_x[...] = jnp.zeros_like(edge_x)
        edge_s[...] = jnp.zeros_like(edge_s)

    def packed(low, high):
        return jnp.where(
            iota(low.shape, 1) < LANES // 2, pltpu.roll(low, LANES // 2, 1), high
        )

    extbc[0:8, :] = packed(edge_s[0], edge_s[1])
    extbc[8:, :] = packed(small_ref[0:block, :], small_ref[block:, :])
    conv = vec_ref[4:5, :]
    for k in range(KER):
        conv = conv + vec_ref[k : k + 1, :] * extbc[pl.ds(8 - (KER - 1) + k, block), :]
    convbc_ref[...] = conv
    bc_all[head] = (conv * sigmoid(conv)).astype(BF16)
    share = head_copy(parts, lambda _: bc_all.at[head], lambda k: bc_all.at[k], bc_send, bc_recv)
    loop(1, parts, lambda i: share(i).start())

    def x_chunk(t):
        rows = ds(t * CHUNK, CHUNK)
        s, c = t // chunks, lax.rem(t, chunks)
        before = pl.ds(pl.multiple_of(jnp.maximum(t * CHUNK - 8, 0), 8), 8)
        for b in range(inner // LANES):
            lane = slice(b * LANES, (b + 1) * LANES)
            ext[0:8, lane] = jnp.where(c == 0, edge_x[s, :, lane], x_ref[before, lane])
            ext[8:, lane] = x_ref[rows, lane]
            conv = chan_ref[4:5, lane]
            for k in range(KER):
                conv = conv + chan_ref[k : k + 1, lane] * ext[pl.ds(8 - (KER - 1) + k, CHUNK), lane]
            conv_ref[rows, lane] = conv
            xact_ref[rows, lane] = (conv * sigmoid(conv)).astype(BF16)

    loop(0, total, x_chunk)

    loop(1, parts, lambda i: share(i).wait())
    everything = jnp.concatenate([bc_all[k] for k in range(parts)], axis=1)
    for s in range(seqs):
        bc_ref[s * block : (s + 1) * block, :] = mul(everything, unpack_ref[s], NN).astype(BF16)

    for s in range(seqs):

        def add(c, held):
            t = s * chunks + c
            rows = ds(t * CHUNK, CHUNK)
            cum, dt = cum_ref[rows, :], dt_ref[rows, :]
            end = cum[CHUNK - 1 :, :]
            tail = jnp.exp(end - cum) * dt
            weighted = jnp.concatenate(
                [
                    (
                        xact_ref[rows, p * LANES : (p + 1) * LANES].astype(F32) * pair_of(tail, p)
                    ).astype(BF16)
                    for p in range(pairs)
                ],
                axis=1,
            )
            new = mul(bc_ref[rows, 0:state], weighted, TN)
            fresh[t] = new
            return spread(jnp.exp(end), pairs) * held + new

        held = lax.fori_loop(0, chunks, add, jnp.zeros((state, inner), F32))
        local[s] = held.astype(local.dtype)

    start, carry, finish = carry_exchange(
        dims,
        local,
        arrived,
        passed,
        handed,
        incoming,
        decay_ref,
        (st_send, st_recv, back_send, back_recv, over_send, over_recv),
        False,
    )
    start()
    for copy in keeps[:5]:
        copy.start()

    def within(t):
        rows = ds(t * CHUNK, CHUNK)
        cum, dt = cum_ref[rows, :], dt_ref[rows, :]
        cum_t = cum.T
        scores = mul(bc_ref[rows, state:], bc_ref[rows, 0:state], NT)
        seen = iota((CHUNK, CHUNK), 0) >= iota((CHUNK, CHUNK), 1)
        side = iota((CHUNK, LANES), 1) < LANES // 2
        for p in range(pairs):
            lane = slice(p * LANES, (p + 1) * LANES)
            stepped = (xact_ref[rows, lane].astype(F32) * pair_of(dt, p)).astype(BF16)
            halves = []
            for h in (2 * p, 2 * p + 1):
                gap = cum[:, h : h + 1] - cum_t[h : h + 1, :]
                mixing = (scores * jnp.exp(jnp.where(seen, gap, -1e30))).astype(BF16)
                halves.append(mul(mixing, stepped, NN))
            y_ref[rows, lane] = jnp.where(side, halves[0], halves[1])

    loop(0, total, within)

    loop(1, count, lambda i: dec(i).wait())
    for s in range(seqs):
        decay_ref[s] = mul(decays[:, s, :], expand_ref[...], NN, EXACT)
    for copy in fetches:
        copy.wait()
    wide = 2 * LANES
    leads = place < count // 2

    def back_project(i):
        s, b = i // (inner // wide), lax.rem(i, inner // wide)
        rows, lane = ds(s * block, block), ds(b * wide, wide)
        dng_ref[rows, lane] = mul(cot_ref[rows, :], wout_ref[lane, :], NT)

    def gate_project(i):
        rows = ds(i * wide, wide)
        gate_ref[rows, :] = mul(normed_t_ref[:, rows], weight_ref[...], TN)

    def meanwhile():
        loop(0, seqs * (inner // wide), back_project)
        loop(0, seqs * block // wide, gate_project)

    @pl.when(~leads)
    def _():
        meanwhile()

    carry()

    @pl.when(leads)
    def _():
        meanwhile()

    finish()

    for s in range(seqs):

        def gate(c, held):
            t = s * chunks + c
            rows = ds(t * CHUNK, CHUNK)
            cum = cum_ref[rows, :]
            grown = jnp.exp(cum)
            states_ref[t] = held
            high, low = halves_of(held)
            c_rows = bc_ref[rows, state:]
            carried = mul(c_rows, high, NN) + mul(c_rows, low, NN)
            square = jnp.zeros((CHUNK, LANES), F32)
            cross = jnp.zeros((CHUNK, LANES), F32)
            for p in range(pairs):
                lane = slice(p * LANES, (p + 1) * LANES)
                y = y_ref[rows, lane] + carried[:, lane] * pair_of(grown, p)
                y_ref[rows, lane] = y
                out = y + chan_ref[6:7, lane] * xact_ref[rows, lane].astype(F32)
                pre = gate_ref[rows, lane]
                gated = out * (pre * sigmoid(pre))
                gated_ref[rows, lane] = gated
                square = square + gated * gated
                cross = cross + dng_ref[rows, lane] * chan_ref[5:6, lane] * gated
            at = iota((CHUNK, LANES), 1)
            both = jnp.where(
                at == 0,
                jnp.sum(square, axis=1, keepdims=True),
                jnp.where(at == 1, jnp.sum(cross, axis=1, keepdims=True), 0.0),
            )
            rowsum[head, t] = both.T[0:8, :]
            return spread(grown[CHUNK - 1 :, :], pairs) * held + fresh[t]

        lax.fori_loop(0, chunks, gate, incoming[s].astype(F32))

    keeps[5].start()
    rows_copy = head_copy(
        parts, lambda _: rowsum.at[head], lambda k: rowsum.at[k], row_send, row_recv
    )
    loop(1, parts, lambda i: rows_copy(i).start())
    loop(1, parts, lambda i: rows_copy(i).wait())
    sums_ref[...] = jnp.zeros_like(sums_ref)
    channels = inner * parts

    def outputs(t):
        rows = ds(t * CHUNK, CHUNK)
        sums = rowsum[0, t]
        for k in range(1, parts):
            sums = sums + rowsum[k, t]
        turned = jnp.concatenate([sums, jnp.zeros((CHUNK - 8, LANES), F32)], axis=0).T
        scale = lax.rsqrt(turned[:, 0:1] / channels + EPSILON)
        pull = scale * scale * scale * (turned[:, 1:2] / channels)
        dyy = jnp.zeros((CHUNK, LANES), F32)
        for p in range(pairs):
            lane = slice(p * LANES, (p + 1) * LANES)
            pre = gate_ref[rows, lane]
            sg = sigmoid(pre)
            gated, y = gated_ref[rows, lane], y_ref[rows, lane]
            x = xact_ref[rows, lane].astype(F32)
            gain = chan_ref[5:6, lane]
            scaled = gated * scale
            ng_t_ref[lane, rows] = (scaled * gain).T.astype(BF16)
            dng = dng_ref[rows, lane]
            d_gated = scale * (dng * gain) - gated * pull
            d_ssd = d_gated * (pre * sg)
            out = y + chan_ref[6:7, lane] * x
            dgate_ref[rows, lane] = (d_gated * out * (sg * (1.0 + pre * (1.0 - sg)))).astype(BF16)
            dy = d_ssd.astype(BF16)
            dy_ref[rows, lane] = dy
            sums_ref[0:8, lane] += eights(dng * scaled)
            sums_ref[8:16, lane] += eights(d_ssd * x)
            dyy = dyy + head_sums(dy.astype(F32) * y, gather_ref[lane, :])
        dyy_ref[rows, :] = dyy

    loop(0, total, outputs)
    for copy in keeps[6:]:
        copy.start()
    for copy in keeps:
        copy.wait()

    @pl.when(place < count - 1)
    def _():
        for c in edge_copies(after):
            c.wait_send()


def vmem(shape, kind):
    return pltpu.VMEM(shape, kind)


def forward(dims, *operands):
    count, parts, seqs, block, inner, heads, state = dims
    rows = seqs * block
    chunks = rows // CHUNK
    group, cut_rows = cut_of(count, seqs, state)
    spec, far = pl.BlockSpec(memory_space=pltpu.VMEM), pl.BlockSpec(memory_space=pl.ANY)
    fetched, kept = (1, 2, 9, 10), (0, 1, 2, 4, 5, 6, 7, 8, 9, 10)
    line, ring = pltpu.SemaphoreType.DMA((count,)), pltpu.SemaphoreType.DMA((parts,))
    edge = pltpu.SemaphoreType.DMA((2, seqs))
    outs = [
        ((rows, inner), BF16),
        ((rows, 2 * state), BF16),
        ((rows, inner), F32),
        ((block, LANES), F32),
        ((rows, LANES), F32),
        ((rows, LANES), F32),
        ((chunks, state, inner), F32),
        ((inner, rows), BF16),
        ((rows, inner), BF16),
        ((rows, inner), BF16),
        ((rows, LANES), F32),
        ((seqs, count, inner), F32),
        ((16, inner), F32),
    ]
    return pl.pallas_call(
        functools.partial(forward_kernel, dims),
        out_shape=[jax.ShapeDtypeStruct(*o) for o in outs],
        in_specs=[far if k in fetched else spec for k in range(len(operands))],
        out_specs=[far if k in kept else spec for k in range(len(outs))],
        scratch_shapes=[vmem(operands[k].shape[-2:], operands[k].dtype) for k in fetched]
        + [vmem((rows, inner), F32)]
        + [vmem(*outs[k]) for k in kept]
        + [
            pltpu.SemaphoreType.DMA((len(fetched),)),
            pltpu.SemaphoreType.DMA((len(kept),)),
            vmem((seqs, 8, inner), F32),
            vmem((seqs, 8, LANES), F32),
            vmem((CHUNK + 8, inner), F32),
            vmem((block + 8, LANES), F32),
            vmem((parts, block, LANES), BF16),
            vmem((chunks, state, inner), F32),
            vmem((rows, inner), F32),
            vmem((rows, inner), F32),
            vmem((rows, inner), F32),
            vmem((count, 8, LANES), F32),
            vmem((seqs, state, inner), BF16),
            vmem((group, cut_rows, inner), BF16),
            vmem((group, cut_rows, inner), F32),
            vmem((2, cut_rows, inner), F32),
            vmem((seqs, state, inner), F32),
            vmem((parts, chunks, 8, LANES), F32),
            edge,
            edge,
            line,
            line,
            ring,
            ring,
            line,
            line,
            line,
            line,
            pltpu.SemaphoreType.DMA,
            pltpu.SemaphoreType.DMA,
            ring,
            ring,
        ],
        compiler_params=pltpu.CompilerParams(
            collective_id=2, has_side_effects=True, vmem_limit_bytes=VMEM_LIMIT
        ),
        name="mixer_forward",
    )(*operands)


def project_kernel(
    tokens_ref,
    gain_ref,
    weight_ref,
    step_ref,
    coef_ref,
    taps_ref,
    taps_bc_ref,
    bias_ref,
    bias_bc_ref,
    dt_bias_ref,
    a_log_ref,
    skip_ref,
    gate_gain_ref,
    x_ref,
    small_ref,
    turned_ref,
    scale_ref,
    small_weight_ref,
    chan_ref,
    vec_ref,
    gain_row,
):
    heads, state_part = step_ref.shape[0], coef_ref.shape[1]

    def flat(ref):
        return jnp.concatenate([ref[k : k + 1, :] for k in range(ref.shape[0])], axis=1)

    @pl.when(pl.program_id(0) == 0)
    def _():
        small_weight_ref[...] = jnp.zeros_like(small_weight_ref)
        small_weight_ref[0:heads, :] = step_ref[...]
        for k in range(2):
            low = LANES // 2 + k * state_part
            small_weight_ref[low : low + state_part, :] = coef_ref[k]
        gain_row[...] = flat(gain_ref)
        chan_ref[...] = jnp.zeros_like(chan_ref)
        chan_ref[0:KER, :] = taps_ref[...]
        chan_ref[4:5, :] = flat(bias_ref)
        chan_ref[5:6, :] = flat(gate_gain_ref)
        chan_ref[6:7, :] = spread(skip_ref[...], heads // 2)
        vec_ref[...] = jnp.zeros_like(vec_ref)
        for k in range(4):
            at = slice(k * state_part, (k + 1) * state_part)
            vec_ref[0:KER, at] = taps_bc_ref[:, k % 2, :]
            vec_ref[4:5, at] = bias_bc_ref[k % 2 : k % 2 + 1, :]
        vec_ref[5:6, 0:heads] = dt_bias_ref[...]
        vec_ref[6:7, 0:heads] = -jnp.exp(a_log_ref[...])

    tokens = tokens_ref[...].astype(F32)
    scale = lax.rsqrt(jnp.mean(tokens * tokens, axis=1, keepdims=True) + EPSILON)
    scale_ref[...] = scale
    low = (tokens * scale * gain_row[...]).astype(BF16)
    turned_ref[...] = low.T
    x_ref[...] = mul(low, weight_ref[0], NN)
    small_ref[...] = mul(low, small_weight_ref[...], NT)


def project(tokens, gain, weights, *params):
    rows, width = tokens.shape
    inner = weights.shape[2]
    tall = 4 * CHUNK

    def by_rows(cols):
        return pl.BlockSpec((tall, cols), lambda i: (i, 0))

    def whole(shape):
        return pl.BlockSpec(shape, lambda i: (0,) * len(shape))

    return pl.pallas_call(
        project_kernel,
        grid=(rows // tall,),
        in_specs=[
            by_rows(width),
            whole(gain.shape),
            pl.BlockSpec((1, width, inner), lambda i: (1, 0, 0)),
        ]
        + [whole(a.shape) for a in params],
        out_specs=[
            by_rows(inner),
            by_rows(LANES),
            pl.BlockSpec((width, tall), lambda i: (0, i)),
            by_rows(1),
            whole((LANES, width)),
            whole((8, inner)),
            whole((8, LANES)),
            whole((1, width)),
        ],
        out_shape=[
            jax.ShapeDtypeStruct((rows, inner), F32),
            jax.ShapeDtypeStruct((rows, LANES), F32),
            jax.ShapeDtypeStruct((width, rows), BF16),
            jax.ShapeDtypeStruct((rows, 1), F32),
            jax.ShapeDtypeStruct((LANES, width), BF16),
            jax.ShapeDtypeStruct((8, inner), F32),
            jax.ShapeDtypeStruct((8, LANES), F32),
            jax.ShapeDtypeStruct((1, width), F32),
        ],
        compiler_params=pltpu.CompilerParams(vmem_limit_bytes=VMEM_LIMIT),
        name="project",
    )(tokens, gain, weights, *params)


def ring_place(count):
    place = lax.axis_index("seq")
    row, col = place // 2, place % 2
    return jnp.where(col == 0, row, count - 1 - row)


def ring_device(rank, count):
    return jnp.where(rank < count // 2, 2 * rank, 2 * (count - 1 - rank) + 1)


def ring_steps(count, plan, outs, bufs, stages, sems):
    rs_send, rs_recv, ag_send, ag_recv, keep_sem = sems
    far = count // 2
    head = lax.axis_index("head")
    rank = ring_place(count)
    arms = (1, -1)
    peers = [ring_device(lax.rem(rank + a + count, count), count) for a in arms]

    def chunk_at(distance):
        return lax.rem(rank + distance + 2 * count, count)

    def partial(i, chunk):
        left, right, first, cols, _ = plan[i]
        rows = left.shape[0] // count
        return mul(left[ds(chunk * rows, rows), :], right[:, first : first + cols], NN)

    def half(i, arm):
        cols, cut = plan[i][3:]
        return slice(0, cut) if arm == 0 else slice(cut, cols)

    def block_of(i, chunk):
        rows = plan[i][0].shape[0] // count
        return outs[i].at[ds(chunk * rows, rows)]

    def rs(i, arm, step, first=False):
        here = stages[i] if first else bufs[i].at[arm, step - 1]
        there = bufs[i].at[arm, step]
        if first:
            here, there = here.at[:, half(i, arm)], there.at[:, half(i, arm)]
        return remote(
            here, there, rs_send.at[i, arm, step], rs_recv.at[i, arm, step], peers[arm], head
        )

    def ag(i, arm, step, kind="middle"):
        there = block_of(i, chunk_at(-arms[arm] * step))
        here = bufs[i].at[0, far - 1] if kind == "first" else there
        if kind == "last":
            here, there = here.at[:, half(i, arm)], there.at[:, half(i, arm)]
        return remote(
            here, there, ag_send.at[i, arm, step], ag_recv.at[i, arm, step], peers[arm], head
        )

    def keep(i):
        return pltpu.make_async_copy(
            bufs[i].at[0, far - 1], block_of(i, chunk_at(0)), keep_sem.at[i]
        )

    def begin(i):
        stages[i][...] = partial(i, chunk_at(far)).astype(BF16)
        for arm in range(2):
            rs(i, arm, 0, True).start()

    def advance(streams, slot, slots):
        def second(i, arm):
            own = partial(i, chunk_at(arms[arm] * (far - 1)))
            rs(i, arm, 0, True).wait_recv()
            mine, other = half(i, arm), half(i, 1 - arm)
            bufs[i][arm, 0, :, other] = own[:, other].astype(BF16)
            bufs[i][arm, 0, :, mine] = (
                own[:, mine] + bufs[i][arm, 0, :, mine].astype(F32)
            ).astype(BF16)
            rs(i, arm, 1).start()

        def later(i, arm, step):
            own = partial(i, chunk_at(arms[arm] * (far - step)))
            rs(i, arm, step - 1).wait_recv()
            bufs[i][arm, step - 1] = (own + bufs[i][arm, step - 1].astype(F32)).astype(BF16)
            rs(i, arm, step).start()

        def last(i):
            own = partial(i, chunk_at(0))
            for arm in range(2):
                rs(i, arm, far - 1).wait_recv()
                own = own + bufs[i][arm, far - 1].astype(F32)
            bufs[i][0, far - 1] = own.astype(BF16)
            for arm in range(2):
                ag(i, arm, 0, "first").start()
            keep(i).start()

        low, high = slot * far // slots, (slot + 1) * far // slots
        if low == 0 < high:
            for i in streams:
                for arm in range(2):
                    second(i, arm)

        def middle(step):
            for i in streams:
                for arm in range(2):
                    later(i, arm, step)

        if min(high, far - 1) > max(low, 1):
            loop(max(low, 1) + 1, min(high, far - 1) + 1, middle)
        if high == far:
            for i in streams:
                last(i)

    def pass_on(streams, slot, slots):
        def middle(step):
            for i in streams:
                for arm in range(2):
                    ag(i, arm, step - 1).wait_recv()
                    ag(i, arm, step).start()

        steps = far - 1
        low, high = slot * steps // slots, (slot + 1) * steps // slots
        if min(high, steps - 1) > low:
            loop(low + 1, min(high, steps - 1) + 1, middle)
        if low < high == steps:
            for i in streams:
                for arm in range(2):
                    ag(i, arm, steps - 1).wait_recv()
                    ag(i, arm, steps, "last").start()

    def pass_end(streams):
        for i in streams:
            for arm in range(2):
                ag(i, arm, far - 1, "last").wait_recv()

    def drain(streams):
        for i in streams:
            for arm in range(2):
                rs(i, arm, 0, True).wait_send()
                ag(i, arm, 0, "first").wait_send()
                ag(i, arm, far - 1, "last").wait_send()
            keep(i).wait()

        def one(step):
            for i in streams:
                for arm in range(2):
                    rs(i, arm, step).wait_send()

                    @pl.when(step < far - 1)
                    def _():
                        ag(i, arm, step).wait_send()

        loop(1, far, one)

    return begin, advance, pass_on, pass_end, drain


def finish_kernel(
    gate,
    narrow_low,
    narrow,
    out,
    sums_ref,
    gather_ref,
    block_far,
    input_far,
    gin_ref,
    wout_ref,
    coef_ref,
    step_ref,
    taps_ref,
    taps_bc_ref,
    bias_ref,
    bias_bc_ref,
    dt_ref,
    log_ref,
    skip_ref,
    gain_ref,
    norm_ref,
    block_out,
    input_out,
):
    inner, half = gate.shape[1], narrow_low.shape[1]
    heads, state_part = step_ref.shape[0], bias_bc_ref.shape[1]
    block_out[...] = block_far[...]
    input_out[...] = input_far[...]

    @pl.when(pl.program_id(0) == 0)
    def _():
        lanes = sums_ref[:, inner:]
        both = lanes + pltpu.roll(lanes, LANES // 2, 1)
        taps_ref[...] = sums_ref[0:KER, 0:inner]
        for ref, row in ((bias_ref, KER), (gain_ref, KER + 1), (norm_ref, KER + 3)):
            for k in range(ref.shape[0]):
                ref[k : k + 1, :] = sums_ref[row : row + 1, k * LANES : (k + 1) * LANES]
        for k in range(2):
            at = slice(k * state_part, (k + 1) * state_part)
            taps_bc_ref[:, k, :] = both[0:KER, at]
            bias_bc_ref[k : k + 1, :] = both[KER : KER + 1, at]
        dt_ref[...] = lanes[KER + 1 : KER + 2, 0:heads]
        log_ref[...] = lanes[KER + 2 : KER + 3, 0:heads]
        skip_ref[...] = head_sums(sums_ref[:, 0:inner], gather_ref[...])[KER + 2 : KER + 3, 0:heads]

    gin_ref[:, 0, :] = gate[...].astype(F32)
    gin_ref[:, 1, 0:half] = narrow_low[...].astype(F32)
    gin_ref[:, 1, half:] = narrow[:, 0 : inner - half].astype(F32)
    small = narrow[:, inner - half :].astype(F32).T
    step_ref[...] = small[0:heads]
    for k in range(2):
        low = LANES // 2 + k * state_part
        coef_ref[k] = small[low : low + state_part]
    wout_ref[...] = out[...].astype(F32)


def finish(width, inner, heads, state_part, streams, sums, gather, block_out, grad_input):
    steps = 4
    tall, low, part = width // steps, inner // steps, grad_input.shape[0] // steps
    out, gate, narrow_low, narrow = streams
    cols = grad_input.shape[1]
    mine = pl.BlockSpec((part, cols), lambda i: (i, 0))

    def block(array_in, rows):
        return pl.BlockSpec((rows, array_in.shape[1]), lambda i: (i, 0))

    def whole(shape):
        return pl.BlockSpec(shape, lambda i: (0,) * len(shape))

    little = [
        (KER, inner),
        (KER, 2, state_part),
        (inner // LANES, LANES),
        (2, state_part),
        (1, heads),
        (1, heads),
        (1, heads),
        (inner // LANES, LANES),
        (cols // LANES, LANES),
    ]
    return pl.pallas_call(
        finish_kernel,
        grid=(steps,),
        in_specs=[block(gate, tall), block(narrow_low, tall), block(narrow, tall), block(out, low)]
        + [whole(sums.shape), whole(gather.shape), mine, mine],
        out_specs=[
            pl.BlockSpec((tall, 2, inner), lambda i: (i, 0, 0)),
            pl.BlockSpec((low, width), lambda i: (i, 0)),
            pl.BlockSpec((2, state_part, tall), lambda i: (0, 0, i)),
            pl.BlockSpec((heads, tall), lambda i: (0, i)),
        ]
        + [whole(s) for s in little]
        + [mine, mine],
        out_shape=[
            jax.ShapeDtypeStruct((width, 2, inner), F32),
            jax.ShapeDtypeStruct((inner, width), F32),
            jax.ShapeDtypeStruct((2, state_part, width), F32),
            jax.ShapeDtypeStruct((heads, width), F32),
        ]
        + [jax.ShapeDtypeStruct(s, F32) for s in little]
        + [
            jax.ShapeDtypeStruct(block_out.shape, BF16),
            jax.ShapeDtypeStruct(grad_input.shape, F32),
        ],
        compiler_params=pltpu.CompilerParams(vmem_limit_bytes=VMEM_LIMIT),
        name="finish",
    )(gate, narrow_low, narrow, out, sums, gather, block_out, grad_input)


STEPS = 4


def backward_kernel(
    dims,
    dy_ref,
    xact_far,
    bc_ref,
    conv_ref,
    convbc_ref,
    dt_ref,
    cum_ref,
    states_far,
    dyy_ref,
    decay_ref,
    x_far,
    small_ref,
    chan_ref,
    vec_ref,
    pack_far,
    gather_ref,
    normed_t_far,
    ng_t_far,
    cot_far,
    dgate_far,
    small_weight_far,
    sums_ref,
    gain_ref,
    row_scale_ref,
    tokens_ref,
    weight_ref,
    wout_far,
    *rest,
):
    count, parts, seqs, block, inner, heads, state = dims
    outs, rest = rest[:4], rest[4:]
    grad_ref, total_ref, mixed_ref, *rest = rest
    bufs, rest = rest[:4], rest[4:]
    stages, rest = rest[:4], rest[4:]
    fetched, rest = rest[:7], rest[7:]
    fetch_sem, *rest = rest
    (
        dx_ref,
        gx_ref,
        gbc_ref,
        gdt_ref,
        weights,
        conv_buf,
        state_buf,
        dn_out,
        dn_in,
        wout,
        mix_in,
        token_buf,
        rowsum,
        shared,
        rs_send,
        rs_recv,
        ag_send,
        ag_recv,
        keep_sem,
        weight_sem,
        conv_sem,
        state_sem,
        x_sem,
        token_sem,
        dn_send,
        dn_recv,
        wout_sem,
        mix_send,
        mix_recv,
        row_send,
        row_recv,
        sum_send,
        sum_recv,
        *rest,
    ) = rest
    (
        dconv,
        dconvbc,
        prebc,
        dbc,
        ddt,
        local,
        arrived,
        passed,
        handed,
        incoming,
        bc_out,
        bc_in,
        edge_send,
        edge_recv,
        bc_send,
        bc_recv,
        st_send,
        st_recv,
        back_send,
        back_recv,
        over_send,
        over_recv,
    ) = rest
    sources = (
        ng_t_far,
        cot_far,
        normed_t_far,
        dgate_far,
        xact_far,
        small_weight_far,
        pack_far,
    )
    fetches = [
        pltpu.make_async_copy(src, dst, fetch_sem.at[k])
        for k, (src, dst) in enumerate(zip(sources, fetched))
    ]
    for copy in fetches:
        copy.start()
    (
        ng_t_ref,
        cot_ref,
        normed_t_ref,
        dgate_ref,
        xact_ref,
        small_weight_ref,
        pack_ref,
    ) = fetched
    place, head = lax.axis_index("seq"), lax.axis_index("head")
    chunks = block // CHUNK
    pairs = heads // 2
    total = seqs * chunks
    rows_all = seqs * block
    width = cot_ref.shape[1]
    cols = width // parts
    plan = (
        (ng_t_ref, cot_ref, 0, width, width // 2),
        (normed_t_ref, dgate_ref, 0, inner, inner // 2),
        (normed_t_ref, dx_ref, 0, inner // 2, LANES),
        (normed_t_ref, dx_ref, inner // 2, inner // 2 + LANES, 2 * LANES),
    )
    begin, advance, pass_on, pass_end, drain = ring_steps(
        count, plan, outs, bufs, stages, (rs_send, rs_recv, ag_send, ag_recv, keep_sem)
    )
    out, gate, late = (0,), (1,), (2, 3)
    meet(count, parts)
    gdt_ref[...] = jnp.zeros_like(gdt_ref)

    token_copy = pltpu.make_async_copy(
        tokens_ref.at[:, pl.ds(pl.multiple_of(head * cols, cols), cols)], token_buf, token_sem
    )
    token_copy.start()

    def weight_copy(i):
        other = lax.rem(head + i, parts)
        return pltpu.make_async_copy(
            weight_ref.at[:, pl.ds(pl.multiple_of(other * cols, cols), cols)],
            weights.at[lax.rem(i + 1, 2)],
            weight_sem.at[lax.rem(i + 1, 2)],
        )

    def conv_copy(q):
        t = q // chunks * chunks + chunks - 1 - lax.rem(q, chunks)
        slot = lax.rem(q, 2)
        return pltpu.make_async_copy(
            conv_ref.at[ds(t * CHUNK, CHUNK)], conv_buf.at[slot], conv_sem.at[slot]
        )

    def state_copy(q):
        t = q // chunks * chunks + chunks - 1 - lax.rem(q, chunks)
        slot = lax.rem(q, 2)
        return pltpu.make_async_copy(states_far.at[t], state_buf.at[slot], state_sem.at[slot])

    conv_copy(0).start()
    state_copy(0).start()
    weight_copy(1).start()

    tall = 2 * CHUNK

    def wout_copy(i):
        other = lax.rem(head + i, parts)
        return pltpu.make_async_copy(
            wout_far.at[:, pl.ds(pl.multiple_of(other * cols, cols), cols)],
            wout.at[i % 2],
            wout_sem.at[i % 2],
        )

    def mix_copy(i):
        other = lax.rem(head + i, parts)
        return remote(
            dn_out.at[other], mix_in.at[i - 1], mix_send.at[i], mix_recv.at[i], place, other
        )

    def mix(i):
        other = lax.rem(head + i, parts)
        if i < parts:
            wout_copy(i + 1).start()
        wout_copy(i).wait()

        def some(r):
            rows = ds(r * tall, tall)
            dn_out[other, rows, :] = mul(ng_t_ref[0:inner, rows], wout[i % 2], TN).astype(BF16)

        loop(0, rows_all // tall, some)
        if i < parts:
            mix_copy(i).start()

    wout_copy(1).start()

    for s in range(seqs):

        def alone(i, held):
            t = s * chunks + chunks - 1 - i
            rows = ds(t * CHUNK, CHUNK)
            grown = jnp.exp(cum_ref[rows, :])
            weighted = jnp.concatenate(
                [
                    (
                        dy_ref[rows, p * LANES : (p + 1) * LANES].astype(F32) * pair_of(grown, p)
                    ).astype(BF16)
                    for p in range(pairs)
                ],
                axis=1,
            )
            new = mul(bc_ref[rows, state:], weighted, TN)
            return spread(grown[CHUNK - 1 :, :], pairs) * held + new

        held = lax.fori_loop(0, chunks, alone, jnp.zeros((state, inner), F32))
        local[s] = held.astype(BF16)
        if s == 0:
            for copy in fetches[:4]:
                copy.wait()
            for i in out + gate:
                begin(i)

    start, carry, finish = carry_exchange(
        dims,
        local,
        arrived,
        passed,
        handed,
        incoming,
        decay_ref,
        (st_send, st_recv, back_send, back_recv, over_send, over_recv),
        True,
    )
    leads = place >= count // 2
    start()
    advance(out, 0, STEPS)

    @pl.when(leads)
    def _():
        carry()

    mix(1)
    advance(gate, 0, STEPS)
    mix(2)
    advance(out, 1, STEPS)
    advance(gate, 1, STEPS)

    @pl.when(~leads)
    def _():
        carry()

    mix(3)
    advance(out, 2, STEPS)
    for i in range(4, parts + 1):
        mix(i)
    for copy in fetches[4:]:
        copy.wait()
    finish()

    side = iota((CHUNK, LANES), 1) < LANES // 2
    seen = iota((CHUNK, CHUNK), 0) <= iota((CHUNK, CHUNK), 1)
    upper = seen.astype(F32)
    for s in range(seqs):

        def chunk(i, held):
            t = s * chunks + chunks - 1 - i
            rows = ds(t * CHUNK, CHUNK)
            out_rows = ds((s * chunks + chunks - 1 - i) * CHUNK, CHUNK)
            turn = s * chunks + i
            conv_copy(turn).wait()
            state_copy(turn).wait()

            @pl.when(turn + 1 < total)
            def _():
                conv_copy(turn + 1).start()
                state_copy(turn + 1).start()

            cum, dt = cum_ref[rows, :], dt_ref[rows, :]
            cum_t = cum.T
            grown = jnp.exp(cum)
            end = cum[CHUNK - 1 :, :]
            tail = jnp.exp(end - cum)
            b_rows, c_rows = bc_ref[rows, 0:state], bc_ref[rows, state:]
            scores = mul(b_rows, c_rows, NT)
            low = held.astype(BF16)
            begun = state_buf[lax.rem(turn, 2)]
            begun_high, begun_low = halves_of(begun)
            pulled = mul(b_rows, low, NN)
            grad_scores = jnp.zeros((CHUNK, CHUNK), F32)
            d_x_sum = jnp.zeros((CHUNK, LANES), F32)
            d_fall = jnp.zeros((CHUNK, LANES), F32)
            into_x = []
            into_y = []
            last = []
            for p in range(pairs):
                lane = slice(p * LANES, (p + 1) * LANES)
                x, dy = xact_ref[rows, lane], dy_ref[rows, lane]
                xf, dyf = x.astype(F32), dy.astype(F32)
                dt_p, tail_p = pair_of(dt, p), pair_of(tail, p)
                stepped = xf * dt_p
                low_step = stepped.astype(BF16)
                halves = []
                for k, h in enumerate((2 * p, 2 * p + 1)):
                    gap = cum_t[h : h + 1, :] - cum[:, h : h + 1]
                    fade = jnp.exp(jnp.where(seen, gap, -1e30))
                    own = jnp.where(side if k == 0 else ~side, low_step, jnp.zeros_like(low_step))
                    grad_scores = grad_scores + mul(own, dy, NT) * fade
                    halves.append(mul((scores * fade).astype(BF16), dy, NN))
                from_state = pulled[:, lane] * tail_p
                d_step_x = jnp.where(side, halves[0], halves[1]) + from_state
                rounded = low_step.astype(F32)
                d_x_sum = d_x_sum + head_sums(xf * d_step_x, gather_ref[lane, :])
                d_fall = d_fall + head_sums(rounded * d_step_x, gather_ref[lane, :])
                into_x.append(halves_of(stepped * tail_p))
                into_y.append(halves_of(dyf * pair_of(grown, p)))
                last.append(jnp.sum(rounded * from_state, axis=0, keepdims=True))
                conv = conv_buf[lax.rem(turn, 2), :, lane]
                sg = sigmoid(conv)
                d_act = dt_p * d_step_x + chan_ref[6:7, lane] * dyf
                dconv[s, ds((chunks - 1 - i) * CHUNK, CHUNK), lane] = d_act * (
                    sg * (1.0 + conv * (1.0 - sg))
                )
            low_scores = grad_scores.astype(BF16)
            x_high, x_low = (jnp.concatenate([v[k] for v in into_x], axis=1) for k in range(2))
            y_high, y_low = (jnp.concatenate([v[k] for v in into_y], axis=1) for k in range(2))
            d_b = mul(low_scores, c_rows, NN) + mul(x_high, low, NT) + mul(x_low, low, NT)
            d_c = mul(low_scores, b_rows, TN) + mul(y_high, begun_high, NT)
            d_c = d_c + mul(y_high, begun_low, NT) + mul(y_low, begun_high, NT)
            dbc[out_rows, 0:state] = d_b.astype(BF16)
            dbc[out_rows, state:] = d_c.astype(BF16)
            fall = spread(grown[CHUNK - 1 :, :], pairs)
            ends = jnp.concatenate(last, axis=1) + fall * jnp.sum(
                held * begun, axis=0, keepdims=True
            )
            ends = head_sums(jnp.broadcast_to(ends, (8, inner)), gather_ref[...])[0:1, :]
            d_log = mul(upper, dyy_ref[rows, :] - d_fall, NN, EXACT) + ends
            d_step = d_x_sum + vec_ref[6:7, :] * d_log
            d_dt = d_step * sigmoid(small_ref[rows, :] + vec_ref[5:6, :])
            gdt_ref[0:8, :] += eights(d_dt)
            gdt_ref[8:16, :] += eights(d_log * (dt * vec_ref[6:7, :]))
            ddt[out_rows, :] = d_dt


            @pl.when(turn == total * 3 // 8)
            def _():
                advance(gate, 2, STEPS)

            @pl.when(turn == total * 6 // 8)
            def _():
                advance(out, 3, STEPS)

            return fall * held + mul(c_rows, y_high, TN)

        lax.fori_loop(0, chunks, chunk, incoming[s].astype(F32))

    def pack(k):
        piece = mul(dbc[0:block, :], pack_ref[k, 0], NN)
        return (piece + mul(dbc[block:, :], pack_ref[k, 1], NN)).astype(BF16)

    def pack_one(k):
        bc_out[k] = pack(k)

    def x_copy(t):
        slot = lax.rem(t, 2)
        return pltpu.make_async_copy(
            x_far.at[ds(t * CHUNK, CHUNK)], conv_buf.at[slot], x_sem.at[slot]
        )

    x_copy(0).start()
    advance(gate, 3, STEPS)
    loop(0, parts, pack_one)
    share = head_copy(parts, lambda k: bc_out.at[k], lambda k: bc_in.at[k], bc_send, bc_recv)
    loop(1, parts, lambda i: share(i).start())

    before = lax.rem(place + count - 1, count)

    def edge_copy(s):
        return remote(
            dconv.at[s, pl.ds(0, 8)],
            dconv.at[s, pl.ds(block, 8)],
            edge_send.at[s],
            edge_recv.at[s],
            before,
            head,
        )

    def edge_bc():
        return remote(
            dconvbc.at[pl.ds(0, 8)],
            dconvbc.at[pl.ds(block, 8)],
            edge_send.at[seqs],
            edge_recv.at[seqs],
            before,
            head,
        )

    @pl.when(place > 0)
    def _():
        for s in range(seqs):
            edge_copy(s).start()

    pass_on(out, 0, 3)
    loop(1, parts, lambda i: share(i).wait())
    bc_in[head] = bc_out[head]
    d_act = bc_in[0].astype(F32)
    for k in range(1, parts):
        d_act = d_act + bc_in[k].astype(F32)
    conv = convbc_ref[...]
    sg = sigmoid(conv)
    dconvbc[0:block, :] = d_act * (sg * (1.0 + conv * (1.0 - sg)))

    @pl.when(place > 0)
    def _():
        edge_bc().start()

    @pl.when(place < count - 1)
    def _():
        for s in range(seqs):
            edge_copy(s).wait_recv()

    @pl.when(place == count - 1)
    def _():
        for s in range(seqs):
            dconv[s, block : block + 8, :] = jnp.zeros((8, inner), F32)

    gx_ref[...] = jnp.zeros_like(gx_ref)

    def x_chunk(t):
        rows = ds(t * CHUNK, CHUNK)
        s, c = t // chunks, lax.rem(t, chunks)
        x_copy(t).wait()

        @pl.when(t + 1 < total)
        def _():
            x_copy(t + 1).start()

        for p in range(pairs):
            lane = slice(p * LANES, (p + 1) * LANES)
            x = conv_buf[lax.rem(t, 2), :, lane]
            pre = jnp.zeros((CHUNK, LANES), F32)
            here = dconv[s, pl.ds(pl.multiple_of(c * CHUNK, CHUNK), CHUNK + 8), lane]
            for k in range(KER):
                off = KER - 1 - k
                d = pltpu.roll(here, CHUNK + 8 - off, 0)[:CHUNK] if off else here[:CHUNK]
                pre = pre + chan_ref[k : k + 1, lane] * d
                gx_ref[8 * k : 8 * k + 8, lane] += eights(x * d)
                if k == KER - 1:
                    gx_ref[8 * KER : 8 * KER + 8, lane] += eights(d)
            dx_ref[rows, lane] = pre.astype(BF16)

        @pl.when(t == total // 2)
        def _():
            pass_on(gate, 0, 3)

    loop(0, total, x_chunk)

    @pl.when(place < count - 1)
    def _():
        edge_bc().wait_recv()

    @pl.when(place == count - 1)
    def _():
        dconvbc[block : block + 8, :] = jnp.zeros((8, LANES), F32)

    low, high = small_ref[0:block, :], small_ref[block:, :]
    prebc[...] = jnp.where(
        iota(low.shape, 1) < LANES // 2, pltpu.roll(low, LANES // 2, 1), high
    )
    pre = jnp.zeros((block, LANES), F32)
    for k in range(KER):
        d = dconvbc[pl.ds(KER - 1 - k, block), :]
        pre = pre + vec_ref[k : k + 1, :] * d
        gbc_ref[8 * k : 8 * k + 8, :] = eights(prebc[...] * d)
    gbc_ref[8 * KER : 8 * KER + 8, :] = eights(dconvbc[0:block, :])
    at = iota((block, LANES), 1)
    for s in range(seqs):
        rows = slice(s * block, (s + 1) * block)
        mine = pre if s == seqs - 1 else pltpu.roll(pre, LANES // 2, 1)
        step = jnp.where(at < heads, ddt[rows, :], 0.0)
        dx_ref[rows, inner:] = jnp.where(at < LANES // 2, step, mine).astype(BF16)

    for i in late:
        begin(i)

    loop(1, parts, lambda i: mix_copy(i).wait())
    token_copy.wait()

    def add_up(t):
        rows = ds(t * CHUNK, CHUNK)
        d = dn_out[head, rows, :].astype(F32)
        for k in range(parts - 1):
            d = d + mix_in[k, rows, :].astype(F32)
        mixed_ref[rows, :] = (token_buf[rows, :].astype(F32) + d).astype(BF16)

    loop(0, total, add_up)


    def dn_copy(i):
        other = lax.rem(head + i, parts)
        return remote(
            dn_out.at[other], dn_in.at[i - 1], dn_send.at[i], dn_recv.at[i], place, other
        )

    def d_normed(i):
        other = lax.rem(head + i, parts)
        slot = (i + 1) % 2
        if i < parts:
            weight_copy(i + 1).start()

        weight_copy(i).wait()
        mine = small_weight_ref[:, pl.ds(pl.multiple_of(other * cols, cols), cols)]

        def some(r):
            rows = ds(r * tall, tall)
            part = mul(dgate_ref[rows, :], weights[slot, 0], NT)
            part = part + mul(dx_ref[rows, 0:inner], weights[slot, 1], NT)
            part = part + mul(dx_ref[rows, inner:], mine, NN)
            dn_out[other, rows, :] = part.astype(BF16)

        loop(0, rows_all // tall, some)

        if i < parts:
            dn_copy(i).start()

    between = ((out, 1), (), (out, 2), ())
    for k in range(STEPS):
        if k < parts:
            d_normed(k + 1)
        advance(late, k, STEPS)
        if between[k]:
            pass_on(*between[k], 3)
    for k in range(STEPS, parts):
        d_normed(k + 1)

    loop(1, parts, lambda i: dn_copy(i).wait())
    my_cols = pl.ds(pl.multiple_of(head * cols, cols), cols)

    def own(t, grads):
        rows = ds(t * CHUNK, CHUNK)
        d = dn_out[head, rows, :].astype(F32)
        for k in range(parts - 1):
            d = d + dn_in[k, rows, :].astype(F32)
        token = token_buf[rows, :].astype(F32)
        grads = grads + eights(d * (token * row_scale_ref[rows, :]))
        d = d * gain_ref[:, my_cols]
        grad_ref[rows, :] = d
        line = jnp.sum(d * token, axis=1, keepdims=True)
        line = jnp.where(iota((CHUNK, LANES), 1) == 0, line, 0.0)
        rowsum[head, t] = line.T[0:8, :]
        return grads

    norm_grads = lax.fori_loop(0, total, own, jnp.zeros((8, cols), F32))
    rows_copy = head_copy(
        parts, lambda _: rowsum.at[head], lambda k: rowsum.at[k], row_send, row_recv
    )
    loop(1, parts, lambda i: rows_copy(i).start())

    def summed(ref, k):
        return jnp.sum(ref[8 * k : 8 * k + 8, :], axis=0, keepdims=True)

    shared[place] = jnp.zeros(shared.shape[1:], F32)
    for k in range(KER + 1):
        shared[place, k : k + 1, 0:inner] = summed(gx_ref, k)
        shared[place, k : k + 1, inner:] = summed(gbc_ref, k)
    for k in range(2):
        shared[place, KER + 1 + k : KER + 2 + k, 0:inner] = summed(sums_ref, k)
        shared[place, KER + 1 + k : KER + 2 + k, inner:] = summed(gdt_ref, k)
    shared[place, 7:8, 0:cols] = jnp.sum(norm_grads, axis=0, keepdims=True)
    sums_copy = line_copy(
        count, lambda _: shared.at[place], lambda k: shared.at[k], sum_send, sum_recv
    )
    loop(1, count, lambda i: sums_copy(i).start())
    pass_on(late, 0, 3)
    pass_on(gate, 1, 3)
    loop(1, parts, lambda i: rows_copy(i).wait())

    def finish_rows(t):
        rows = ds(t * CHUNK, CHUNK)
        sums = rowsum[0, t]
        for k in range(1, parts):
            sums = sums + rowsum[k, t]
        turned = jnp.concatenate([sums, jnp.zeros((CHUNK - 8, LANES), F32)], axis=0).T
        scale = row_scale_ref[rows, :]
        pull = scale * scale * scale * (turned[:, 0:1] / width)
        grad_ref[rows, :] = (
            scale * grad_ref[rows, :]
            - token_buf[rows, :].astype(F32) * pull
            + cot_ref[rows, my_cols].astype(F32)
        )

    loop(0, total, finish_rows)
    pass_on(late, 1, 3)
    pass_on(gate, 2, 3)
    loop(1, count, lambda i: sums_copy(i).wait())
    everything = shared[0]
    for k in range(1, count):
        everything = everything + shared[k]
    total_ref[...] = everything
    pass_on(late, 2, 3)
    pass_end(out + gate + late)
    drain(out + gate + late)

    @pl.when(place > 0)
    def _():
        for s in range(seqs):
            edge_copy(s).wait_send()
        edge_bc().wait_send()


def backward(dims, *operands):
    count, parts, seqs, block, inner, heads, state = dims
    rows = seqs * block
    chunks = rows // CHUNK
    group, cut_rows = cut_of(count, seqs, state)
    normed_rows, ng_rows, width = (operands[k].shape[d] for k, d in ((16, 0), (17, 0), (18, 1)))
    cols = width // parts
    distant = (1, 3, 7, 10, 14, 16, 17, 18, 19, 20, 24, 25, 26)
    fetched = [operands[k] for k in (17, 18, 16, 19, 1, 20, 14)]
    spec = pl.BlockSpec(memory_space=pltpu.VMEM)
    far = pl.BlockSpec(memory_space=pl.ANY)
    line, ring = pltpu.SemaphoreType.DMA((count,)), pltpu.SemaphoreType.DMA((parts,))
    edge = pltpu.SemaphoreType.DMA((seqs + 1,))
    streams = [
        (ng_rows, width),
        (normed_rows, inner),
        (normed_rows, inner // 2),
        (normed_rows, inner // 2 + LANES),
    ]
    steps = pltpu.SemaphoreType.DMA((len(streams), 2, count // 2))
    outs = [(shape, BF16) for shape in streams]
    outs = outs + [((rows, cols), F32), ((8, inner + LANES), F32), ((rows, cols), BF16)]
    return pl.pallas_call(
        functools.partial(backward_kernel, dims),
        out_shape=[jax.ShapeDtypeStruct(*o) for o in outs],
        in_specs=[far if k in distant else spec for k in range(len(operands))],
        out_specs=[far] * len(streams) + [spec] * 3,
        scratch_shapes=[vmem((2, count // 2, r // count, c), BF16) for r, c in streams]
        + [vmem((r // count, c), BF16) for r, c in streams]
        + [vmem(a.shape, a.dtype) for a in fetched]
        + [
            pltpu.SemaphoreType.DMA((len(fetched),)),
            vmem((rows, inner + LANES), BF16),
            vmem((8 * (KER + 1), inner), F32),
            vmem((8 * (KER + 1), LANES), F32),
            vmem((16, LANES), F32),
            vmem((2, 2, cols, inner), BF16),
            vmem((2, CHUNK, inner), F32),
            vmem((2, state, inner), F32),
            vmem((parts, rows, cols), BF16),
            vmem((parts - 1, rows, cols), BF16),
            vmem((2, inner, cols), BF16),
            vmem((parts - 1, rows, cols), BF16),
            vmem((rows, cols), BF16),
            vmem((parts, chunks, 8, LANES), F32),
            vmem((count, 8, inner + LANES), F32),
            steps,
            steps,
            steps,
            steps,
            pltpu.SemaphoreType.DMA((len(streams),)),
            pltpu.SemaphoreType.DMA((2,)),
            pltpu.SemaphoreType.DMA((2,)),
            pltpu.SemaphoreType.DMA((2,)),
            pltpu.SemaphoreType.DMA((2,)),
            pltpu.SemaphoreType.DMA,
            ring,
            ring,
            pltpu.SemaphoreType.DMA((2,)),
            ring,
            ring,
            ring,
            ring,
            line,
            line,
            vmem((seqs, block + 8, inner), F32),
            vmem((block + 8, LANES), F32),
            vmem((block, LANES), F32),
            vmem((rows, 2 * state), BF16),
            vmem((rows, LANES), F32),
            vmem((seqs, state, inner), BF16),
            vmem((group, cut_rows, inner), BF16),
            vmem((group, cut_rows, inner), BF16),
            vmem((2, cut_rows, inner), BF16),
            vmem((seqs, state, inner), BF16),
            vmem((parts, block, LANES), BF16),
            vmem((parts, block, LANES), BF16),
            edge,
            edge,
            ring,
            ring,
            line,
            line,
            line,
            line,
            pltpu.SemaphoreType.DMA,
            pltpu.SemaphoreType.DMA,
        ],
        compiler_params=pltpu.CompilerParams(
            collective_id=3, has_side_effects=True, vmem_limit_bytes=VMEM_LIMIT
        ),
        name="mixer_backward",
    )(*operands)


def body(
    tokens,
    norm_gain,
    gate_input_weight,
    coefficient_weight,
    step_weight,
    conv_x,
    conv_bc,
    conv_bias_x,
    conv_bias_bc,
    dt_bias,
    a_log,
    d_skip,
    gate_gain,
    output_weight,
    cotangent,
):
    seqs, block, width = tokens.shape
    inner = gate_input_weight.shape[2]
    state_part = coefficient_weight.shape[2]
    heads = step_weight.shape[1]
    count, parts = lax.axis_size("seq"), lax.axis_size("head")
    state = state_part * parts
    rows = seqs * block
    col_count = width // parts
    half = LANES // 2
    dims = (count, parts, seqs, block, inner, heads, state)

    flat_tokens = tokens.reshape(rows, width)
    both_weights = gate_input_weight.transpose(1, 0, 2)
    x_pre, small, normed_t, row_scale, small_weight, chan, vec, gain = project(
        flat_tokens,
        norm_gain.reshape(-1, LANES),
        both_weights,
        step_weight.T,
        coefficient_weight.transpose(1, 2, 0),
        conv_x,
        conv_bc,
        conv_bias_x.reshape(-1, LANES),
        conv_bias_bc,
        dt_bias.reshape(1, heads),
        a_log.reshape(1, heads),
        d_skip.reshape(1, heads),
        gate_gain.reshape(-1, LANES),
    )
    device, lane, channel = np.meshgrid(
        np.arange(parts), np.arange(LANES), np.arange(2 * state), indexing="ij"
    )
    is_c, at = channel // state, channel % state
    unpack = np.stack(
        [
            (lane == s * half + is_c * state_part + at - device * state_part)
            & (at // state_part == device)
            for s in range(seqs)
        ]
    ).astype(np.float32)
    pack = jnp.asarray(unpack.transpose(1, 0, 3, 2), BF16)
    unpack = jnp.asarray(unpack.reshape(seqs, parts * LANES, 2 * state), BF16)
    expand = np.arange(LANES)[:, None] == np.arange(inner)[None, :] // (inner // heads)
    gather = jnp.asarray(expand.T.astype(np.float32), BF16)
    expand = jnp.asarray(expand.astype(np.float32))
    cot = cotangent.reshape(rows, width)

    xact, bc, conv, convbc, dt, cum, states, ng_t, dgate, dy, dyy, decay, sums = forward(
        dims,
        x_pre,
        normed_t,
        both_weights,
        small,
        chan,
        vec,
        unpack,
        expand,
        gather,
        cot,
        output_weight,
    )
    def padded(array_in):
        return jnp.pad(array_in, ((0, -array_in.shape[0] % (count * 16)), (0, 0)))

    *streams, grad_input, sums, block_out = backward(
        dims,
        dy,
        xact,
        bc,
        conv,
        convbc,
        dt,
        cum,
        states,
        dyy,
        decay,
        x_pre,
        small,
        chan,
        vec,
        pack,
        gather,
        padded(normed_t),
        padded(ng_t),
        cot,
        dgate,
        small_weight,
        sums,
        gain,
        row_scale,
        flat_tokens,
        both_weights,
        output_weight,
    )
    (
        g_in,
        g_w_out,
        g_coef,
        g_step,
        taps,
        taps_bc,
        bias,
        bias_bc,
        g_dt,
        g_log,
        g_skip,
        g_gain,
        g_norm,
        block_out,
        grad_input,
    ) = finish(
        width, inner, heads, state_part, streams, sums, gather, block_out, grad_input
    )
    return (
        block_out.reshape(seqs, block, col_count),
        grad_input.reshape(seqs, block, col_count),
        g_norm.reshape(-1),
        g_in,
        g_coef.transpose(2, 0, 1),
        g_step.T,
        taps,
        taps_bc,
        bias.reshape(-1),
        bias_bc,
        g_dt.reshape(-1),
        g_log.reshape(-1),
        g_skip.reshape(-1),
        g_gain.reshape(-1),
        g_w_out,
    )


def solution(mesh):
    placed = (
        P(None, "seq", None),
        P(),
        P(None, None, "head"),
        P(None, None, "head"),
        P(None, "head"),
        P(None, "head"),
        P(None, None, "head"),
        P("head"),
        P(None, "head"),
        P("head"),
        P("head"),
        P("head"),
        P("head"),
        P("head", None),
        P(None, "seq", None),
    )
    return jax.shard_map(
        body,
        mesh=mesh,
        in_specs=placed,
        out_specs=(
            P(None, "seq", "head"),
            P(None, "seq", "head"),
            P("head"),
            P(None, None, "head"),
            P(None, None, "head"),
            P(None, "head"),
            P(None, "head"),
            P(None, None, "head"),
            P("head"),
            P(None, "head"),
            P("head"),
            P("head"),
            P("head"),
            P("head"),
            P("head", None),
        ),
        check_vma=False,
    )
```
